32 devices in a mesh: seq: 8 (over z, y), tp: 4 (over x, core).
Axes of the slice: x: 2, y: 2, z: 4, core: 2. Of those that a mesh axis runs over, the one named last changes fastest.
Arguments:
- query_in: bfloat16 [1024, 8192], P('seq', 'tp'), may hold values from -6 to 6
- key_in: bfloat16 [1024, 8192], P('seq', 'tp'), may hold values from -6 to 6
- value_in: bfloat16 [1024, 8192], P('seq', 'tp'), may hold values from -6 to 6
- stream: bfloat16 [1024, 8192], P('seq', 'tp'), may hold values from -6 to 6
- short_filter: float32 [3, 3, 8192], P(None, None, 'tp'), may hold values from -3 to 3
- decay_rate: float32 [16, 8192], P(None, 'tp'), as said below
- residue: float32 [16, 8192], P(None, 'tp'), as said below
- norm_gain: float32 [8192], P('tp'), may hold values from 0.5 to 1.5
- cotangent: bfloat16 [1024, 8192], P('seq', 'tp'), may hold values from -6 to 6
Outputs:
- normed: bfloat16 [1024, 8192], P('seq', 'tp')
- stream_grad: bfloat16 [1024, 8192], P('seq', 'tp')
- query_grad: bfloat16 [1024, 8192], P('seq', 'tp')
- key_grad: bfloat16 [1024, 8192], P('seq', 'tp')
- value_grad: bfloat16 [1024, 8192], P('seq', 'tp')
The draws below stay inside these ranges and needn't reach their ends.
Inputs may be any that keep to these rules, and one draw needn't show every extreme that they name: The pole of mode m of channel c is exp(-decay_rate[m, c]); every rate is positive and at most 1/30. `residue`: residues are real numbers.
All inputs are finite; a program needn't handle non-finite values.
Results may differ from the reference program's by a relative error of at most 0.0012.
Values may be sent and summed in bfloat16 or wider, within the bound.
No kernel may reach another device: no remote copies, remote signals or barrier semaphores. Data moves between devices by JAX's collectives and lax.ppermute only.
A program may use at most 128 MiB of HBM per device.

```python
import math
import jax
import jax.numpy as jnp
from jax import lax

D = 8192
MODES = 16
SHORT = 3
TOKENS = 1024
N_TP = 4


def mode_rates(key):
    base = jax.random.fold_in(key, 17)
    chooser = jax.random.uniform(jax.random.fold_in(base, 1), (MODES, D), jnp.float32)
    placing = jax.random.uniform(jax.random.fold_in(base, 2), (MODES, D), jnp.float32)
    slow_share = 0.4
    middle_share = 0.3
    top_rate = 1.0 / 30.0
    slow_low = math.log(0.05 / TOKENS)
    slow_high = math.log(min(2.0 / TOKENS, top_rate))
    middle_low = slow_high
    middle_high = math.log(top_rate)
    fast_low = math.log(1.0 / 50.0)
    fast_high = math.log(top_rate)
    slow_rate = jnp.exp(slow_low + placing * (slow_high - slow_low))
    middle_rate = jnp.exp(middle_low + placing * (middle_high - middle_low))
    fast_rate = jnp.exp(fast_low + placing * (fast_high - fast_low))
    return jnp.where(chooser < slow_share, slow_rate, jnp.where(chooser < slow_share + middle_share, middle_rate, fast_rate))


def draw_decay_rate(key, part):
    return mode_rates(key)


def draw_residue(key, part):
    rates = mode_rates(key)
    normals = jax.random.normal(jax.random.fold_in(key, 29), (MODES, D), jnp.float32)
    return normals * jnp.sqrt(2.0 * rates / MODES)


def block_levels(stream_key, shape, pieces, smallest, high):
    gain, own = 1.0, jax.random.fold_in(stream_key, 6)
    for position, blocks in pieces:
        steps = jnp.exp(jax.random.uniform(jax.random.fold_in(own, position), (blocks,), jnp.float32, smallest / len(pieces), high / len(pieces)))
        gain = gain * jnp.repeat(steps, shape[position] // blocks).reshape([-1 if axis == position else 1 for axis in range(len(shape))])
    return gain


def scatter_about(key, extent, scale, limit, shards=(), held_as=jnp.bfloat16):
    factor_of = block_levels(key, extent, shards, -0.22, 0.18) if shards else 1.0
    drawn = jax.random.normal(key, extent, jnp.float32) * scale * factor_of
    return jnp.minimum(jnp.maximum(drawn, -limit), limit).astype(held_as)


def setup_inputs(seed: int = 0) -> dict:
    splits = jax.random.split(jax.random.key(seed), 10)
    return {
        "query_in": scatter_about(splits[0], (TOKENS, D), 1.0, 6.0, ((0, 8), (1, 4))),
        "key_in": scatter_about(splits[1], (TOKENS, D), 1.0, 6.0, ((0, 8), (1, 4))),
        "value_in": scatter_about(splits[2], (TOKENS, D), 1.0, 6.0, ((0, 8), (1, 4))),
        "stream": scatter_about(splits[3], (TOKENS, D), 1.0, 6.0, ((0, 8), (1, 4))),
        "short_filter": scatter_about(splits[4], (3, SHORT, D), 0.6, 3.0, ((2, 4),), jnp.float32),
        "decay_rate": draw_decay_rate(jax.random.fold_in(splits[9], 71), 0),
        "residue": draw_residue(jax.random.fold_in(splits[9], 71), 0),
        "norm_gain": jnp.clip(1.0 + 0.1 * jax.random.normal(splits[7], (D,), jnp.float32), 0.5, 1.5),
        "cotangent": scatter_about(splits[8], (TOKENS, D), 1.0, 6.0, ((0, 8), (1, 4))),
    }


highest = lax.Precision.HIGHEST
epsilon = 1e-05

def modal_parts(signal, decay_rate, residue):
    length, channels = signal.shape
    modes = decay_rate.shape[0]
    block_len = min(64, length)
    count_blocks = length // block_len
    offsets = jnp.arange(block_len, dtype=jnp.int32)
    positions = offsets.astype(jnp.float32)
    rising = jnp.exp(decay_rate[None] * positions[:, None, None])
    falling = jnp.exp(-decay_rate[None] * positions[:, None, None])
    lower = (offsets[:, None] >= offsets[None, :]).astype(jnp.float32)
    blocked = signal.reshape(count_blocks, block_len, channels)
    weighted = (blocked[:, :, None, :] * rising[None]).reshape(count_blocks, block_len, modes * channels)
    summed = jnp.einsum('ts,nsx->ntx', lower, weighted, precision=highest).reshape(count_blocks, block_len, modes, channels)
    states = summed * falling[None]
    inside = lax.optimization_barrier(jnp.sum(states * residue[None, None], axis=2))
    endings = states[:, block_len - 1]
    block_decay = jnp.exp(-decay_rate * block_len)

    def advance(state, ended):
        return (block_decay * state + ended, state)
    final, starting = lax.scan(advance, jnp.zeros(decay_rate.shape, jnp.float32), endings)
    return (inside, starting, final)

def modal_finish(inside, starting, arriving, decay_rate, residue):
    count_blocks, block_len, channels = inside.shape
    positions = jnp.arange(block_len, dtype=jnp.float32)
    block_starts = jnp.arange(count_blocks, dtype=jnp.float32) * block_len
    carried = starting + jnp.exp(-decay_rate[None] * block_starts[:, None, None]) * arriving[None]
    entering = residue[None] * jnp.exp(-decay_rate[None] * (positions + 1.0)[:, None, None])
    output = inside + lax.optimization_barrier(jnp.sum(entering[None] * carried[:, None], axis=2))
    return output.reshape(count_blocks * block_len, channels)

def short_mix(signal, taps):
    padded = jnp.pad(signal, ((2, 0), (0, 0)))
    return taps[0] * padded[2:] + taps[1] * padded[1:-1] + taps[2] * padded[:-2]

def group_mix(query_in, key_in, value_in, taps, decay_rate, residue):
    query_mix = short_mix(query_in, taps[0])
    key_mix = short_mix(key_in, taps[1])
    value_mix = short_mix(value_in, taps[2])
    product = key_mix * value_mix
    inside, starting, final = modal_parts(product, decay_rate, residue)
    conv = modal_finish(inside, starting, jnp.zeros(decay_rate.shape, jnp.float32), decay_rate, residue)
    return query_mix * conv

def reference(query_in, key_in, value_in, stream, short_filter, decay_rate, residue, norm_gain, cotangent):
    groups = N_TP
    channels = D // groups

    def split(array):
        return array.reshape(TOKENS, groups, channels).transpose(1, 0, 2)

    def merge(array):
        return array.transpose(1, 0, 2).reshape(TOKENS, D).astype(jnp.bfloat16)
    taps_grouped = short_filter.reshape(3, SHORT, groups, channels).transpose(2, 0, 1, 3)
    rates_grouped = decay_rate.reshape(MODES, groups, channels).transpose(1, 0, 2)
    residues_grouped = residue.reshape(MODES, groups, channels).transpose(1, 0, 2)
    query_split = split(query_in)
    key_split = split(key_in)
    value_split = split(value_in)

    def forward_group(items):
        query_part, key_part, value_part, stream_part, taps, rates, residues = items
        return stream_part.astype(jnp.float32) + group_mix(query_part.astype(jnp.float32), key_part.astype(jnp.float32), value_part.astype(jnp.float32), taps, rates, residues)
    mixed = lax.map(forward_group, (query_split, key_split, value_split, split(stream), taps_grouped, rates_grouped, residues_grouped))
    squares = lax.optimization_barrier(jnp.sum(mixed * mixed, axis=(0, 2)))
    inverse = lax.rsqrt(squares / D + epsilon)
    gains = norm_gain.reshape(groups, 1, channels)
    normed = mixed * inverse[None, :, None] * gains
    scaled = gains * split(cotangent).astype(jnp.float32)
    inner = lax.optimization_barrier(jnp.sum(scaled * mixed, axis=(0, 2)))
    dmixed = inverse[None, :, None] * scaled - mixed * (inverse ** 3 * inner / D)[None, :, None]

    def backward_group(items):
        query_part, key_part, value_part, taps, rates, residues, upstream = items

        def local_mix(first, second, third):
            return group_mix(first, second, third, taps, rates, residues)
        unused, pullback = jax.vjp(local_mix, query_part.astype(jnp.float32), key_part.astype(jnp.float32), value_part.astype(jnp.float32))
        return pullback(upstream)
    query_grad, key_grad, value_grad = lax.map(backward_group, (query_split, key_split, value_split, taps_grouped, rates_grouped, residues_grouped, dmixed))
    return (merge(normed), merge(dmixed), merge(query_grad), merge(key_grad), merge(value_grad))
```

```python
import functools

import jax
import jax.numpy as jnp
from jax import lax
from jax.experimental import pallas as pl
from jax.experimental.pallas import tpu as pltpu
from jax.sharding import PartitionSpec as P

f32 = jnp.float32
bf16 = jnp.bfloat16
epsilon = 1e-05
LANES = 128
SUB = 8
GROUP = LANES * SUB
FORWARD_EXTRA = 12
BACKWARD_EXTRA = 4


class Sizes:
    def __init__(self, length, channels, modes, devices):
        self.length, self.channels, self.modes, self.devices = length, channels, modes, devices
        self.tiles = channels // LANES
        self.halves = channels // GROUP
        self.direct = devices == SUB

    def chunk_row(self, r, h, extra):
        if r < self.modes:
            return h * self.modes + r
        return self.halves * self.modes + h * extra + r - self.modes

    def chunk_rows(self, extra):
        return self.halves * (self.modes + extra)

    def exchange_shape(self, extra):
        if self.direct:
            return (self.devices * self.chunk_rows(extra), LANES)
        return ((self.modes + extra) * self.tiles, LANES)

    def exchange_slice(self, r, h, extra):
        if self.direct:
            return pl.ds(self.chunk_row(r, h, extra), SUB, stride=self.chunk_rows(extra))
        return pl.ds(r * self.tiles + h * SUB, SUB)


def staged(s, block, offset, h):
    start = block * (s.tiles * SUB) + (h * SUB * SUB + offset)
    return pl.ds(start, SUB, stride=SUB)


def major(s, t, h):
    start = t * s.tiles + h * SUB
    if not isinstance(start, int):
        start = pl.multiple_of(start, SUB)
    return pl.ds(start, SUB)


def stage(s, x_ref, out_ref):
    def step(i, carry):
        rows = x_ref[pl.ds(pl.multiple_of(i * 16, 16), 16), :].astype(f32)
        base = i * (2 * s.tiles * SUB)
        for part in range(2):
            for j in range(s.tiles):
                start = pl.multiple_of(base + (part * s.tiles + j) * SUB, SUB)
                out_ref[pl.ds(start, SUB), :] = rows[
                    part * SUB : (part + 1) * SUB, j * LANES : (j + 1) * LANES
                ]
        return carry

    lax.fori_loop(0, s.length // 16, step, 0)


def unstage(s, in_ref, x_ref):
    def step(i, carry):
        base = i * (2 * s.tiles * SUB)
        for j in range(s.tiles):
            parts = [
                in_ref[pl.ds(pl.multiple_of(base + (part * s.tiles + j) * SUB, SUB), SUB), :]
                for part in range(2)
            ]
            x_ref[pl.ds(pl.multiple_of(i * 16, 16), 16), j * LANES : (j + 1) * LANES] = (
                jnp.concatenate(parts, axis=0).astype(bf16)
            )
        return carry

    lax.fori_loop(0, s.length // 16, step, 0)


def stage_modes(s, x_ref, out_ref, f):
    for g in range(s.modes // SUB):
        rows = f(x_ref[g * SUB : (g + 1) * SUB, :])
        for j in range(s.tiles):
            start = (g * s.tiles + j) * SUB
            out_ref[start : start + SUB, :] = rows[:, j * LANES : (j + 1) * LANES]


def mode_tiles(s, ref, h):
    return [ref[staged(s, m // SUB, m % SUB, h), :] for m in range(s.modes)]


def stage_taps(s, filter_ref, out_ref):
    for i in range(3):
        rows = filter_ref[i]
        for j in range(s.tiles):
            start = (i * s.tiles + j) * SUB
            out_ref[start : start + 3, :] = rows[:, j * LANES : (j + 1) * LANES]


def tap_tiles(s, ref, i, h):
    return [ref[staged(s, i, tap, h), :] for tap in range(3)]


def total(parts):
    while len(parts) > 1:
        parts = [
            parts[i] + parts[i + 1] if i + 1 < len(parts) else parts[i]
            for i in range(0, len(parts), 2)
        ]
    return parts[0]


def mix(taps, now, before, before2):
    return taps[0] * now + taps[1] * before + taps[2] * before2


def begin_kernel(
    s, q_ref, k_ref, v_ref, filter_ref, decay_ref, qmix_ref, prod_ref, pay_ref, qs, ks, vs, taps, poles
):
    stage(s, k_ref, ks)
    stage(s, v_ref, vs)
    stage(s, q_ref, qs)
    stage_modes(s, decay_ref, poles, lambda x: jnp.exp(-x))
    stage_taps(s, filter_ref, taps)
    last = s.length // SUB - 1
    blank = jnp.zeros((SUB, LANES), f32)
    for h in range(s.halves):
        p = mode_tiles(s, poles, h)
        taps_q, taps_k, taps_v = (tap_tiles(s, taps, i, h) for i in range(3))

        def position(block, offset, held, states, first):
            rows = staged(s, block, offset, h)
            q0, k0, v0 = qs[rows, :], ks[rows, :], vs[rows, :]
            q1, q2, k1, k2, v1, v2 = held
            product = mix(taps_k, k0, k1, k2) * mix(taps_v, v0, v1, v2)
            out = major(s, block * SUB + offset, h)
            qmix_ref[out, :] = mix(taps_q, q0, q1, q2)
            prod_ref[out, :] = product
            if not first:
                states = [p[m] * states[m] + product for m in range(s.modes)]
            return (q0, q1, k0, k1, v0, v1), states

        held, states = (blank,) * 6, [blank] * s.modes
        for offset in range(SUB):
            held, states = position(0, offset, held, states, offset < 2)

        def step(block, carry):
            held, states = carry
            for offset in range(SUB):
                held, states = position(block, offset, held, states, False)
            return held, states

        held, states = lax.fori_loop(1, s.length // SUB, step, (held, states))
        for m in range(s.modes):
            pay_ref[s.exchange_slice(m, h, FORWARD_EXTRA), :] = states[m]
        q1, q2, k1, k2, v1, v2 = held
        first = [staged(s, 0, offset, h) for offset in range(2)]
        extra = [
            ks[first[0], :], ks[first[1], :], k2, k1,
            vs[first[0], :], vs[first[1], :], v2, v1,
            q2, q1, blank, blank,
        ]
        for r, value in enumerate(extra):
            pay_ref[s.exchange_slice(s.modes + r, h, FORWARD_EXTRA), :] = value


def forward_middle(length, rates, taps, ends, extras):
    devices = len(ends)
    whole, step0, step1 = (jnp.exp(-float(length - i) * rates) for i in range(3))
    blank = jnp.zeros_like(extras[0][0])
    arriving = jnp.zeros_like(ends[0])
    result = []
    for i in range(devices):
        k0, k1, _, _, v0, v1 = extras[i][:6]
        if i:
            _, _, ka, kb, _, _, va, vb, qa, qb = extras[i - 1][:10]
        else:
            ka = kb = va = vb = qa = qb = blank
        if i + 1 < devices:
            kc, kd, _, _, vc, vd = extras[i + 1][:6]
        else:
            kc = kd = vc = vd = blank
        prod0 = mix(taps[1], k0, kb, ka) * mix(taps[2], v0, vb, va)
        prod1 = mix(taps[1], k1, k0, kb) * mix(taps[2], v1, v0, vb)
        result.append((arriving, [prod0, prod1, ka, kb, va, vb, qa, qb, kc, kd, vc, vd]))
        arriving = whole * arriving + (ends[i] + step0 * prod0 + step1 * prod1)
    return result


def backward_middle(length, rates, ends, extras):
    devices = len(ends)
    whole = jnp.exp(-float(length) * rates)
    blank = jnp.zeros_like(extras[0][0])
    arriving = jnp.zeros_like(ends[0])
    result = [None] * devices
    for i in reversed(range(devices)):
        result[i] = (arriving, extras[i + 1] if i + 1 < devices else [blank] * len(extras[0]))
        arriving = whole * arriving + ends[i]
    return result


def middle_kernel(s, extra, in_ref, decay_ref, filter_ref, out_ref):
    me = lax.axis_index("seq")
    rows = s.chunk_rows(extra)
    for h in range(s.halves):
        lanes = pl.ds(pl.multiple_of((me + h * SUB) * LANES, LANES), LANES)
        rates = decay_ref[:, lanes]
        ends, extras = [], []
        for i in range(s.devices):
            base = i * rows
            e = base + s.chunk_row(0, h, extra)
            ends.append(in_ref[e : e + s.modes, :])
            x = base + s.chunk_row(s.modes, h, extra)
            extras.append([in_ref[x + r : x + r + 1, :] for r in range(extra)])
        if extra == FORWARD_EXTRA:
            taps = [[filter_ref[i, tap : tap + 1, lanes] for tap in range(3)] for i in range(3)]
            result = forward_middle(s.length, rates, taps, ends, extras)
        else:
            result = backward_middle(s.length, rates, ends, extras)
        for i in range(s.devices):
            base = i * rows
            e = base + s.chunk_row(0, h, extra)
            out_ref[e : e + s.modes, :] = result[i][0]
            x = base + s.chunk_row(s.modes, h, extra)
            for r in range(extra):
                out_ref[x + r : x + r + 1, :] = result[i][1][r]


def exchange(s, pay, decay_rate, short_filter, extra):
    if s.direct:
        got = lax.all_to_all(pay, "seq", 0, 0, tiled=True)
        back = pl.pallas_call(
            functools.partial(middle_kernel, s, extra),
            out_shape=jax.ShapeDtypeStruct(pay.shape, f32),
        )(got, decay_rate, short_filter)
        return lax.all_to_all(back, "seq", 0, 0, tiled=True)
    rows = s.modes + extra
    width = s.channels // s.devices
    start = lax.axis_index("seq") * width
    rates = lax.dynamic_slice_in_dim(decay_rate, start, width, 1)
    part = lax.dynamic_slice_in_dim(short_filter, start, width, 2)
    pay = pay.reshape(rows, s.devices, width).transpose(1, 0, 2)
    got = lax.all_to_all(pay, "seq", 0, 0, tiled=True)
    ends = [got[i, : s.modes] for i in range(s.devices)]
    extras = [[got[i, s.modes + r][None] for r in range(extra)] for i in range(s.devices)]
    if extra == FORWARD_EXTRA:
        taps = [[part[i, tap][None] for tap in range(3)] for i in range(3)]
        result = forward_middle(s.length, rates, taps, ends, extras)
    else:
        result = backward_middle(s.length, rates, ends, extras)
    back = jnp.stack([jnp.concatenate([state] + list(more)) for state, more in result])
    back = lax.all_to_all(back, "seq", 0, 0, tiled=True)
    return back.transpose(1, 0, 2).reshape(rows * s.tiles, LANES)


def forward_kernel(
    s, qmix_in, prod_ref, stream_ref, cot_ref, back_ref, filter_ref, decay_ref, residue_ref, gain_ref,
    conv_ref, mixed_ref, scaled_ref, sums_ref,
    xs, gs, taps, poles, weights, squares, inners,
):
    stage(s, stream_ref, xs)
    stage(s, cot_ref, gs)
    stage_modes(s, decay_ref, poles, lambda x: jnp.exp(-x))
    stage_modes(s, residue_ref, weights, lambda x: x)
    stage_taps(s, filter_ref, taps)

    def back(r, h):
        return back_ref[s.exchange_slice(r, h, FORWARD_EXTRA), :]

    for h in range(s.halves):
        p = mode_tiles(s, poles, h)
        w = mode_tiles(s, weights, h)
        gain = gain_ref[h * SUB : (h + 1) * SUB, :]
        taps_q = tap_tiles(s, taps, 0, h)
        qa, qb = back(s.modes + 6, h), back(s.modes + 7, h)
        ahead = [taps_q[1] * qb + taps_q[2] * qa, taps_q[2] * qb]

        def position(block, offset, states, first):
            rows = staged(s, block, offset, h)
            t = block * SUB + offset
            out = major(s, t, h)
            qmix = qmix_in[out, :]
            if first:
                product = back(s.modes + offset, h)
                qmix = qmix + ahead[offset]
            else:
                product = prod_ref[out, :]
            states = [p[m] * states[m] + product for m in range(s.modes)]
            conv = total([w[m] * states[m] for m in range(s.modes)])
            mixed = xs[rows, :] + qmix * conv
            scaled = gain * gs[rows, :]
            conv_ref[out, :] = conv
            mixed_ref[out, :] = mixed
            scaled_ref[out, :] = scaled
            square, inner = mixed * mixed, scaled * mixed
            part = pl.ds(t * SUB if isinstance(t, int) else pl.multiple_of(t * SUB, SUB), SUB)
            if h:
                square, inner = square + squares[part, :], inner + inners[part, :]
            squares[part, :] = square
            inners[part, :] = inner
            return states

        states = [back(m, h) for m in range(s.modes)]
        for offset in range(SUB):
            states = position(0, offset, states, offset < 2)

        def step(block, states):
            for offset in range(SUB):
                states = position(block, offset, states, False)
            return states

        lax.fori_loop(1, s.length // SUB, step, states)
    for r, ref in enumerate((squares, inners)):
        parts = []
        for b in range(s.length // SUB):
            parts.append(
                total([ref[pl.ds(b * SUB * SUB + i, SUB, stride=SUB), :] for i in range(SUB)])
            )
        rows = jnp.concatenate(parts, axis=0)
        sums_ref[r : r + 1, :] = jnp.sum(rows.T, axis=0, keepdims=True)


def norm_kernel(
    s, width, sums_ref, conv_ref, mixed_ref, scaled_ref, qmix_in, back_ref, filter_ref, decay_ref, gain_ref,
    normed_ref, dstream_ref, dconv_ref, dq_ref, pay_ref,
    normed_s, dstream_s, taps, poles, inv_s, coef_s,
):
    stage_modes(s, decay_ref, poles, lambda x: jnp.exp(-x))
    stage_taps(s, filter_ref, taps)
    inverse = lax.rsqrt(sums_ref[0:1, :] / width + epsilon)
    coef = inverse * inverse * inverse * sums_ref[1:2, :] / width
    inv_s[...] = jnp.broadcast_to(inverse, (s.length, s.length)).T
    coef_s[...] = jnp.broadcast_to(coef, (s.length, s.length)).T
    blocks = s.length // SUB

    def back(r, h):
        return back_ref[s.exchange_slice(r, h, FORWARD_EXTRA), :]

    for h in range(s.halves):
        p = mode_tiles(s, poles, h)
        gain = gain_ref[h * SUB : (h + 1) * SUB, :]
        taps_q = tap_tiles(s, taps, 0, h)
        qa, qb = back(s.modes + 6, h), back(s.modes + 7, h)
        ahead = [taps_q[1] * qb + taps_q[2] * qa, taps_q[2] * qb]

        def position(block, offset, states, first):
            rows = staged(s, block, offset, h)
            t = block * SUB + offset
            out = major(s, t, h)
            inv = jnp.broadcast_to(inv_s[pl.ds(t, 1), :], (SUB, LANES))
            cf = jnp.broadcast_to(coef_s[pl.ds(t, 1), :], (SUB, LANES))
            mixed = mixed_ref[out, :]
            qmix = qmix_in[out, :]
            if first:
                qmix = qmix + ahead[offset]
            dmixed = inv * scaled_ref[out, :] - mixed * cf
            normed_s[rows, :] = mixed * inv * gain
            dstream_s[rows, :] = dmixed
            dq = dmixed * conv_ref[out, :]
            dconv = dmixed * qmix
            dq_ref[out, :] = dq
            dconv_ref[out, :] = dconv
            if first:
                pay_ref[s.exchange_slice(s.modes + 1 + offset, h, BACKWARD_EXTRA), :] = dq
                if offset == 0:
                    pay_ref[s.exchange_slice(s.modes, h, BACKWARD_EXTRA), :] = dconv
            return [p[m] * states[m] + dconv for m in range(s.modes)]

        def step(i, states):
            for offset in reversed(range(SUB)):
                states = position(blocks - 1 - i, offset, states, False)
            return states

        states = [jnp.zeros((SUB, LANES), f32)] * s.modes
        states = lax.fori_loop(0, blocks - 1, step, states)
        for offset in reversed(range(SUB)):
            states = position(0, offset, states, offset < 2)
        for m in range(s.modes):
            pay_ref[s.exchange_slice(m, h, BACKWARD_EXTRA), :] = states[m]
        pay_ref[s.exchange_slice(s.modes + 3, h, BACKWARD_EXTRA), :] = jnp.zeros((SUB, LANES), f32)
    unstage(s, normed_s, normed_ref)
    unstage(s, dstream_s, dstream_ref)


def backward_kernel(
    s, k_ref, v_ref, dconv_ref, dq_ref, ahead_ref, back_ref, filter_ref, decay_ref, residue_ref,
    qgrad_ref, kgrad_ref, vgrad_ref,
    ks, vs, kmix, vmix, dprod, taps, poles, weights,
):
    stage(s, k_ref, ks)
    stage(s, v_ref, vs)
    stage_modes(s, decay_ref, poles, lambda x: jnp.exp(-x))
    stage_modes(s, residue_ref, weights, lambda x: x)
    stage_taps(s, filter_ref, taps)
    blocks = s.length // SUB

    def near(r, h):
        return ahead_ref[s.exchange_slice(s.modes + r, h, FORWARD_EXTRA), :]

    def back(r, h):
        return back_ref[s.exchange_slice(r, h, BACKWARD_EXTRA), :]

    after = []
    for h in range(s.halves):
        taps_k, taps_v = (tap_tiles(s, taps, i, h) for i in (1, 2))

        def features(block, held):
            for offset in range(SUB):
                rows = staged(s, block, offset, h)
                k0, v0 = ks[rows, :], vs[rows, :]
                k1, k2, v1, v2 = held
                out = major(s, block * SUB + offset, h)
                kmix[out, :] = mix(taps_k, k0, k1, k2)
                vmix[out, :] = mix(taps_v, v0, v1, v2)
                held = (k0, k1, v0, v1)
            return held

        ka, kb, va, vb, _, _, kc, kd, vc, vd = (near(2 + r, h) for r in range(10))
        k1, k2, v1, v2 = lax.fori_loop(0, blocks, features, (kb, ka, vb, va))
        after.append(
            (
                mix(taps_k, kc, k1, k2), mix(taps_k, kd, kc, k1),
                mix(taps_v, vc, v1, v2), mix(taps_v, vd, vc, v1),
            )
        )
    for h in range(s.halves):
        p = mode_tiles(s, poles, h)
        w = mode_tiles(s, weights, h)

        def step(i, states):
            block = blocks - 1 - i
            for offset in reversed(range(SUB)):
                out = major(s, block * SUB + offset, h)
                dconv = dconv_ref[out, :]
                states = [p[m] * states[m] + dconv for m in range(s.modes)]
                dprod[out, :] = total([w[m] * states[m] for m in range(s.modes)])
            return states

        lax.fori_loop(0, blocks, step, [back(m, h) for m in range(s.modes)])
    for h in range(s.halves):
        taps_q, taps_k, taps_v = (tap_tiles(s, taps, i, h) for i in range(3))
        w = mode_tiles(s, weights, h)
        arriving = [back(m, h) for m in range(s.modes)]
        dconv0, dq0, dq1 = (back(s.modes + r, h) for r in range(3))
        dprod0 = total([w[m] * arriving[m] for m in range(s.modes)])
        p = mode_tiles(s, poles, h)
        dprod1 = total([w[m] * ((arriving[m] - dconv0) / p[m]) for m in range(s.modes)])
        kmix0, kmix1, vmix0, vmix1 = after[h]
        held = (dq0, dq1, dprod0 * vmix0, dprod1 * vmix1, dprod0 * kmix0, dprod1 * kmix1)

        def grads(i, held):
            block = blocks - 1 - i
            for offset in reversed(range(SUB)):
                out = major(s, block * SUB + offset, h)
                rows = staged(s, block, offset, h)
                q1, q2, k1, k2, v1, v2 = held
                d = dprod[out, :]
                q0, k0, v0 = dq_ref[out, :], d * vmix[out, :], d * kmix[out, :]
                ks[rows, :] = mix(taps_k, k0, k1, k2)
                vs[rows, :] = mix(taps_v, v0, v1, v2)
                dprod[out, :] = mix(taps_q, q0, q1, q2)
                held = (q0, q1, k0, k1, v0, v1)
            return held

        lax.fori_loop(0, blocks, grads, held)
    unstage(s, ks, kgrad_ref)
    unstage(s, vs, vgrad_ref)
    def restage(block, carry):
        for h in range(s.halves):
            for offset in range(SUB):
                ks[staged(s, block, offset, h), :] = dprod[major(s, block * SUB + offset, h), :]
        return carry

    lax.fori_loop(0, blocks, restage, 0)
    unstage(s, ks, qgrad_ref)


def body(
    query_in, key_in, value_in, stream, short_filter, decay_rate, residue, norm_gain, cotangent
):
    length, channels = query_in.shape
    modes = decay_rate.shape[0]
    s = Sizes(length, channels, modes, lax.axis_size("seq"))
    total_width = channels * lax.axis_size("tp")
    wide = jax.ShapeDtypeStruct((length * s.tiles, LANES), f32)
    narrow = jax.ShapeDtypeStruct((length, channels), bf16)
    wide_scratch = pltpu.VMEM((length * s.tiles, LANES), f32)
    tap_scratch = pltpu.VMEM((3 * s.tiles * SUB, LANES), f32)
    mode_scratch = pltpu.VMEM((modes * s.tiles, LANES), f32)
    sum_scratch = pltpu.VMEM((length * SUB, LANES), f32)
    square_scratch = pltpu.VMEM((length, length), f32)
    params = pltpu.CompilerParams(vmem_limit_bytes=40 * 1024 * 1024)
    gain = norm_gain.reshape(s.tiles, LANES)

    def call(kernel, out_shape, scratch_shapes, *operands):
        return pl.pallas_call(
            functools.partial(kernel, s),
            out_shape=out_shape,
            scratch_shapes=scratch_shapes,
            compiler_params=params,
        )(*operands)

    qmix, product, pay = call(
        begin_kernel,
        (wide, wide, jax.ShapeDtypeStruct(s.exchange_shape(FORWARD_EXTRA), f32)),
        [wide_scratch] * 3 + [tap_scratch, mode_scratch],
        query_in, key_in, value_in, short_filter, decay_rate,
    )
    back = exchange(s, pay, decay_rate, short_filter, FORWARD_EXTRA)
    conv, mixed, scaled, sums = call(
        forward_kernel,
        (wide, wide, wide, jax.ShapeDtypeStruct((2, length), f32)),
        [wide_scratch] * 2 + [tap_scratch, mode_scratch, mode_scratch, sum_scratch, sum_scratch],
        qmix, product, stream, cotangent, back, short_filter, decay_rate, residue, gain,
    )
    sums = lax.psum(sums, "tp")
    normed, dstream, dconv, dq, pay_back = call(
        lambda s, *refs: norm_kernel(s, total_width, *refs),
        (narrow, narrow, wide, wide, jax.ShapeDtypeStruct(s.exchange_shape(BACKWARD_EXTRA), f32)),
        [wide_scratch] * 2 + [tap_scratch, mode_scratch, square_scratch, square_scratch],
        sums, conv, mixed, scaled, qmix, back, short_filter, decay_rate, gain,
    )
    back_back = exchange(s, pay_back, decay_rate, short_filter, BACKWARD_EXTRA)
    query_grad, key_grad, value_grad = call(
        backward_kernel,
        (narrow, narrow, narrow),
        [wide_scratch] * 5 + [tap_scratch, mode_scratch, mode_scratch],
        key_in, value_in, dconv, dq, back, back_back, short_filter, decay_rate, residue,
    )
    return (normed, dstream, query_grad, key_grad, value_grad)


def solution(mesh):
    cut = P("seq", "tp")
    return jax.shard_map(
        body,
        mesh=mesh,
        in_specs=(cut, cut, cut, cut, P(None, None, "tp"), P(None, "tp"), P(None, "tp"), P("tp"), cut),
        out_specs=(cut,) * 5,
        check_vma=False,
    )
```

```python
import functools

import jax
import jax.numpy as jnp
from jax import lax
from jax.experimental import pallas as pl
from jax.experimental.pallas import tpu as pltpu
from jax.sharding import PartitionSpec as P

f32 = jnp.float32
bf16 = jnp.bfloat16
epsilon = 1e-05
LANES = 128
SUB = 8
GROUP = LANES * SUB
FORWARD_EXTRA = 12
BACKWARD_EXTRA = 4
GRANT = 20 * 1024 * 1024


class Sizes:
    def __init__(self, length, channels, modes, devices):
        self.length, self.channels, self.modes, self.devices = length, channels, modes, devices
        self.tiles = channels // LANES
        self.halves = channels // GROUP
        self.direct = devices == SUB

    def chunk_row(self, r, h, extra):
        if r < self.modes:
            return h * self.modes + r
        return self.halves * self.modes + h * extra + r - self.modes

    def chunk_rows(self, extra):
        return self.halves * (self.modes + extra)

    def exchange_shape(self, extra):
        if self.direct:
            return (self.devices * self.chunk_rows(extra), LANES)
        return ((self.modes + extra) * self.tiles, LANES)

    def exchange_slice(self, r, h, extra):
        if self.direct:
            return pl.ds(self.chunk_row(r, h, extra), SUB, stride=self.chunk_rows(extra))
        return pl.ds(r * self.tiles + h * SUB, SUB)


def staged(s, block, offset, h):
    start = block * (s.tiles * SUB) + (h * SUB * SUB + offset)
    return pl.ds(start, SUB, stride=SUB)


def major(s, t, h):
    start = t * s.tiles + h * SUB
    if not isinstance(start, int):
        start = pl.multiple_of(start, SUB)
    return pl.ds(start, SUB)


def staged_before(s, block, offset, h):
    if offset < 2:
        return staged(s, block - 1, offset + SUB - 2, h)
    return staged(s, block, offset - 2, h)


def stage_rows(s, rows, out_ref, base, tiles):
    for part in range(2):
        for i, j in enumerate(tiles):
            start = base + (part * s.tiles + j) * SUB
            if not isinstance(start, int):
                start = pl.multiple_of(start, SUB)
            out_ref[pl.ds(start, SUB), :] = rows[
                part * SUB : (part + 1) * SUB, i * LANES : (i + 1) * LANES
            ]


def stage(s, x_ref, out_ref, h):
    def step(i, carry):
        rows = x_ref[pl.ds(pl.multiple_of(i * 16, 16), 16), h * GROUP : (h + 1) * GROUP]
        base = i * (2 * s.tiles * SUB)
        stage_rows(s, rows.astype(f32), out_ref, base, range(h * SUB, (h + 1) * SUB))
        return carry

    lax.fori_loop(0, s.length // 16, step, 0)


def unstage(s, in_ref, x_ref, h, length):
    def step(i, carry):
        base = i * (2 * s.tiles * SUB)
        for j in range(h * SUB, (h + 1) * SUB):
            parts = [
                in_ref[pl.ds(pl.multiple_of(base + (part * s.tiles + j) * SUB, SUB), SUB), :]
                for part in range(2)
            ]
            x_ref[pl.ds(pl.multiple_of(i * 16, 16), 16), j * LANES : (j + 1) * LANES] = (
                jnp.concatenate(parts, axis=0).astype(bf16)
            )
        return carry

    lax.fori_loop(0, length // 16, step, 0)


def stage_modes(s, x_ref, out_ref, f):
    for g in range(s.modes // SUB):
        rows = f(x_ref[g * SUB : (g + 1) * SUB, :])
        for j in range(s.tiles):
            start = (g * s.tiles + j) * SUB
            out_ref[start : start + SUB, :] = rows[:, j * LANES : (j + 1) * LANES]


def mode_tiles(s, ref, h):
    return [ref[staged(s, m // SUB, m % SUB, h), :] for m in range(s.modes)]


def stage_taps(s, filter_ref, out_ref):
    for i in range(3):
        rows = filter_ref[i]
        for j in range(s.tiles):
            start = (i * s.tiles + j) * SUB
            out_ref[start : start + 3, :] = rows[:, j * LANES : (j + 1) * LANES]


def tap_tiles(s, ref, i, h):
    return [ref[staged(s, i, tap, h), :] for tap in range(3)]


def total(parts):
    while len(parts) > 1:
        parts = [
            parts[i] + parts[i + 1] if i + 1 < len(parts) else parts[i]
            for i in range(0, len(parts), 2)
        ]
    return parts[0]


def mix(taps, now, before, before2):
    return taps[0] * now + taps[1] * before + taps[2] * before2


def begin_kernel(
    s, q_hbm, k_hbm, v_hbm, filter_hbm, decay_hbm, prod_ref, pay_ref,
    kb, vb, qb, fb, db, ks, vs, qs, taps, poles, sems,
):
    half = GROUP
    copies = [(decay_hbm, db), (filter_hbm, fb)]
    for h in range(s.halves):
        cut = pl.ds(h * half, half)
        copies += [(k_hbm.at[:, cut], kb.at[:, cut]), (v_hbm.at[:, cut], vb.at[:, cut])]
    copies.append((q_hbm.at[pl.ds(s.length - 16, 16), :], qb))
    copies = [pltpu.make_async_copy(a, b, sems.at[i]) for i, (a, b) in enumerate(copies)]
    for copy in copies:
        copy.start()
    copies[0].wait()
    stage_modes(s, db, poles, lambda x: jnp.exp(-x))
    copies[1].wait()
    stage_taps(s, fb, taps)
    blank = jnp.zeros((SUB, LANES), f32)
    for h in range(s.halves):
        copies[2 + 2 * h].wait()
        stage(s, kb, ks, h)
        copies[3 + 2 * h].wait()
        stage(s, vb, vs, h)
        p = mode_tiles(s, poles, h)
        taps_k, taps_v = (tap_tiles(s, taps, i, h) for i in (1, 2))

        def position(block, offset, held, states, first):
            rows = staged(s, block, offset, h)
            k0, v0 = ks[rows, :], vs[rows, :]
            k1, k2, v1, v2 = held
            product = mix(taps_k, k0, k1, k2) * mix(taps_v, v0, v1, v2)
            prod_ref[major(s, block * SUB + offset, h), :] = product
            if not first:
                states = [p[m] * states[m] + product for m in range(s.modes)]
            return (k0, k1, v0, v1), states

        held, states = (blank,) * 4, [blank] * s.modes
        for offset in range(SUB):
            held, states = position(0, offset, held, states, offset < 2)

        def step(block, carry):
            held, states = carry
            for offset in range(SUB):
                held, states = position(block, offset, held, states, False)
            return held, states

        held, states = lax.fori_loop(1, s.length // SUB, step, (held, states))
        for m in range(s.modes):
            pay_ref[s.exchange_slice(m, h, FORWARD_EXTRA), :] = states[m]
        if h == 0:
            copies[-1].wait()
            stage_rows(s, qb[...].astype(f32), qs, 0, range(s.tiles))
        k1, k2, v1, v2 = held
        first = [staged(s, 0, offset, h) for offset in range(2)]
        last = [staged(s, 1, offset, h) for offset in (6, 7)]
        extra = [
            ks[first[0], :], ks[first[1], :], k2, k1,
            vs[first[0], :], vs[first[1], :], v2, v1,
            qs[last[0], :], qs[last[1], :], blank, blank,
        ]
        for r, value in enumerate(extra):
            pay_ref[s.exchange_slice(s.modes + r, h, FORWARD_EXTRA), :] = value


def forward_middle(length, rates, taps, ends, extras):
    devices = len(ends)
    whole, step0, step1 = (jnp.exp(-float(length - i) * rates) for i in range(3))
    blank = jnp.zeros_like(extras[0][0])
    arriving = jnp.zeros_like(ends[0])
    result = []
    for i in range(devices):
        k0, k1, _, _, v0, v1 = extras[i][:6]
        if i:
            _, _, ka, kb, _, _, va, vb, qa, qb = extras[i - 1][:10]
        else:
            ka = kb = va = vb = qa = qb = blank
        if i + 1 < devices:
            kc, kd, _, _, vc, vd = extras[i + 1][:6]
        else:
            kc = kd = vc = vd = blank
        prod0 = mix(taps[1], k0, kb, ka) * mix(taps[2], v0, vb, va)
        prod1 = mix(taps[1], k1, k0, kb) * mix(taps[2], v1, v0, vb)
        result.append((arriving, [prod0, prod1, ka, kb, va, vb, qa, qb, kc, kd, vc, vd]))
        arriving = whole * arriving + (ends[i] + step0 * prod0 + step1 * prod1)
    return result


def backward_middle(length, rates, ends, extras):
    devices = len(ends)
    whole = jnp.exp(-float(length) * rates)
    blank = jnp.zeros_like(extras[0][0])
    arriving = jnp.zeros_like(ends[0])
    result = [None] * devices
    for i in reversed(range(devices)):
        result[i] = (arriving, extras[i + 1] if i + 1 < devices else [blank] * len(extras[0]))
        arriving = whole * arriving + ends[i]
    return result


def middle_kernel(s, extra, in_ref, decay_ref, filter_ref, out_ref):
    me = lax.axis_index("seq")
    rows = s.chunk_rows(extra)
    for h in range(s.halves):
        lanes = pl.ds(pl.multiple_of((me + h * SUB) * LANES, LANES), LANES)
        rates = decay_ref[:, lanes]
        ends, extras = [], []
        for i in range(s.devices):
            base = i * rows
            e = base + s.chunk_row(0, h, extra)
            ends.append(in_ref[e : e + s.modes, :])
            x = base + s.chunk_row(s.modes, h, extra)
            extras.append([in_ref[x + r : x + r + 1, :] for r in range(extra)])
        if extra == FORWARD_EXTRA:
            taps = [[filter_ref[i, tap : tap + 1, lanes] for tap in range(3)] for i in range(3)]
            result = forward_middle(s.length, rates, taps, ends, extras)
        else:
            result = backward_middle(s.length, rates, ends, extras)
        for i in range(s.devices):
            base = i * rows
            e = base + s.chunk_row(0, h, extra)
            out_ref[e : e + s.modes, :] = result[i][0]
            x = base + s.chunk_row(s.modes, h, extra)
            for r in range(extra):
                out_ref[x + r : x + r + 1, :] = result[i][1][r]


def exchange(s, pay, decay_rate, short_filter, extra):
    if s.direct:
        got = lax.all_to_all(pay, "seq", 0, 0, tiled=True)
        back = pl.pallas_call(
            functools.partial(middle_kernel, s, extra),
            out_shape=jax.ShapeDtypeStruct(pay.shape, f32),
            compiler_params=pltpu.CompilerParams(vmem_limit_bytes=GRANT),
        )(got, decay_rate, short_filter)
        return lax.all_to_all(back, "seq", 0, 0, tiled=True)
    rows = s.modes + extra
    width = s.channels // s.devices
    start = lax.axis_index("seq") * width
    rates = lax.dynamic_slice_in_dim(decay_rate, start, width, 1)
    part = lax.dynamic_slice_in_dim(short_filter, start, width, 2)
    pay = pay.reshape(rows, s.devices, width).transpose(1, 0, 2)
    got = lax.all_to_all(pay, "seq", 0, 0, tiled=True)
    ends = [got[i, : s.modes] for i in range(s.devices)]
    extras = [[got[i, s.modes + r][None] for r in range(extra)] for i in range(s.devices)]
    if extra == FORWARD_EXTRA:
        taps = [[part[i, tap][None] for tap in range(3)] for i in range(3)]
        result = forward_middle(s.length, rates, taps, ends, extras)
    else:
        result = backward_middle(s.length, rates, ends, extras)
    back = jnp.stack([jnp.concatenate([state] + list(more)) for state, more in result])
    back = lax.all_to_all(back, "seq", 0, 0, tiled=True)
    return back.transpose(1, 0, 2).reshape(rows * s.tiles, LANES)


def forward_kernel(
    s, prod_ref, q_ref, stream_ref, cot_ref, back_ref, filter_ref, decay_ref, residue_ref, gain_ref,
    conv_ref, sums_ref,
    qs, xs, gs, taps, poles, weights, squares, inners,
):
    stage_modes(s, decay_ref, poles, lambda x: jnp.exp(-x))
    stage_modes(s, residue_ref, weights, lambda x: x)
    stage_taps(s, filter_ref, taps)

    def back(r, h):
        return back_ref[s.exchange_slice(r, h, FORWARD_EXTRA), :]

    for h in range(s.halves):
        p = mode_tiles(s, poles, h)
        w = mode_tiles(s, weights, h)

        def position(block, offset, states, first):
            out = major(s, block * SUB + offset, h)
            product = back(s.modes + offset, h) if first else prod_ref[out, :]
            states = [p[m] * states[m] + product for m in range(s.modes)]
            conv_ref[out, :] = total([w[m] * states[m] for m in range(s.modes)])
            return states

        states = [back(m, h) for m in range(s.modes)]
        for offset in range(SUB):
            states = position(0, offset, states, offset < 2)

        def step(block, states):
            for offset in range(SUB):
                states = position(block, offset, states, False)
            return states

        lax.fori_loop(1, s.length // SUB, step, states)

        stage(s, q_ref, qs, h)
        stage(s, stream_ref, xs, h)
        stage(s, cot_ref, gs, h)
        gain = gain_ref[h * SUB : (h + 1) * SUB, :]
        taps_q = tap_tiles(s, taps, 0, h)

        def sums(block, held):
            q1, q2 = held
            for offset in range(SUB):
                rows = staged(s, block, offset, h)
                t = block * SUB + offset
                q0 = qs[rows, :]
                mixed = xs[rows, :] + mix(taps_q, q0, q1, q2) * conv_ref[major(s, t, h), :]
                square, inner = mixed * mixed, gain * gs[rows, :] * mixed
                part = pl.ds(pl.multiple_of(t * SUB, SUB), SUB)
                if h:
                    square, inner = square + squares[part, :], inner + inners[part, :]
                squares[part, :] = square
                inners[part, :] = inner
                q1, q2 = q0, q1
            return q1, q2

        before = (back(s.modes + 7, h), back(s.modes + 6, h))
        lax.fori_loop(0, s.length // SUB, sums, before)
    for r, ref in enumerate((squares, inners)):
        parts = []
        for b in range(s.length // SUB):
            parts.append(
                total([ref[pl.ds(b * SUB * SUB + i, SUB, stride=SUB), :] for i in range(SUB)])
            )
        rows = jnp.concatenate(parts, axis=0)
        sums_ref[r : r + 1, :] = jnp.sum(rows.T, axis=0, keepdims=True)


def norm_kernel(
    s, width, sums_ref, conv_ref, q_ref, stream_ref, cot_ref, back_ref, filter_ref, decay_ref, gain_ref,
    normed_hbm, dstream_hbm, qgrad_hbm, dconv_ref, tail_ref, pay_ref,
    qs, xs, gs, ns, ds, normed_b, dstream_b, qgrad_b, taps, poles, inv_s, coef_s, sems,
):
    inverse = lax.rsqrt(sums_ref[0:1, :] / width + epsilon)
    coef = inverse * inverse * inverse * sums_ref[1:2, :] / width
    inv_s[...] = jnp.broadcast_to(inverse, (LANES, s.length)).T
    coef_s[...] = jnp.broadcast_to(coef, (LANES, s.length)).T
    stage_modes(s, decay_ref, poles, lambda x: jnp.exp(-x))
    stage_taps(s, filter_ref, taps)
    blocks = s.length // SUB
    blank = jnp.zeros((SUB, LANES), f32)
    copies = []

    def back(r, h):
        return back_ref[s.exchange_slice(r, h, FORWARD_EXTRA), :]

    for h in range(s.halves):
        stage(s, q_ref, qs, h)
        stage(s, stream_ref, xs, h)
        stage(s, cot_ref, gs, h)
        gain = gain_ref[h * SUB : (h + 1) * SUB, :]
        taps_q = tap_tiles(s, taps, 0, h)

        def position(block, offset, held, first):
            q1, q2, dq1, dq2 = held
            rows = staged(s, block, offset, h)
            t = block * SUB + offset
            out = major(s, t, h)
            inv = jnp.broadcast_to(inv_s[pl.ds(t, 1), :], (SUB, LANES))
            cf = jnp.broadcast_to(coef_s[pl.ds(t, 1), :], (SUB, LANES))
            q0 = qs[rows, :]
            qmix = mix(taps_q, q0, q1, q2)
            conv = conv_ref[out, :]
            mixed = xs[rows, :] + qmix * conv
            dmixed = inv * (gain * gs[rows, :]) - mixed * cf
            ns[rows, :] = mixed * inv * gain
            ds[rows, :] = dmixed
            dq0 = dmixed * conv
            dconv = dmixed * qmix
            dconv_ref[out, :] = dconv
            if first:
                pay_ref[s.exchange_slice(s.modes + 1 + offset, h, BACKWARD_EXTRA), :] = dq0
                if offset == 0:
                    pay_ref[s.exchange_slice(s.modes, h, BACKWARD_EXTRA), :] = dconv
            else:
                qs[staged_before(s, block, offset, h), :] = mix(taps_q, dq2, dq1, dq0)
            return q0, q1, dq0, dq1

        held = (back(s.modes + 7, h), back(s.modes + 6, h), blank, blank)
        for offset in range(SUB):
            held = position(0, offset, held, offset < 2)

        def step(block, held):
            for offset in range(SUB):
                held = position(block, offset, held, False)
            return held

        _, _, dq1, dq2 = lax.fori_loop(1, blocks, step, held)
        qs[staged(s, blocks - 1, 6, h), :] = taps_q[0] * dq2 + taps_q[1] * dq1
        qs[staged(s, blocks - 1, 7, h), :] = taps_q[0] * dq1
        pieces = [
            (ns, normed_b, normed_hbm, s.length),
            (ds, dstream_b, dstream_hbm, s.length),
            (qs, qgrad_b, qgrad_hbm, s.length - 16),
        ]
        for i, (from_ref, block_ref, to_hbm, rows) in enumerate(pieces):
            unstage(s, from_ref, block_ref, h, rows)
            cut = (pl.ds(0, rows), pl.ds(h * GROUP, GROUP))
            copy = pltpu.make_async_copy(block_ref.at[cut], to_hbm.at[cut], sems.at[3 * h + i])
            copy.start()
            copies.append(copy)
    start = (blocks - 2) * s.tiles * SUB
    tail_ref[...] = qs[start : start + 2 * s.tiles * SUB, :]
    for h in range(s.halves):
        p = mode_tiles(s, poles, h)

        def ends(i, states):
            for offset in reversed(range(SUB)):
                dconv = dconv_ref[major(s, (blocks - 1 - i) * SUB + offset, h), :]
                states = [p[m] * states[m] + dconv for m in range(s.modes)]
            return states

        states = lax.fori_loop(0, blocks, ends, [blank] * s.modes)
        for m in range(s.modes):
            pay_ref[s.exchange_slice(m, h, BACKWARD_EXTRA), :] = states[m]
        pay_ref[s.exchange_slice(s.modes + 3, h, BACKWARD_EXTRA), :] = blank
    for copy in copies:
        copy.wait()


def backward_kernel(
    s, k_ref, v_ref, dconv_ref, tail_ref, ahead_ref, back_ref, filter_ref, decay_ref, residue_ref, qgrad_in,
    qgrad_hbm, kgrad_hbm, vgrad_hbm,
    ks, vs, dprod, qs, kgrad_b, vgrad_b, qgrad_b, taps, poles, weights, sems,
):
    del qgrad_in
    stage_modes(s, decay_ref, poles, lambda x: jnp.exp(-x))
    stage_modes(s, residue_ref, weights, lambda x: x)
    stage_taps(s, filter_ref, taps)
    blocks = s.length // SUB
    copies = []

    def near(r, h):
        return ahead_ref[s.exchange_slice(s.modes + r, h, FORWARD_EXTRA), :]

    def back(r, h):
        return back_ref[s.exchange_slice(r, h, BACKWARD_EXTRA), :]

    qs[...] = tail_ref[...]
    for h in range(s.halves):
        taps_q = tap_tiles(s, taps, 0, h)
        dq0, dq1 = back(s.modes + 1, h), back(s.modes + 2, h)
        rows = [staged(s, 1, offset, h) for offset in (6, 7)]
        qs[rows[0], :] = qs[rows[0], :] + taps_q[2] * dq0
        qs[rows[1], :] = qs[rows[1], :] + (taps_q[1] * dq0 + taps_q[2] * dq1)
        unstage(s, qs, qgrad_b, h, 16)
    copy = pltpu.make_async_copy(qgrad_b, qgrad_hbm.at[pl.ds(s.length - 16, 16), :], sems.at[0])
    copy.start()
    copies.append(copy)
    for h in range(s.halves):
        p = mode_tiles(s, poles, h)
        w = mode_tiles(s, weights, h)

        def step(i, states):
            block = blocks - 1 - i
            for offset in reversed(range(SUB)):
                out = major(s, block * SUB + offset, h)
                dconv = dconv_ref[out, :]
                states = [p[m] * states[m] + dconv for m in range(s.modes)]
                dprod[out, :] = total([w[m] * states[m] for m in range(s.modes)])
            return states

        arriving = [back(m, h) for m in range(s.modes)]
        lax.fori_loop(0, blocks, step, arriving)

        stage(s, k_ref, ks, h)
        stage(s, v_ref, vs, h)
        taps_k, taps_v = (tap_tiles(s, taps, i, h) for i in (1, 2))

        def advance(held, k0, v0, d):
            k1, k2, v1, v2, dk1, dk2, dv1, dv2 = held
            dk0 = d * mix(taps_v, v0, v1, v2)
            dv0 = d * mix(taps_k, k0, k1, k2)
            grads = mix(taps_k, dk2, dk1, dk0), mix(taps_v, dv2, dv1, dv0)
            return (k0, k1, v0, v1, dk0, dk1, dv0, dv1), grads

        def position(block, offset, held, first):
            rows = staged(s, block, offset, h)
            d = dprod[major(s, block * SUB + offset, h), :]
            held, grads = advance(held, ks[rows, :], vs[rows, :], d)
            if not first:
                out = staged_before(s, block, offset, h)
                ks[out, :], vs[out, :] = grads
            return held

        ka, kb, va, vb, _, _, kc, kd, vc, vd = (near(2 + r, h) for r in range(10))
        blank = jnp.zeros((SUB, LANES), f32)
        held = (kb, ka, vb, va, blank, blank, blank, blank)
        for offset in range(SUB):
            held = position(0, offset, held, offset < 2)

        def features(block, held):
            for offset in range(SUB):
                held = position(block, offset, held, False)
            return held

        held = lax.fori_loop(1, blocks, features, held)
        arriving = [back(m, h) for m in range(s.modes)]
        dconv0 = back(s.modes, h)
        d0 = total([w[m] * arriving[m] for m in range(s.modes)])
        d1 = total([w[m] * ((arriving[m] - dconv0) / p[m]) for m in range(s.modes)])
        for offset, k0, v0, d in ((6, kc, vc, d0), (7, kd, vd, d1)):
            held, grads = advance(held, k0, v0, d)
            out = staged(s, blocks - 1, offset, h)
            ks[out, :], vs[out, :] = grads
        pieces = [(ks, kgrad_b, kgrad_hbm), (vs, vgrad_b, vgrad_hbm)]
        for i, (from_ref, block_ref, to_hbm) in enumerate(pieces):
            unstage(s, from_ref, block_ref, h, s.length)
            cut = (pl.ds(0, s.length), pl.ds(h * GROUP, GROUP))
            copy = pltpu.make_async_copy(block_ref.at[cut], to_hbm.at[cut], sems.at[1 + 2 * h + i])
            copy.start()
            copies.append(copy)
    for copy in copies:
        copy.wait()


def body(
    query_in, key_in, value_in, stream, short_filter, decay_rate, residue, norm_gain, cotangent
):
    length, channels = query_in.shape
    modes = decay_rate.shape[0]
    s = Sizes(length, channels, modes, lax.axis_size("seq"))
    total_width = channels * lax.axis_size("tp")
    wide = jax.ShapeDtypeStruct((length * s.tiles, LANES), f32)
    narrow = jax.ShapeDtypeStruct((length, channels), bf16)
    rows = 16 * s.tiles
    wide_s = pltpu.VMEM(wide.shape, f32)
    narrow_s = pltpu.VMEM(narrow.shape, bf16)
    last_s = pltpu.VMEM((16, channels), bf16)
    tail_s = pltpu.VMEM((rows, LANES), f32)
    taps_s = pltpu.VMEM((3 * s.tiles * SUB, LANES), f32)
    mode_s = pltpu.VMEM((modes * s.tiles, LANES), f32)
    sum_s = pltpu.VMEM((length * SUB, LANES), f32)
    square_s = pltpu.VMEM((length, LANES), f32)
    gain = norm_gain.reshape(s.tiles, LANES)
    there = pl.BlockSpec(memory_space=pltpu.HBM)
    here = pl.BlockSpec(memory_space=pltpu.VMEM)

    def call(kernel, ins, outs, out_shape, scratch_shapes, operands, aliases={}):
        return pl.pallas_call(
            functools.partial(kernel, s),
            in_specs=[there if c == "h" else here for c in ins],
            out_specs=[there if c == "h" else here for c in outs],
            out_shape=out_shape,
            scratch_shapes=scratch_shapes,
            input_output_aliases=aliases,
            compiler_params=pltpu.CompilerParams(vmem_limit_bytes=GRANT),
        )(*operands)

    def pay_shape(extra):
        return jax.ShapeDtypeStruct(s.exchange_shape(extra), f32)

    product, pay = call(
        begin_kernel, "hhhhh", "vv",
        (wide, pay_shape(FORWARD_EXTRA)),
        [narrow_s, narrow_s, last_s, pltpu.VMEM(short_filter.shape, f32), pltpu.VMEM(decay_rate.shape, f32)]
        + [wide_s, wide_s, tail_s, taps_s, mode_s, pltpu.SemaphoreType.DMA((3 + 2 * s.halves,))],
        (query_in, key_in, value_in, short_filter, decay_rate),
    )
    back = exchange(s, pay, decay_rate, short_filter, FORWARD_EXTRA)
    conv, sums = call(
        forward_kernel, "v" * 9, "vv",
        (wide, jax.ShapeDtypeStruct((2, length), f32)),
        [wide_s] * 3 + [taps_s, mode_s, mode_s, sum_s, sum_s],
        (product, query_in, stream, cotangent, back, short_filter, decay_rate, residue, gain),
    )
    sums = lax.psum(sums, "tp")
    normed, dstream, query_grad, dconv, tail, pay_back = call(
        lambda s, *refs: norm_kernel(s, total_width, *refs), "v" * 9, "hhhvvv",
        (narrow, narrow, narrow, wide, jax.ShapeDtypeStruct((rows, LANES), f32), pay_shape(BACKWARD_EXTRA)),
        [wide_s] * 5 + [narrow_s] * 3
        + [taps_s, mode_s, square_s, square_s, pltpu.SemaphoreType.DMA((3 * s.halves,))],
        (sums, conv, query_in, stream, cotangent, back, short_filter, decay_rate, gain),
    )
    back_back = exchange(s, pay_back, decay_rate, short_filter, BACKWARD_EXTRA)
    query_grad, key_grad, value_grad = call(
        backward_kernel, "v" * 9 + "h", "hhh",
        (narrow, narrow, narrow),
        [wide_s] * 3 + [tail_s] + [narrow_s] * 2 + [last_s, taps_s, mode_s, mode_s]
        + [pltpu.SemaphoreType.DMA((1 + 2 * s.halves,))],
        (key_in, value_in, dconv, tail, back, back_back, short_filter, decay_rate, residue, query_grad),
        {9: 0},
    )
    return (normed, dstream, query_grad, key_grad, value_grad)


def solution(mesh):
    cut = P("seq", "tp")
    return jax.shard_map(
        body,
        mesh=mesh,
        in_specs=(cut, cut, cut, cut, P(None, None, "tp"), P(None, "tp"), P(None, "tp"), P("tp"), cut),
        out_specs=(cut,) * 5,
        check_vma=False,
    )
```

```python
import functools

import jax
import jax.numpy as jnp
from jax import lax
from jax.experimental import pallas as pl
from jax.experimental.pallas import tpu as pltpu
from jax.sharding import PartitionSpec as P

f32 = jnp.float32
bf16 = jnp.bfloat16
epsilon = 1e-05
LANES = 128
SUB = 8
GROUP = LANES * SUB
FORWARD_EXTRA = 12
BACKWARD_EXTRA = 4
GRANT = 20 * 1024 * 1024


class Sizes:
    def __init__(self, length, channels, modes, devices):
        self.length, self.channels, self.modes, self.devices = length, channels, modes, devices
        self.tiles = channels // LANES
        self.halves = channels // GROUP
        self.direct = devices == SUB

    def chunk_row(self, r, h, extra):
        if r < self.modes:
            return h * self.modes + r
        return self.halves * self.modes + h * extra + r - self.modes

    def chunk_rows(self, extra):
        return self.halves * (self.modes + extra)

    def exchange_shape(self, extra):
        if self.direct:
            return (self.devices * self.chunk_rows(extra), LANES)
        return ((self.modes + extra) * self.tiles, LANES)

    def exchange_slice(self, r, h, extra):
        if self.direct:
            return pl.ds(self.chunk_row(r, h, extra), SUB, stride=self.chunk_rows(extra))
        return pl.ds(r * self.tiles + h * SUB, SUB)


def staged(s, block, offset, h):
    start = block * (s.tiles * SUB) + (h * SUB * SUB + offset)
    return pl.ds(start, SUB, stride=SUB)


def major(s, t, h):
    start = t * s.tiles + h * SUB
    if not isinstance(start, int):
        start = pl.multiple_of(start, SUB)
    return pl.ds(start, SUB)


def staged_before(s, block, offset, h):
    if offset < 2:
        return staged(s, block - 1, offset + SUB - 2, h)
    return staged(s, block, offset - 2, h)


def stage_rows(s, rows, out_ref, base, tiles):
    for part in range(2):
        for i, j in enumerate(tiles):
            start = base + (part * s.tiles + j) * SUB
            if not isinstance(start, int):
                start = pl.multiple_of(start, SUB)
            out_ref[pl.ds(start, SUB), :] = rows[
                part * SUB : (part + 1) * SUB, i * LANES : (i + 1) * LANES
            ]


def stage(s, x_ref, out_ref, h):
    def step(i, carry):
        rows = x_ref[pl.ds(pl.multiple_of(i * 16, 16), 16), h * GROUP : (h + 1) * GROUP]
        base = i * (2 * s.tiles * SUB)
        stage_rows(s, rows.astype(f32), out_ref, base, range(h * SUB, (h + 1) * SUB))
        return carry

    lax.fori_loop(0, s.length // 16, step, 0)


def unstage(s, in_ref, x_ref, h, length):
    def step(i, carry):
        base = i * (2 * s.tiles * SUB)
        for j in range(h * SUB, (h + 1) * SUB):
            parts = [
                in_ref[pl.ds(pl.multiple_of(base + (part * s.tiles + j) * SUB, SUB), SUB), :]
                for part in range(2)
            ]
            x_ref[pl.ds(pl.multiple_of(i * 16, 16), 16), j * LANES : (j + 1) * LANES] = (
                jnp.concatenate(parts, axis=0).astype(bf16)
            )
        return carry

    lax.fori_loop(0, length // 16, step, 0)


def stage_modes(s, x_ref, out_ref, f):
    for g in range(s.modes // SUB):
        rows = f(x_ref[g * SUB : (g + 1) * SUB, :])
        for j in range(s.tiles):
            start = (g * s.tiles + j) * SUB
            out_ref[start : start + SUB, :] = rows[:, j * LANES : (j + 1) * LANES]


def mode_tiles(s, ref, h):
    return [ref[staged(s, m // SUB, m % SUB, h), :] for m in range(s.modes)]


def stage_taps(s, filter_ref, out_ref):
    for i in range(3):
        rows = filter_ref[i]
        for j in range(s.tiles):
            start = (i * s.tiles + j) * SUB
            out_ref[start : start + 3, :] = rows[:, j * LANES : (j + 1) * LANES]


def tap_tiles(s, ref, i, h):
    return [ref[staged(s, i, tap, h), :] for tap in range(3)]


def total(parts):
    while len(parts) > 1:
        parts = [
            parts[i] + parts[i + 1] if i + 1 < len(parts) else parts[i]
            for i in range(0, len(parts), 2)
        ]
    return parts[0]


def mix(taps, now, before, before2):
    return taps[0] * now + taps[1] * before + taps[2] * before2


def begin_kernel(
    s, q_hbm, k_hbm, v_hbm, filter_hbm, decay_hbm, prod_ref, pay_ref,
    kb, vb, qb, fb, db, ks, vs, qs, taps, poles, sems,
):
    half = GROUP
    copies = [(decay_hbm, db), (filter_hbm, fb)]
    for h in range(s.halves):
        cut = pl.ds(h * half, half)
        copies += [(k_hbm.at[:, cut], kb.at[:, cut]), (v_hbm.at[:, cut], vb.at[:, cut])]
    copies.append((q_hbm.at[pl.ds(s.length - 16, 16), :], qb))
    copies = [pltpu.make_async_copy(a, b, sems.at[i]) for i, (a, b) in enumerate(copies)]
    for copy in copies:
        copy.start()
    copies[0].wait()
    stage_modes(s, db, poles, lambda x: jnp.exp(-x))
    copies[1].wait()
    stage_taps(s, fb, taps)
    blank = jnp.zeros((SUB, LANES), f32)
    for h in range(s.halves):
        copies[2 + 2 * h].wait()
        stage(s, kb, ks, h)
        copies[3 + 2 * h].wait()
        stage(s, vb, vs, h)
        p = mode_tiles(s, poles, h)
        taps_k, taps_v = (tap_tiles(s, taps, i, h) for i in (1, 2))

        def position(block, offset, held, states, first):
            rows = staged(s, block, offset, h)
            k0, v0 = ks[rows, :], vs[rows, :]
            k1, k2, v1, v2 = held
            product = mix(taps_k, k0, k1, k2) * mix(taps_v, v0, v1, v2)
            prod_ref[major(s, block * SUB + offset, h), :] = product
            if not first:
                states = [p[m] * states[m] + product for m in range(s.modes)]
            return (k0, k1, v0, v1), states

        held, states = (blank,) * 4, [blank] * s.modes
        for offset in range(SUB):
            held, states = position(0, offset, held, states, offset < 2)

        def step(block, carry):
            held, states = carry
            for offset in range(SUB):
                held, states = position(block, offset, held, states, False)
            return held, states

        held, states = lax.fori_loop(1, s.length // SUB, step, (held, states))
        for m in range(s.modes):
            pay_ref[s.exchange_slice(m, h, FORWARD_EXTRA), :] = states[m]
        if h == 0:
            copies[-1].wait()
            stage_rows(s, qb[...].astype(f32), qs, 0, range(s.tiles))
        k1, k2, v1, v2 = held
        first = [staged(s, 0, offset, h) for offset in range(2)]
        last = [staged(s, 1, offset, h) for offset in (6, 7)]
        extra = [
            ks[first[0], :], ks[first[1], :], k2, k1,
            vs[first[0], :], vs[first[1], :], v2, v1,
            qs[last[0], :], qs[last[1], :], blank, blank,
        ]
        for r, value in enumerate(extra):
            pay_ref[s.exchange_slice(s.modes + r, h, FORWARD_EXTRA), :] = value


def forward_middle(length, rates, taps, ends, extras):
    devices = len(ends)
    whole, step0, step1 = (jnp.exp(-float(length - i) * rates) for i in range(3))
    blank = jnp.zeros_like(extras[0][0])
    arriving = jnp.zeros_like(ends[0])
    result = []
    for i in range(devices):
        k0, k1, _, _, v0, v1 = extras[i][:6]
        if i:
            _, _, ka, kb, _, _, va, vb, qa, qb = extras[i - 1][:10]
        else:
            ka = kb = va = vb = qa = qb = blank
        if i + 1 < devices:
            kc, kd, _, _, vc, vd = extras[i + 1][:6]
        else:
            kc = kd = vc = vd = blank
        prod0 = mix(taps[1], k0, kb, ka) * mix(taps[2], v0, vb, va)
        prod1 = mix(taps[1], k1, k0, kb) * mix(taps[2], v1, v0, vb)
        result.append((arriving, [prod0, prod1, ka, kb, va, vb, qa, qb, kc, kd, vc, vd]))
        arriving = whole * arriving + (ends[i] + step0 * prod0 + step1 * prod1)
    return result


def backward_middle(length, rates, ends, extras):
    devices = len(ends)
    whole = jnp.exp(-float(length) * rates)
    blank = jnp.zeros_like(extras[0][0])
    arriving = jnp.zeros_like(ends[0])
    result = [None] * devices
    for i in reversed(range(devices)):
        result[i] = (arriving, extras[i + 1] if i + 1 < devices else [blank] * len(extras[0]))
        arriving = whole * arriving + ends[i]
    return result


def middle_kernel(s, extra, in_ref, decay_ref, filter_ref, out_ref):
    me = lax.axis_index("seq")
    rows = s.chunk_rows(extra)
    for h in range(s.halves):
        lanes = pl.ds(pl.multiple_of((me + h * SUB) * LANES, LANES), LANES)
        rates = decay_ref[:, lanes]
        ends, extras = [], []
        for i in range(s.devices):
            base = i * rows
            e = base + s.chunk_row(0, h, extra)
            ends.append(in_ref[e : e + s.modes, :])
            x = base + s.chunk_row(s.modes, h, extra)
            extras.append([in_ref[x + r : x + r + 1, :] for r in range(extra)])
        if extra == FORWARD_EXTRA:
            taps = [[filter_ref[i, tap : tap + 1, lanes] for tap in range(3)] for i in range(3)]
            result = forward_middle(s.length, rates, taps, ends, extras)
        else:
            result = backward_middle(s.length, rates, ends, extras)
        for i in range(s.devices):
            base = i * rows
            e = base + s.chunk_row(0, h, extra)
            out_ref[e : e + s.modes, :] = result[i][0]
            x = base + s.chunk_row(s.modes, h, extra)
            for r in range(extra):
                out_ref[x + r : x + r + 1, :] = result[i][1][r]


def exchange(s, pay, decay_rate, short_filter, extra):
    if s.direct:
        got = lax.all_to_all(pay, "seq", 0, 0, tiled=True)
        back = pl.pallas_call(
            functools.partial(middle_kernel, s, extra),
            out_shape=jax.ShapeDtypeStruct(pay.shape, f32),
            compiler_params=pltpu.CompilerParams(vmem_limit_bytes=GRANT),
        )(got, decay_rate, short_filter)
        return lax.all_to_all(back, "seq", 0, 0, tiled=True)
    rows = s.modes + extra
    width = s.channels // s.devices
    start = lax.axis_index("seq") * width
    rates = lax.dynamic_slice_in_dim(decay_rate, start, width, 1)
    part = lax.dynamic_slice_in_dim(short_filter, start, width, 2)
    pay = pay.reshape(rows, s.devices, width).transpose(1, 0, 2)
    got = lax.all_to_all(pay, "seq", 0, 0, tiled=True)
    ends = [got[i, : s.modes] for i in range(s.devices)]
    extras = [[got[i, s.modes + r][None] for r in range(extra)] for i in range(s.devices)]
    if extra == FORWARD_EXTRA:
        taps = [[part[i, tap][None] for tap in range(3)] for i in range(3)]
        result = forward_middle(s.length, rates, taps, ends, extras)
    else:
        result = backward_middle(s.length, rates, ends, extras)
    back = jnp.stack([jnp.concatenate([state] + list(more)) for state, more in result])
    back = lax.all_to_all(back, "seq", 0, 0, tiled=True)
    return back.transpose(1, 0, 2).reshape(rows * s.tiles, LANES)


def forward_kernel(
    s, prod_ref, q_ref, stream_ref, cot_ref, back_ref, filter_ref, decay_ref, residue_ref, gain_ref,
    conv_ref, sums_ref,
    qs, xs, gs, taps, poles, weights, squares, inners,
):
    stage_modes(s, decay_ref, poles, lambda x: jnp.exp(-x))
    stage_modes(s, residue_ref, weights, lambda x: x)
    stage_taps(s, filter_ref, taps)

    def back(r, h):
        return back_ref[s.exchange_slice(r, h, FORWARD_EXTRA), :]

    for h in range(s.halves):
        p = mode_tiles(s, poles, h)
        w = mode_tiles(s, weights, h)

        def position(block, offset, states, first):
            out = major(s, block * SUB + offset, h)
            product = back(s.modes + offset, h) if first else prod_ref[out, :]
            states = [p[m] * states[m] + product for m in range(s.modes)]
            conv_ref[out, :] = total([w[m] * states[m] for m in range(s.modes)])
            return states

        states = [back(m, h) for m in range(s.modes)]
        for offset in range(SUB):
            states = position(0, offset, states, offset < 2)

        def step(block, states):
            for offset in range(SUB):
                states = position(block, offset, states, False)
            return states

        lax.fori_loop(1, s.length // SUB, step, states)

        stage(s, q_ref, qs, h)
        stage(s, stream_ref, xs, h)
        stage(s, cot_ref, gs, h)
        gain = gain_ref[h * SUB : (h + 1) * SUB, :]
        taps_q = tap_tiles(s, taps, 0, h)

        def sums(block, held):
            q1, q2 = held
            for offset in range(SUB):
                rows = staged(s, block, offset, h)
                t = block * SUB + offset
                q0 = qs[rows, :]
                mixed = xs[rows, :] + mix(taps_q, q0, q1, q2) * conv_ref[major(s, t, h), :]
                square, inner = mixed * mixed, gain * gs[rows, :] * mixed
                part = pl.ds(pl.multiple_of(t * SUB, SUB), SUB)
                if h:
                    square, inner = square + squares[part, :], inner + inners[part, :]
                squares[part, :] = square
                inners[part, :] = inner
                q1, q2 = q0, q1
            return q1, q2

        before = (back(s.modes + 7, h), back(s.modes + 6, h))
        lax.fori_loop(0, s.length // SUB, sums, before)
    for r, ref in enumerate((squares, inners)):
        parts = []
        for b in range(s.length // SUB):
            parts.append(
                total([ref[pl.ds(b * SUB * SUB + i, SUB, stride=SUB), :] for i in range(SUB)])
            )
        rows = jnp.concatenate(parts, axis=0)
        row = jnp.sum(rows.T, axis=0, keepdims=True)
        for i in range(sums_ref.shape[0]):
            sums_ref[i, r : r + 1, :] = row


def norm_kernel(
    s, width, sums_ref, conv_ref, q_ref, stream_ref, cot_ref, back_ref, filter_ref, decay_ref, gain_ref,
    normed_hbm, dstream_hbm, qgrad_hbm, dconv_ref, tail_ref, pay_ref,
    qs, xs, gs, ns, ds, normed_b, dstream_b, qgrad_b, taps, poles, inv_s, coef_s, sems,
):
    sums = total([sums_ref[i] for i in range(sums_ref.shape[0])])
    inverse = lax.rsqrt(sums[0:1, :] / width + epsilon)
    coef = inverse * inverse * inverse * sums[1:2, :] / width
    inv_s[...] = jnp.broadcast_to(inverse, (LANES, s.length)).T
    coef_s[...] = jnp.broadcast_to(coef, (LANES, s.length)).T
    stage_modes(s, decay_ref, poles, lambda x: jnp.exp(-x))
    stage_taps(s, filter_ref, taps)
    blocks = s.length // SUB
    blank = jnp.zeros((SUB, LANES), f32)
    copies = []

    def back(r, h):
        return back_ref[s.exchange_slice(r, h, FORWARD_EXTRA), :]

    for h in range(s.halves):
        stage(s, q_ref, qs, h)
        stage(s, stream_ref, xs, h)
        stage(s, cot_ref, gs, h)
        gain = gain_ref[h * SUB : (h + 1) * SUB, :]
        taps_q = tap_tiles(s, taps, 0, h)

        def position(block, offset, held, first):
            q1, q2, dq1, dq2 = held
            rows = staged(s, block, offset, h)
            t = block * SUB + offset
            out = major(s, t, h)
            inv = jnp.broadcast_to(inv_s[pl.ds(t, 1), :], (SUB, LANES))
            cf = jnp.broadcast_to(coef_s[pl.ds(t, 1), :], (SUB, LANES))
            q0 = qs[rows, :]
            qmix = mix(taps_q, q0, q1, q2)
            conv = conv_ref[out, :]
            mixed = xs[rows, :] + qmix * conv
            dmixed = inv * (gain * gs[rows, :]) - mixed * cf
            ns[rows, :] = mixed * inv * gain
            ds[rows, :] = dmixed
            dq0 = dmixed * conv
            dconv = dmixed * qmix
            dconv_ref[out, :] = dconv
            if first:
                pay_ref[s.exchange_slice(s.modes + 1 + offset, h, BACKWARD_EXTRA), :] = dq0
                if offset == 0:
                    pay_ref[s.exchange_slice(s.modes, h, BACKWARD_EXTRA), :] = dconv
            else:
                qs[staged_before(s, block, offset, h), :] = mix(taps_q, dq2, dq1, dq0)
            return q0, q1, dq0, dq1

        held = (back(s.modes + 7, h), back(s.modes + 6, h), blank, blank)
        for offset in range(SUB):
            held = position(0, offset, held, offset < 2)

        def step(block, held):
            for offset in range(SUB):
                held = position(block, offset, held, False)
            return held

        _, _, dq1, dq2 = lax.fori_loop(1, blocks, step, held)
        qs[staged(s, blocks - 1, 6, h), :] = taps_q[0] * dq2 + taps_q[1] * dq1
        qs[staged(s, blocks - 1, 7, h), :] = taps_q[0] * dq1
        pieces = [
            (ns, normed_b, normed_hbm, s.length),
            (ds, dstream_b, dstream_hbm, s.length),
            (qs, qgrad_b, qgrad_hbm, s.length - 16),
        ]
        for i, (from_ref, block_ref, to_hbm, rows) in enumerate(pieces):
            unstage(s, from_ref, block_ref, h, rows)
            cut = (pl.ds(0, rows), pl.ds(h * GROUP, GROUP))
            copy = pltpu.make_async_copy(block_ref.at[cut], to_hbm.at[cut], sems.at[3 * h + i])
            copy.start()
            copies.append(copy)
    start = (blocks - 2) * s.tiles * SUB
    tail_ref[...] = qs[start : start + 2 * s.tiles * SUB, :]
    for h in range(s.halves):
        p = mode_tiles(s, poles, h)

        def ends(i, states):
            for offset in reversed(range(SUB)):
                dconv = dconv_ref[major(s, (blocks - 1 - i) * SUB + offset, h), :]
                states = [p[m] * states[m] + dconv for m in range(s.modes)]
            return states

        states = lax.fori_loop(0, blocks, ends, [blank] * s.modes)
        for m in range(s.modes):
            pay_ref[s.exchange_slice(m, h, BACKWARD_EXTRA), :] = states[m]
        pay_ref[s.exchange_slice(s.modes + 3, h, BACKWARD_EXTRA), :] = blank
    for copy in copies:
        copy.wait()


def backward_kernel(
    s, k_ref, v_ref, dconv_ref, tail_ref, ahead_ref, back_ref, filter_ref, decay_ref, residue_ref, qgrad_in,
    qgrad_hbm, kgrad_hbm, vgrad_hbm,
    ks, vs, dprod, qs, kgrad_b, vgrad_b, qgrad_b, taps, poles, weights, sems,
):
    del qgrad_in
    stage_modes(s, decay_ref, poles, lambda x: jnp.exp(-x))
    stage_modes(s, residue_ref, weights, lambda x: x)
    stage_taps(s, filter_ref, taps)
    blocks = s.length // SUB
    copies = []

    def near(r, h):
        return ahead_ref[s.exchange_slice(s.modes + r, h, FORWARD_EXTRA), :]

    def back(r, h):
        return back_ref[s.exchange_slice(r, h, BACKWARD_EXTRA), :]

    qs[...] = tail_ref[...]
    for h in range(s.halves):
        taps_q = tap_tiles(s, taps, 0, h)
        dq0, dq1 = back(s.modes + 1, h), back(s.modes + 2, h)
        rows = [staged(s, 1, offset, h) for offset in (6, 7)]
        qs[rows[0], :] = qs[rows[0], :] + taps_q[2] * dq0
        qs[rows[1], :] = qs[rows[1], :] + (taps_q[1] * dq0 + taps_q[2] * dq1)
        unstage(s, qs, qgrad_b, h, 16)
    copy = pltpu.make_async_copy(qgrad_b, qgrad_hbm.at[pl.ds(s.length - 16, 16), :], sems.at[0])
    copy.start()
    copies.append(copy)
    for h in range(s.halves):
        p = mode_tiles(s, poles, h)
        w = mode_tiles(s, weights, h)

        def step(i, states):
            block = blocks - 1 - i
            for offset in reversed(range(SUB)):
                out = major(s, block * SUB + offset, h)
                dconv = dconv_ref[out, :]
                states = [p[m] * states[m] + dconv for m in range(s.modes)]
                dprod[out, :] = total([w[m] * states[m] for m in range(s.modes)])
            return states

        arriving = [back(m, h) for m in range(s.modes)]
        lax.fori_loop(0, blocks, step, arriving)

        stage(s, k_ref, ks, h)
        stage(s, v_ref, vs, h)
        taps_k, taps_v = (tap_tiles(s, taps, i, h) for i in (1, 2))

        def advance(held, k0, v0, d):
            k1, k2, v1, v2, dk1, dk2, dv1, dv2 = held
            dk0 = d * mix(taps_v, v0, v1, v2)
            dv0 = d * mix(taps_k, k0, k1, k2)
            grads = mix(taps_k, dk2, dk1, dk0), mix(taps_v, dv2, dv1, dv0)
            return (k0, k1, v0, v1, dk0, dk1, dv0, dv1), grads

        def position(block, offset, held, first):
            rows = staged(s, block, offset, h)
            d = dprod[major(s, block * SUB + offset, h), :]
            held, grads = advance(held, ks[rows, :], vs[rows, :], d)
            if not first:
                out = staged_before(s, block, offset, h)
                ks[out, :], vs[out, :] = grads
            return held

        ka, kb, va, vb, _, _, kc, kd, vc, vd = (near(2 + r, h) for r in range(10))
        blank = jnp.zeros((SUB, LANES), f32)
        held = (kb, ka, vb, va, blank, blank, blank, blank)
        for offset in range(SUB):
            held = position(0, offset, held, offset < 2)

        def features(block, held):
            for offset in range(SUB):
                held = position(block, offset, held, False)
            return held

        held = lax.fori_loop(1, blocks, features, held)
        arriving = [back(m, h) for m in range(s.modes)]
        dconv0 = back(s.modes, h)
        d0 = total([w[m] * arriving[m] for m in range(s.modes)])
        d1 = total([w[m] * ((arriving[m] - dconv0) / p[m]) for m in range(s.modes)])
        for offset, k0, v0, d in ((6, kc, vc, d0), (7, kd, vd, d1)):
            held, grads = advance(held, k0, v0, d)
            out = staged(s, blocks - 1, offset, h)
            ks[out, :], vs[out, :] = grads
        pieces = [(ks, kgrad_b, kgrad_hbm), (vs, vgrad_b, vgrad_hbm)]
        for i, (from_ref, block_ref, to_hbm) in enumerate(pieces):
            unstage(s, from_ref, block_ref, h, s.length)
            cut = (pl.ds(0, s.length), pl.ds(h * GROUP, GROUP))
            copy = pltpu.make_async_copy(block_ref.at[cut], to_hbm.at[cut], sems.at[1 + 2 * h + i])
            copy.start()
            copies.append(copy)
    for copy in copies:
        copy.wait()


def body(
    query_in, key_in, value_in, stream, short_filter, decay_rate, residue, norm_gain, cotangent
):
    length, channels = query_in.shape
    modes = decay_rate.shape[0]
    s = Sizes(length, channels, modes, lax.axis_size("seq"))
    total_width = channels * lax.axis_size("tp")
    wide = jax.ShapeDtypeStruct((length * s.tiles, LANES), f32)
    narrow = jax.ShapeDtypeStruct((length, channels), bf16)
    rows = 16 * s.tiles
    wide_s = pltpu.VMEM(wide.shape, f32)
    narrow_s = pltpu.VMEM(narrow.shape, bf16)
    last_s = pltpu.VMEM((16, channels), bf16)
    tail_s = pltpu.VMEM((rows, LANES), f32)
    taps_s = pltpu.VMEM((3 * s.tiles * SUB, LANES), f32)
    mode_s = pltpu.VMEM((modes * s.tiles, LANES), f32)
    sum_s = pltpu.VMEM((length * SUB, LANES), f32)
    square_s = pltpu.VMEM((length, LANES), f32)
    gain = norm_gain.reshape(s.tiles, LANES)
    there = pl.BlockSpec(memory_space=pltpu.HBM)
    here = pl.BlockSpec(memory_space=pltpu.VMEM)

    def call(kernel, ins, outs, out_shape, scratch_shapes, operands, aliases={}):
        return pl.pallas_call(
            functools.partial(kernel, s),
            in_specs=[there if c == "h" else here for c in ins],
            out_specs=[there if c == "h" else here for c in outs],
            out_shape=out_shape,
            scratch_shapes=scratch_shapes,
            input_output_aliases=aliases,
            compiler_params=pltpu.CompilerParams(vmem_limit_bytes=GRANT),
        )(*operands)

    def pay_shape(extra):
        return jax.ShapeDtypeStruct(s.exchange_shape(extra), f32)

    near_inputs = [
        pltpu.with_memory_space_constraint(x, pltpu.HBM)
        for x in (query_in, key_in, value_in, short_filter, decay_rate)
    ]
    product, pay = call(
        begin_kernel, "hhhhh", "vv",
        (wide, pay_shape(FORWARD_EXTRA)),
        [narrow_s, narrow_s, last_s, pltpu.VMEM(short_filter.shape, f32), pltpu.VMEM(decay_rate.shape, f32)]
        + [wide_s, wide_s, tail_s, taps_s, mode_s, pltpu.SemaphoreType.DMA((3 + 2 * s.halves,))],
        near_inputs,
    )
    back = exchange(s, pay, decay_rate, short_filter, FORWARD_EXTRA)
    conv, sums = call(
        forward_kernel, "v" * 9, "vv",
        (wide, jax.ShapeDtypeStruct((lax.axis_size("tp"), 2, length), f32)),
        [wide_s] * 3 + [taps_s, mode_s, mode_s, sum_s, sum_s],
        (product, query_in, stream, cotangent, back, short_filter, decay_rate, residue, gain),
    )
    sums = lax.all_to_all(sums, "tp", 0, 0, tiled=True)
    normed, dstream, query_grad, dconv, tail, pay_back = call(
        lambda s, *refs: norm_kernel(s, total_width, *refs), "v" * 9, "hhhvvv",
        (narrow, narrow, narrow, wide, jax.ShapeDtypeStruct((rows, LANES), f32), pay_shape(BACKWARD_EXTRA)),
        [wide_s] * 5 + [narrow_s] * 3
        + [taps_s, mode_s, square_s, square_s, pltpu.SemaphoreType.DMA((3 * s.halves,))],
        (sums, conv, query_in, stream, cotangent, back, short_filter, decay_rate, gain),
    )
    back_back = exchange(s, pay_back, decay_rate, short_filter, BACKWARD_EXTRA)
    query_grad, key_grad, value_grad = call(
        backward_kernel, "v" * 9 + "h", "hhh",
        (narrow, narrow, narrow),
        [wide_s] * 3 + [tail_s] + [narrow_s] * 2 + [last_s, taps_s, mode_s, mode_s]
        + [pltpu.SemaphoreType.DMA((1 + 2 * s.halves,))],
        (key_in, value_in, dconv, tail, back, back_back, short_filter, decay_rate, residue, query_grad),
        {9: 0},
    )
    return (normed, dstream, query_grad, key_grad, value_grad)


def solution(mesh):
    cut = P("seq", "tp")
    return jax.shard_map(
        body,
        mesh=mesh,
        in_specs=(cut, cut, cut, cut, P(None, None, "tp"), P(None, "tp"), P(None, "tp"), P("tp"), cut),
        out_specs=(cut,) * 5,
        check_vma=False,
    )
```

```python
import functools

import jax
import jax.numpy as jnp
from jax import lax
from jax.experimental import pallas as pl
from jax.experimental.pallas import tpu as pltpu
from jax.sharding import PartitionSpec as P

f32 = jnp.float32
bf16 = jnp.bfloat16
epsilon = 1e-05
LANES = 128
SUB = 8
GROUP = LANES * SUB
FORWARD_EXTRA = 12
BACKWARD_EXTRA = 4
GRANT = 20 * 1024 * 1024


class Sizes:
    def __init__(self, length, channels, modes, devices):
        self.length, self.channels, self.modes, self.devices = length, channels, modes, devices
        self.tiles = channels // LANES
        self.halves = channels // GROUP
        self.direct = devices == SUB

    def chunk_row(self, r, h, extra):
        if r < self.modes:
            return h * self.modes + r
        return self.halves * self.modes + h * extra + r - self.modes

    def chunk_rows(self, extra):
        return self.halves * (self.modes + extra)

    def exchange_shape(self, extra):
        if self.direct:
            return (self.devices * self.chunk_rows(extra), LANES)
        return ((self.modes + extra) * self.tiles, LANES)

    def exchange_slice(self, r, h, extra):
        if self.direct:
            return pl.ds(self.chunk_row(r, h, extra), SUB, stride=self.chunk_rows(extra))
        return pl.ds(r * self.tiles + h * SUB, SUB)


def staged(s, block, offset, h):
    start = block * (s.tiles * SUB) + (h * SUB * SUB + offset)
    return pl.ds(start, SUB, stride=SUB)


def major(s, t, h):
    start = t * s.tiles + h * SUB
    if not isinstance(start, int):
        start = pl.multiple_of(start, SUB)
    return pl.ds(start, SUB)


def staged_before(s, block, offset, h):
    if offset < 2:
        return staged(s, block - 1, offset + SUB - 2, h)
    return staged(s, block, offset - 2, h)


def stage_rows(s, rows, out_ref, base, tiles):
    for part in range(2):
        for i, j in enumerate(tiles):
            start = base + (part * s.tiles + j) * SUB
            if not isinstance(start, int):
                start = pl.multiple_of(start, SUB)
            out_ref[pl.ds(start, SUB), :] = rows[
                part * SUB : (part + 1) * SUB, i * LANES : (i + 1) * LANES
            ]


def stage(s, x_ref, out_ref, i, h):
    start = i * 16 if isinstance(i, int) else pl.multiple_of(i * 16, 16)
    rows = x_ref[pl.ds(start, 16), h * GROUP : (h + 1) * GROUP]
    base = i * (2 * s.tiles * SUB)
    stage_rows(s, rows.astype(f32), out_ref, base, range(h * SUB, (h + 1) * SUB))


def unstage(s, in_ref, x_ref, i, h):
    base = i * (2 * s.tiles * SUB)
    row = i * 16 if isinstance(i, int) else pl.multiple_of(i * 16, 16)
    for j in range(h * SUB, (h + 1) * SUB):
        parts = []
        for part in range(2):
            start = base + (part * s.tiles + j) * SUB
            start = start if isinstance(start, int) else pl.multiple_of(start, SUB)
            parts.append(in_ref[pl.ds(start, SUB), :])
        x_ref[pl.ds(row, 16), j * LANES : (j + 1) * LANES] = jnp.concatenate(parts, axis=0).astype(bf16)


def sixteen(i, reverse=False):
    pairs = [(2 * i + part, offset) for part in range(2) for offset in range(SUB)]
    return pairs[::-1] if reverse else pairs


def stage_modes(s, x_ref, out_ref, f):
    for g in range(s.modes // SUB):
        rows = f(x_ref[g * SUB : (g + 1) * SUB, :])
        for j in range(s.tiles):
            start = (g * s.tiles + j) * SUB
            out_ref[start : start + SUB, :] = rows[:, j * LANES : (j + 1) * LANES]


def mode_tiles(s, ref, h):
    return [ref[staged(s, m // SUB, m % SUB, h), :] for m in range(s.modes)]


def stage_taps(s, filter_ref, out_ref):
    for i in range(3):
        rows = filter_ref[i]
        for j in range(s.tiles):
            start = (i * s.tiles + j) * SUB
            out_ref[start : start + 3, :] = rows[:, j * LANES : (j + 1) * LANES]


def tap_tiles(s, ref, i, h):
    return [ref[staged(s, i, tap, h), :] for tap in range(3)]


def total(parts):
    while len(parts) > 1:
        parts = [
            parts[i] + parts[i + 1] if i + 1 < len(parts) else parts[i]
            for i in range(0, len(parts), 2)
        ]
    return parts[0]


def mix(taps, now, before, before2):
    return taps[0] * now + taps[1] * before + taps[2] * before2


def begin_kernel(
    s, q_hbm, k_hbm, v_hbm, filter_hbm, decay_hbm, prod_ref, pay_ref,
    kb, vb, qb, fb, db, ks, vs, qs, taps, poles, sems,
):
    half = GROUP
    copies = [(decay_hbm, db), (filter_hbm, fb)]
    for h in range(s.halves):
        cut = pl.ds(h * half, half)
        copies += [(k_hbm.at[:, cut], kb.at[:, cut]), (v_hbm.at[:, cut], vb.at[:, cut])]
    copies.append((q_hbm.at[pl.ds(s.length - 16, 16), :], qb))
    copies = [pltpu.make_async_copy(a, b, sems.at[i]) for i, (a, b) in enumerate(copies)]
    for copy in copies:
        copy.start()
    copies[0].wait()
    stage_modes(s, db, poles, lambda x: jnp.exp(-x))
    copies[1].wait()
    stage_taps(s, fb, taps)
    blank = jnp.zeros((SUB, LANES), f32)
    steps = s.length // 16
    for h in range(s.halves):
        copies[2 + 2 * h].wait()
        copies[3 + 2 * h].wait()
        p = mode_tiles(s, poles, h)
        taps_k, taps_v = (tap_tiles(s, taps, i, h) for i in (1, 2))

        def position(block, offset, held, states, first):
            rows = staged(s, block, offset, h)
            k0, v0 = ks[rows, :], vs[rows, :]
            k1, k2, v1, v2 = held
            product = mix(taps_k, k0, k1, k2) * mix(taps_v, v0, v1, v2)
            prod_ref[major(s, block * SUB + offset, h), :] = product
            if not first:
                states = [p[m] * states[m] + product for m in range(s.modes)]
            return (k0, k1, v0, v1), states

        def bring(i):
            stage(s, kb, ks, i, h)
            stage(s, vb, vs, i, h)

        held, states = (blank,) * 4, [blank] * s.modes
        bring(0)
        for block, offset in sixteen(0):
            held, states = position(block, offset, held, states, block == 0 and offset < 2)
        bring(1)

        def step(i, carry):
            held, states = carry
            for block, offset in sixteen(i):
                held, states = position(block, offset, held, states, False)
            bring(jnp.minimum(i + 1, steps - 1))
            return held, states

        held, states = lax.fori_loop(1, steps, step, (held, states))
        for m in range(s.modes):
            pay_ref[s.exchange_slice(m, h, FORWARD_EXTRA), :] = states[m]
        if h == 0:
            copies[-1].wait()
            stage_rows(s, qb[...].astype(f32), qs, 0, range(s.tiles))
        k1, k2, v1, v2 = held
        first = [staged(s, 0, offset, h) for offset in range(2)]
        last = [staged(s, 1, offset, h) for offset in (6, 7)]
        extra = [
            ks[first[0], :], ks[first[1], :], k2, k1,
            vs[first[0], :], vs[first[1], :], v2, v1,
            qs[last[0], :], qs[last[1], :], blank, blank,
        ]
        for r, value in enumerate(extra):
            pay_ref[s.exchange_slice(s.modes + r, h, FORWARD_EXTRA), :] = value


def forward_middle(length, rates, taps, ends, extras):
    devices = len(ends)
    whole, step0, step1 = (jnp.exp(-float(length - i) * rates) for i in range(3))
    blank = jnp.zeros_like(extras[0][0])
    arriving = jnp.zeros_like(ends[0])
    result = []
    for i in range(devices):
        k0, k1, _, _, v0, v1 = extras[i][:6]
        if i:
            _, _, ka, kb, _, _, va, vb, qa, qb = extras[i - 1][:10]
        else:
            ka = kb = va = vb = qa = qb = blank
        if i + 1 < devices:
            kc, kd, _, _, vc, vd = extras[i + 1][:6]
        else:
            kc = kd = vc = vd = blank
        prod0 = mix(taps[1], k0, kb, ka) * mix(taps[2], v0, vb, va)
        prod1 = mix(taps[1], k1, k0, kb) * mix(taps[2], v1, v0, vb)
        result.append((arriving, [prod0, prod1, ka, kb, va, vb, qa, qb, kc, kd, vc, vd]))
        arriving = whole * arriving + (ends[i] + step0 * prod0 + step1 * prod1)
    return result


def backward_middle(length, rates, ends, extras):
    devices = len(ends)
    whole = jnp.exp(-float(length) * rates)
    blank = jnp.zeros_like(extras[0][0])
    arriving = jnp.zeros_like(ends[0])
    result = [None] * devices
    for i in reversed(range(devices)):
        result[i] = (arriving, extras[i + 1] if i + 1 < devices else [blank] * len(extras[0]))
        arriving = whole * arriving + ends[i]
    return result


def middle_kernel(s, extra, in_ref, decay_ref, filter_ref, out_ref):
    me = lax.axis_index("seq")
    rows = s.chunk_rows(extra)
    for h in range(s.halves):
        lanes = pl.ds(pl.multiple_of((me + h * SUB) * LANES, LANES), LANES)
        rates = decay_ref[:, lanes]
        ends, extras = [], []
        for i in range(s.devices):
            base = i * rows
            e = base + s.chunk_row(0, h, extra)
            ends.append(in_ref[e : e + s.modes, :])
            x = base + s.chunk_row(s.modes, h, extra)
            extras.append([in_ref[x + r : x + r + 1, :] for r in range(extra)])
        if extra == FORWARD_EXTRA:
            taps = [[filter_ref[i, tap : tap + 1, lanes] for tap in range(3)] for i in range(3)]
            result = forward_middle(s.length, rates, taps, ends, extras)
        else:
            result = backward_middle(s.length, rates, ends, extras)
        for i in range(s.devices):
            base = i * rows
            e = base + s.chunk_row(0, h, extra)
            out_ref[e : e + s.modes, :] = result[i][0]
            x = base + s.chunk_row(s.modes, h, extra)
            for r in range(extra):
                out_ref[x + r : x + r + 1, :] = result[i][1][r]


def exchange(s, pay, decay_rate, short_filter, extra):
    if s.direct:
        got = lax.all_to_all(pay, "seq", 0, 0, tiled=True)
        back = pl.pallas_call(
            functools.partial(middle_kernel, s, extra),
            out_shape=jax.ShapeDtypeStruct(pay.shape, f32),
            compiler_params=pltpu.CompilerParams(vmem_limit_bytes=GRANT),
        )(got, decay_rate, short_filter)
        return lax.all_to_all(back, "seq", 0, 0, tiled=True)
    rows = s.modes + extra
    width = s.channels // s.devices
    start = lax.axis_index("seq") * width
    rates = lax.dynamic_slice_in_dim(decay_rate, start, width, 1)
    part = lax.dynamic_slice_in_dim(short_filter, start, width, 2)
    pay = pay.reshape(rows, s.devices, width).transpose(1, 0, 2)
    got = lax.all_to_all(pay, "seq", 0, 0, tiled=True)
    ends = [got[i, : s.modes] for i in range(s.devices)]
    extras = [[got[i, s.modes + r][None] for r in range(extra)] for i in range(s.devices)]
    if extra == FORWARD_EXTRA:
        taps = [[part[i, tap][None] for tap in range(3)] for i in range(3)]
        result = forward_middle(s.length, rates, taps, ends, extras)
    else:
        result = backward_middle(s.length, rates, ends, extras)
    back = jnp.stack([jnp.concatenate([state] + list(more)) for state, more in result])
    back = lax.all_to_all(back, "seq", 0, 0, tiled=True)
    return back.transpose(1, 0, 2).reshape(rows * s.tiles, LANES)


def forward_kernel(
    s, prod_ref, q_ref, stream_ref, cot_ref, back_ref, filter_ref, decay_ref, residue_ref, gain_ref,
    conv_ref, sums_ref,
    qs, xs, gs, taps, poles, weights, squares, inners,
):
    stage_modes(s, decay_ref, poles, lambda x: jnp.exp(-x))
    stage_modes(s, residue_ref, weights, lambda x: x)
    stage_taps(s, filter_ref, taps)

    def back(r, h):
        return back_ref[s.exchange_slice(r, h, FORWARD_EXTRA), :]

    steps = s.length // 16
    for h in range(s.halves):
        p = mode_tiles(s, poles, h)
        w = mode_tiles(s, weights, h)
        gain = gain_ref[h * SUB : (h + 1) * SUB, :]
        taps_q = tap_tiles(s, taps, 0, h)

        def position(block, offset, held, states, first):
            q1, q2 = held
            rows = staged(s, block, offset, h)
            t = block * SUB + offset
            out = major(s, t, h)
            product = back(s.modes + offset, h) if first else prod_ref[out, :]
            states = [p[m] * states[m] + product for m in range(s.modes)]
            conv = total([w[m] * states[m] for m in range(s.modes)])
            conv_ref[out, :] = conv
            q0 = qs[rows, :]
            mixed = xs[rows, :] + mix(taps_q, q0, q1, q2) * conv
            square, inner = mixed * mixed, gain * gs[rows, :] * mixed
            part = pl.ds(t * SUB if isinstance(t, int) else pl.multiple_of(t * SUB, SUB), SUB)
            if h:
                square, inner = square + squares[part, :], inner + inners[part, :]
            squares[part, :] = square
            inners[part, :] = inner
            return (q0, q1), states

        def bring(i):
            stage(s, q_ref, qs, i, h)
            stage(s, stream_ref, xs, i, h)
            stage(s, cot_ref, gs, i, h)

        held = (back(s.modes + 7, h), back(s.modes + 6, h))
        states = [back(m, h) for m in range(s.modes)]
        bring(0)
        for block, offset in sixteen(0):
            held, states = position(block, offset, held, states, block == 0 and offset < 2)
        bring(1)

        def step(i, carry):
            held, states = carry
            for block, offset in sixteen(i):
                held, states = position(block, offset, held, states, False)
            bring(jnp.minimum(i + 1, steps - 1))
            return held, states

        lax.fori_loop(1, steps, step, (held, states))
    for r, ref in enumerate((squares, inners)):
        parts = []
        for b in range(s.length // SUB):
            parts.append(
                total([ref[pl.ds(b * SUB * SUB + i, SUB, stride=SUB), :] for i in range(SUB)])
            )
        rows = jnp.concatenate(parts, axis=0)
        sums_ref[r : r + 1, :] = jnp.sum(rows.T, axis=0, keepdims=True)


def norm_kernel(
    s, width, sums_ref, conv_ref, q_ref, stream_ref, cot_ref, back_ref, filter_ref, decay_ref, gain_ref,
    normed_hbm, dstream_hbm, qgrad_hbm, dconv_ref, tail_ref, pay_ref,
    qs, xs, gs, ns, ds, normed_b, dstream_b, qgrad_b, taps, poles, inv_s, coef_s, sems,
):
    inverse = lax.rsqrt(sums_ref[0:1, :] / width + epsilon)
    coef = inverse * inverse * inverse * sums_ref[1:2, :] / width
    inv_s[...] = jnp.broadcast_to(inverse, (LANES, s.length)).T
    coef_s[...] = jnp.broadcast_to(coef, (LANES, s.length)).T
    stage_modes(s, decay_ref, poles, lambda x: jnp.exp(-x))
    stage_taps(s, filter_ref, taps)
    blocks = s.length // SUB
    blank = jnp.zeros((SUB, LANES), f32)
    copies = []

    def back(r, h):
        return back_ref[s.exchange_slice(r, h, FORWARD_EXTRA), :]

    steps = s.length // 16
    for h in range(s.halves):
        gain = gain_ref[h * SUB : (h + 1) * SUB, :]
        taps_q = tap_tiles(s, taps, 0, h)

        def position(block, offset, held, first):
            q1, q2, dq1, dq2 = held
            rows = staged(s, block, offset, h)
            t = block * SUB + offset
            out = major(s, t, h)
            inv = jnp.broadcast_to(inv_s[pl.ds(t, 1), :], (SUB, LANES))
            cf = jnp.broadcast_to(coef_s[pl.ds(t, 1), :], (SUB, LANES))
            q0 = qs[rows, :]
            qmix = mix(taps_q, q0, q1, q2)
            conv = conv_ref[out, :]
            mixed = xs[rows, :] + qmix * conv
            dmixed = inv * (gain * gs[rows, :]) - mixed * cf
            ns[rows, :] = mixed * inv * gain
            ds[rows, :] = dmixed
            dq0 = dmixed * conv
            dconv = dmixed * qmix
            dconv_ref[out, :] = dconv
            if first:
                pay_ref[s.exchange_slice(s.modes + 1 + offset, h, BACKWARD_EXTRA), :] = dq0
                if offset == 0:
                    pay_ref[s.exchange_slice(s.modes, h, BACKWARD_EXTRA), :] = dconv
            else:
                qs[staged_before(s, block, offset, h), :] = mix(taps_q, dq2, dq1, dq0)
            return q0, q1, dq0, dq1

        def bring(i):
            stage(s, q_ref, qs, i, h)
            stage(s, stream_ref, xs, i, h)
            stage(s, cot_ref, gs, i, h)

        def leave(i):
            unstage(s, ns, normed_b, i, h)
            unstage(s, ds, dstream_b, i, h)
            unstage(s, qs, qgrad_b, i, h)

        held = (back(s.modes + 7, h), back(s.modes + 6, h), blank, blank)
        bring(0)
        for block, offset in sixteen(0):
            held = position(block, offset, held, block == 0 and offset < 2)
        bring(1)

        def step(i, held):
            for block, offset in sixteen(i):
                held = position(block, offset, held, False)
            leave(i - 1)
            bring(jnp.minimum(i + 1, steps - 1))
            return held

        held = lax.fori_loop(1, steps - 1, step, held)
        for block, offset in sixteen(steps - 1):
            held = position(block, offset, held, False)
        _, _, dq1, dq2 = held
        qs[staged(s, blocks - 1, 6, h), :] = taps_q[0] * dq2 + taps_q[1] * dq1
        qs[staged(s, blocks - 1, 7, h), :] = taps_q[0] * dq1
        leave(steps - 2)
        leave(steps - 1)
        pieces = [
            (normed_b, normed_hbm, s.length),
            (dstream_b, dstream_hbm, s.length),
            (qgrad_b, qgrad_hbm, s.length - 16),
        ]
        for i, (block_ref, to_hbm, rows) in enumerate(pieces):
            cut = (pl.ds(0, rows), pl.ds(h * GROUP, GROUP))
            copy = pltpu.make_async_copy(block_ref.at[cut], to_hbm.at[cut], sems.at[3 * h + i])
            copy.start()
            copies.append(copy)
    start = (blocks - 2) * s.tiles * SUB
    tail_ref[...] = qs[start : start + 2 * s.tiles * SUB, :]
    for h in range(s.halves):
        p = mode_tiles(s, poles, h)

        def ends(i, states):
            for block, offset in sixteen(steps - 1 - i, reverse=True):
                dconv = dconv_ref[major(s, block * SUB + offset, h), :]
                states = [p[m] * states[m] + dconv for m in range(s.modes)]
            return states

        states = lax.fori_loop(0, steps, ends, [blank] * s.modes)
        for m in range(s.modes):
            pay_ref[s.exchange_slice(m, h, BACKWARD_EXTRA), :] = states[m]
        pay_ref[s.exchange_slice(s.modes + 3, h, BACKWARD_EXTRA), :] = blank
    for copy in copies:
        copy.wait()


def backward_kernel(
    s, k_ref, v_ref, dconv_ref, tail_ref, ahead_ref, back_ref, filter_ref, decay_ref, residue_ref, qgrad_in,
    qgrad_hbm, kgrad_hbm, vgrad_hbm,
    ks, vs, qs, kgrad_b, vgrad_b, qgrad_b, taps, poles, weights, sems,
):
    del qgrad_in
    stage_modes(s, decay_ref, poles, lambda x: jnp.exp(-x))
    stage_modes(s, residue_ref, weights, lambda x: x)
    stage_taps(s, filter_ref, taps)
    blocks = s.length // SUB
    copies = []

    def near(r, h):
        return ahead_ref[s.exchange_slice(s.modes + r, h, FORWARD_EXTRA), :]

    def back(r, h):
        return back_ref[s.exchange_slice(r, h, BACKWARD_EXTRA), :]

    qs[...] = tail_ref[...]
    for h in range(s.halves):
        taps_q = tap_tiles(s, taps, 0, h)
        dq0, dq1 = back(s.modes + 1, h), back(s.modes + 2, h)
        rows = [staged(s, 1, offset, h) for offset in (6, 7)]
        qs[rows[0], :] = qs[rows[0], :] + taps_q[2] * dq0
        qs[rows[1], :] = qs[rows[1], :] + (taps_q[1] * dq0 + taps_q[2] * dq1)
        unstage(s, qs, qgrad_b, 0, h)
    copy = pltpu.make_async_copy(qgrad_b, qgrad_hbm.at[pl.ds(s.length - 16, 16), :], sems.at[0])
    copy.start()
    copies.append(copy)
    steps = s.length // 16
    for h in range(s.halves):
        p = mode_tiles(s, poles, h)
        w = mode_tiles(s, weights, h)
        taps_k, taps_v = (tap_tiles(s, taps, i, h) for i in (1, 2))

        def bring(i):
            stage(s, k_ref, ks, i, h)
            stage(s, v_ref, vs, i, h)

        def leave(i):
            unstage(s, ks, kgrad_b, i, h)
            unstage(s, vs, vgrad_b, i, h)

        def advance(inputs, grads, k2, v2, d):
            k0, k1, v0, v1 = inputs
            dk1, dk2, dv1, dv2 = grads
            dk0 = d * mix(taps_v, v0, v1, v2)
            dv0 = d * mix(taps_k, k0, k1, k2)
            out = mix(taps_k, dk0, dk1, dk2), mix(taps_v, dv0, dv1, dv2)
            return (k1, k2, v1, v2), (dk0, dk1, dv0, dv1), out

        def position(block, offset, carry, before=None):
            states, inputs, grads = carry
            dconv = dconv_ref[major(s, block * SUB + offset, h), :]
            states = [p[m] * states[m] + dconv for m in range(s.modes)]
            d = total([w[m] * states[m] for m in range(s.modes)])
            if before is None:
                rows = staged_before(s, block, offset, h)
                before = ks[rows, :], vs[rows, :]
            inputs, grads, out = advance(inputs, grads, *before, d)
            rows = staged(s, block, offset, h)
            ks[rows, :], vs[rows, :] = out
            return states, inputs, grads

        bring(steps - 1)
        bring(steps - 2)
        ka, kb, va, vb, _, _, kc, kd, vc, vd = (near(2 + r, h) for r in range(10))
        arriving = [back(m, h) for m in range(s.modes)]
        dconv0 = back(s.modes, h)
        d0 = total([w[m] * arriving[m] for m in range(s.modes)])
        d1 = total([w[m] * ((arriving[m] - dconv0) / p[m]) for m in range(s.modes)])
        ends = [staged(s, blocks - 1, offset, h) for offset in (6, 7)]
        inputs = (kd, kc, vd, vc)
        grads = (jnp.zeros((SUB, LANES), f32),) * 4
        inputs, grads, _ = advance(inputs, grads, ks[ends[1], :], vs[ends[1], :], d1)
        inputs, grads, _ = advance(inputs, grads, ks[ends[0], :], vs[ends[0], :], d0)

        def step(i, carry):
            i = steps - 1 - i
            for block, offset in sixteen(i, reverse=True):
                carry = position(block, offset, carry)
            leave(i)
            bring(jnp.maximum(i - 2, 0))
            return carry

        carry = lax.fori_loop(0, steps - 1, step, (arriving, inputs, grads))
        for block, offset in sixteen(0, reverse=True):
            first = block == 0 and offset < 2
            carry = position(block, offset, carry, ((ka, va), (kb, vb))[offset] if first else None)
        leave(0)
        for i, (block_ref, to_hbm) in enumerate([(kgrad_b, kgrad_hbm), (vgrad_b, vgrad_hbm)]):
            cut = (pl.ds(0, s.length), pl.ds(h * GROUP, GROUP))
            copy = pltpu.make_async_copy(block_ref.at[cut], to_hbm.at[cut], sems.at[1 + 2 * h + i])
            copy.start()
            copies.append(copy)
    for copy in copies:
        copy.wait()


def body(
    query_in, key_in, value_in, stream, short_filter, decay_rate, residue, norm_gain, cotangent
):
    length, channels = query_in.shape
    modes = decay_rate.shape[0]
    s = Sizes(length, channels, modes, lax.axis_size("seq"))
    total_width = channels * lax.axis_size("tp")
    wide = jax.ShapeDtypeStruct((length * s.tiles, LANES), f32)
    narrow = jax.ShapeDtypeStruct((length, channels), bf16)
    rows = 16 * s.tiles
    wide_s = pltpu.VMEM(wide.shape, f32)
    narrow_s = pltpu.VMEM(narrow.shape, bf16)
    last_s = pltpu.VMEM((16, channels), bf16)
    tail_s = pltpu.VMEM((rows, LANES), f32)
    taps_s = pltpu.VMEM((3 * s.tiles * SUB, LANES), f32)
    mode_s = pltpu.VMEM((modes * s.tiles, LANES), f32)
    sum_s = pltpu.VMEM((length * SUB, LANES), f32)
    square_s = pltpu.VMEM((length, LANES), f32)
    gain = norm_gain.reshape(s.tiles, LANES)
    there = pl.BlockSpec(memory_space=pltpu.HBM)
    here = pl.BlockSpec(memory_space=pltpu.VMEM)

    def call(kernel, ins, outs, out_shape, scratch_shapes, operands, aliases={}):
        return pl.pallas_call(
            functools.partial(kernel, s),
            in_specs=[there if c == "h" else here for c in ins],
            out_specs=[there if c == "h" else here for c in outs],
            out_shape=out_shape,
            scratch_shapes=scratch_shapes,
            input_output_aliases=aliases,
            compiler_params=pltpu.CompilerParams(vmem_limit_bytes=GRANT),
        )(*operands)

    def pay_shape(extra):
        return jax.ShapeDtypeStruct(s.exchange_shape(extra), f32)

    near_inputs = [
        pltpu.with_memory_space_constraint(x, pltpu.HBM)
        for x in (query_in, key_in, value_in, short_filter, decay_rate)
    ]
    product, pay = call(
        begin_kernel, "hhhhh", "vv",
        (wide, pay_shape(FORWARD_EXTRA)),
        [narrow_s, narrow_s, last_s, pltpu.VMEM(short_filter.shape, f32), pltpu.VMEM(decay_rate.shape, f32)]
        + [wide_s, wide_s, tail_s, taps_s, mode_s, pltpu.SemaphoreType.DMA((3 + 2 * s.halves,))],
        near_inputs,
    )
    back = exchange(s, pay, decay_rate, short_filter, FORWARD_EXTRA)
    conv, sums = call(
        forward_kernel, "v" * 9, "vv",
        (wide, jax.ShapeDtypeStruct((2, length), f32)),
        [wide_s] * 3 + [taps_s, mode_s, mode_s, sum_s, sum_s],
        (product, query_in, stream, cotangent, back, short_filter, decay_rate, residue, gain),
    )
    sums = lax.psum(sums, "tp")
    normed, dstream, query_grad, dconv, tail, pay_back = call(
        lambda s, *refs: norm_kernel(s, total_width, *refs), "v" * 9, "hhhvvv",
        (narrow, narrow, narrow, wide, jax.ShapeDtypeStruct((rows, LANES), f32), pay_shape(BACKWARD_EXTRA)),
        [wide_s] * 5 + [narrow_s] * 3
        + [taps_s, mode_s, square_s, square_s, pltpu.SemaphoreType.DMA((3 * s.halves,))],
        (sums, conv, query_in, stream, cotangent, back, short_filter, decay_rate, gain),
    )
    back_back = exchange(s, pay_back, decay_rate, short_filter, BACKWARD_EXTRA)
    query_grad, key_grad, value_grad = call(
        backward_kernel, "v" * 9 + "h", "hhh",
        (narrow, narrow, narrow),
        [wide_s] * 2 + [tail_s] + [narrow_s] * 2 + [last_s, taps_s, mode_s, mode_s]
        + [pltpu.SemaphoreType.DMA((1 + 2 * s.halves,))],
        (key_in, value_in, dconv, tail, back, back_back, short_filter, decay_rate, residue, query_grad),
        {9: 0},
    )
    return (normed, dstream, query_grad, key_grad, value_grad)


def solution(mesh):
    cut = P("seq", "tp")
    return jax.shard_map(
        body,
        mesh=mesh,
        in_specs=(cut, cut, cut, cut, P(None, None, "tp"), P(None, "tp"), P(None, "tp"), P("tp"), cut),
        out_specs=(cut,) * 5,
        check_vma=False,
    )
```

```python
import functools

import jax
import jax.numpy as jnp
from jax import lax
from jax.experimental import pallas as pl
from jax.experimental.pallas import tpu as pltpu
from jax.sharding import PartitionSpec as P

f32 = jnp.float32
bf16 = jnp.bfloat16
epsilon = 1e-05
LANES = 128
SUB = 8
GROUP = LANES * SUB
FORWARD_EXTRA = 12
BACKWARD_EXTRA = 4
GRANT = 20 * 1024 * 1024


class Sizes:
    def __init__(self, length, channels, modes, devices):
        self.length, self.channels, self.modes, self.devices = length, channels, modes, devices
        self.tiles = channels // LANES
        self.halves = channels // GROUP
        self.direct = devices == SUB

    def chunk_row(self, r, h, extra):
        if r < self.modes:
            return h * self.modes + r
        return self.halves * self.modes + h * extra + r - self.modes

    def chunk_rows(self, extra):
        return self.halves * (self.modes + extra)

    def exchange_shape(self, extra):
        if self.direct:
            return (self.devices * self.chunk_rows(extra), LANES)
        return ((self.modes + extra) * self.tiles, LANES)

    def exchange_slice(self, r, h, extra):
        if self.direct:
            return pl.ds(self.chunk_row(r, h, extra), SUB, stride=self.chunk_rows(extra))
        return pl.ds(r * self.tiles + h * SUB, SUB)


def staged(s, block, offset, h):
    start = block * (s.tiles * SUB) + (h * SUB * SUB + offset)
    return pl.ds(start, SUB, stride=SUB)


def major(s, t, h):
    start = t * s.tiles + h * SUB
    if not isinstance(start, int):
        start = pl.multiple_of(start, SUB)
    return pl.ds(start, SUB)


def staged_before(s, block, offset, h):
    if offset < 2:
        return staged(s, block - 1, offset + SUB - 2, h)
    return staged(s, block, offset - 2, h)


def stage_rows(s, rows, out_ref, base, tiles):
    for part in range(2):
        for i, j in enumerate(tiles):
            start = base + (part * s.tiles + j) * SUB
            if not isinstance(start, int):
                start = pl.multiple_of(start, SUB)
            out_ref[pl.ds(start, SUB), :] = rows[
                part * SUB : (part + 1) * SUB, i * LANES : (i + 1) * LANES
            ]


def stage(s, x_ref, out_ref, i, h):
    start = i * 16 if isinstance(i, int) else pl.multiple_of(i * 16, 16)
    rows = x_ref[pl.ds(start, 16), h * GROUP : (h + 1) * GROUP]
    base = i * (2 * s.tiles * SUB)
    stage_rows(s, rows.astype(f32), out_ref, base, range(h * SUB, (h + 1) * SUB))


def unstage(s, in_ref, x_ref, i, h):
    base = i * (2 * s.tiles * SUB)
    row = i * 16 if isinstance(i, int) else pl.multiple_of(i * 16, 16)
    for j in range(h * SUB, (h + 1) * SUB):
        parts = []
        for part in range(2):
            start = base + (part * s.tiles + j) * SUB
            start = start if isinstance(start, int) else pl.multiple_of(start, SUB)
            parts.append(in_ref[pl.ds(start, SUB), :])
        x_ref[pl.ds(row, 16), j * LANES : (j + 1) * LANES] = jnp.concatenate(parts, axis=0).astype(bf16)


def sixteen(i, reverse=False):
    pairs = [(2 * i + part, offset) for part in range(2) for offset in range(SUB)]
    return pairs[::-1] if reverse else pairs


def stage_modes(s, x_ref, out_ref, f):
    for g in range(s.modes // SUB):
        rows = f(x_ref[g * SUB : (g + 1) * SUB, :])
        for j in range(s.tiles):
            start = (g * s.tiles + j) * SUB
            out_ref[start : start + SUB, :] = rows[:, j * LANES : (j + 1) * LANES]


def mode_tiles(s, ref, h):
    return [ref[staged(s, m // SUB, m % SUB, h), :] for m in range(s.modes)]


def stage_taps(s, filter_ref, out_ref):
    for i in range(3):
        rows = filter_ref[i]
        for j in range(s.tiles):
            start = (i * s.tiles + j) * SUB
            out_ref[start : start + 3, :] = rows[:, j * LANES : (j + 1) * LANES]


def tap_tiles(s, ref, i, h):
    return [ref[staged(s, i, tap, h), :] for tap in range(3)]


def total(parts):
    while len(parts) > 1:
        parts = [
            parts[i] + parts[i + 1] if i + 1 < len(parts) else parts[i]
            for i in range(0, len(parts), 2)
        ]
    return parts[0]


def mix(taps, now, before, before2):
    return taps[0] * now + taps[1] * before + taps[2] * before2


def begin_kernel(
    s, q_hbm, k_hbm, v_hbm, filter_hbm, decay_hbm, prod_ref, pay_ref,
    kb, vb, qb, fb, db, ks, vs, qs, taps, poles, sems,
):
    half = GROUP
    copies = [(decay_hbm, db), (filter_hbm, fb)]
    for h in range(s.halves):
        cut = pl.ds(h * half, half)
        copies += [(k_hbm.at[:, cut], kb.at[:, cut]), (v_hbm.at[:, cut], vb.at[:, cut])]
    copies.append((q_hbm.at[pl.ds(s.length - 16, 16), :], qb))
    copies = [pltpu.make_async_copy(a, b, sems.at[i]) for i, (a, b) in enumerate(copies)]
    for copy in copies:
        copy.start()
    copies[0].wait()
    stage_modes(s, db, poles, lambda x: jnp.exp(-x))
    copies[1].wait()
    stage_taps(s, fb, taps)
    blank = jnp.zeros((SUB, LANES), f32)
    steps = s.length // 16
    for h in range(s.halves):
        copies[2 + 2 * h].wait()
        copies[3 + 2 * h].wait()
        p = mode_tiles(s, poles, h)
        taps_k, taps_v = (tap_tiles(s, taps, i, h) for i in (1, 2))

        def position(block, offset, held, states, first):
            rows = staged(s, block, offset, h)
            k0, v0 = ks[rows, :], vs[rows, :]
            k1, k2, v1, v2 = held
            product = mix(taps_k, k0, k1, k2) * mix(taps_v, v0, v1, v2)
            prod_ref[major(s, block * SUB + offset, h), :] = product
            if not first:
                states = [p[m] * states[m] + product for m in range(s.modes)]
            return (k0, k1, v0, v1), states

        def bring(i):
            stage(s, kb, ks, i, h)
            stage(s, vb, vs, i, h)

        held, states = (blank,) * 4, [blank] * s.modes
        bring(0)
        for block, offset in sixteen(0):
            held, states = position(block, offset, held, states, block == 0 and offset < 2)
        bring(1)

        def step(i, carry):
            held, states = carry
            for block, offset in sixteen(i):
                held, states = position(block, offset, held, states, False)
            bring(jnp.minimum(i + 1, steps - 1))
            return held, states

        held, states = lax.fori_loop(1, steps, step, (held, states))
        for m in range(s.modes):
            pay_ref[s.exchange_slice(m, h, FORWARD_EXTRA), :] = states[m]
        if h == 0:
            copies[-1].wait()
            stage_rows(s, qb[...].astype(f32), qs, 0, range(s.tiles))
        k1, k2, v1, v2 = held
        first = [staged(s, 0, offset, h) for offset in range(2)]
        last = [staged(s, 1, offset, h) for offset in (6, 7)]
        extra = [
            ks[first[0], :], ks[first[1], :], k2, k1,
            vs[first[0], :], vs[first[1], :], v2, v1,
            qs[last[0], :], qs[last[1], :], blank, blank,
        ]
        for r, value in enumerate(extra):
            pay_ref[s.exchange_slice(s.modes + r, h, FORWARD_EXTRA), :] = value


def forward_middle(length, rates, taps, ends, extras):
    devices = len(ends)
    whole, step0, step1 = (jnp.exp(-float(length - i) * rates) for i in range(3))
    blank = jnp.zeros_like(extras[0][0])
    arriving = jnp.zeros_like(ends[0])
    result = []
    for i in range(devices):
        k0, k1, _, _, v0, v1 = extras[i][:6]
        if i:
            _, _, ka, kb, _, _, va, vb, qa, qb = extras[i - 1][:10]
        else:
            ka = kb = va = vb = qa = qb = blank
        if i + 1 < devices:
            kc, kd, _, _, vc, vd = extras[i + 1][:6]
        else:
            kc = kd = vc = vd = blank
        prod0 = mix(taps[1], k0, kb, ka) * mix(taps[2], v0, vb, va)
        prod1 = mix(taps[1], k1, k0, kb) * mix(taps[2], v1, v0, vb)
        result.append((arriving, [prod0, prod1, ka, kb, va, vb, qa, qb, kc, kd, vc, vd]))
        arriving = whole * arriving + (ends[i] + step0 * prod0 + step1 * prod1)
    return result


def backward_middle(length, rates, ends, extras):
    devices = len(ends)
    whole = jnp.exp(-float(length) * rates)
    blank = jnp.zeros_like(extras[0][0])
    arriving = jnp.zeros_like(ends[0])
    result = [None] * devices
    for i in reversed(range(devices)):
        result[i] = (arriving, extras[i + 1] if i + 1 < devices else [blank] * len(extras[0]))
        arriving = whole * arriving + ends[i]
    return result


def middle_kernel(s, extra, in_ref, decay_ref, filter_ref, out_ref):
    me = lax.axis_index("seq")
    rows = s.chunk_rows(extra)
    for h in range(s.halves):
        lanes = pl.ds(pl.multiple_of((me + h * SUB) * LANES, LANES), LANES)
        rates = decay_ref[:, lanes]
        ends, extras = [], []
        for i in range(s.devices):
            base = i * rows
            e = base + s.chunk_row(0, h, extra)
            ends.append(in_ref[e : e + s.modes, :])
            x = base + s.chunk_row(s.modes, h, extra)
            extras.append([in_ref[x + r : x + r + 1, :] for r in range(extra)])
        if extra == FORWARD_EXTRA:
            taps = [[filter_ref[i, tap : tap + 1, lanes] for tap in range(3)] for i in range(3)]
            result = forward_middle(s.length, rates, taps, ends, extras)
        else:
            result = backward_middle(s.length, rates, ends, extras)
        for i in range(s.devices):
            base = i * rows
            e = base + s.chunk_row(0, h, extra)
            out_ref[e : e + s.modes, :] = result[i][0]
            x = base + s.chunk_row(s.modes, h, extra)
            for r in range(extra):
                out_ref[x + r : x + r + 1, :] = result[i][1][r]


def exchange(s, pay, decay_rate, short_filter, extra):
    if s.direct:
        got = lax.all_to_all(pay, "seq", 0, 0, tiled=True)
        back = pl.pallas_call(
            functools.partial(middle_kernel, s, extra),
            out_shape=jax.ShapeDtypeStruct(pay.shape, f32),
            compiler_params=pltpu.CompilerParams(vmem_limit_bytes=GRANT),
        )(got, decay_rate, short_filter)
        return lax.all_to_all(back, "seq", 0, 0, tiled=True)
    rows = s.modes + extra
    width = s.channels // s.devices
    start = lax.axis_index("seq") * width
    rates = lax.dynamic_slice_in_dim(decay_rate, start, width, 1)
    part = lax.dynamic_slice_in_dim(short_filter, start, width, 2)
    pay = pay.reshape(rows, s.devices, width).transpose(1, 0, 2)
    got = lax.all_to_all(pay, "seq", 0, 0, tiled=True)
    ends = [got[i, : s.modes] for i in range(s.devices)]
    extras = [[got[i, s.modes + r][None] for r in range(extra)] for i in range(s.devices)]
    if extra == FORWARD_EXTRA:
        taps = [[part[i, tap][None] for tap in range(3)] for i in range(3)]
        result = forward_middle(s.length, rates, taps, ends, extras)
    else:
        result = backward_middle(s.length, rates, ends, extras)
    back = jnp.stack([jnp.concatenate([state] + list(more)) for state, more in result])
    back = lax.all_to_all(back, "seq", 0, 0, tiled=True)
    return back.transpose(1, 0, 2).reshape(rows * s.tiles, LANES)


def inside_kernel(s, prod_ref, decay_ref, residue_ref, inside_ref, poles, weights):
    stage_modes(s, decay_ref, poles, lambda x: jnp.exp(-x))
    stage_modes(s, residue_ref, weights, lambda x: x)
    steps = s.length // 16
    for h in range(s.halves):
        p = mode_tiles(s, poles, h)
        w = mode_tiles(s, weights, h)

        def position(block, offset, states):
            out = major(s, block * SUB + offset, h)
            product = prod_ref[out, :]
            states = [p[m] * states[m] + product for m in range(s.modes)]
            inside_ref[out, :] = total([w[m] * states[m] for m in range(s.modes)])
            return states

        states = [jnp.zeros((SUB, LANES), f32)] * s.modes
        for block, offset in sixteen(0)[2:]:
            states = position(block, offset, states)

        def step(i, states):
            for block, offset in sixteen(i):
                states = position(block, offset, states)
            return states

        lax.fori_loop(1, steps, step, states)


def forward_kernel(
    s, inside_ref, q_ref, stream_ref, cot_ref, back_ref, filter_ref, decay_ref, residue_ref, gain_ref,
    conv_ref, sums_ref,
    qs, xs, gs, taps, poles, weights, squares, inners,
):
    stage_modes(s, decay_ref, poles, lambda x: jnp.exp(-x))
    stage_modes(s, residue_ref, weights, lambda x: x)
    stage_taps(s, filter_ref, taps)

    def back(r, h):
        return back_ref[s.exchange_slice(r, h, FORWARD_EXTRA), :]

    steps = s.length // 16
    for h in range(s.halves):
        p = mode_tiles(s, poles, h)
        w = mode_tiles(s, weights, h)
        gain = gain_ref[h * SUB : (h + 1) * SUB, :]
        taps_q = tap_tiles(s, taps, 0, h)

        def position(block, offset, held, states, first):
            q1, q2 = held
            rows = staged(s, block, offset, h)
            t = block * SUB + offset
            out = major(s, t, h)
            if first:
                product = back(s.modes + offset, h)
                states = [p[m] * states[m] + product for m in range(s.modes)]
                conv = total([w[m] * states[m] for m in range(s.modes)])
                if offset == 1:
                    states = [w[m] * states[m] for m in range(s.modes)]
            else:
                states = [p[m] * states[m] for m in range(s.modes)]
                conv = inside_ref[out, :] + total(states)
            conv_ref[out, :] = conv
            q0 = qs[rows, :]
            mixed = xs[rows, :] + mix(taps_q, q0, q1, q2) * conv
            square, inner = mixed * mixed, gain * gs[rows, :] * mixed
            part = pl.ds(t * SUB if isinstance(t, int) else pl.multiple_of(t * SUB, SUB), SUB)
            if h:
                square, inner = square + squares[part, :], inner + inners[part, :]
            squares[part, :] = square
            inners[part, :] = inner
            return (q0, q1), states

        def bring(i):
            stage(s, q_ref, qs, i, h)
            stage(s, stream_ref, xs, i, h)
            stage(s, cot_ref, gs, i, h)

        held = (back(s.modes + 7, h), back(s.modes + 6, h))
        states = [back(m, h) for m in range(s.modes)]
        bring(0)
        for block, offset in sixteen(0):
            held, states = position(block, offset, held, states, block == 0 and offset < 2)
        bring(1)

        def step(i, carry):
            held, states = carry
            for block, offset in sixteen(i):
                held, states = position(block, offset, held, states, False)
            bring(jnp.minimum(i + 1, steps - 1))
            return held, states

        lax.fori_loop(1, steps, step, (held, states))
    for r, ref in enumerate((squares, inners)):
        parts = []
        for b in range(s.length // SUB):
            parts.append(
                total([ref[pl.ds(b * SUB * SUB + i, SUB, stride=SUB), :] for i in range(SUB)])
            )
        rows = jnp.concatenate(parts, axis=0)
        sums_ref[r : r + 1, :] = jnp.sum(rows.T, axis=0, keepdims=True)


def norm_kernel(
    s, width, sums_ref, conv_ref, q_ref, stream_ref, cot_ref, back_ref, filter_ref, decay_ref, gain_ref,
    normed_hbm, dstream_hbm, qgrad_hbm, dconv_ref, tail_ref, pay_ref,
    qs, xs, gs, ns, ds, normed_b, dstream_b, qgrad_b, taps, poles, inv_s, coef_s, sems,
):
    inverse = lax.rsqrt(sums_ref[0:1, :] / width + epsilon)
    coef = inverse * inverse * inverse * sums_ref[1:2, :] / width
    inv_s[...] = jnp.broadcast_to(inverse, (LANES, s.length)).T
    coef_s[...] = jnp.broadcast_to(coef, (LANES, s.length)).T
    stage_modes(s, decay_ref, poles, lambda x: jnp.exp(-x))
    stage_taps(s, filter_ref, taps)
    blocks = s.length // SUB
    blank = jnp.zeros((SUB, LANES), f32)
    copies = []

    def back(r, h):
        return back_ref[s.exchange_slice(r, h, FORWARD_EXTRA), :]

    steps = s.length // 16
    for h in range(s.halves):
        gain = gain_ref[h * SUB : (h + 1) * SUB, :]
        taps_q = tap_tiles(s, taps, 0, h)

        def position(block, offset, held, first):
            q1, q2, dq1, dq2 = held
            rows = staged(s, block, offset, h)
            t = block * SUB + offset
            out = major(s, t, h)
            inv = jnp.broadcast_to(inv_s[pl.ds(t, 1), :], (SUB, LANES))
            cf = jnp.broadcast_to(coef_s[pl.ds(t, 1), :], (SUB, LANES))
            q0 = qs[rows, :]
            qmix = mix(taps_q, q0, q1, q2)
            conv = conv_ref[out, :]
            mixed = xs[rows, :] + qmix * conv
            dmixed = inv * (gain * gs[rows, :]) - mixed * cf
            ns[rows, :] = mixed * inv * gain
            ds[rows, :] = dmixed
            dq0 = dmixed * conv
            dconv = dmixed * qmix
            dconv_ref[out, :] = dconv
            if first:
                pay_ref[s.exchange_slice(s.modes + 1 + offset, h, BACKWARD_EXTRA), :] = dq0
                if offset == 0:
                    pay_ref[s.exchange_slice(s.modes, h, BACKWARD_EXTRA), :] = dconv
            else:
                qs[staged_before(s, block, offset, h), :] = mix(taps_q, dq2, dq1, dq0)
            return q0, q1, dq0, dq1

        def bring(i):
            stage(s, q_ref, qs, i, h)
            stage(s, stream_ref, xs, i, h)
            stage(s, cot_ref, gs, i, h)

        def leave(i):
            unstage(s, ns, normed_b, i, h)
            unstage(s, ds, dstream_b, i, h)
            unstage(s, qs, qgrad_b, i, h)

        held = (back(s.modes + 7, h), back(s.modes + 6, h), blank, blank)
        bring(0)
        for block, offset in sixteen(0):
            held = position(block, offset, held, block == 0 and offset < 2)
        bring(1)

        def step(i, held):
            for block, offset in sixteen(i):
                held = position(block, offset, held, False)
            leave(i - 1)
            bring(jnp.minimum(i + 1, steps - 1))
            return held

        held = lax.fori_loop(1, steps - 1, step, held)
        for block, offset in sixteen(steps - 1):
            held = position(block, offset, held, False)
        _, _, dq1, dq2 = held
        qs[staged(s, blocks - 1, 6, h), :] = taps_q[0] * dq2 + taps_q[1] * dq1
        qs[staged(s, blocks - 1, 7, h), :] = taps_q[0] * dq1
        leave(steps - 2)
        leave(steps - 1)
        pieces = [
            (normed_b, normed_hbm, s.length),
            (dstream_b, dstream_hbm, s.length),
            (qgrad_b, qgrad_hbm, s.length - 16),
        ]
        for i, (block_ref, to_hbm, rows) in enumerate(pieces):
            cut = (pl.ds(0, rows), pl.ds(h * GROUP, GROUP))
            copy = pltpu.make_async_copy(block_ref.at[cut], to_hbm.at[cut], sems.at[3 * h + i])
            copy.start()
            copies.append(copy)
    start = (blocks - 2) * s.tiles * SUB
    tail_ref[...] = qs[start : start + 2 * s.tiles * SUB, :]
    for h in range(s.halves):
        p = mode_tiles(s, poles, h)

        def ends(i, states):
            for block, offset in sixteen(steps - 1 - i, reverse=True):
                dconv = dconv_ref[major(s, block * SUB + offset, h), :]
                states = [p[m] * states[m] + dconv for m in range(s.modes)]
            return states

        states = lax.fori_loop(0, steps, ends, [blank] * s.modes)
        for m in range(s.modes):
            pay_ref[s.exchange_slice(m, h, BACKWARD_EXTRA), :] = states[m]
        pay_ref[s.exchange_slice(s.modes + 3, h, BACKWARD_EXTRA), :] = blank
    for copy in copies:
        copy.wait()


def backward_kernel(
    s, k_ref, v_ref, dconv_ref, tail_ref, ahead_ref, back_ref, filter_ref, decay_ref, residue_ref, qgrad_in,
    qgrad_hbm, kgrad_hbm, vgrad_hbm,
    ks, vs, qs, kgrad_b, vgrad_b, qgrad_b, taps, poles, weights, sems,
):
    del qgrad_in
    stage_modes(s, decay_ref, poles, lambda x: jnp.exp(-x))
    stage_modes(s, residue_ref, weights, lambda x: x)
    stage_taps(s, filter_ref, taps)
    blocks = s.length // SUB
    copies = []

    def near(r, h):
        return ahead_ref[s.exchange_slice(s.modes + r, h, FORWARD_EXTRA), :]

    def back(r, h):
        return back_ref[s.exchange_slice(r, h, BACKWARD_EXTRA), :]

    qs[...] = tail_ref[...]
    for h in range(s.halves):
        taps_q = tap_tiles(s, taps, 0, h)
        dq0, dq1 = back(s.modes + 1, h), back(s.modes + 2, h)
        rows = [staged(s, 1, offset, h) for offset in (6, 7)]
        qs[rows[0], :] = qs[rows[0], :] + taps_q[2] * dq0
        qs[rows[1], :] = qs[rows[1], :] + (taps_q[1] * dq0 + taps_q[2] * dq1)
        unstage(s, qs, qgrad_b, 0, h)
    copy = pltpu.make_async_copy(qgrad_b, qgrad_hbm.at[pl.ds(s.length - 16, 16), :], sems.at[0])
    copy.start()
    copies.append(copy)
    steps = s.length // 16
    for h in range(s.halves):
        p = mode_tiles(s, poles, h)
        w = mode_tiles(s, weights, h)
        taps_k, taps_v = (tap_tiles(s, taps, i, h) for i in (1, 2))

        def bring(i):
            stage(s, k_ref, ks, i, h)
            stage(s, v_ref, vs, i, h)

        def leave(i):
            unstage(s, ks, kgrad_b, i, h)
            unstage(s, vs, vgrad_b, i, h)

        def advance(inputs, grads, k2, v2, d):
            k0, k1, v0, v1 = inputs
            dk1, dk2, dv1, dv2 = grads
            dk0 = d * mix(taps_v, v0, v1, v2)
            dv0 = d * mix(taps_k, k0, k1, k2)
            out = mix(taps_k, dk0, dk1, dk2), mix(taps_v, dv0, dv1, dv2)
            return (k1, k2, v1, v2), (dk0, dk1, dv0, dv1), out

        def position(block, offset, carry, before=None):
            states, inputs, grads = carry
            dconv = dconv_ref[major(s, block * SUB + offset, h), :]
            states = [p[m] * states[m] + dconv for m in range(s.modes)]
            d = total([w[m] * states[m] for m in range(s.modes)])
            if before is None:
                rows = staged_before(s, block, offset, h)
                before = ks[rows, :], vs[rows, :]
            inputs, grads, out = advance(inputs, grads, *before, d)
            rows = staged(s, block, offset, h)
            ks[rows, :], vs[rows, :] = out
            return states, inputs, grads

        bring(steps - 1)
        bring(steps - 2)
        ka, kb, va, vb, _, _, kc, kd, vc, vd = (near(2 + r, h) for r in range(10))
        arriving = [back(m, h) for m in range(s.modes)]
        dconv0 = back(s.modes, h)
        d0 = total([w[m] * arriving[m] for m in range(s.modes)])
        d1 = total([w[m] * ((arriving[m] - dconv0) / p[m]) for m in range(s.modes)])
        ends = [staged(s, blocks - 1, offset, h) for offset in (6, 7)]
        inputs = (kd, kc, vd, vc)
        grads = (jnp.zeros((SUB, LANES), f32),) * 4
        inputs, grads, _ = advance(inputs, grads, ks[ends[1], :], vs[ends[1], :], d1)
        inputs, grads, _ = advance(inputs, grads, ks[ends[0], :], vs[ends[0], :], d0)

        def step(i, carry):
            i = steps - 1 - i
            for block, offset in sixteen(i, reverse=True):
                carry = position(block, offset, carry)
            leave(i)
            bring(jnp.maximum(i - 2, 0))
            return carry

        carry = lax.fori_loop(0, steps - 1, step, (arriving, inputs, grads))
        for block, offset in sixteen(0, reverse=True):
            first = block == 0 and offset < 2
            carry = position(block, offset, carry, ((ka, va), (kb, vb))[offset] if first else None)
        leave(0)
        for i, (block_ref, to_hbm) in enumerate([(kgrad_b, kgrad_hbm), (vgrad_b, vgrad_hbm)]):
            cut = (pl.ds(0, s.length), pl.ds(h * GROUP, GROUP))
            copy = pltpu.make_async_copy(block_ref.at[cut], to_hbm.at[cut], sems.at[1 + 2 * h + i])
            copy.start()
            copies.append(copy)
    for copy in copies:
        copy.wait()


def body(
    query_in, key_in, value_in, stream, short_filter, decay_rate, residue, norm_gain, cotangent
):
    length, channels = query_in.shape
    modes = decay_rate.shape[0]
    s = Sizes(length, channels, modes, lax.axis_size("seq"))
    total_width = channels * lax.axis_size("tp")
    wide = jax.ShapeDtypeStruct((length * s.tiles, LANES), f32)
    narrow = jax.ShapeDtypeStruct((length, channels), bf16)
    rows = 16 * s.tiles
    wide_s = pltpu.VMEM(wide.shape, f32)
    narrow_s = pltpu.VMEM(narrow.shape, bf16)
    last_s = pltpu.VMEM((16, channels), bf16)
    tail_s = pltpu.VMEM((rows, LANES), f32)
    taps_s = pltpu.VMEM((3 * s.tiles * SUB, LANES), f32)
    mode_s = pltpu.VMEM((modes * s.tiles, LANES), f32)
    sum_s = pltpu.VMEM((length * SUB, LANES), f32)
    square_s = pltpu.VMEM((length, LANES), f32)
    gain = norm_gain.reshape(s.tiles, LANES)
    there = pl.BlockSpec(memory_space=pltpu.HBM)
    here = pl.BlockSpec(memory_space=pltpu.VMEM)

    def call(kernel, ins, outs, out_shape, scratch_shapes, operands, aliases={}, cost=None):
        return pl.pallas_call(
            functools.partial(kernel, s),
            in_specs=[there if c == "h" else here for c in ins],
            out_specs=[there if c == "h" else here for c in outs],
            out_shape=out_shape,
            scratch_shapes=scratch_shapes,
            input_output_aliases=aliases,
            cost_estimate=cost,
            compiler_params=pltpu.CompilerParams(vmem_limit_bytes=GRANT),
        )(*operands)

    def pay_shape(extra):
        return jax.ShapeDtypeStruct(s.exchange_shape(extra), f32)

    near_inputs = [
        pltpu.with_memory_space_constraint(x, pltpu.HBM)
        for x in (query_in, key_in, value_in, short_filter, decay_rate)
    ]
    product, pay = call(
        begin_kernel, "hhhhh", "vv",
        (wide, pay_shape(FORWARD_EXTRA)),
        [narrow_s, narrow_s, last_s, pltpu.VMEM(short_filter.shape, f32), pltpu.VMEM(decay_rate.shape, f32)]
        + [wide_s, wide_s, tail_s, taps_s, mode_s, pltpu.SemaphoreType.DMA((3 + 2 * s.halves,))],
        near_inputs,
    )
    inside = call(
        inside_kernel, "vvv", "v", (wide,), [mode_s, mode_s], (product, decay_rate, residue),
        cost=pl.CostEstimate(flops=64 * length * channels, bytes_accessed=3 * 4 * length * channels, transcendentals=0),
    )[0]
    back = exchange(s, pay, decay_rate, short_filter, FORWARD_EXTRA)
    conv, sums = call(
        forward_kernel, "v" * 9, "vv",
        (wide, jax.ShapeDtypeStruct((2, length), f32)),
        [wide_s] * 3 + [taps_s, mode_s, mode_s, sum_s, sum_s],
        (inside, query_in, stream, cotangent, back, short_filter, decay_rate, residue, gain),
    )
    sums = lax.psum(sums, "tp")
    normed, dstream, query_grad, dconv, tail, pay_back = call(
        lambda s, *refs: norm_kernel(s, total_width, *refs), "v" * 9, "hhhvvv",
        (narrow, narrow, narrow, wide, jax.ShapeDtypeStruct((rows, LANES), f32), pay_shape(BACKWARD_EXTRA)),
        [wide_s] * 5 + [narrow_s] * 3
        + [taps_s, mode_s, square_s, square_s, pltpu.SemaphoreType.DMA((3 * s.halves,))],
        (sums, conv, query_in, stream, cotangent, back, short_filter, decay_rate, gain),
    )
    back_back = exchange(s, pay_back, decay_rate, short_filter, BACKWARD_EXTRA)
    query_grad, key_grad, value_grad = call(
        backward_kernel, "v" * 9 + "h", "hhh",
        (narrow, narrow, narrow),
        [wide_s] * 2 + [tail_s] + [narrow_s] * 2 + [last_s, taps_s, mode_s, mode_s]
        + [pltpu.SemaphoreType.DMA((1 + 2 * s.halves,))],
        (key_in, value_in, dconv, tail, back, back_back, short_filter, decay_rate, residue, query_grad),
        {9: 0},
    )
    return (normed, dstream, query_grad, key_grad, value_grad)


def solution(mesh):
    cut = P("seq", "tp")
    return jax.shard_map(
        body,
        mesh=mesh,
        in_specs=(cut, cut, cut, cut, P(None, None, "tp"), P(None, "tp"), P(None, "tp"), P("tp"), cut),
        out_specs=(cut,) * 5,
        check_vma=False,
    )
```

```python
import functools

import jax
import jax.numpy as jnp
from jax import lax
from jax.experimental import pallas as pl
from jax.experimental.pallas import tpu as pltpu
from jax.sharding import PartitionSpec as P

f32 = jnp.float32
bf16 = jnp.bfloat16
epsilon = 1e-05
LANES = 128
SUB = 8
GROUP = LANES * SUB
FORWARD_EXTRA = 16
BACKWARD_EXTRA = 8
GRANT = 20 * 1024 * 1024


class Sizes:
    def __init__(self, length, modes, devices, base):
        self.length, self.modes, self.devices, self.base = length, modes, devices, base
        self.direct = devices == SUB

    def exchange_shape(self, extra):
        return (SUB * (self.modes + extra), LANES)

    def exchange_slice(self, r, extra):
        if self.direct:
            return pl.ds(r, SUB, stride=self.modes + extra)
        return pl.ds(r * SUB, SUB)


def staged(block, offset):
    return pl.ds(block * (SUB * SUB) + offset, SUB, stride=SUB)


def major(t):
    start = t * SUB
    return pl.ds(start if isinstance(start, int) else pl.multiple_of(start, SUB), SUB)


def staged_before(block, offset):
    if offset < 2:
        return staged(block - 1, offset + SUB - 2)
    return staged(block, offset - 2)


def aligned(start, unit):
    return start if isinstance(start, int) else pl.multiple_of(start, unit)


def stage(s, x_ref, out_ref, i):
    rows = x_ref[pl.ds(aligned(i * 16, 16), 16), s.base : s.base + GROUP].astype(f32)
    for part in range(2):
        for j in range(SUB):
            start = aligned(i * (2 * SUB * SUB) + (part * SUB + j) * SUB, SUB)
            out_ref[pl.ds(start, SUB), :] = rows[
                part * SUB : (part + 1) * SUB, j * LANES : (j + 1) * LANES
            ]


def unstage(in_ref, x_ref, i):
    for j in range(SUB):
        parts = []
        for part in range(2):
            start = aligned(i * (2 * SUB * SUB) + (part * SUB + j) * SUB, SUB)
            parts.append(in_ref[pl.ds(start, SUB), :])
        x_ref[pl.ds(aligned(i * 16, 16), 16), j * LANES : (j + 1) * LANES] = jnp.concatenate(
            parts, axis=0
        ).astype(bf16)


def sixteen(i, reverse=False):
    pairs = [(2 * i + part, offset) for part in range(2) for offset in range(SUB)]
    return pairs[::-1] if reverse else pairs


def stage_modes(s, x_ref, out_ref, f):
    for g in range(s.modes // SUB):
        rows = f(x_ref[g * SUB : (g + 1) * SUB, s.base : s.base + GROUP])
        for j in range(SUB):
            start = (g * SUB + j) * SUB
            out_ref[start : start + SUB, :] = rows[:, j * LANES : (j + 1) * LANES]


def mode_tiles(s, ref):
    return [ref[staged(m // SUB, m % SUB), :] for m in range(s.modes)]


def stage_taps(s, filter_ref, out_ref):
    for i in range(3):
        rows = filter_ref[i][:, s.base : s.base + GROUP]
        for j in range(SUB):
            start = (i * SUB + j) * SUB
            out_ref[start : start + 3, :] = rows[:, j * LANES : (j + 1) * LANES]


def tap_tiles(ref, i):
    return [ref[staged(i, tap), :] for tap in range(3)]


def gain_tile(s, gain_ref):
    return gain_ref[s.base // LANES : s.base // LANES + SUB, :]


def total(parts):
    while len(parts) > 1:
        parts = [
            parts[i] + parts[i + 1] if i + 1 < len(parts) else parts[i]
            for i in range(0, len(parts), 2)
        ]
    return parts[0]


def mix(taps, now, before, before2):
    return taps[0] * now + taps[1] * before + taps[2] * before2


def begin_kernel(
    s, q_hbm, k_hbm, v_hbm, filter_hbm, decay_hbm, pay_ref, kb, vb, qb, fb, db, ks, vs, qs, taps, poles, sems
):
    cut = pl.ds(s.base, GROUP)
    copies = [
        (decay_hbm.at[:, cut], db),
        (filter_hbm.at[:, :, cut], fb),
        (k_hbm.at[:, cut], kb),
        (v_hbm.at[:, cut], vb),
        (q_hbm.at[pl.ds(s.length - 16, 16), cut], qb),
    ]
    copies = [pltpu.make_async_copy(a, b, sems.at[i]) for i, (a, b) in enumerate(copies)]
    for copy in copies:
        copy.start()
    own = Sizes(s.length, s.modes, s.devices, 0)
    copies[0].wait()
    stage_modes(own, db, poles, lambda x: jnp.exp(-x))
    copies[1].wait()
    stage_taps(own, fb, taps)
    blank = jnp.zeros((SUB, LANES), f32)
    steps = s.length // 16
    copies[2].wait()
    copies[3].wait()
    p = mode_tiles(s, poles)
    taps_k, taps_v = (tap_tiles(taps, i) for i in (1, 2))

    def position(block, offset, held, states, first):
        rows = staged(block, offset)
        k0, v0 = ks[rows, :], vs[rows, :]
        k1, k2, v1, v2 = held
        if not first:
            product = mix(taps_k, k0, k1, k2) * mix(taps_v, v0, v1, v2)
            states = [p[m] * states[m] + product for m in range(s.modes)]
        return (k0, k1, v0, v1), states

    def bring(i):
        stage(own, kb, ks, i)
        stage(own, vb, vs, i)

    held, states = (blank,) * 4, [blank] * s.modes
    bring(0)
    for block, offset in sixteen(0):
        held, states = position(block, offset, held, states, block == 0 and offset < 2)
    bring(1)

    def step(i, carry):
        held, states = carry
        for block, offset in sixteen(i):
            held, states = position(block, offset, held, states, False)
        bring(jnp.minimum(i + 1, steps - 1))
        return held, states

    held, states = lax.fori_loop(1, steps, step, (held, states))
    for m in range(s.modes):
        pay_ref[s.exchange_slice(m, FORWARD_EXTRA), :] = states[m]
    copies[4].wait()
    stage(own, qb, qs, 0)
    k1, k2, v1, v2 = held
    first = [staged(0, offset) for offset in range(2)]
    last = [staged(1, offset) for offset in (6, 7)]
    extra = [
        ks[first[0], :], ks[first[1], :], k2, k1,
        vs[first[0], :], vs[first[1], :], v2, v1,
        qs[last[0], :], qs[last[1], :],
    ]
    extra += [blank] * (FORWARD_EXTRA - len(extra))
    for r, value in enumerate(extra):
        pay_ref[s.exchange_slice(s.modes + r, FORWARD_EXTRA), :] = value


def forward_middle(length, rates, taps, ends, extras):
    devices = len(ends)
    whole, step0, step1 = (jnp.exp(-float(length - i) * rates) for i in range(3))
    blank = jnp.zeros_like(extras[0][0])
    arriving = jnp.zeros_like(ends[0])
    result = []
    for i in range(devices):
        k0, k1, _, _, v0, v1 = extras[i][:6]
        if i:
            _, _, ka, kb, _, _, va, vb, qa, qb = extras[i - 1][:10]
        else:
            ka = kb = va = vb = qa = qb = blank
        if i + 1 < devices:
            kc, kd, _, _, vc, vd = extras[i + 1][:6]
        else:
            kc = kd = vc = vd = blank
        prod0 = mix(taps[1], k0, kb, ka) * mix(taps[2], v0, vb, va)
        prod1 = mix(taps[1], k1, k0, kb) * mix(taps[2], v1, v0, vb)
        result.append((arriving, [ka, kb, va, vb, qa, qb, kc, kd, vc, vd]))
        arriving = whole * arriving + (ends[i] + step0 * prod0 + step1 * prod1)
    return result


def backward_middle(length, rates, ends, extras):
    devices = len(ends)
    whole = jnp.exp(-float(length) * rates)
    blank = jnp.zeros_like(extras[0][0])
    arriving = jnp.zeros_like(ends[0])
    result = [None] * devices
    for i in reversed(range(devices)):
        result[i] = (arriving, extras[i + 1][:3] if i + 1 < devices else [blank] * 3)
        arriving = whole * arriving + ends[i]
    return result


def middle_kernel(s, extra, in_ref, decay_ref, filter_ref, out_ref):
    me = lax.axis_index("seq")
    lanes = pl.ds(pl.multiple_of(s.base + me * LANES, LANES), LANES)
    rates = decay_ref[:, lanes]
    rows = s.modes + extra
    ends = [in_ref[i * rows : i * rows + s.modes, :] for i in range(s.devices)]
    extras = [
        [in_ref[i * rows + s.modes + r : i * rows + s.modes + r + 1, :] for r in range(10 if extra == FORWARD_EXTRA else 3)]
        for i in range(s.devices)
    ]
    if extra == FORWARD_EXTRA:
        taps = [[filter_ref[i, tap : tap + 1, lanes] for tap in range(3)] for i in range(3)]
        result = forward_middle(s.length, rates, taps, ends, extras)
    else:
        result = backward_middle(s.length, rates, ends, extras)
    for i, (state, more) in enumerate(result):
        out_ref[i * rows : i * rows + s.modes, :] = state
        more = list(more) + [jnp.zeros((1, LANES), f32)] * (extra - len(more))
        out_ref[i * rows + s.modes : (i + 1) * rows, :] = jnp.concatenate(more, axis=0)


def exchange(s, pay, decay_rate, short_filter, extra):
    rows = s.modes + extra
    if s.direct:
        got = lax.all_to_all(pay.reshape(s.devices, rows, LANES), "seq", 0, 0, tiled=True)
        back = pl.pallas_call(
            functools.partial(middle_kernel, s, extra),
            out_shape=jax.ShapeDtypeStruct(pay.shape, f32),
            compiler_params=pltpu.CompilerParams(vmem_limit_bytes=GRANT),
        )(got.reshape(pay.shape), decay_rate, short_filter)
        back = lax.all_to_all(back.reshape(s.devices, rows, LANES), "seq", 0, 0, tiled=True)
        return back.reshape(pay.shape)
    width = GROUP // s.devices
    start = s.base + lax.axis_index("seq") * width
    rates = lax.dynamic_slice_in_dim(decay_rate, start, width, 1)
    part = lax.dynamic_slice_in_dim(short_filter, start, width, 2)
    pay = pay.reshape(rows, s.devices, width).transpose(1, 0, 2)
    got = lax.all_to_all(pay, "seq", 0, 0, tiled=True)
    ends = [got[i, : s.modes] for i in range(s.devices)]
    extras = [[got[i, s.modes + r][None] for r in range(extra)] for i in range(s.devices)]
    if extra == FORWARD_EXTRA:
        taps = [[part[i, tap][None] for tap in range(3)] for i in range(3)]
        result = forward_middle(s.length, rates, taps, ends, extras)
    else:
        result = backward_middle(s.length, rates, ends, extras)
    back = jnp.stack(
        [
            jnp.concatenate([state] + list(more) + [jnp.zeros((extra - len(more), width), f32)])
            for state, more in result
        ]
    )
    back = lax.all_to_all(back, "seq", 0, 0, tiled=True)
    return back.transpose(1, 0, 2).reshape(rows * SUB, LANES)


def forward_kernel(
    s, *refs
):
    if s.base:
        before_ref, *refs = refs
    (
        q_ref, k_ref, v_ref, stream_ref, cot_ref, back_ref, filter_ref, decay_ref, residue_ref, gain_ref,
        conv_ref, sums_ref,
        qs, ks, vs, xs, gs, taps, poles, weights, squares, inners,
    ) = refs
    stage_modes(s, decay_ref, poles, lambda x: jnp.exp(-x))
    stage_modes(s, residue_ref, weights, lambda x: x)
    stage_taps(s, filter_ref, taps)
    back = [back_ref[s.exchange_slice(r, FORWARD_EXTRA), :] for r in range(s.modes + 6)]
    steps = s.length // 16
    p = mode_tiles(s, poles)
    w = mode_tiles(s, weights)
    gain = gain_tile(s, gain_ref)
    taps_q, taps_k, taps_v = (tap_tiles(taps, i) for i in range(3))

    def position(block, offset, held, states):
        q1, q2, k1, k2, v1, v2 = held
        rows = staged(block, offset)
        t = block * SUB + offset
        q0, k0, v0 = qs[rows, :], ks[rows, :], vs[rows, :]
        product = mix(taps_k, k0, k1, k2) * mix(taps_v, v0, v1, v2)
        states = [p[m] * states[m] + product for m in range(s.modes)]
        conv = total([w[m] * states[m] for m in range(s.modes)])
        conv_ref[major(t), :] = conv
        mixed = xs[rows, :] + mix(taps_q, q0, q1, q2) * conv
        squares[major(t), :] = mixed * mixed
        inners[major(t), :] = gain * gs[rows, :] * mixed
        return (q0, q1, k0, k1, v0, v1), states

    def bring(i):
        for from_ref, to_ref in ((q_ref, qs), (k_ref, ks), (v_ref, vs), (stream_ref, xs), (cot_ref, gs)):
            stage(s, from_ref, to_ref, i)

    ka, kb, va, vb, qa, qb = back[s.modes :]
    bring(0)

    def step(i, carry):
        held, states = carry
        for block, offset in sixteen(i):
            held, states = position(block, offset, held, states)
        bring(jnp.minimum(i + 1, steps - 1))
        return held, states

    lax.fori_loop(0, steps, step, ((qb, qa, kb, ka, vb, va), back[: s.modes]))
    for r, ref in enumerate((squares, inners)):
        parts = []
        for b in range(s.length // SUB):
            parts.append(
                total([ref[pl.ds(b * SUB * SUB + i, SUB, stride=SUB), :] for i in range(SUB)])
            )
        row = jnp.sum(jnp.concatenate(parts, axis=0).T, axis=0, keepdims=True)
        sums_ref[r : r + 1, :] = row + before_ref[r : r + 1, :] if s.base else row


def norm_kernel(s, width, *refs):
    if s.base:
        refs = refs[3:]
    (
        sums_ref, conv_ref, q_ref, stream_ref, cot_ref, back_ref, filter_ref, decay_ref, gain_ref,
        normed_hbm, dstream_hbm, qgrad_hbm, dconv_hbm, tail_ref, pay_ref,
        qs, xs, gs, ns, ds, cs, normed_b, dstream_b, qgrad_b, taps, poles, inv_s, coef_s, sems,
    ) = refs
    inverse = lax.rsqrt(sums_ref[0:1, :] / width + epsilon)
    coef = inverse * inverse * inverse * sums_ref[1:2, :] / width
    inv_s[...] = jnp.broadcast_to(inverse, (LANES, s.length)).T
    coef_s[...] = jnp.broadcast_to(coef, (LANES, s.length)).T
    stage_modes(s, decay_ref, poles, lambda x: jnp.exp(-x))
    stage_taps(s, filter_ref, taps)
    blocks = s.length // SUB
    steps = s.length // 16
    blank = jnp.zeros((SUB, LANES), f32)
    qa, qb = (back_ref[s.exchange_slice(s.modes + r, FORWARD_EXTRA), :] for r in (4, 5))
    gain = gain_tile(s, gain_ref)
    taps_q = tap_tiles(taps, 0)

    def position(block, offset, held, first):
        q1, q2, dq1, dq2 = held
        rows = staged(block, offset)
        t = block * SUB + offset
        inv = jnp.broadcast_to(inv_s[pl.ds(t, 1), :], (SUB, LANES))
        cf = jnp.broadcast_to(coef_s[pl.ds(t, 1), :], (SUB, LANES))
        q0 = qs[rows, :]
        qmix = mix(taps_q, q0, q1, q2)
        conv = conv_ref[major(t), :]
        mixed = xs[rows, :] + qmix * conv
        dmixed = inv * (gain * gs[rows, :]) - mixed * cf
        ns[rows, :] = mixed * inv * gain
        ds[rows, :] = dmixed
        dq0 = dmixed * conv
        dconv = dmixed * qmix
        cs[major(t), :] = dconv
        if first:
            pay_ref[s.exchange_slice(s.modes + 1 + offset, BACKWARD_EXTRA), :] = dq0
            if offset == 0:
                pay_ref[s.exchange_slice(s.modes, BACKWARD_EXTRA), :] = dconv
        else:
            qs[staged_before(block, offset), :] = mix(taps_q, dq2, dq1, dq0)
        return q0, q1, dq0, dq1

    def bring(i):
        for from_ref, to_ref in ((q_ref, qs), (stream_ref, xs), (cot_ref, gs)):
            stage(s, from_ref, to_ref, i)

    def leave(i):
        for from_ref, to_ref in ((ns, normed_b), (ds, dstream_b), (qs, qgrad_b)):
            unstage(from_ref, to_ref, i)

    held = (qb, qa, blank, blank)
    bring(0)
    for block, offset in sixteen(0):
        held = position(block, offset, held, block == 0 and offset < 2)
    bring(1)

    def step(i, held):
        for block, offset in sixteen(i):
            held = position(block, offset, held, False)
        leave(i - 1)
        bring(i + 1)
        return held

    held = lax.fori_loop(1, steps - 1, step, held)
    for block, offset in sixteen(steps - 1):
        held = position(block, offset, held, False)
    _, _, dq1, dq2 = held
    qs[staged(blocks - 1, 6), :] = taps_q[0] * dq2 + taps_q[1] * dq1
    qs[staged(blocks - 1, 7), :] = taps_q[0] * dq1
    copies = [pltpu.make_async_copy(cs, dconv_hbm, sems.at[0])]
    copies[0].start()
    leave(steps - 2)
    leave(steps - 1)
    pieces = [
        (normed_b, normed_hbm, s.length),
        (dstream_b, dstream_hbm, s.length),
        (qgrad_b, qgrad_hbm, s.length - 16),
    ]
    for i, (block_ref, to_hbm, rows) in enumerate(pieces):
        copy = pltpu.make_async_copy(
            block_ref.at[pl.ds(0, rows), :], to_hbm.at[pl.ds(0, rows), pl.ds(s.base, GROUP)], sems.at[1 + i]
        )
        copy.start()
        copies.append(copy)
    start = (blocks - 2) * SUB * SUB
    tail_ref[...] = qs[start : start + 2 * SUB * SUB, :]
    p = mode_tiles(s, poles)

    def ends(i, states):
        for block, offset in sixteen(steps - 1 - i, reverse=True):
            dconv = cs[major(block * SUB + offset), :]
            states = [p[m] * states[m] + dconv for m in range(s.modes)]
        return states

    states = lax.fori_loop(0, steps, ends, [blank] * s.modes)
    for m in range(s.modes):
        pay_ref[s.exchange_slice(m, BACKWARD_EXTRA), :] = states[m]
    for r in range(3, BACKWARD_EXTRA):
        pay_ref[s.exchange_slice(s.modes + r, BACKWARD_EXTRA), :] = blank
    for copy in copies:
        copy.wait()


def backward_kernel(s, *refs):
    refs = refs[3 if s.base else 1 :]
    (
        k_ref, v_ref, dconv_ref, tail_ref, ahead_ref, back_ref, filter_ref, decay_ref, residue_ref,
        qgrad_hbm, kgrad_hbm, vgrad_hbm,
        ks, vs, qs, kgrad_b, vgrad_b, qgrad_b, taps, poles, weights, sems,
    ) = refs
    stage_modes(s, decay_ref, poles, lambda x: jnp.exp(-x))
    stage_modes(s, residue_ref, weights, lambda x: x)
    stage_taps(s, filter_ref, taps)
    blocks = s.length // SUB
    steps = s.length // 16
    copies = []

    def near(r):
        return ahead_ref[s.exchange_slice(s.modes + r, FORWARD_EXTRA), :]

    def back(r):
        return back_ref[s.exchange_slice(r, BACKWARD_EXTRA), :]

    def send(block_ref, to, i):
        copy = pltpu.make_async_copy(block_ref, to, sems.at[i])
        copy.start()
        copies.append(copy)

    taps_q, taps_k, taps_v = (tap_tiles(taps, i) for i in range(3))
    qs[...] = tail_ref[...]
    dq0, dq1 = back(s.modes + 1), back(s.modes + 2)
    rows = [staged(1, offset) for offset in (6, 7)]
    qs[rows[0], :] = qs[rows[0], :] + taps_q[2] * dq0
    qs[rows[1], :] = qs[rows[1], :] + (taps_q[1] * dq0 + taps_q[2] * dq1)
    unstage(qs, qgrad_b, 0)
    cut = pl.ds(s.base, GROUP)
    send(qgrad_b, qgrad_hbm.at[pl.ds(s.length - 16, 16), cut], 0)
    p = mode_tiles(s, poles)
    w = mode_tiles(s, weights)

    def bring(i):
        stage(s, k_ref, ks, i)
        stage(s, v_ref, vs, i)

    def leave(i):
        unstage(ks, kgrad_b, i)
        unstage(vs, vgrad_b, i)

    def advance(inputs, grads, k2, v2, d):
        k0, k1, v0, v1 = inputs
        dk1, dk2, dv1, dv2 = grads
        dk0 = d * mix(taps_v, v0, v1, v2)
        dv0 = d * mix(taps_k, k0, k1, k2)
        out = mix(taps_k, dk0, dk1, dk2), mix(taps_v, dv0, dv1, dv2)
        return (k1, k2, v1, v2), (dk0, dk1, dv0, dv1), out

    def position(block, offset, carry, before=None):
        states, inputs, grads = carry
        dconv = dconv_ref[major(block * SUB + offset), :]
        states = [p[m] * states[m] + dconv for m in range(s.modes)]
        d = total([w[m] * states[m] for m in range(s.modes)])
        if before is None:
            rows = staged_before(block, offset)
            before = ks[rows, :], vs[rows, :]
        inputs, grads, out = advance(inputs, grads, *before, d)
        rows = staged(block, offset)
        ks[rows, :], vs[rows, :] = out
        return states, inputs, grads

    bring(steps - 1)
    bring(steps - 2)
    ka, kb, va, vb, _, _, kc, kd, vc, vd = (near(r) for r in range(10))
    arriving = [back(m) for m in range(s.modes)]
    dconv0 = back(s.modes)
    d0 = total([w[m] * arriving[m] for m in range(s.modes)])
    d1 = total([w[m] * ((arriving[m] - dconv0) / p[m]) for m in range(s.modes)])
    ends = [staged(blocks - 1, offset) for offset in (6, 7)]
    inputs = (kd, kc, vd, vc)
    grads = (jnp.zeros((SUB, LANES), f32),) * 4
    inputs, grads, _ = advance(inputs, grads, ks[ends[1], :], vs[ends[1], :], d1)
    inputs, grads, _ = advance(inputs, grads, ks[ends[0], :], vs[ends[0], :], d0)

    def step(i, carry):
        i = steps - 1 - i
        for block, offset in sixteen(i, reverse=True):
            carry = position(block, offset, carry)
        leave(i)
        bring(jnp.maximum(i - 2, 0))
        return carry

    carry = lax.fori_loop(0, steps - 1, step, (arriving, inputs, grads))
    for block, offset in sixteen(0, reverse=True):
        first = block == 0 and offset < 2
        carry = position(block, offset, carry, ((ka, va), (kb, vb))[offset] if first else None)
    leave(0)
    send(kgrad_b, kgrad_hbm.at[:, cut], 1)
    send(vgrad_b, vgrad_hbm.at[:, cut], 2)
    for copy in copies:
        copy.wait()


def body(
    query_in, key_in, value_in, stream, short_filter, decay_rate, residue, norm_gain, cotangent
):
    length, channels = query_in.shape
    modes = decay_rate.shape[0]
    parts = [Sizes(length, modes, lax.axis_size("seq"), base) for base in range(0, channels, GROUP)]
    total_width = channels * lax.axis_size("tp")
    wide = jax.ShapeDtypeStruct((length * SUB, LANES), f32)
    narrow = jax.ShapeDtypeStruct((length, channels), bf16)
    wide_s = pltpu.VMEM(wide.shape, f32)
    narrow_s = pltpu.VMEM((length, GROUP), bf16)
    last_s = pltpu.VMEM((16, GROUP), bf16)
    tail_s = pltpu.VMEM((16 * SUB, LANES), f32)
    taps_s = pltpu.VMEM((3 * SUB * SUB, LANES), f32)
    mode_s = pltpu.VMEM((modes * SUB, LANES), f32)
    square_s = pltpu.VMEM((length, LANES), f32)
    gain = norm_gain.reshape(channels // LANES, LANES)
    there = pl.BlockSpec(memory_space=pltpu.HBM)
    here = pl.BlockSpec(memory_space=pltpu.VMEM)

    def far(*arrays):
        return [pltpu.with_memory_space_constraint(x, pltpu.HBM) for x in arrays]

    def call(kernel, s, ins, outs, out_shape, scratch_shapes, operands, aliases={}):
        return pl.pallas_call(
            functools.partial(kernel, s),
            in_specs=[there if c == "h" else here for c in ins],
            out_specs=[there if c == "h" else here for c in outs],
            out_shape=out_shape,
            scratch_shapes=scratch_shapes,
            input_output_aliases=aliases,
            compiler_params=pltpu.CompilerParams(vmem_limit_bytes=GRANT),
        )(*operands)

    def semaphores(count):
        return pltpu.SemaphoreType.DMA((count,))

    def pay_shape(extra):
        return jax.ShapeDtypeStruct(parts[0].exchange_shape(extra), f32)

    backs = []
    for s in parts:
        (pay,) = call(
            begin_kernel, s, "hhhhh", "v",
            (pay_shape(FORWARD_EXTRA),),
            [narrow_s, narrow_s, last_s, pltpu.VMEM((3, 3, GROUP), f32), pltpu.VMEM((modes, GROUP), f32)]
            + [wide_s, wide_s, tail_s, taps_s, mode_s, semaphores(5)],
            far(query_in, key_in, value_in, short_filter, decay_rate),
        )
        backs.append(exchange(s, pay, decay_rate, short_filter, FORWARD_EXTRA))

    convs, sums = [], []
    for s, back in zip(parts, backs):
        conv, part_sums = call(
            forward_kernel, s, "v" * (10 + len(sums)), "vv",
            (wide, jax.ShapeDtypeStruct((2, length), f32)),
            [wide_s] * 5 + [taps_s, mode_s, mode_s, wide_s, wide_s],
            (*sums, query_in, key_in, value_in, stream, cotangent, back)
            + (short_filter, decay_rate, residue, gain),
        )
        convs.append(conv)
        sums = [part_sums]
    sums = lax.psum(sums[0], "tp")

    held, after = [], []
    for s, back, conv in zip(parts, backs, convs):
        *held, dconv, tail, pay = call(
            lambda s, *refs: norm_kernel(s, total_width, *refs), s, "h" * len(held) + "v" * 9, "hhhhvv",
            (narrow, narrow, narrow, wide, jax.ShapeDtypeStruct((16 * SUB, LANES), f32), pay_shape(BACKWARD_EXTRA)),
            [wide_s] * 6 + [narrow_s] * 3 + [taps_s, mode_s, square_s, square_s, semaphores(4)],
            (*held, sums, conv, query_in, stream, cotangent, back, short_filter, decay_rate, gain),
            {i: i for i in range(len(held))},
        )
        after.append((dconv, tail, exchange(s, pay, decay_rate, short_filter, BACKWARD_EXTRA)))
    normed, dstream, query_grad = held

    held = [query_grad]
    for s, back, (dconv, tail, back_back) in zip(parts, backs, after):
        held = call(
            backward_kernel, s, "h" * len(held) + "v" * 9, "hhh",
            (narrow, narrow, narrow),
            [wide_s] * 2 + [tail_s] + [narrow_s] * 2 + [last_s, taps_s, mode_s, mode_s, semaphores(3)],
            (*held, key_in, value_in, dconv, tail, back, back_back, short_filter, decay_rate, residue),
            {i: i for i in range(len(held))},
        )
    query_grad, key_grad, value_grad = held
    return (normed, dstream, query_grad, key_grad, value_grad)


def solution(mesh):
    cut = P("seq", "tp")
    return jax.shard_map(
        body,
        mesh=mesh,
        in_specs=(cut, cut, cut, cut, P(None, None, "tp"), P(None, "tp"), P(None, "tp"), P("tp"), cut),
        out_specs=(cut,) * 5,
        check_vma=False,
    )
```

```python
import functools

import jax
import jax.numpy as jnp
from jax import lax
from jax.experimental import pallas as pl
from jax.experimental.pallas import tpu as pltpu
from jax.sharding import PartitionSpec as P

f32 = jnp.float32
bf16 = jnp.bfloat16
epsilon = 1e-05
LANES = 128
SUB = 8
GROUP = LANES * SUB
FORWARD_EXTRA = 12
BACKWARD_EXTRA = 4
GRANT = 20 * 1024 * 1024


class Sizes:
    def __init__(self, length, channels, modes, devices):
        self.length, self.channels, self.modes, self.devices = length, channels, modes, devices
        self.tiles = channels // LANES
        self.halves = channels // GROUP
        self.direct = devices == SUB

    def chunk_row(self, r, h, extra):
        if r < self.modes:
            return h * self.modes + r
        return self.halves * self.modes + h * extra + r - self.modes

    def chunk_rows(self, extra):
        return self.halves * (self.modes + extra)

    def exchange_shape(self, extra):
        if self.direct:
            return (self.devices * self.chunk_rows(extra), LANES)
        return ((self.modes + extra) * self.tiles, LANES)

    def exchange_slice(self, r, h, extra):
        if self.direct:
            return pl.ds(self.chunk_row(r, h, extra), SUB, stride=self.chunk_rows(extra))
        return pl.ds(r * self.tiles + h * SUB, SUB)


def staged(s, block, offset, h):
    start = block * (s.tiles * SUB) + (h * SUB * SUB + offset)
    return pl.ds(start, SUB, stride=SUB)


def major(s, t, h):
    start = t * s.tiles + h * SUB
    if not isinstance(start, int):
        start = pl.multiple_of(start, SUB)
    return pl.ds(start, SUB)


def staged_before(s, block, offset, h):
    if offset < 2:
        return staged(s, block - 1, offset + SUB - 2, h)
    return staged(s, block, offset - 2, h)


def stage_rows(s, rows, out_ref, base, tiles):
    for part in range(2):
        for i, j in enumerate(tiles):
            start = base + (part * s.tiles + j) * SUB
            if not isinstance(start, int):
                start = pl.multiple_of(start, SUB)
            out_ref[pl.ds(start, SUB), :] = rows[
                part * SUB : (part + 1) * SUB, i * LANES : (i + 1) * LANES
            ]


def stage(s, x_ref, out_ref, i, h):
    start = i * 16 if isinstance(i, int) else pl.multiple_of(i * 16, 16)
    rows = x_ref[pl.ds(start, 16), h * GROUP : (h + 1) * GROUP]
    base = i * (2 * s.tiles * SUB)
    stage_rows(s, rows.astype(f32), out_ref, base, range(h * SUB, (h + 1) * SUB))


def unstage(s, in_ref, x_ref, i, h):
    base = i * (2 * s.tiles * SUB)
    row = i * 16 if isinstance(i, int) else pl.multiple_of(i * 16, 16)
    for j in range(h * SUB, (h + 1) * SUB):
        parts = []
        for part in range(2):
            start = base + (part * s.tiles + j) * SUB
            start = start if isinstance(start, int) else pl.multiple_of(start, SUB)
            parts.append(in_ref[pl.ds(start, SUB), :])
        x_ref[pl.ds(row, 16), j * LANES : (j + 1) * LANES] = jnp.concatenate(parts, axis=0).astype(bf16)


def sixteen(i, reverse=False):
    pairs = [(2 * i + part, offset) for part in range(2) for offset in range(SUB)]
    return pairs[::-1] if reverse else pairs


def stage_modes(s, x_ref, out_ref, f):
    for g in range(s.modes // SUB):
        rows = f(x_ref[g * SUB : (g + 1) * SUB, :])
        for j in range(s.tiles):
            start = (g * s.tiles + j) * SUB
            out_ref[start : start + SUB, :] = rows[:, j * LANES : (j + 1) * LANES]


def mode_tiles(s, ref, h):
    return [ref[staged(s, m // SUB, m % SUB, h), :] for m in range(s.modes)]


def stage_taps(s, filter_ref, out_ref):
    for i in range(3):
        rows = filter_ref[i]
        for j in range(s.tiles):
            start = (i * s.tiles + j) * SUB
            out_ref[start : start + 3, :] = rows[:, j * LANES : (j + 1) * LANES]


def tap_tiles(s, ref, i, h):
    return [ref[staged(s, i, tap, h), :] for tap in range(3)]


def total(parts):
    while len(parts) > 1:
        parts = [
            parts[i] + parts[i + 1] if i + 1 < len(parts) else parts[i]
            for i in range(0, len(parts), 2)
        ]
    return parts[0]


def mix(taps, now, before, before2):
    return taps[0] * now + taps[1] * before + taps[2] * before2


def begin_kernel(
    s, q_hbm, k_hbm, v_hbm, filter_hbm, decay_hbm, pay_ref,
    kb, vb, qb, fb, db, ks, vs, qs, taps, poles, sems,
):
    half = GROUP
    copies = [(decay_hbm, db), (filter_hbm, fb)]
    for h in range(s.halves):
        cut = pl.ds(h * half, half)
        copies += [(k_hbm.at[:, cut], kb.at[:, cut]), (v_hbm.at[:, cut], vb.at[:, cut])]
    copies.append((q_hbm.at[pl.ds(s.length - 16, 16), :], qb))
    copies = [pltpu.make_async_copy(a, b, sems.at[i]) for i, (a, b) in enumerate(copies)]
    for copy in copies:
        copy.start()
    copies[0].wait()
    stage_modes(s, db, poles, lambda x: jnp.exp(-x))
    copies[1].wait()
    stage_taps(s, fb, taps)
    blank = jnp.zeros((SUB, LANES), f32)
    steps = s.length // 16
    for h in range(s.halves):
        copies[2 + 2 * h].wait()
        copies[3 + 2 * h].wait()
        p = mode_tiles(s, poles, h)
        taps_k, taps_v = (tap_tiles(s, taps, i, h) for i in (1, 2))

        def position(block, offset, held, states, first):
            rows = staged(s, block, offset, h)
            k0, v0 = ks[rows, :], vs[rows, :]
            k1, k2, v1, v2 = held
            if not first:
                product = mix(taps_k, k0, k1, k2) * mix(taps_v, v0, v1, v2)
                states = [p[m] * states[m] + product for m in range(s.modes)]
            return (k0, k1, v0, v1), states

        def bring(i):
            stage(s, kb, ks, i, h)
            stage(s, vb, vs, i, h)

        held, states = (blank,) * 4, [blank] * s.modes
        bring(0)
        for block, offset in sixteen(0):
            held, states = position(block, offset, held, states, block == 0 and offset < 2)
        bring(1)

        def step(i, carry):
            held, states = carry
            for block, offset in sixteen(i):
                held, states = position(block, offset, held, states, False)
            bring(jnp.minimum(i + 1, steps - 1))
            return held, states

        held, states = lax.fori_loop(1, steps, step, (held, states))
        for m in range(s.modes):
            pay_ref[s.exchange_slice(m, h, FORWARD_EXTRA), :] = states[m]
        if h == 0:
            copies[-1].wait()
            stage_rows(s, qb[...].astype(f32), qs, 0, range(s.tiles))
        k1, k2, v1, v2 = held
        first = [staged(s, 0, offset, h) for offset in range(2)]
        last = [staged(s, 1, offset, h) for offset in (6, 7)]
        extra = [
            ks[first[0], :], ks[first[1], :], k2, k1,
            vs[first[0], :], vs[first[1], :], v2, v1,
            qs[last[0], :], qs[last[1], :], blank, blank,
        ]
        for r, value in enumerate(extra):
            pay_ref[s.exchange_slice(s.modes + r, h, FORWARD_EXTRA), :] = value


def forward_middle(length, rates, taps, ends, extras):
    devices = len(ends)
    whole, step0, step1 = (jnp.exp(-float(length - i) * rates) for i in range(3))
    blank = jnp.zeros_like(extras[0][0])
    arriving = jnp.zeros_like(ends[0])
    result = []
    for i in range(devices):
        k0, k1, _, _, v0, v1 = extras[i][:6]
        if i:
            _, _, ka, kb, _, _, va, vb, qa, qb = extras[i - 1][:10]
        else:
            ka = kb = va = vb = qa = qb = blank
        if i + 1 < devices:
            kc, kd, _, _, vc, vd = extras[i + 1][:6]
        else:
            kc = kd = vc = vd = blank
        prod0 = mix(taps[1], k0, kb, ka) * mix(taps[2], v0, vb, va)
        prod1 = mix(taps[1], k1, k0, kb) * mix(taps[2], v1, v0, vb)
        result.append((arriving, [prod0, prod1, ka, kb, va, vb, qa, qb, kc, kd, vc, vd]))
        arriving = whole * arriving + (ends[i] + step0 * prod0 + step1 * prod1)
    return result


def backward_middle(length, rates, ends, extras):
    devices = len(ends)
    whole = jnp.exp(-float(length) * rates)
    blank = jnp.zeros_like(extras[0][0])
    arriving = jnp.zeros_like(ends[0])
    result = [None] * devices
    for i in reversed(range(devices)):
        result[i] = (arriving, extras[i + 1] if i + 1 < devices else [blank] * len(extras[0]))
        arriving = whole * arriving + ends[i]
    return result


def middle_kernel(s, extra, in_ref, decay_ref, filter_ref, out_ref):
    me = lax.axis_index("seq")
    rows = s.chunk_rows(extra)
    for h in range(s.halves):
        lanes = pl.ds(pl.multiple_of((me + h * SUB) * LANES, LANES), LANES)
        rates = decay_ref[:, lanes]
        ends, extras = [], []
        for i in range(s.devices):
            base = i * rows
            e = base + s.chunk_row(0, h, extra)
            ends.append(in_ref[e : e + s.modes, :])
            x = base + s.chunk_row(s.modes, h, extra)
            extras.append([in_ref[x + r : x + r + 1, :] for r in range(extra)])
        if extra == FORWARD_EXTRA:
            taps = [[filter_ref[i, tap : tap + 1, lanes] for tap in range(3)] for i in range(3)]
            result = forward_middle(s.length, rates, taps, ends, extras)
        else:
            result = backward_middle(s.length, rates, ends, extras)
        for i in range(s.devices):
            base = i * rows
            e = base + s.chunk_row(0, h, extra)
            out_ref[e : e + s.modes, :] = result[i][0]
            x = base + s.chunk_row(s.modes, h, extra)
            for r in range(extra):
                out_ref[x + r : x + r + 1, :] = result[i][1][r]


def exchange(s, pay, decay_rate, short_filter, extra):
    if s.direct:
        got = lax.all_to_all(pay, "seq", 0, 0, tiled=True)
        back = pl.pallas_call(
            functools.partial(middle_kernel, s, extra),
            out_shape=jax.ShapeDtypeStruct(pay.shape, f32),
            compiler_params=pltpu.CompilerParams(vmem_limit_bytes=GRANT),
        )(got, decay_rate, short_filter)
        return lax.all_to_all(back, "seq", 0, 0, tiled=True)
    rows = s.modes + extra
    width = s.channels // s.devices
    start = lax.axis_index("seq") * width
    rates = lax.dynamic_slice_in_dim(decay_rate, start, width, 1)
    part = lax.dynamic_slice_in_dim(short_filter, start, width, 2)
    pay = pay.reshape(rows, s.devices, width).transpose(1, 0, 2)
    got = lax.all_to_all(pay, "seq", 0, 0, tiled=True)
    ends = [got[i, : s.modes] for i in range(s.devices)]
    extras = [[got[i, s.modes + r][None] for r in range(extra)] for i in range(s.devices)]
    if extra == FORWARD_EXTRA:
        taps = [[part[i, tap][None] for tap in range(3)] for i in range(3)]
        result = forward_middle(s.length, rates, taps, ends, extras)
    else:
        result = backward_middle(s.length, rates, ends, extras)
    back = jnp.stack([jnp.concatenate([state] + list(more)) for state, more in result])
    back = lax.all_to_all(back, "seq", 0, 0, tiled=True)
    return back.transpose(1, 0, 2).reshape(rows * s.tiles, LANES)


def inside_kernel(
    s, k_hbm, v_hbm, filter_hbm, decay_hbm, residue_hbm, inside_ref,
    kb, vb, fb, db, rb, ks, vs, prod, taps, poles, weights, sems,
):
    pairs = [(decay_hbm, db), (residue_hbm, rb), (filter_hbm, fb), (k_hbm, kb), (v_hbm, vb)]
    copies = [pltpu.make_async_copy(a, b, sems.at[i]) for i, (a, b) in enumerate(pairs)]
    for copy in copies:
        copy.start()
    for copy in copies:
        copy.wait()
    stage_modes(s, db, poles, lambda x: jnp.exp(-x))
    stage_modes(s, rb, weights, lambda x: x)
    stage_taps(s, fb, taps)
    blank = jnp.zeros((SUB, LANES), f32)
    steps = s.length // 16
    for h in range(s.halves):
        taps_k, taps_v = (tap_tiles(s, taps, i, h) for i in (1, 2))

        def products(i, held):
            stage(s, kb, ks, i, h)
            stage(s, vb, vs, i, h)
            for block, offset in sixteen(i):
                rows = staged(s, block, offset, h)
                k0, v0 = ks[rows, :], vs[rows, :]
                k1, k2, v1, v2 = held
                prod[major(s, block * SUB + offset, h), :] = (
                    mix(taps_k, k0, k1, k2) * mix(taps_v, v0, v1, v2)
                )
                held = (k0, k1, v0, v1)
            return held

        lax.fori_loop(0, steps, products, (blank,) * 4)
        p = mode_tiles(s, poles, h)
        w = mode_tiles(s, weights, h)

        def position(block, offset, states):
            out = major(s, block * SUB + offset, h)
            product = prod[out, :]
            states = [p[m] * states[m] + product for m in range(s.modes)]
            inside_ref[out, :] = total([w[m] * states[m] for m in range(s.modes)])
            return states

        states = [blank] * s.modes
        for block, offset in sixteen(0)[2:]:
            states = position(block, offset, states)

        def step(i, states):
            for block, offset in sixteen(i):
                states = position(block, offset, states)
            return states

        lax.fori_loop(1, steps, step, states)


def forward_kernel(
    s, inside_ref, q_ref, stream_ref, cot_ref, back_ref, filter_ref, decay_ref, residue_ref, gain_ref,
    conv_ref, sums_ref,
    qs, xs, gs, taps, poles, weights, squares, inners,
):
    stage_modes(s, decay_ref, poles, lambda x: jnp.exp(-x))
    stage_modes(s, residue_ref, weights, lambda x: x)
    stage_taps(s, filter_ref, taps)

    def back(r, h):
        return back_ref[s.exchange_slice(r, h, FORWARD_EXTRA), :]

    steps = s.length // 16
    for h in range(s.halves):
        p = mode_tiles(s, poles, h)
        w = mode_tiles(s, weights, h)
        gain = gain_ref[h * SUB : (h + 1) * SUB, :]
        taps_q = tap_tiles(s, taps, 0, h)

        def position(block, offset, held, states, first):
            q1, q2 = held
            rows = staged(s, block, offset, h)
            t = block * SUB + offset
            out = major(s, t, h)
            if first:
                product = back(s.modes + offset, h)
                states = [p[m] * states[m] + product for m in range(s.modes)]
                conv = total([w[m] * states[m] for m in range(s.modes)])
                if offset == 1:
                    states = [w[m] * states[m] for m in range(s.modes)]
            else:
                states = [p[m] * states[m] for m in range(s.modes)]
                conv = inside_ref[out, :] + total(states)
            conv_ref[out, :] = conv
            q0 = qs[rows, :]
            mixed = xs[rows, :] + mix(taps_q, q0, q1, q2) * conv
            square, inner = mixed * mixed, gain * gs[rows, :] * mixed
            part = pl.ds(t * SUB if isinstance(t, int) else pl.multiple_of(t * SUB, SUB), SUB)
            if h:
                square, inner = square + squares[part, :], inner + inners[part, :]
            squares[part, :] = square
            inners[part, :] = inner
            return (q0, q1), states

        def bring(i):
            stage(s, q_ref, qs, i, h)
            stage(s, stream_ref, xs, i, h)
            stage(s, cot_ref, gs, i, h)

        held = (back(s.modes + 7, h), back(s.modes + 6, h))
        states = [back(m, h) for m in range(s.modes)]
        bring(0)
        for block, offset in sixteen(0):
            held, states = position(block, offset, held, states, block == 0 and offset < 2)
        bring(1)

        def step(i, carry):
            held, states = carry
            for block, offset in sixteen(i):
                held, states = position(block, offset, held, states, False)
            bring(jnp.minimum(i + 1, steps - 1))
            return held, states

        lax.fori_loop(1, steps, step, (held, states))
    for r, ref in enumerate((squares, inners)):
        parts = []
        for b in range(s.length // SUB):
            parts.append(
                total([ref[pl.ds(b * SUB * SUB + i, SUB, stride=SUB), :] for i in range(SUB)])
            )
        rows = jnp.concatenate(parts, axis=0)
        sums_ref[r : r + 1, :] = jnp.sum(rows.T, axis=0, keepdims=True)


def norm_kernel(
    s, width, sums_ref, conv_ref, q_ref, stream_ref, cot_ref, back_ref, filter_ref, decay_ref, gain_ref,
    normed_hbm, dstream_hbm, qgrad_hbm, dconv_hbm, tail_ref, pay_ref,
    qs, xs, gs, ns, ds, dconv_ref, normed_b, dstream_b, qgrad_b, taps, poles, inv_s, coef_s, sems,
):
    inverse = lax.rsqrt(sums_ref[0:1, :] / width + epsilon)
    coef = inverse * inverse * inverse * sums_ref[1:2, :] / width
    inv_s[...] = jnp.broadcast_to(inverse, (LANES, s.length)).T
    coef_s[...] = jnp.broadcast_to(coef, (LANES, s.length)).T
    stage_modes(s, decay_ref, poles, lambda x: jnp.exp(-x))
    stage_taps(s, filter_ref, taps)
    blocks = s.length // SUB
    blank = jnp.zeros((SUB, LANES), f32)
    copies = []

    def back(r, h):
        return back_ref[s.exchange_slice(r, h, FORWARD_EXTRA), :]

    steps = s.length // 16
    for h in range(s.halves):
        gain = gain_ref[h * SUB : (h + 1) * SUB, :]
        taps_q = tap_tiles(s, taps, 0, h)

        def position(block, offset, held, first):
            q1, q2, dq1, dq2 = held
            rows = staged(s, block, offset, h)
            t = block * SUB + offset
            out = major(s, t, h)
            inv = jnp.broadcast_to(inv_s[pl.ds(t, 1), :], (SUB, LANES))
            cf = jnp.broadcast_to(coef_s[pl.ds(t, 1), :], (SUB, LANES))
            q0 = qs[rows, :]
            qmix = mix(taps_q, q0, q1, q2)
            conv = conv_ref[out, :]
            mixed = xs[rows, :] + qmix * conv
            dmixed = inv * (gain * gs[rows, :]) - mixed * cf
            ns[rows, :] = mixed * inv * gain
            ds[rows, :] = dmixed
            dq0 = dmixed * conv
            dconv = dmixed * qmix
            dconv_ref[out, :] = dconv
            if first:
                pay_ref[s.exchange_slice(s.modes + 1 + offset, h, BACKWARD_EXTRA), :] = dq0
                if offset == 0:
                    pay_ref[s.exchange_slice(s.modes, h, BACKWARD_EXTRA), :] = dconv
            else:
                qs[staged_before(s, block, offset, h), :] = mix(taps_q, dq2, dq1, dq0)
            return q0, q1, dq0, dq1

        def bring(i):
            stage(s, q_ref, qs, i, h)
            stage(s, stream_ref, xs, i, h)
            stage(s, cot_ref, gs, i, h)

        def leave(i):
            unstage(s, ns, normed_b, i, h)
            unstage(s, ds, dstream_b, i, h)
            unstage(s, qs, qgrad_b, i, h)

        held = (back(s.modes + 7, h), back(s.modes + 6, h), blank, blank)
        bring(0)
        for block, offset in sixteen(0):
            held = position(block, offset, held, block == 0 and offset < 2)
        bring(1)

        def step(i, held):
            for block, offset in sixteen(i):
                held = position(block, offset, held, False)
            leave(i - 1)
            bring(jnp.minimum(i + 1, steps - 1))
            return held

        held = lax.fori_loop(1, steps - 1, step, held)
        for block, offset in sixteen(steps - 1):
            held = position(block, offset, held, False)
        _, _, dq1, dq2 = held
        qs[staged(s, blocks - 1, 6, h), :] = taps_q[0] * dq2 + taps_q[1] * dq1
        qs[staged(s, blocks - 1, 7, h), :] = taps_q[0] * dq1
        leave(steps - 2)
        leave(steps - 1)
        pieces = [
            (normed_b, normed_hbm, s.length),
            (dstream_b, dstream_hbm, s.length),
            (qgrad_b, qgrad_hbm, s.length - 16),
        ]
        for i, (block_ref, to_hbm, rows) in enumerate(pieces):
            cut = (pl.ds(0, rows), pl.ds(h * GROUP, GROUP))
            copy = pltpu.make_async_copy(block_ref.at[cut], to_hbm.at[cut], sems.at[3 * h + i])
            copy.start()
            copies.append(copy)
    copies.append(pltpu.make_async_copy(dconv_ref, dconv_hbm, sems.at[3 * s.halves]))
    copies[-1].start()
    start = (blocks - 2) * s.tiles * SUB
    tail_ref[...] = qs[start : start + 2 * s.tiles * SUB, :]
    for h in range(s.halves):
        p = mode_tiles(s, poles, h)

        def ends(i, states):
            for block, offset in sixteen(steps - 1 - i, reverse=True):
                dconv = dconv_ref[major(s, block * SUB + offset, h), :]
                states = [p[m] * states[m] + dconv for m in range(s.modes)]
            return states

        states = lax.fori_loop(0, steps, ends, [blank] * s.modes)
        for m in range(s.modes):
            pay_ref[s.exchange_slice(m, h, BACKWARD_EXTRA), :] = states[m]
        pay_ref[s.exchange_slice(s.modes + 3, h, BACKWARD_EXTRA), :] = blank
    for copy in copies:
        copy.wait()


def inside_back_kernel(
    s, dconv_hbm, decay_hbm, residue_hbm, inside_ref, cs, db, rb, poles, weights, sems
):
    pairs = [(decay_hbm, db), (residue_hbm, rb), (dconv_hbm, cs)]
    copies = [pltpu.make_async_copy(a, b, sems.at[i]) for i, (a, b) in enumerate(pairs)]
    for copy in copies:
        copy.start()
    for copy in copies:
        copy.wait()
    stage_modes(s, db, poles, lambda x: jnp.exp(-x))
    stage_modes(s, rb, weights, lambda x: x)
    steps = s.length // 16
    for h in range(s.halves):
        p = mode_tiles(s, poles, h)
        w = mode_tiles(s, weights, h)

        def step(i, states):
            for block, offset in sixteen(steps - 1 - i, reverse=True):
                out = major(s, block * SUB + offset, h)
                dconv = cs[out, :]
                states = [p[m] * states[m] + dconv for m in range(s.modes)]
                inside_ref[out, :] = total([w[m] * states[m] for m in range(s.modes)])
            return states

        lax.fori_loop(0, steps, step, [jnp.zeros((SUB, LANES), f32)] * s.modes)


def backward_kernel(
    s, k_ref, v_ref, inside_ref, tail_ref, ahead_ref, back_ref, filter_ref, decay_ref, residue_ref, qgrad_in,
    qgrad_hbm, kgrad_hbm, vgrad_hbm,
    ks, vs, qs, kgrad_b, vgrad_b, qgrad_b, taps, poles, weights, sems,
):
    del qgrad_in
    stage_modes(s, decay_ref, poles, lambda x: jnp.exp(-x))
    stage_modes(s, residue_ref, weights, lambda x: x)
    stage_taps(s, filter_ref, taps)
    blocks = s.length // SUB
    copies = []

    def near(r, h):
        return ahead_ref[s.exchange_slice(s.modes + r, h, FORWARD_EXTRA), :]

    def back(r, h):
        return back_ref[s.exchange_slice(r, h, BACKWARD_EXTRA), :]

    qs[...] = tail_ref[...]
    for h in range(s.halves):
        taps_q = tap_tiles(s, taps, 0, h)
        dq0, dq1 = back(s.modes + 1, h), back(s.modes + 2, h)
        rows = [staged(s, 1, offset, h) for offset in (6, 7)]
        qs[rows[0], :] = qs[rows[0], :] + taps_q[2] * dq0
        qs[rows[1], :] = qs[rows[1], :] + (taps_q[1] * dq0 + taps_q[2] * dq1)
        unstage(s, qs, qgrad_b, 0, h)
    copy = pltpu.make_async_copy(qgrad_b, qgrad_hbm.at[pl.ds(s.length - 16, 16), :], sems.at[0])
    copy.start()
    copies.append(copy)
    steps = s.length // 16
    for h in range(s.halves):
        p = mode_tiles(s, poles, h)
        w = mode_tiles(s, weights, h)
        taps_k, taps_v = (tap_tiles(s, taps, i, h) for i in (1, 2))

        def bring(i):
            stage(s, k_ref, ks, i, h)
            stage(s, v_ref, vs, i, h)

        def leave(i):
            unstage(s, ks, kgrad_b, i, h)
            unstage(s, vs, vgrad_b, i, h)

        def advance(inputs, grads, k2, v2, d):
            k0, k1, v0, v1 = inputs
            dk1, dk2, dv1, dv2 = grads
            dk0 = d * mix(taps_v, v0, v1, v2)
            dv0 = d * mix(taps_k, k0, k1, k2)
            out = mix(taps_k, dk0, dk1, dk2), mix(taps_v, dv0, dv1, dv2)
            return (k1, k2, v1, v2), (dk0, dk1, dv0, dv1), out

        def position(block, offset, carry, before=None):
            states, inputs, grads = carry
            states = [p[m] * states[m] for m in range(s.modes)]
            d = inside_ref[major(s, block * SUB + offset, h), :] + total(states)
            if before is None:
                rows = staged_before(s, block, offset, h)
                before = ks[rows, :], vs[rows, :]
            inputs, grads, out = advance(inputs, grads, *before, d)
            rows = staged(s, block, offset, h)
            ks[rows, :], vs[rows, :] = out
            return states, inputs, grads

        bring(steps - 1)
        bring(steps - 2)
        ka, kb, va, vb, _, _, kc, kd, vc, vd = (near(2 + r, h) for r in range(10))
        arriving = [back(m, h) for m in range(s.modes)]
        dconv0 = back(s.modes, h)
        d0 = total([w[m] * arriving[m] for m in range(s.modes)])
        d1 = total([w[m] * ((arriving[m] - dconv0) / p[m]) for m in range(s.modes)])
        ends = [staged(s, blocks - 1, offset, h) for offset in (6, 7)]
        inputs = (kd, kc, vd, vc)
        grads = (jnp.zeros((SUB, LANES), f32),) * 4
        inputs, grads, _ = advance(inputs, grads, ks[ends[1], :], vs[ends[1], :], d1)
        inputs, grads, _ = advance(inputs, grads, ks[ends[0], :], vs[ends[0], :], d0)

        def step(i, carry):
            i = steps - 1 - i
            for block, offset in sixteen(i, reverse=True):
                carry = position(block, offset, carry)
            leave(i)
            bring(jnp.maximum(i - 2, 0))
            return carry

        states = [w[m] * arriving[m] for m in range(s.modes)]
        carry = lax.fori_loop(0, steps - 1, step, (states, inputs, grads))
        for block, offset in sixteen(0, reverse=True):
            first = block == 0 and offset < 2
            carry = position(block, offset, carry, ((ka, va), (kb, vb))[offset] if first else None)
        leave(0)
        for i, (block_ref, to_hbm) in enumerate([(kgrad_b, kgrad_hbm), (vgrad_b, vgrad_hbm)]):
            cut = (pl.ds(0, s.length), pl.ds(h * GROUP, GROUP))
            copy = pltpu.make_async_copy(block_ref.at[cut], to_hbm.at[cut], sems.at[1 + 2 * h + i])
            copy.start()
            copies.append(copy)
    for copy in copies:
        copy.wait()


def body(
    query_in, key_in, value_in, stream, short_filter, decay_rate, residue, norm_gain, cotangent
):
    length, channels = query_in.shape
    modes = decay_rate.shape[0]
    s = Sizes(length, channels, modes, lax.axis_size("seq"))
    total_width = channels * lax.axis_size("tp")
    wide = jax.ShapeDtypeStruct((length * s.tiles, LANES), f32)
    narrow = jax.ShapeDtypeStruct((length, channels), bf16)
    rows = 16 * s.tiles
    wide_s = pltpu.VMEM(wide.shape, f32)
    narrow_s = pltpu.VMEM(narrow.shape, bf16)
    last_s = pltpu.VMEM((16, channels), bf16)
    tail_s = pltpu.VMEM((rows, LANES), f32)
    taps_s = pltpu.VMEM((3 * s.tiles * SUB, LANES), f32)
    mode_s = pltpu.VMEM((modes * s.tiles, LANES), f32)
    sum_s = pltpu.VMEM((length * SUB, LANES), f32)
    square_s = pltpu.VMEM((length, LANES), f32)
    gain = norm_gain.reshape(s.tiles, LANES)
    there = pl.BlockSpec(memory_space=pltpu.HBM)
    here = pl.BlockSpec(memory_space=pltpu.VMEM)

    def call(kernel, ins, outs, out_shape, scratch_shapes, operands, aliases={}, cost=None):
        return pl.pallas_call(
            functools.partial(kernel, s),
            in_specs=[there if c == "h" else here for c in ins],
            out_specs=[there if c == "h" else here for c in outs],
            out_shape=out_shape,
            scratch_shapes=scratch_shapes,
            input_output_aliases=aliases,
            cost_estimate=cost,
            compiler_params=pltpu.CompilerParams(vmem_limit_bytes=GRANT),
        )(*operands)

    def pay_shape(extra):
        return jax.ShapeDtypeStruct(s.exchange_shape(extra), f32)

    def far(*arrays):
        return [pltpu.with_memory_space_constraint(x, pltpu.HBM) for x in arrays]

    def cost(per_element, arrays):
        return pl.CostEstimate(
            flops=per_element * length * channels, bytes_accessed=arrays * 4 * length * channels, transcendentals=0
        )

    filter_s = pltpu.VMEM(short_filter.shape, f32)
    rates_s = pltpu.VMEM(decay_rate.shape, f32)
    (pay,) = call(
        begin_kernel, "hhhhh", "v",
        (pay_shape(FORWARD_EXTRA),),
        [narrow_s, narrow_s, last_s, filter_s, rates_s]
        + [wide_s, wide_s, tail_s, taps_s, mode_s, pltpu.SemaphoreType.DMA((3 + 2 * s.halves,))],
        far(query_in, key_in, value_in, short_filter, decay_rate),
    )
    (inside,) = call(
        inside_kernel, "hhhhh", "v", (wide,),
        [narrow_s, narrow_s, filter_s, rates_s, rates_s]
        + [wide_s] * 3 + [taps_s, mode_s, mode_s, pltpu.SemaphoreType.DMA((5,))],
        far(key_in, value_in, short_filter, decay_rate, residue),
        cost=cost(75, 3),
    )
    back = exchange(s, pay, decay_rate, short_filter, FORWARD_EXTRA)
    conv, sums = call(
        forward_kernel, "v" * 9, "vv",
        (wide, jax.ShapeDtypeStruct((2, length), f32)),
        [wide_s] * 3 + [taps_s, mode_s, mode_s, sum_s, sum_s],
        (inside, query_in, stream, cotangent, back, short_filter, decay_rate, residue, gain),
        {0: 0},
    )
    sums = lax.psum(sums, "tp")
    normed, dstream, query_grad, dconv, tail, pay_back = call(
        lambda s, *refs: norm_kernel(s, total_width, *refs), "v" * 9, "hhhhvv",
        (narrow, narrow, narrow, wide, jax.ShapeDtypeStruct((rows, LANES), f32), pay_shape(BACKWARD_EXTRA)),
        [wide_s] * 6 + [narrow_s] * 3
        + [taps_s, mode_s, square_s, square_s, pltpu.SemaphoreType.DMA((3 * s.halves + 1,))],
        (sums, conv, query_in, stream, cotangent, back, short_filter, decay_rate, gain),
    )
    (inside_back,) = call(
        inside_back_kernel, "hhh", "v", (wide,),
        [wide_s, rates_s, rates_s, mode_s, mode_s, pltpu.SemaphoreType.DMA((3,))],
        far(dconv, decay_rate, residue),
        cost=cost(64, 3),
    )
    back_back = exchange(s, pay_back, decay_rate, short_filter, BACKWARD_EXTRA)
    query_grad, key_grad, value_grad = call(
        backward_kernel, "v" * 9 + "h", "hhh",
        (narrow, narrow, narrow),
        [wide_s] * 2 + [tail_s] + [narrow_s] * 2 + [last_s, taps_s, mode_s, mode_s]
        + [pltpu.SemaphoreType.DMA((1 + 2 * s.halves,))],
        (key_in, value_in, inside_back, tail, back, back_back, short_filter, decay_rate, residue, query_grad),
        {9: 0},
    )
    return (normed, dstream, query_grad, key_grad, value_grad)


def solution(mesh):
    cut = P("seq", "tp")
    return jax.shard_map(
        body,
        mesh=mesh,
        in_specs=(cut, cut, cut, cut, P(None, None, "tp"), P(None, "tp"), P(None, "tp"), P("tp"), cut),
        out_specs=(cut,) * 5,
        check_vma=False,
    )
```

```python
import functools

import jax
import jax.numpy as jnp
from jax import lax
from jax.experimental import pallas as pl
from jax.experimental.pallas import tpu as pltpu
from jax.sharding import PartitionSpec as P

f32 = jnp.float32
bf16 = jnp.bfloat16
epsilon = 1e-05
LANES = 128
SUB = 8
GROUP = LANES * SUB
FORWARD_EXTRA = 12
BACKWARD_EXTRA = 4
GRANT = 20 * 1024 * 1024


class Sizes:
    def __init__(self, length, channels, modes, devices):
        self.length, self.channels, self.modes, self.devices = length, channels, modes, devices
        self.tiles = channels // LANES
        self.halves = channels // GROUP
        self.direct = devices == SUB

    def chunk_row(self, r, h, extra):
        if r < self.modes:
            return h * self.modes + r
        return self.halves * self.modes + h * extra + r - self.modes

    def chunk_rows(self, extra):
        return self.halves * (self.modes + extra)

    def exchange_shape(self, extra):
        if self.direct:
            return (self.devices * self.chunk_rows(extra), LANES)
        return ((self.modes + extra) * self.tiles, LANES)

    def exchange_slice(self, r, h, extra):
        if self.direct:
            return pl.ds(self.chunk_row(r, h, extra), SUB, stride=self.chunk_rows(extra))
        return pl.ds(r * self.tiles + h * SUB, SUB)


def staged(s, block, offset, h):
    start = block * (s.tiles * SUB) + (h * SUB * SUB + offset)
    return pl.ds(start, SUB, stride=SUB)


def major(s, t, h):
    start = t * s.tiles + h * SUB
    if not isinstance(start, int):
        start = pl.multiple_of(start, SUB)
    return pl.ds(start, SUB)


def staged_before(s, block, offset, h):
    if offset < 2:
        return staged(s, block - 1, offset + SUB - 2, h)
    return staged(s, block, offset - 2, h)


def aligned(start, unit):
    return start if isinstance(start, int) else pl.multiple_of(start, unit)


def columns(h):
    return pl.ds(aligned(h * GROUP, GROUP), GROUP)


def stage(s, x_ref, out_ref, i, h, pad=0):
    rows = x_ref[pl.ds(aligned(i * 16, 16), 16), columns(h)].astype(f32)
    base = (i + pad) * (2 * s.tiles * SUB) + h * (SUB * SUB)
    for part in range(2):
        for j in range(SUB):
            out_ref[pl.ds(aligned(base + (part * s.tiles + j) * SUB, SUB), SUB), :] = rows[
                part * SUB : (part + 1) * SUB, j * LANES : (j + 1) * LANES
            ]


def unstage(s, in_ref, x_ref, i, h, to=None):
    base = i * (2 * s.tiles * SUB) + h * (SUB * SUB)
    rows = [
        jnp.concatenate(
            [
                in_ref[pl.ds(aligned(base + (part * s.tiles + j) * SUB, SUB), SUB), :]
                for part in range(2)
            ],
            axis=0,
        )
        for j in range(SUB)
    ]
    to = i if to is None else to
    x_ref[pl.ds(aligned(to * 16, 16), 16), columns(h)] = jnp.concatenate(rows, axis=1).astype(bf16)


def stage_wide(s, x_ref, out_ref):
    for h in range(s.halves):
        stage(s, x_ref, out_ref, 0, h)


def each_half(s, body):
    def step(h, carry):
        body(h)
        return carry

    lax.fori_loop(0, s.halves, step, 0)


def sixteen(i, reverse=False):
    pairs = [(2 * i + part, offset) for part in range(2) for offset in range(SUB)]
    return pairs[::-1] if reverse else pairs


def stage_modes(s, x_ref, out_ref, f):
    for g in range(s.modes // SUB):
        rows = f(x_ref[g * SUB : (g + 1) * SUB, :])
        for j in range(s.tiles):
            start = (g * s.tiles + j) * SUB
            out_ref[start : start + SUB, :] = rows[:, j * LANES : (j + 1) * LANES]


def mode_tiles(s, ref, h):
    return [ref[staged(s, m // SUB, m % SUB, h), :] for m in range(s.modes)]


def stage_taps(s, filter_ref, out_ref):
    for i in range(3):
        rows = filter_ref[i]
        for j in range(s.tiles):
            start = (i * s.tiles + j) * SUB
            out_ref[start : start + 3, :] = rows[:, j * LANES : (j + 1) * LANES]


def tap_tiles(s, ref, i, h):
    return [ref[staged(s, i, tap, h), :] for tap in range(3)]


def total(parts):
    while len(parts) > 1:
        parts = [
            parts[i] + parts[i + 1] if i + 1 < len(parts) else parts[i]
            for i in range(0, len(parts), 2)
        ]
    return parts[0]


def mix(taps, now, before, before2):
    return taps[0] * now + taps[1] * before + taps[2] * before2


def recur(s, from_ref, to_ref, p, w, states, h, reverse=False):
    steps = s.length // 16

    def step(i, states):
        i = steps - 1 - i if reverse else i
        for block, offset in sixteen(0, reverse):
            rows = major(s, (2 * i + block) * SUB + offset, h)
            signal = from_ref[rows, :]
            states = [p[m] * states[m] + signal for m in range(s.modes)]
            to_ref[rows, :] = total([w[m] * states[m] for m in range(s.modes)])
        return states

    lax.fori_loop(0, steps, step, states)


def begin_kernel(
    s, q_hbm, k_hbm, v_hbm, filter_hbm, decay_hbm, pay_ref,
    kb, vb, qb, fb, db, ks, vs, qs, taps, poles, sems,
):
    copies = [(decay_hbm, db), (filter_hbm, fb), (q_hbm.at[pl.ds(s.length - 16, 16), :], qb)]
    for h in range(s.halves):
        cut = pl.ds(h * GROUP, GROUP)
        copies += [(k_hbm.at[:, cut], kb.at[:, cut]), (v_hbm.at[:, cut], vb.at[:, cut])]
    copies = [pltpu.make_async_copy(a, b, sems.at[i]) for i, (a, b) in enumerate(copies)]
    for copy in copies:
        copy.start()
    copies[0].wait()
    stage_modes(s, db, poles, lambda x: jnp.exp(-x))
    copies[1].wait()
    stage_taps(s, fb, taps)
    blank = jnp.zeros((SUB, LANES), f32)
    steps = s.length // 16
    copies[2].wait()
    stage_wide(s, qb, qs)

    def half(h):
        for i, (from_hbm, to) in enumerate(((k_hbm, kb), (v_hbm, vb))):
            cut = columns(h)
            pltpu.make_async_copy(from_hbm.at[:, cut], to.at[:, cut], sems.at[3 + 2 * h + i]).wait()
        p = mode_tiles(s, poles, h)
        taps_k, taps_v = (tap_tiles(s, taps, i, h) for i in (1, 2))

        def bring(i):
            stage(s, kb, ks, i, h)
            stage(s, vb, vs, i, h)

        def step(i, carry):
            (k1, k2, v1, v2), states = carry
            for block, offset in sixteen(0):
                rows = staged(s, 2 * i + block, offset, h)
                k0, v0 = ks[rows, :], vs[rows, :]
                product = mix(taps_k, k0, k1, k2) * mix(taps_v, v0, v1, v2)
                if block == 0 and offset < 2:
                    product = jnp.where(i == 0, 0.0, product)
                states = [p[m] * states[m] + product for m in range(s.modes)]
                k1, k2, v1, v2 = k0, k1, v0, v1
            bring(jnp.minimum(i + 1, steps - 1))
            return (k1, k2, v1, v2), states

        bring(0)
        held, states = lax.fori_loop(0, steps, step, ((blank,) * 4, [blank] * s.modes))
        for m in range(s.modes):
            pay_ref[s.exchange_slice(m, h, FORWARD_EXTRA), :] = states[m]
        k1, k2, v1, v2 = held
        first = [staged(s, 0, offset, h) for offset in range(2)]
        last = [staged(s, 1, offset, h) for offset in (6, 7)]
        extra = [
            ks[first[0], :], ks[first[1], :], k2, k1,
            vs[first[0], :], vs[first[1], :], v2, v1,
            qs[last[0], :], qs[last[1], :], blank, blank,
        ]
        for r, value in enumerate(extra):
            pay_ref[s.exchange_slice(s.modes + r, h, FORWARD_EXTRA), :] = value

    each_half(s, half)


def forward_middle(length, rates, taps, ends, extras):
    devices = len(ends)
    whole, step0, step1 = (jnp.exp(-float(length - i) * rates) for i in range(3))
    blank = jnp.zeros_like(extras[0][0])
    arriving = jnp.zeros_like(ends[0])
    result = []
    for i in range(devices):
        k0, k1, _, _, v0, v1 = extras[i][:6]
        if i:
            _, _, ka, kb, _, _, va, vb, qa, qb = extras[i - 1][:10]
        else:
            ka = kb = va = vb = qa = qb = blank
        if i + 1 < devices:
            kc, kd, _, _, vc, vd = extras[i + 1][:6]
        else:
            kc = kd = vc = vd = blank
        prod0 = mix(taps[1], k0, kb, ka) * mix(taps[2], v0, vb, va)
        prod1 = mix(taps[1], k1, k0, kb) * mix(taps[2], v1, v0, vb)
        result.append((arriving, [prod0, prod1, ka, kb, va, vb, qa, qb, kc, kd, vc, vd]))
        arriving = whole * arriving + (ends[i] + step0 * prod0 + step1 * prod1)
    return result


def backward_middle(length, rates, ends, extras):
    devices = len(ends)
    whole = jnp.exp(-float(length) * rates)
    blank = jnp.zeros_like(extras[0][0])
    arriving = jnp.zeros_like(ends[0])
    result = [None] * devices
    for i in reversed(range(devices)):
        result[i] = (arriving, extras[i + 1] if i + 1 < devices else [blank] * len(extras[0]))
        arriving = whole * arriving + ends[i]
    return result


def middle_kernel(s, extra, in_ref, decay_ref, filter_ref, out_ref):
    me = lax.axis_index("seq")
    rows = s.chunk_rows(extra)
    for h in range(s.halves):
        lanes = pl.ds(pl.multiple_of((me + h * SUB) * LANES, LANES), LANES)
        rates = decay_ref[:, lanes]
        ends, extras = [], []
        for i in range(s.devices):
            base = i * rows
            e = base + s.chunk_row(0, h, extra)
            ends.append(in_ref[e : e + s.modes, :])
            x = base + s.chunk_row(s.modes, h, extra)
            extras.append([in_ref[x + r : x + r + 1, :] for r in range(extra)])
        if extra == FORWARD_EXTRA:
            taps = [[filter_ref[i, tap : tap + 1, lanes] for tap in range(3)] for i in range(3)]
            result = forward_middle(s.length, rates, taps, ends, extras)
        else:
            result = backward_middle(s.length, rates, ends, extras)
        for i in range(s.devices):
            base = i * rows
            e = base + s.chunk_row(0, h, extra)
            out_ref[e : e + s.modes, :] = result[i][0]
            x = base + s.chunk_row(s.modes, h, extra)
            for r in range(extra):
                out_ref[x + r : x + r + 1, :] = result[i][1][r]


def exchange(s, pay, decay_rate, short_filter, extra):
    if s.direct:
        got = lax.all_to_all(pay, "seq", 0, 0, tiled=True)
        back = pl.pallas_call(
            functools.partial(middle_kernel, s, extra),
            out_shape=jax.ShapeDtypeStruct(pay.shape, f32),
            compiler_params=pltpu.CompilerParams(vmem_limit_bytes=GRANT),
        )(got, decay_rate, short_filter)
        return lax.all_to_all(back, "seq", 0, 0, tiled=True)
    rows = s.modes + extra
    width = s.channels // s.devices
    start = lax.axis_index("seq") * width
    rates = lax.dynamic_slice_in_dim(decay_rate, start, width, 1)
    part = lax.dynamic_slice_in_dim(short_filter, start, width, 2)
    pay = pay.reshape(rows, s.devices, width).transpose(1, 0, 2)
    got = lax.all_to_all(pay, "seq", 0, 0, tiled=True)
    ends = [got[i, : s.modes] for i in range(s.devices)]
    extras = [[got[i, s.modes + r][None] for r in range(extra)] for i in range(s.devices)]
    if extra == FORWARD_EXTRA:
        taps = [[part[i, tap][None] for tap in range(3)] for i in range(3)]
        result = forward_middle(s.length, rates, taps, ends, extras)
    else:
        result = backward_middle(s.length, rates, ends, extras)
    back = jnp.stack([jnp.concatenate([state] + list(more)) for state, more in result])
    back = lax.all_to_all(back, "seq", 0, 0, tiled=True)
    return back.transpose(1, 0, 2).reshape(rows * s.tiles, LANES)


def inside_kernel(
    s, k_hbm, v_hbm, filter_hbm, decay_hbm, residue_hbm, inside_ref,
    kb, vb, fb, db, rb, ks, vs, prod, taps, poles, weights, sems,
):
    pairs = [(decay_hbm, db), (residue_hbm, rb), (filter_hbm, fb), (k_hbm, kb), (v_hbm, vb)]
    copies = [pltpu.make_async_copy(a, b, sems.at[i]) for i, (a, b) in enumerate(pairs)]
    for copy in copies:
        copy.start()
    for copy in copies:
        copy.wait()
    stage_modes(s, db, poles, lambda x: jnp.exp(-x))
    stage_modes(s, rb, weights, lambda x: x)
    stage_taps(s, fb, taps)
    blank = jnp.zeros((SUB, LANES), f32)
    steps = s.length // 16

    def half(h):
        taps_k, taps_v = (tap_tiles(s, taps, i, h) for i in (1, 2))

        def products(i, held):
            stage(s, kb, ks, i, h)
            stage(s, vb, vs, i, h)
            k1, k2, v1, v2 = held
            for block, offset in sixteen(0):
                rows = staged(s, 2 * i + block, offset, h)
                k0, v0 = ks[rows, :], vs[rows, :]
                product = mix(taps_k, k0, k1, k2) * mix(taps_v, v0, v1, v2)
                if block == 0 and offset < 2:
                    product = jnp.where(i == 0, 0.0, product)
                prod[major(s, (2 * i + block) * SUB + offset, h), :] = product
                k1, k2, v1, v2 = k0, k1, v0, v1
            return k1, k2, v1, v2

        lax.fori_loop(0, steps, products, (blank,) * 4)
        recur(s, prod, inside_ref, mode_tiles(s, poles, h), mode_tiles(s, weights, h), [blank] * s.modes, h)

    each_half(s, half)


def forward_kernel(
    s, inside_ref, q_ref, stream_ref, cot_ref, back_ref, filter_ref, decay_ref, residue_ref, gain_ref,
    conv_ref, sums_ref,
    qs, xs, gs, taps, poles, weights, squares, inners,
):
    stage_modes(s, decay_ref, poles, lambda x: jnp.exp(-x))
    stage_modes(s, residue_ref, weights, lambda x: x)
    stage_taps(s, filter_ref, taps)

    def back(r, h):
        return back_ref[s.exchange_slice(r, h, FORWARD_EXTRA), :]

    steps = s.length // 16

    def half(h):
        p = mode_tiles(s, poles, h)
        w = mode_tiles(s, weights, h)
        gain = gain_ref[pl.ds(aligned(h * SUB, SUB), SUB), :]
        taps_q = tap_tiles(s, taps, 0, h)
        conv, states = [], [back(m, h) for m in range(s.modes)]
        for offset in range(2):
            product = back(s.modes + offset, h)
            states = [p[m] * states[m] + product for m in range(s.modes)]
            conv.append(total([w[m] * states[m] for m in range(s.modes)]))
        states = [w[m] * states[m] / (p[m] * p[m]) for m in range(s.modes)]
        first, ahead = [], states
        for offset in range(2):
            ahead = [p[m] * ahead[m] for m in range(s.modes)]
            first.append(conv[offset] - total(ahead))

        def bring(i):
            stage(s, q_ref, qs, i, h)
            stage(s, stream_ref, xs, i, h)
            stage(s, cot_ref, gs, i, h)

        def step(i, carry):
            (q1, q2), states = carry
            for block, offset in sixteen(0):
                rows = staged(s, 2 * i + block, offset, h)
                t = (2 * i + block) * SUB + offset
                out = major(s, t, h)
                inside = inside_ref[out, :]
                if block == 0 and offset < 2:
                    inside = jnp.where(i == 0, first[offset], inside)
                states = [p[m] * states[m] for m in range(s.modes)]
                conv = inside + total(states)
                conv_ref[out, :] = conv
                q0 = qs[rows, :]
                mixed = xs[rows, :] + mix(taps_q, q0, q1, q2) * conv
                part = pl.ds(pl.multiple_of(t * SUB, SUB), SUB)
                square, inner = mixed * mixed, gain * gs[rows, :] * mixed
                squares[part, :] = square + jnp.where(h == 0, 0.0, squares[part, :])
                inners[part, :] = inner + jnp.where(h == 0, 0.0, inners[part, :])
                q1, q2 = q0, q1
            bring(jnp.minimum(i + 1, steps - 1))
            return (q1, q2), states

        bring(0)
        lax.fori_loop(0, steps, step, ((back(s.modes + 7, h), back(s.modes + 6, h)), states))

    each_half(s, half)
    for r, ref in enumerate((squares, inners)):
        parts = []
        for b in range(s.length // SUB):
            parts.append(
                total([ref[pl.ds(b * SUB * SUB + i, SUB, stride=SUB), :] for i in range(SUB)])
            )
        rows = jnp.concatenate(parts, axis=0)
        sums_ref[r : r + 1, :] = jnp.sum(rows.T, axis=0, keepdims=True)


def norm_kernel(
    s, width, sums_ref, conv_ref, q_ref, stream_ref, cot_ref, back_ref, filter_ref, decay_ref, gain_ref,
    normed_hbm, dstream_hbm, qgrad_hbm, dconv_ref, tail_ref, pay_ref,
    qs, xs, gs, ns, ds, normed_b, dstream_b, qgrad_b, taps, poles, inv_s, coef_s, sems,
):
    inverse = lax.rsqrt(sums_ref[0:1, :] / width + epsilon)
    coef = inverse * inverse * inverse * sums_ref[1:2, :] / width
    inv_s[...] = jnp.broadcast_to(inverse, (LANES, s.length)).T
    coef_s[...] = jnp.broadcast_to(coef, (LANES, s.length)).T
    stage_modes(s, decay_ref, poles, lambda x: jnp.exp(-x))
    stage_taps(s, filter_ref, taps)
    blank = jnp.zeros((SUB, LANES), f32)
    steps = s.length // 16

    def back(r, h):
        return back_ref[s.exchange_slice(r, h, FORWARD_EXTRA), :]

    def pieces(h):
        cut = columns(h)
        sources = [
            (normed_b.at[:, cut], normed_hbm.at[:, cut]),
            (dstream_b.at[:, cut], dstream_hbm.at[:, cut]),
            (qgrad_b.at[pl.ds(16, s.length - 16), cut], qgrad_hbm.at[pl.ds(0, s.length - 16), cut]),
        ]
        return [pltpu.make_async_copy(a, b, sems.at[3 * h + i]) for i, (a, b) in enumerate(sources)]

    def half(h):
        gain = gain_ref[pl.ds(aligned(h * SUB, SUB), SUB), :]
        taps_q = tap_tiles(s, taps, 0, h)

        def bring(i):
            rows = jnp.minimum(i, steps - 1)
            stage(s, q_ref, qs, rows, h, i - rows + 1)
            stage(s, stream_ref, xs, rows, h)
            stage(s, cot_ref, gs, rows, h)

        def step(i, held):
            q1, q2, dq1, dq2 = held
            for block, offset in sixteen(0):
                rows = staged(s, 2 * i + block, offset, h)
                t = (2 * i + block) * SUB + offset
                out = major(s, t, h)
                inv = jnp.broadcast_to(inv_s[pl.ds(t, 1), :], (SUB, LANES))
                cf = jnp.broadcast_to(coef_s[pl.ds(t, 1), :], (SUB, LANES))
                q0 = qs[staged(s, 2 * i + block + 2, offset, h), :]
                qmix = mix(taps_q, q0, q1, q2)
                conv = conv_ref[out, :]
                mixed = xs[rows, :] + qmix * conv
                dmixed = inv * (gain * gs[rows, :]) - mixed * cf
                ns[rows, :] = mixed * inv * gain
                ds[rows, :] = dmixed
                dq0 = dmixed * conv
                dconv_ref[out, :] = dmixed * qmix
                qs[staged_before(s, 2 * i + block + 2, offset, h), :] = mix(taps_q, dq2, dq1, dq0)
                q1, q2, dq1, dq2 = q0, q1, dq0, dq1
            unstage(s, ns, normed_b, i, h)
            unstage(s, ds, dstream_b, i, h)
            unstage(s, qs, qgrad_b, i, h)
            bring(i + 1)
            return q1, q2, dq1, dq2

        bring(0)
        held = (back(s.modes + 7, h), back(s.modes + 6, h), blank, blank)
        _, _, dq1, dq2 = lax.fori_loop(0, steps, step, held)
        qs[staged(s, 2 * steps + 1, 6, h), :] = taps_q[0] * dq2 + taps_q[1] * dq1
        qs[staged(s, 2 * steps + 1, 7, h), :] = taps_q[0] * dq1
        for copy in pieces(h):
            copy.start()

    each_half(s, half)
    start = steps * 2 * s.tiles * SUB
    tail_ref[...] = qs[start : start + 2 * s.tiles * SUB, :]

    def ends(h):
        p = mode_tiles(s, poles, h)

        def step(i, states):
            for block, offset in sixteen(0, True):
                t = (2 * (steps - 1 - i) + block) * SUB + offset
                dconv = dconv_ref[major(s, t, h), :]
                states = [p[m] * states[m] + dconv for m in range(s.modes)]
            return states

        states = lax.fori_loop(0, steps, step, [blank] * s.modes)
        for m in range(s.modes):
            pay_ref[s.exchange_slice(m, h, BACKWARD_EXTRA), :] = states[m]
        first = [ds[staged(s, 0, offset, h), :] * conv_ref[major(s, offset, h), :] for offset in range(2)]
        for r, value in enumerate([dconv_ref[major(s, 0, h), :], *first, blank]):
            pay_ref[s.exchange_slice(s.modes + r, h, BACKWARD_EXTRA), :] = value

    each_half(s, ends)

    def finish(h):
        for copy in pieces(h):
            copy.wait()

    each_half(s, finish)


def backward_kernel(
    s, k_ref, v_ref, dconv_ref, tail_ref, ahead_ref, back_ref, filter_ref, decay_ref, residue_ref, qgrad_in,
    qgrad_hbm, kgrad_hbm, vgrad_hbm,
    ks, vs, dprod, qs, kgrad_b, vgrad_b, qgrad_b, taps, poles, weights, sems,
):
    del qgrad_in
    stage_modes(s, decay_ref, poles, lambda x: jnp.exp(-x))
    stage_modes(s, residue_ref, weights, lambda x: x)
    stage_taps(s, filter_ref, taps)
    steps = s.length // 16

    def near(r, h):
        return ahead_ref[s.exchange_slice(s.modes + r, h, FORWARD_EXTRA), :]

    def back(r, h):
        return back_ref[s.exchange_slice(r, h, BACKWARD_EXTRA), :]

    qs[...] = tail_ref[...]

    def tails(h):
        taps_q = tap_tiles(s, taps, 0, h)
        dq0, dq1 = back(s.modes + 1, h), back(s.modes + 2, h)
        rows = [staged(s, 1, offset, h) for offset in (6, 7)]
        qs[rows[0], :] = qs[rows[0], :] + taps_q[2] * dq0
        qs[rows[1], :] = qs[rows[1], :] + (taps_q[1] * dq0 + taps_q[2] * dq1)
        unstage(s, qs, qgrad_b, 0, h)

    each_half(s, tails)
    last = pltpu.make_async_copy(qgrad_b, qgrad_hbm.at[pl.ds(s.length - 16, 16), :], sems.at[2 * s.halves])
    last.start()

    def pieces(h):
        cut = columns(h)
        sources = [(kgrad_b, kgrad_hbm), (vgrad_b, vgrad_hbm)]
        return [
            pltpu.make_async_copy(a.at[:, cut], b.at[:, cut], sems.at[2 * h + i])
            for i, (a, b) in enumerate(sources)
        ]

    def half(h):
        p = mode_tiles(s, poles, h)
        w = mode_tiles(s, weights, h)
        arriving = [back(m, h) for m in range(s.modes)]
        recur(s, dconv_ref, dprod, p, w, arriving, h, reverse=True)
        taps_k, taps_v = (tap_tiles(s, taps, i, h) for i in (1, 2))

        def bring(i):
            stage(s, k_ref, ks, i, h, 1)
            stage(s, v_ref, vs, i, h, 1)

        def advance(inputs, grads, k2, v2, d):
            k0, k1, v0, v1 = inputs
            dk1, dk2, dv1, dv2 = grads
            dk0 = d * mix(taps_v, v0, v1, v2)
            dv0 = d * mix(taps_k, k0, k1, k2)
            out = mix(taps_k, dk0, dk1, dk2), mix(taps_v, dv0, dv1, dv2)
            return (k1, k2, v1, v2), (dk0, dk1, dv0, dv1), out

        bring(steps - 1)
        ka, kb, va, vb, _, _, kc, kd, vc, vd = (near(2 + r, h) for r in range(10))
        for ref, rows in ((ks, (ka, kb)), (vs, (va, vb))):
            for offset in range(2):
                ref[staged(s, 1, 6 + offset, h), :] = rows[offset]
        arriving = [back(m, h) for m in range(s.modes)]
        dconv0 = back(s.modes, h)
        d0 = total([w[m] * arriving[m] for m in range(s.modes)])
        d1 = total([w[m] * ((arriving[m] - dconv0) / p[m]) for m in range(s.modes)])
        ends = [staged(s, 2 * steps + 1, offset, h) for offset in (6, 7)]
        inputs = (kd, kc, vd, vc)
        grads = (jnp.zeros((SUB, LANES), f32),) * 4
        inputs, grads, _ = advance(inputs, grads, ks[ends[1], :], vs[ends[1], :], d1)
        inputs, grads, _ = advance(inputs, grads, ks[ends[0], :], vs[ends[0], :], d0)

        def step(i, carry):
            inputs, grads = carry
            i = steps - 1 - i

            @pl.when(i > 0)
            def _():
                bring(jnp.maximum(i - 1, 0))

            for block, offset in sixteen(0, True):
                d = dprod[major(s, (2 * i + block) * SUB + offset, h), :]
                rows = staged_before(s, 2 * i + block + 2, offset, h)
                inputs, grads, out = advance(inputs, grads, ks[rows, :], vs[rows, :], d)
                rows = staged(s, 2 * i + block + 2, offset, h)
                ks[rows, :], vs[rows, :] = out
            unstage(s, ks, kgrad_b, i + 1, h, i)
            unstage(s, vs, vgrad_b, i + 1, h, i)
            return inputs, grads

        lax.fori_loop(0, steps, step, (inputs, grads))
        for copy in pieces(h):
            copy.start()

    each_half(s, half)
    last.wait()

    def finish(h):
        for copy in pieces(h):
            copy.wait()

    each_half(s, finish)


def body(
    query_in, key_in, value_in, stream, short_filter, decay_rate, residue, norm_gain, cotangent
):
    length, channels = query_in.shape
    modes = decay_rate.shape[0]
    s = Sizes(length, channels, modes, lax.axis_size("seq"))
    total_width = channels * lax.axis_size("tp")
    wide = jax.ShapeDtypeStruct((length * s.tiles, LANES), f32)
    narrow = jax.ShapeDtypeStruct((length, channels), bf16)
    rows = 16 * s.tiles
    wide_s = pltpu.VMEM(wide.shape, f32)
    longer_s = pltpu.VMEM(((length + 16) * s.tiles, LANES), f32)
    narrow_s = pltpu.VMEM(narrow.shape, bf16)
    last_s = pltpu.VMEM((16, channels), bf16)
    tail_s = pltpu.VMEM((rows, LANES), f32)
    taps_s = pltpu.VMEM((3 * s.tiles * SUB, LANES), f32)
    mode_s = pltpu.VMEM((modes * s.tiles, LANES), f32)
    sum_s = pltpu.VMEM((length * SUB, LANES), f32)
    square_s = pltpu.VMEM((length, LANES), f32)
    gain = norm_gain.reshape(s.tiles, LANES)
    there = pl.BlockSpec(memory_space=pltpu.HBM)
    here = pl.BlockSpec(memory_space=pltpu.VMEM)

    def call(kernel, ins, outs, out_shape, scratch_shapes, operands, aliases={}, cost=None):
        return pl.pallas_call(
            functools.partial(kernel, s),
            in_specs=[there if c == "h" else here for c in ins],
            out_specs=[there if c == "h" else here for c in outs],
            out_shape=out_shape,
            scratch_shapes=scratch_shapes,
            input_output_aliases=aliases,
            cost_estimate=cost,
            compiler_params=pltpu.CompilerParams(vmem_limit_bytes=GRANT),
        )(*operands)

    def pay_shape(extra):
        return jax.ShapeDtypeStruct(s.exchange_shape(extra), f32)

    def far(*arrays):
        return [pltpu.with_memory_space_constraint(x, pltpu.HBM) for x in arrays]

    def cost(per_element, arrays):
        return pl.CostEstimate(
            flops=per_element * length * channels, bytes_accessed=arrays * 4 * length * channels, transcendentals=0
        )

    filter_s = pltpu.VMEM(short_filter.shape, f32)
    rates_s = pltpu.VMEM(decay_rate.shape, f32)
    (pay,) = call(
        begin_kernel, "hhhhh", "v",
        (pay_shape(FORWARD_EXTRA),),
        [narrow_s, narrow_s, last_s, filter_s, rates_s]
        + [wide_s, wide_s, tail_s, taps_s, mode_s, pltpu.SemaphoreType.DMA((3 + 2 * s.halves,))],
        far(query_in, key_in, value_in, short_filter, decay_rate),
    )
    (inside,) = call(
        inside_kernel, "hhhhh", "v", (wide,),
        [narrow_s, narrow_s, filter_s, rates_s, rates_s]
        + [wide_s] * 3 + [taps_s, mode_s, mode_s, pltpu.SemaphoreType.DMA((5,))],
        far(key_in, value_in, short_filter, decay_rate, residue),
        cost=cost(75, 3),
    )
    back = exchange(s, pay, decay_rate, short_filter, FORWARD_EXTRA)
    conv, sums = call(
        forward_kernel, "v" * 9, "vv",
        (wide, jax.ShapeDtypeStruct((2, length), f32)),
        [wide_s] * 3 + [taps_s, mode_s, mode_s, sum_s, sum_s],
        (inside, query_in, stream, cotangent, back, short_filter, decay_rate, residue, gain),
        {0: 0},
    )
    sums = lax.psum(sums, "tp")
    normed, dstream, query_grad, dconv, tail, pay_back = call(
        lambda s, *refs: norm_kernel(s, total_width, *refs), "v" * 9, "hhhvvv",
        (narrow, narrow, narrow, wide, jax.ShapeDtypeStruct((rows, LANES), f32), pay_shape(BACKWARD_EXTRA)),
        [pltpu.VMEM(((length + 32) * s.tiles, LANES), f32)] + [longer_s] * 2 + [wide_s] * 2 + [narrow_s] * 2
        + [pltpu.VMEM((length + 16, channels), bf16)]
        + [taps_s, mode_s, square_s, square_s, pltpu.SemaphoreType.DMA((3 * s.halves,))],
        (sums, conv, query_in, stream, cotangent, back, short_filter, decay_rate, gain),
    )
    back_back = exchange(s, pay_back, decay_rate, short_filter, BACKWARD_EXTRA)
    query_grad, key_grad, value_grad = call(
        backward_kernel, "v" * 9 + "h", "hhh",
        (narrow, narrow, narrow),
        [longer_s] * 2 + [wide_s, tail_s] + [narrow_s] * 2 + [last_s, taps_s, mode_s, mode_s]
        + [pltpu.SemaphoreType.DMA((1 + 2 * s.halves,))],
        (key_in, value_in, dconv, tail, back, back_back, short_filter, decay_rate, residue, query_grad),
        {9: 0},
    )
    return (normed, dstream, query_grad, key_grad, value_grad)


def solution(mesh):
    cut = P("seq", "tp")
    return jax.shard_map(
        body,
        mesh=mesh,
        in_specs=(cut, cut, cut, cut, P(None, None, "tp"), P(None, "tp"), P(None, "tp"), P("tp"), cut),
        out_specs=(cut,) * 5,
        check_vma=False,
    )
```

```python
import functools

import jax
import jax.numpy as jnp
from jax import lax
from jax.experimental import pallas as pl
from jax.experimental.pallas import tpu as pltpu
from jax.sharding import PartitionSpec as P

f32 = jnp.float32
bf16 = jnp.bfloat16
epsilon = 1e-05
LANES = 128
SUB = 8
GROUP = LANES * SUB
FORWARD_EXTRA = 10
BACKWARD_EXTRA = 4
GRANT = 20 * 1024 * 1024


class Sizes:
    def __init__(self, length, channels, modes, devices):
        self.length, self.channels, self.modes, self.devices = length, channels, modes, devices
        self.tiles = channels // LANES
        self.halves = channels // GROUP
        self.direct = devices == SUB

    def chunk_row(self, r, h, lead, extra):
        if r < lead:
            return h * lead + r
        return self.halves * lead + h * extra + r - lead

    def chunk_rows(self, lead, extra):
        return -(-self.halves * (lead + extra) // SUB) * SUB

    def exchange_shape(self, lead, extra):
        if self.direct:
            return (self.devices * self.chunk_rows(lead, extra), LANES)
        return ((lead + extra) * self.tiles, LANES)

    def exchange_slice(self, r, h, lead, extra):
        if self.direct:
            return pl.ds(self.chunk_row(r, h, lead, extra), SUB, stride=self.chunk_rows(lead, extra))
        return pl.ds(r * self.tiles + h * SUB, SUB)


def staged(s, block, offset, h):
    start = block * (s.tiles * SUB) + (h * SUB * SUB + offset)
    return pl.ds(start, SUB, stride=SUB)


def major(s, t, h):
    start = t * s.tiles + h * SUB
    if not isinstance(start, int):
        start = pl.multiple_of(start, SUB)
    return pl.ds(start, SUB)


def staged_before(s, block, offset, h):
    if offset < 2:
        return staged(s, block - 1, offset + SUB - 2, h)
    return staged(s, block, offset - 2, h)


def aligned(start, unit):
    return start if isinstance(start, int) else pl.multiple_of(start, unit)


def columns(h):
    return pl.ds(aligned(h * GROUP, GROUP), GROUP)


def stage(s, x_ref, out_ref, i, h, pad=0):
    rows = x_ref[pl.ds(aligned(i * 16, 16), 16), columns(h)].astype(f32)
    base = (i + pad) * (2 * s.tiles * SUB) + h * (SUB * SUB)
    for part in range(2):
        for j in range(SUB):
            out_ref[pl.ds(aligned(base + (part * s.tiles + j) * SUB, SUB), SUB), :] = rows[
                part * SUB : (part + 1) * SUB, j * LANES : (j + 1) * LANES
            ]


def unstage(s, in_ref, x_ref, i, h, to=None):
    base = i * (2 * s.tiles * SUB) + h * (SUB * SUB)
    rows = [
        jnp.concatenate(
            [
                in_ref[pl.ds(aligned(base + (part * s.tiles + j) * SUB, SUB), SUB), :]
                for part in range(2)
            ],
            axis=0,
        )
        for j in range(SUB)
    ]
    to = i if to is None else to
    x_ref[pl.ds(aligned(to * 16, 16), 16), columns(h)] = jnp.concatenate(rows, axis=1).astype(bf16)


def stage_wide(s, x_ref, out_ref):
    for h in range(s.halves):
        stage(s, x_ref, out_ref, 0, h)


def each_half(s, body):
    def step(h, carry):
        body(h)
        return carry

    lax.fori_loop(0, s.halves, step, 0)


def sixteen(i, reverse=False):
    pairs = [(2 * i + part, offset) for part in range(2) for offset in range(SUB)]
    return pairs[::-1] if reverse else pairs


def stage_modes(s, x_ref, out_ref, f):
    for g in range(s.modes // SUB):
        rows = f(x_ref[g * SUB : (g + 1) * SUB, :])
        for j in range(s.tiles):
            start = (g * s.tiles + j) * SUB
            out_ref[start : start + SUB, :] = rows[:, j * LANES : (j + 1) * LANES]


def mode_tiles(s, ref, h):
    return [ref[staged(s, m // SUB, m % SUB, h), :] for m in range(s.modes)]


def stage_taps(s, filter_ref, out_ref):
    for i in range(3):
        rows = filter_ref[i]
        for j in range(s.tiles):
            start = (i * s.tiles + j) * SUB
            out_ref[start : start + 3, :] = rows[:, j * LANES : (j + 1) * LANES]


def tap_tiles(s, ref, i, h):
    return [ref[staged(s, i, tap, h), :] for tap in range(3)]


def total(parts):
    while len(parts) > 1:
        parts = [
            parts[i] + parts[i + 1] if i + 1 < len(parts) else parts[i]
            for i in range(0, len(parts), 2)
        ]
    return parts[0]


def mix(taps, now, before, before2):
    return taps[0] * now + taps[1] * before + taps[2] * before2


def recur(s, from_ref, to_ref, p, w, states, h, reverse=False):
    steps = s.length // 16

    def step(i, states):
        i = steps - 1 - i if reverse else i
        for block, offset in sixteen(0, reverse):
            rows = major(s, (2 * i + block) * SUB + offset, h)
            signal = from_ref[rows, :]
            states = [p[m] * states[m] + signal for m in range(s.modes)]
            to_ref[rows, :] = total([w[m] * states[m] for m in range(s.modes)])
        return states

    lax.fori_loop(0, steps, step, states)


def forward_slice(s, r, h):
    return s.exchange_slice(r, h, 2 * s.modes, FORWARD_EXTRA)


def split(x):
    high = x.astype(bf16).astype(f32)
    return high, x - high


def put_states(s, ref, states, h):
    for m in range(s.modes):
        high, low = split(states[m])
        ref[forward_slice(s, m, h), :] = high
        ref[forward_slice(s, s.modes + m, h), :] = low


def narrowed(from_ref, to_ref):
    rows = from_ref.shape[0]
    for i in range(0, rows, 16):
        to_ref[i : min(i + 16, rows), :] = from_ref[i : min(i + 16, rows), :].astype(bf16)


def widened(from_ref, to_ref):
    rows = from_ref.shape[0]
    for i in range(0, rows, 16):
        to_ref[i : min(i + 16, rows), :] = from_ref[i : min(i + 16, rows), :].astype(f32)


def backward_slice(s, r, h):
    return s.exchange_slice(r, h, s.modes, BACKWARD_EXTRA)


def begin_kernel(
    s, q_hbm, k_hbm, v_hbm, filter_hbm, decay_hbm, pay_ref,
    kb, vb, qb, fb, db, ks, vs, qs, pay_s, taps, poles, sems,
):
    copies = [(decay_hbm, db), (filter_hbm, fb), (q_hbm.at[pl.ds(s.length - 16, 16), :], qb)]
    for h in range(s.halves):
        cut = pl.ds(h * GROUP, GROUP)
        copies += [(k_hbm.at[:, cut], kb.at[:, cut]), (v_hbm.at[:, cut], vb.at[:, cut])]
    copies = [pltpu.make_async_copy(a, b, sems.at[i]) for i, (a, b) in enumerate(copies)]
    for copy in copies:
        copy.start()
    copies[0].wait()
    stage_modes(s, db, poles, lambda x: jnp.exp(-x))
    copies[1].wait()
    stage_taps(s, fb, taps)
    blank = jnp.zeros((SUB, LANES), f32)
    steps = s.length // 16
    copies[2].wait()
    stage_wide(s, qb, qs)

    def half(h):
        for i, (from_hbm, to) in enumerate(((k_hbm, kb), (v_hbm, vb))):
            cut = columns(h)
            pltpu.make_async_copy(from_hbm.at[:, cut], to.at[:, cut], sems.at[3 + 2 * h + i]).wait()
        p = mode_tiles(s, poles, h)
        taps_k, taps_v = (tap_tiles(s, taps, i, h) for i in (1, 2))

        def bring(i):
            stage(s, kb, ks, i, h)
            stage(s, vb, vs, i, h)

        def step(i, carry):
            (k1, k2, v1, v2), states = carry
            for block, offset in sixteen(0):
                rows = staged(s, 2 * i + block, offset, h)
                k0, v0 = ks[rows, :], vs[rows, :]
                product = mix(taps_k, k0, k1, k2) * mix(taps_v, v0, v1, v2)
                if block == 0 and offset < 2:
                    product = jnp.where(i == 0, 0.0, product)
                states = [p[m] * states[m] + product for m in range(s.modes)]
                k1, k2, v1, v2 = k0, k1, v0, v1
            bring(jnp.minimum(i + 1, steps - 1))
            return (k1, k2, v1, v2), states

        bring(0)
        held, states = lax.fori_loop(0, steps, step, ((blank,) * 4, [blank] * s.modes))
        put_states(s, pay_s, states, h)
        k1, k2, v1, v2 = held
        first = [staged(s, 0, offset, h) for offset in range(2)]
        last = [staged(s, 1, offset, h) for offset in (6, 7)]
        extra = [
            ks[first[0], :], ks[first[1], :], k2, k1,
            vs[first[0], :], vs[first[1], :], v2, v1,
            qs[last[0], :], qs[last[1], :],
        ]
        for r, value in enumerate(extra):
            pay_s[forward_slice(s, 2 * s.modes + r, h), :] = value

    each_half(s, half)
    narrowed(pay_s, pay_ref)


def forward_middle(length, rates, taps, ends, extras):
    devices = len(ends)
    whole, step0, step1 = (jnp.exp(-float(length - i) * rates) for i in range(3))
    blank = jnp.zeros_like(extras[0][0])
    arriving = jnp.zeros_like(ends[0])
    result = []
    for i in range(devices):
        k0, k1, _, _, v0, v1 = extras[i][:6]
        if i:
            _, _, ka, kb, _, _, va, vb, qa, qb = extras[i - 1][:10]
        else:
            ka = kb = va = vb = qa = qb = blank
        if i + 1 < devices:
            kc, kd, _, _, vc, vd = extras[i + 1][:6]
        else:
            kc = kd = vc = vd = blank
        prod0 = mix(taps[1], k0, kb, ka) * mix(taps[2], v0, vb, va)
        prod1 = mix(taps[1], k1, k0, kb) * mix(taps[2], v1, v0, vb)
        result.append((arriving, [ka, kb, va, vb, qa, qb, kc, kd, vc, vd]))
        arriving = whole * arriving + (ends[i] + step0 * prod0 + step1 * prod1)
    return result


def backward_middle(length, rates, ends, extras):
    devices = len(ends)
    whole = jnp.exp(-float(length) * rates)
    blank = jnp.zeros_like(extras[0][0])
    arriving = jnp.zeros_like(ends[0])
    result = [None] * devices
    for i in reversed(range(devices)):
        result[i] = (arriving, extras[i + 1] if i + 1 < devices else [blank] * len(extras[0]))
        arriving = whole * arriving + ends[i]
    return result


def middle_kernel(s, forward, pay_ref, decay_ref, filter_ref, back_ref, *wide):
    me = lax.axis_index("seq")
    lead, extra = (2 * s.modes, FORWARD_EXTRA) if forward else (s.modes, BACKWARD_EXTRA)
    in_ref, out_ref = wide if forward else (pay_ref, back_ref)
    if forward:
        widened(pay_ref, in_ref)
    rows = s.chunk_rows(lead, extra)
    for h in range(s.halves):
        lanes = pl.ds(pl.multiple_of((me + h * SUB) * LANES, LANES), LANES)
        rates = decay_ref[:, lanes]
        ends, extras = [], []
        for i in range(s.devices):
            e = i * rows + s.chunk_row(0, h, lead, extra)
            end = in_ref[e : e + s.modes, :]
            ends.append(end + in_ref[e + s.modes : e + lead, :] if forward else end)
            x = i * rows + s.chunk_row(lead, h, lead, extra)
            extras.append([in_ref[x + r : x + r + 1, :] for r in range(extra)])
        if forward:
            taps = [[filter_ref[i, tap : tap + 1, lanes] for tap in range(3)] for i in range(3)]
            result = forward_middle(s.length, rates, taps, ends, extras)
        else:
            result = backward_middle(s.length, rates, ends, extras)
        for i, (state, more) in enumerate(result):
            e = i * rows + s.chunk_row(0, h, lead, extra)
            if forward:
                out_ref[e : e + s.modes, :], out_ref[e + s.modes : e + lead, :] = split(state)
            else:
                out_ref[e : e + s.modes, :] = state
            x = i * rows + s.chunk_row(lead, h, lead, extra)
            for r in range(extra):
                out_ref[x + r : x + r + 1, :] = more[r]
    if forward:
        narrowed(out_ref, back_ref)


def exchange(s, pay, decay_rate, short_filter, forward):
    lead, extra = (2 * s.modes, FORWARD_EXTRA) if forward else (s.modes, BACKWARD_EXTRA)
    if s.direct:
        chunks = (s.devices, s.chunk_rows(lead, extra), LANES)
        got = lax.all_to_all(pay.reshape(chunks), "seq", 0, 0, tiled=True)
        back = pl.pallas_call(
            functools.partial(middle_kernel, s, forward),
            out_shape=jax.ShapeDtypeStruct(pay.shape, pay.dtype),
            scratch_shapes=[pltpu.VMEM(pay.shape, f32)] * 2 if forward else [],
            compiler_params=pltpu.CompilerParams(vmem_limit_bytes=GRANT),
        )(got.reshape(pay.shape), decay_rate, short_filter)
        return lax.all_to_all(back.reshape(chunks), "seq", 0, 0, tiled=True).reshape(pay.shape)
    rows = lead + extra
    width = s.channels // s.devices
    start = lax.axis_index("seq") * width
    rates = lax.dynamic_slice_in_dim(decay_rate, start, width, 1)
    part = lax.dynamic_slice_in_dim(short_filter, start, width, 2)
    pay = pay.reshape(rows, s.devices, width).transpose(1, 0, 2)
    got = lax.all_to_all(pay, "seq", 0, 0, tiled=True).astype(f32)
    ends = [got[i, : s.modes] for i in range(s.devices)]
    extras = [[got[i, lead + r][None] for r in range(extra)] for i in range(s.devices)]
    if forward:
        ends = [end + got[i, s.modes : lead] for i, end in enumerate(ends)]
        taps = [[part[i, tap][None] for tap in range(3)] for i in range(3)]
        result = forward_middle(s.length, rates, taps, ends, extras)
        highs = [lax.reduce_precision(state, 8, 7) for state, _ in result]
        result = [
            (jnp.concatenate([high, state - high]), more) for high, (state, more) in zip(highs, result)
        ]
    else:
        result = backward_middle(s.length, rates, ends, extras)
    back = jnp.stack([jnp.concatenate([state] + list(more)) for state, more in result])
    back = lax.all_to_all(back.astype(pay.dtype), "seq", 0, 0, tiled=True)
    return back.transpose(1, 0, 2).reshape(rows * s.tiles, LANES)


def inside_kernel(
    s, k_hbm, v_hbm, filter_hbm, decay_hbm, residue_hbm, inside_ref, first_ref,
    kb, vb, fb, db, rb, ks, vs, prod, taps, poles, weights, sems,
):
    pairs = [(decay_hbm, db), (residue_hbm, rb), (filter_hbm, fb), (k_hbm, kb), (v_hbm, vb)]
    copies = [pltpu.make_async_copy(a, b, sems.at[i]) for i, (a, b) in enumerate(pairs)]
    for copy in copies:
        copy.start()
    for copy in copies:
        copy.wait()
    stage_modes(s, db, poles, lambda x: jnp.exp(-x))
    stage_modes(s, rb, weights, lambda x: x)
    stage_taps(s, fb, taps)
    blank = jnp.zeros((SUB, LANES), f32)
    steps = s.length // 16

    def half(h):
        taps_k, taps_v = (tap_tiles(s, taps, i, h) for i in (1, 2))

        def products(i, held):
            stage(s, kb, ks, i, h)
            stage(s, vb, vs, i, h)
            k1, k2, v1, v2 = held
            for block, offset in sixteen(0):
                rows = staged(s, 2 * i + block, offset, h)
                k0, v0 = ks[rows, :], vs[rows, :]
                product = mix(taps_k, k0, k1, k2) * mix(taps_v, v0, v1, v2)
                if block == 0 and offset < 2:
                    product = jnp.where(i == 0, 0.0, product)
                prod[major(s, (2 * i + block) * SUB + offset, h), :] = product
                k1, k2, v1, v2 = k0, k1, v0, v1
            return k1, k2, v1, v2

        lax.fori_loop(0, steps, products, (blank,) * 4)
        for i, (ref, part) in enumerate(((ks, taps_k), (vs, taps_v))):
            x0, x1 = (ref[staged(s, 0, offset, h), :] for offset in range(2))
            first_ref[major(s, 2 * i, h), :] = part[0] * x0
            first_ref[major(s, 2 * i + 1, h), :] = part[0] * x1 + part[1] * x0
        recur(s, prod, inside_ref, mode_tiles(s, poles, h), mode_tiles(s, weights, h), [blank] * s.modes, h)

    each_half(s, half)


def forward_kernel(
    s, inside_ref, first_ref, q_ref, stream_ref, cot_ref, back_ref, filter_ref, decay_ref, residue_ref, gain_ref,
    conv_ref, sums_ref, near_ref,
    qs, xs, gs, back_s, taps, poles, weights, squares, inners,
):
    stage_modes(s, decay_ref, poles, lambda x: jnp.exp(-x))
    stage_modes(s, residue_ref, weights, lambda x: x)
    stage_taps(s, filter_ref, taps)

    widened(back_ref, back_s)
    steps = s.length // 16

    def half(h):
        p = mode_tiles(s, poles, h)
        w = mode_tiles(s, weights, h)
        gain = gain_ref[pl.ds(aligned(h * SUB, SUB), SUB), :]
        taps_q, taps_k, taps_v = (tap_tiles(s, taps, i, h) for i in range(3))
        near = [back_s[forward_slice(s, 2 * s.modes + r, h), :] for r in range(FORWARD_EXTRA)]
        for r, value in enumerate(near):
            near_ref[major(s, r, h), :] = value
        ka, kb, va, vb, qa, qb = near[:6]
        k0, k1, v0, v1 = (first_ref[major(s, r, h), :] for r in range(4))
        products = [
            (k0 + taps_k[1] * kb + taps_k[2] * ka) * (v0 + taps_v[1] * vb + taps_v[2] * va),
            (k1 + taps_k[2] * kb) * (v1 + taps_v[2] * vb),
        ]
        conv = []
        states = [
            back_s[forward_slice(s, m, h), :] + back_s[forward_slice(s, s.modes + m, h), :]
            for m in range(s.modes)
        ]
        for offset in range(2):
            states = [p[m] * states[m] + products[offset] for m in range(s.modes)]
            conv.append(total([w[m] * states[m] for m in range(s.modes)]))
        states = [w[m] * states[m] / (p[m] * p[m]) for m in range(s.modes)]
        first, ahead = [], states
        for offset in range(2):
            ahead = [p[m] * ahead[m] for m in range(s.modes)]
            first.append(conv[offset] - total(ahead))

        def bring(i):
            stage(s, q_ref, qs, i, h)
            stage(s, stream_ref, xs, i, h)
            stage(s, cot_ref, gs, i, h)

        def step(i, carry):
            (q1, q2), states = carry
            for block, offset in sixteen(0):
                rows = staged(s, 2 * i + block, offset, h)
                t = (2 * i + block) * SUB + offset
                out = major(s, t, h)
                inside = inside_ref[out, :]
                if block == 0 and offset < 2:
                    inside = jnp.where(i == 0, first[offset], inside)
                states = [p[m] * states[m] for m in range(s.modes)]
                conv = inside + total(states)
                conv_ref[out, :] = conv
                q0 = qs[rows, :]
                mixed = xs[rows, :] + mix(taps_q, q0, q1, q2) * conv
                part = pl.ds(pl.multiple_of(t * SUB, SUB), SUB)
                square, inner = mixed * mixed, gain * gs[rows, :] * mixed
                squares[part, :] = square + jnp.where(h == 0, 0.0, squares[part, :])
                inners[part, :] = inner + jnp.where(h == 0, 0.0, inners[part, :])
                q1, q2 = q0, q1
            bring(jnp.minimum(i + 1, steps - 1))
            return (q1, q2), states

        bring(0)
        lax.fori_loop(0, steps, step, ((qb, qa), states))

    each_half(s, half)
    for r, ref in enumerate((squares, inners)):
        parts = []
        for b in range(s.length // SUB):
            parts.append(
                total([ref[pl.ds(b * SUB * SUB + i, SUB, stride=SUB), :] for i in range(SUB)])
            )
        rows = jnp.concatenate(parts, axis=0)
        sums_ref[r : r + 1, :] = jnp.sum(rows.T, axis=0, keepdims=True)


def norm_kernel(
    s, width, sums_ref, conv_ref, q_ref, stream_ref, cot_ref, near_ref, filter_ref, decay_ref, gain_ref,
    normed_hbm, dstream_hbm, qgrad_hbm, dconv_ref, tail_ref, pay_ref,
    qs, xs, gs, ns, ds, normed_b, dstream_b, qgrad_b, taps, poles, inv_s, coef_s, sems,
):
    inverse = lax.rsqrt(sums_ref[0:1, :] / width + epsilon)
    coef = inverse * inverse * inverse * sums_ref[1:2, :] / width
    inv_s[...] = jnp.broadcast_to(inverse, (LANES, s.length)).T
    coef_s[...] = jnp.broadcast_to(coef, (LANES, s.length)).T
    stage_modes(s, decay_ref, poles, lambda x: jnp.exp(-x))
    stage_taps(s, filter_ref, taps)
    blank = jnp.zeros((SUB, LANES), f32)
    steps = s.length // 16

    def pieces(h):
        cut = columns(h)
        sources = [
            (normed_b.at[:, cut], normed_hbm.at[:, cut]),
            (dstream_b.at[:, cut], dstream_hbm.at[:, cut]),
            (qgrad_b.at[pl.ds(16, s.length - 16), cut], qgrad_hbm.at[pl.ds(0, s.length - 16), cut]),
        ]
        return [pltpu.make_async_copy(a, b, sems.at[3 * h + i]) for i, (a, b) in enumerate(sources)]

    def half(h):
        gain = gain_ref[pl.ds(aligned(h * SUB, SUB), SUB), :]
        taps_q = tap_tiles(s, taps, 0, h)

        def bring(i):
            rows = jnp.minimum(i, steps - 1)
            stage(s, q_ref, qs, rows, h, i - rows + 1)
            stage(s, stream_ref, xs, rows, h)
            stage(s, cot_ref, gs, rows, h)

        def step(i, held):
            q1, q2, dq1, dq2 = held
            for block, offset in sixteen(0):
                rows = staged(s, 2 * i + block, offset, h)
                t = (2 * i + block) * SUB + offset
                out = major(s, t, h)
                inv = jnp.broadcast_to(inv_s[pl.ds(t, 1), :], (SUB, LANES))
                cf = jnp.broadcast_to(coef_s[pl.ds(t, 1), :], (SUB, LANES))
                q0 = qs[staged(s, 2 * i + block + 2, offset, h), :]
                qmix = mix(taps_q, q0, q1, q2)
                conv = conv_ref[out, :]
                mixed = xs[rows, :] + qmix * conv
                dmixed = inv * (gain * gs[rows, :]) - mixed * cf
                ns[rows, :] = mixed * inv * gain
                ds[rows, :] = dmixed
                dq0 = dmixed * conv
                dconv_ref[out, :] = dmixed * qmix
                qs[staged_before(s, 2 * i + block + 2, offset, h), :] = mix(taps_q, dq2, dq1, dq0)
                q1, q2, dq1, dq2 = q0, q1, dq0, dq1
            unstage(s, ns, normed_b, i, h)
            unstage(s, ds, dstream_b, i, h)
            unstage(s, qs, qgrad_b, i, h)
            bring(i + 1)
            return q1, q2, dq1, dq2

        bring(0)
        held = (near_ref[major(s, 5, h), :], near_ref[major(s, 4, h), :], blank, blank)
        _, _, dq1, dq2 = lax.fori_loop(0, steps, step, held)
        qs[staged(s, 2 * steps + 1, 6, h), :] = taps_q[0] * dq2 + taps_q[1] * dq1
        qs[staged(s, 2 * steps + 1, 7, h), :] = taps_q[0] * dq1
        for copy in pieces(h):
            copy.start()

    each_half(s, half)
    start = steps * 2 * s.tiles * SUB
    tail_ref[...] = qs[start : start + 2 * s.tiles * SUB, :]

    def ends(h):
        p = mode_tiles(s, poles, h)

        def step(i, states):
            for block, offset in sixteen(0, True):
                t = (2 * (steps - 1 - i) + block) * SUB + offset
                dconv = dconv_ref[major(s, t, h), :]
                states = [p[m] * states[m] + dconv for m in range(s.modes)]
            return states

        states = lax.fori_loop(0, steps, step, [blank] * s.modes)
        for m in range(s.modes):
            pay_ref[backward_slice(s, m, h), :] = states[m]
        first = [ds[staged(s, 0, offset, h), :] * conv_ref[major(s, offset, h), :] for offset in range(2)]
        for r, value in enumerate([dconv_ref[major(s, 0, h), :], *first, blank]):
            pay_ref[backward_slice(s, s.modes + r, h), :] = value

    each_half(s, ends)

    def finish(h):
        for copy in pieces(h):
            copy.wait()

    each_half(s, finish)


def backward_kernel(
    s, k_ref, v_ref, dconv_ref, tail_ref, near_ref, back_ref, filter_ref, decay_ref, residue_ref, qgrad_in,
    qgrad_hbm, kgrad_hbm, vgrad_hbm,
    ks, vs, dprod, qs, kgrad_b, vgrad_b, qgrad_b, taps, poles, weights, sems,
):
    del qgrad_in
    stage_modes(s, decay_ref, poles, lambda x: jnp.exp(-x))
    stage_modes(s, residue_ref, weights, lambda x: x)
    stage_taps(s, filter_ref, taps)
    steps = s.length // 16

    def back(r, h):
        return back_ref[backward_slice(s, r, h), :]

    qs[...] = tail_ref[...]

    def tails(h):
        taps_q = tap_tiles(s, taps, 0, h)
        dq0, dq1 = back(s.modes + 1, h), back(s.modes + 2, h)
        rows = [staged(s, 1, offset, h) for offset in (6, 7)]
        qs[rows[0], :] = qs[rows[0], :] + taps_q[2] * dq0
        qs[rows[1], :] = qs[rows[1], :] + (taps_q[1] * dq0 + taps_q[2] * dq1)
        unstage(s, qs, qgrad_b, 0, h)

    each_half(s, tails)
    last = pltpu.make_async_copy(qgrad_b, qgrad_hbm.at[pl.ds(s.length - 16, 16), :], sems.at[2 * s.halves])
    last.start()

    def pieces(h):
        cut = columns(h)
        sources = [(kgrad_b, kgrad_hbm), (vgrad_b, vgrad_hbm)]
        return [
            pltpu.make_async_copy(a.at[:, cut], b.at[:, cut], sems.at[2 * h + i])
            for i, (a, b) in enumerate(sources)
        ]

    def half(h):
        p = mode_tiles(s, poles, h)
        w = mode_tiles(s, weights, h)
        arriving = [back(m, h) for m in range(s.modes)]
        recur(s, dconv_ref, dprod, p, w, arriving, h, reverse=True)
        taps_k, taps_v = (tap_tiles(s, taps, i, h) for i in (1, 2))

        def bring(i):
            stage(s, k_ref, ks, i, h, 1)
            stage(s, v_ref, vs, i, h, 1)

        def advance(inputs, grads, k2, v2, d):
            k0, k1, v0, v1 = inputs
            dk1, dk2, dv1, dv2 = grads
            dk0 = d * mix(taps_v, v0, v1, v2)
            dv0 = d * mix(taps_k, k0, k1, k2)
            out = mix(taps_k, dk0, dk1, dk2), mix(taps_v, dv0, dv1, dv2)
            return (k1, k2, v1, v2), (dk0, dk1, dv0, dv1), out

        bring(steps - 1)
        ka, kb, va, vb, _, _, kc, kd, vc, vd = (near_ref[major(s, r, h), :] for r in range(10))
        for ref, rows in ((ks, (ka, kb)), (vs, (va, vb))):
            for offset in range(2):
                ref[staged(s, 1, 6 + offset, h), :] = rows[offset]
        arriving = [back(m, h) for m in range(s.modes)]
        dconv0 = back(s.modes, h)
        d0 = total([w[m] * arriving[m] for m in range(s.modes)])
        d1 = total([w[m] * ((arriving[m] - dconv0) / p[m]) for m in range(s.modes)])
        ends = [staged(s, 2 * steps + 1, offset, h) for offset in (6, 7)]
        inputs = (kd, kc, vd, vc)
        grads = (jnp.zeros((SUB, LANES), f32),) * 4
        inputs, grads, _ = advance(inputs, grads, ks[ends[1], :], vs[ends[1], :], d1)
        inputs, grads, _ = advance(inputs, grads, ks[ends[0], :], vs[ends[0], :], d0)

        def step(i, carry):
            inputs, grads = carry
            i = steps - 1 - i

            @pl.when(i > 0)
            def _():
                bring(jnp.maximum(i - 1, 0))

            for block, offset in sixteen(0, True):
                d = dprod[major(s, (2 * i + block) * SUB + offset, h), :]
                rows = staged_before(s, 2 * i + block + 2, offset, h)
                inputs, grads, out = advance(inputs, grads, ks[rows, :], vs[rows, :], d)
                rows = staged(s, 2 * i + block + 2, offset, h)
                ks[rows, :], vs[rows, :] = out
            unstage(s, ks, kgrad_b, i + 1, h, i)
            unstage(s, vs, vgrad_b, i + 1, h, i)
            return inputs, grads

        lax.fori_loop(0, steps, step, (inputs, grads))
        for copy in pieces(h):
            copy.start()

    each_half(s, half)
    last.wait()

    def finish(h):
        for copy in pieces(h):
            copy.wait()

    each_half(s, finish)


def body(
    query_in, key_in, value_in, stream, short_filter, decay_rate, residue, norm_gain, cotangent
):
    length, channels = query_in.shape
    modes = decay_rate.shape[0]
    s = Sizes(length, channels, modes, lax.axis_size("seq"))
    total_width = channels * lax.axis_size("tp")
    wide = jax.ShapeDtypeStruct((length * s.tiles, LANES), f32)
    narrow = jax.ShapeDtypeStruct((length, channels), bf16)
    rows = 16 * s.tiles
    wide_s = pltpu.VMEM(wide.shape, f32)
    longer_s = pltpu.VMEM(((length + 16) * s.tiles, LANES), f32)
    narrow_s = pltpu.VMEM(narrow.shape, bf16)
    last_s = pltpu.VMEM((16, channels), bf16)
    tail_s = pltpu.VMEM((rows, LANES), f32)
    taps_s = pltpu.VMEM((3 * s.tiles * SUB, LANES), f32)
    mode_s = pltpu.VMEM((modes * s.tiles, LANES), f32)
    sum_s = pltpu.VMEM((length * SUB, LANES), f32)
    square_s = pltpu.VMEM((length, LANES), f32)
    gain = norm_gain.reshape(s.tiles, LANES)
    there = pl.BlockSpec(memory_space=pltpu.HBM)
    here = pl.BlockSpec(memory_space=pltpu.VMEM)

    def call(kernel, ins, outs, out_shape, scratch_shapes, operands, aliases={}, cost=None):
        return pl.pallas_call(
            functools.partial(kernel, s),
            in_specs=[there if c == "h" else here for c in ins],
            out_specs=[there if c == "h" else here for c in outs],
            out_shape=out_shape,
            scratch_shapes=scratch_shapes,
            input_output_aliases=aliases,
            cost_estimate=cost,
            compiler_params=pltpu.CompilerParams(vmem_limit_bytes=GRANT),
        )(*operands)

    forward_shape = s.exchange_shape(2 * modes, FORWARD_EXTRA)
    near_shape = jax.ShapeDtypeStruct((FORWARD_EXTRA * s.tiles, LANES), f32)

    def far(*arrays):
        return [pltpu.with_memory_space_constraint(x, pltpu.HBM) for x in arrays]

    def cost(per_element, arrays):
        return pl.CostEstimate(
            flops=per_element * length * channels, bytes_accessed=arrays * 4 * length * channels, transcendentals=0
        )

    filter_s = pltpu.VMEM(short_filter.shape, f32)
    rates_s = pltpu.VMEM(decay_rate.shape, f32)
    (pay,) = call(
        begin_kernel, "hhhhh", "v",
        (jax.ShapeDtypeStruct(forward_shape, bf16),),
        [narrow_s, narrow_s, last_s, filter_s, rates_s]
        + [wide_s, wide_s, tail_s, pltpu.VMEM(forward_shape, f32), taps_s, mode_s]
        + [pltpu.SemaphoreType.DMA((3 + 2 * s.halves,))],
        far(query_in, key_in, value_in, short_filter, decay_rate),
    )
    inside, first = call(
        inside_kernel, "hhhhh", "vv", (wide, jax.ShapeDtypeStruct((4 * s.tiles, LANES), f32)),
        [narrow_s, narrow_s, filter_s, rates_s, rates_s]
        + [wide_s] * 3 + [taps_s, mode_s, mode_s, pltpu.SemaphoreType.DMA((5,))],
        far(key_in, value_in, short_filter, decay_rate, residue),
        cost=cost(75, 3),
    )
    back = exchange(s, pay, decay_rate, short_filter, True)
    conv, sums, near = call(
        forward_kernel, "v" * 10, "vvv",
        (wide, jax.ShapeDtypeStruct((2, length), f32), near_shape),
        [wide_s] * 3 + [pltpu.VMEM(forward_shape, f32), taps_s, mode_s, mode_s, sum_s, sum_s],
        (inside, first, query_in, stream, cotangent, back, short_filter, decay_rate, residue, gain),
        {0: 0},
    )
    sums = lax.psum(sums, "tp")
    normed, dstream, query_grad, dconv, tail, pay_back = call(
        lambda s, *refs: norm_kernel(s, total_width, *refs), "v" * 9, "hhhvvv",
        (narrow, narrow, narrow, wide, jax.ShapeDtypeStruct((rows, LANES), f32), jax.ShapeDtypeStruct(s.exchange_shape(modes, BACKWARD_EXTRA), f32)),
        [pltpu.VMEM(((length + 32) * s.tiles, LANES), f32)] + [longer_s] * 2 + [wide_s] * 2 + [narrow_s] * 2
        + [pltpu.VMEM((length + 16, channels), bf16)]
        + [taps_s, mode_s, square_s, square_s, pltpu.SemaphoreType.DMA((3 * s.halves,))],
        (sums, conv, query_in, stream, cotangent, near, short_filter, decay_rate, gain),
    )
    back_back = exchange(s, pay_back, decay_rate, short_filter, False)
    query_grad, key_grad, value_grad = call(
        backward_kernel, "v" * 9 + "h", "hhh",
        (narrow, narrow, narrow),
        [longer_s] * 2 + [wide_s, tail_s] + [narrow_s] * 2 + [last_s, taps_s, mode_s, mode_s]
        + [pltpu.SemaphoreType.DMA((1 + 2 * s.halves,))],
        (key_in, value_in, dconv, tail, near, back_back, short_filter, decay_rate, residue, query_grad),
        {9: 0},
    )
    return (normed, dstream, query_grad, key_grad, value_grad)


def solution(mesh):
    cut = P("seq", "tp")
    return jax.shard_map(
        body,
        mesh=mesh,
        in_specs=(cut, cut, cut, cut, P(None, None, "tp"), P(None, "tp"), P(None, "tp"), P("tp"), cut),
        out_specs=(cut,) * 5,
        check_vma=False,
    )
```

```python
import functools

import jax
import jax.numpy as jnp
from jax import lax
from jax.experimental import pallas as pl
from jax.experimental.pallas import tpu as pltpu
from jax.sharding import PartitionSpec as P

f32 = jnp.float32
bf16 = jnp.bfloat16
epsilon = 1e-05
LANES = 128
SUB = 8
GROUP = LANES * SUB
FORWARD_EXTRA = 10
BACKWARD_EXTRA = 4
GRANT = 20 * 1024 * 1024


class Sizes:
    def __init__(self, length, channels, modes, devices):
        self.length, self.channels, self.modes, self.devices = length, channels, modes, devices
        self.tiles = channels // LANES
        self.halves = channels // GROUP
        self.direct = devices == SUB

    def chunk_row(self, r, h, lead, extra):
        if r < lead:
            return h * lead + r
        return self.halves * lead + h * extra + r - lead

    def chunk_rows(self, lead, extra):
        return -(-self.halves * (lead + extra) // SUB) * SUB

    def exchange_shape(self, lead, extra):
        if self.direct:
            return (self.devices * self.chunk_rows(lead, extra), LANES)
        return ((lead + extra) * self.tiles, LANES)

    def exchange_slice(self, r, h, lead, extra):
        if self.direct:
            return pl.ds(self.chunk_row(r, h, lead, extra), SUB, stride=self.chunk_rows(lead, extra))
        return pl.ds(r * self.tiles + h * SUB, SUB)


def staged(s, block, offset, h):
    start = block * (s.tiles * SUB) + (h * SUB * SUB + offset)
    return pl.ds(start, SUB, stride=SUB)


def major(s, t, h):
    start = t * s.tiles + h * SUB
    if not isinstance(start, int):
        start = pl.multiple_of(start, SUB)
    return pl.ds(start, SUB)


def staged_before(s, block, offset, h):
    if offset < 2:
        return staged(s, block - 1, offset + SUB - 2, h)
    return staged(s, block, offset - 2, h)


def aligned(start, unit):
    return start if isinstance(start, int) else pl.multiple_of(start, unit)


def columns(h):
    return pl.ds(aligned(h * GROUP, GROUP), GROUP)


def stage(s, x_ref, out_ref, i, h, pad=0):
    rows = x_ref[pl.ds(aligned(i * 16, 16), 16), columns(h)].astype(f32)
    base = (i + pad) * (2 * s.tiles * SUB) + h * (SUB * SUB)
    for part in range(2):
        for j in range(SUB):
            out_ref[pl.ds(aligned(base + (part * s.tiles + j) * SUB, SUB), SUB), :] = rows[
                part * SUB : (part + 1) * SUB, j * LANES : (j + 1) * LANES
            ]


def unstage(s, in_ref, x_ref, i, h, to=None):
    base = i * (2 * s.tiles * SUB) + h * (SUB * SUB)
    rows = [
        jnp.concatenate(
            [
                in_ref[pl.ds(aligned(base + (part * s.tiles + j) * SUB, SUB), SUB), :]
                for part in range(2)
            ],
            axis=0,
        )
        for j in range(SUB)
    ]
    to = i if to is None else to
    x_ref[pl.ds(aligned(to * 16, 16), 16), columns(h)] = jnp.concatenate(rows, axis=1).astype(bf16)


def stage_wide(s, x_ref, out_ref):
    for h in range(s.halves):
        stage(s, x_ref, out_ref, 0, h)


def each_half(s, body):
    def step(h, carry):
        body(h)
        return carry

    lax.fori_loop(0, s.halves, step, 0)


def sixteen(i, reverse=False):
    pairs = [(2 * i + part, offset) for part in range(2) for offset in range(SUB)]
    return pairs[::-1] if reverse else pairs


def stage_modes(s, x_ref, out_ref, f):
    for g in range(s.modes // SUB):
        rows = f(x_ref[g * SUB : (g + 1) * SUB, :])
        for j in range(s.tiles):
            start = (g * s.tiles + j) * SUB
            out_ref[start : start + SUB, :] = rows[:, j * LANES : (j + 1) * LANES]


def mode_tiles(s, ref, h):
    return [ref[staged(s, m // SUB, m % SUB, h), :] for m in range(s.modes)]


def stage_taps(s, filter_ref, out_ref):
    for i in range(3):
        rows = filter_ref[i]
        for j in range(s.tiles):
            start = (i * s.tiles + j) * SUB
            out_ref[start : start + 3, :] = rows[:, j * LANES : (j + 1) * LANES]


def tap_tiles(s, ref, i, h):
    return [ref[staged(s, i, tap, h), :] for tap in range(3)]


def total(parts):
    while len(parts) > 1:
        parts = [
            parts[i] + parts[i + 1] if i + 1 < len(parts) else parts[i]
            for i in range(0, len(parts), 2)
        ]
    return parts[0]


def mix(taps, now, before, before2):
    return taps[0] * now + taps[1] * before + taps[2] * before2


def products(s, k_ref, v_ref, ks, vs, to_ref, taps_k, taps_v, h):
    def step(i, held):
        stage(s, k_ref, ks, i, h)
        stage(s, v_ref, vs, i, h)
        k1, k2, v1, v2 = held
        for block, offset in sixteen(0):
            rows = staged(s, 2 * i + block, offset, h)
            k0, v0 = ks[rows, :], vs[rows, :]
            product = mix(taps_k, k0, k1, k2) * mix(taps_v, v0, v1, v2)
            if block == 0 and offset < 2:
                product = jnp.where(i == 0, 0.0, product)
            to_ref[major(s, (2 * i + block) * SUB + offset, h), :] = product
            k1, k2, v1, v2 = k0, k1, v0, v1
        return k1, k2, v1, v2

    return lax.fori_loop(0, s.length // 16, step, (jnp.zeros((SUB, LANES), f32),) * 4)


def recur(s, from_ref, to_ref, p, w, states, h, reverse=False):
    steps = s.length // 16

    def step(i, states):
        i = steps - 1 - i if reverse else i
        for block, offset in sixteen(0, reverse):
            rows = major(s, (2 * i + block) * SUB + offset, h)
            signal = from_ref[rows, :]
            states = [p[m] * states[m] + signal for m in range(s.modes)]
            to_ref[rows, :] = total([w[m] * states[m] for m in range(s.modes)])
        return states

    lax.fori_loop(0, steps, step, states)


def forward_slice(s, r, h):
    return s.exchange_slice(r, h, 2 * s.modes, FORWARD_EXTRA)


def split(x):
    high = x.astype(bf16).astype(f32)
    return high, x - high


def put_states(s, ref, states, h):
    for m in range(s.modes):
        high, low = split(states[m])
        ref[forward_slice(s, m, h), :] = high
        ref[forward_slice(s, s.modes + m, h), :] = low


def narrowed(from_ref, to_ref):
    rows = from_ref.shape[0]
    for i in range(0, rows, 16):
        to_ref[i : min(i + 16, rows), :] = from_ref[i : min(i + 16, rows), :].astype(bf16)


def widened(from_ref, to_ref):
    rows = from_ref.shape[0]
    for i in range(0, rows, 16):
        to_ref[i : min(i + 16, rows), :] = from_ref[i : min(i + 16, rows), :].astype(f32)


def backward_slice(s, r, h):
    return s.exchange_slice(r, h, s.modes, BACKWARD_EXTRA)


def begin_kernel(
    s, q_hbm, k_hbm, v_hbm, filter_hbm, decay_hbm, pay_ref,
    kb, vb, qb, fb, db, ks, vs, prod, qs, pay_s, taps, poles, sems,
):
    copies = [(decay_hbm, db), (filter_hbm, fb), (q_hbm.at[pl.ds(s.length - 16, 16), :], qb)]
    for h in range(s.halves):
        cut = pl.ds(h * GROUP, GROUP)
        copies += [(k_hbm.at[:, cut], kb.at[:, cut]), (v_hbm.at[:, cut], vb.at[:, cut])]
    copies = [pltpu.make_async_copy(a, b, sems.at[i]) for i, (a, b) in enumerate(copies)]
    for copy in copies:
        copy.start()
    copies[0].wait()
    stage_modes(s, db, poles, lambda x: jnp.exp(-x))
    copies[1].wait()
    stage_taps(s, fb, taps)
    blank = jnp.zeros((SUB, LANES), f32)
    copies[2].wait()
    stage_wide(s, qb, qs)

    def half(h):
        for i, (from_hbm, to) in enumerate(((k_hbm, kb), (v_hbm, vb))):
            cut = columns(h)
            pltpu.make_async_copy(from_hbm.at[:, cut], to.at[:, cut], sems.at[3 + 2 * h + i]).wait()
        p = mode_tiles(s, poles, h)
        taps_k, taps_v = (tap_tiles(s, taps, i, h) for i in (1, 2))

        held = products(s, kb, vb, ks, vs, prod, taps_k, taps_v, h)

        def step(i, states):
            for block, offset in sixteen(0):
                product = prod[major(s, (2 * i + block) * SUB + offset, h), :]
                states = [p[m] * states[m] + product for m in range(s.modes)]
            return states

        states = lax.fori_loop(0, s.length // 16, step, [blank] * s.modes)
        put_states(s, pay_s, states, h)
        k1, k2, v1, v2 = held
        first = [staged(s, 0, offset, h) for offset in range(2)]
        last = [staged(s, 1, offset, h) for offset in (6, 7)]
        extra = [
            ks[first[0], :], ks[first[1], :], k2, k1,
            vs[first[0], :], vs[first[1], :], v2, v1,
            qs[last[0], :], qs[last[1], :],
        ]
        for r, value in enumerate(extra):
            pay_s[forward_slice(s, 2 * s.modes + r, h), :] = value

    each_half(s, half)
    narrowed(pay_s, pay_ref)


def forward_middle(length, rates, taps, ends, extras):
    devices = len(ends)
    whole, step0, step1 = (jnp.exp(-float(length - i) * rates) for i in range(3))
    blank = jnp.zeros_like(extras[0][0])
    arriving = jnp.zeros_like(ends[0])
    result = []
    for i in range(devices):
        k0, k1, _, _, v0, v1 = extras[i][:6]
        if i:
            _, _, ka, kb, _, _, va, vb, qa, qb = extras[i - 1][:10]
        else:
            ka = kb = va = vb = qa = qb = blank
        if i + 1 < devices:
            kc, kd, _, _, vc, vd = extras[i + 1][:6]
        else:
            kc = kd = vc = vd = blank
        prod0 = mix(taps[1], k0, kb, ka) * mix(taps[2], v0, vb, va)
        prod1 = mix(taps[1], k1, k0, kb) * mix(taps[2], v1, v0, vb)
        result.append((arriving, [ka, kb, va, vb, qa, qb, kc, kd, vc, vd]))
        arriving = whole * arriving + (ends[i] + step0 * prod0 + step1 * prod1)
    return result


def backward_middle(length, rates, ends, extras):
    devices = len(ends)
    whole = jnp.exp(-float(length) * rates)
    blank = jnp.zeros_like(extras[0][0])
    arriving = jnp.zeros_like(ends[0])
    result = [None] * devices
    for i in reversed(range(devices)):
        result[i] = (arriving, extras[i + 1] if i + 1 < devices else [blank] * len(extras[0]))
        arriving = whole * arriving + ends[i]
    return result


def middle_kernel(s, forward, pay_ref, decay_ref, filter_ref, back_ref, *wide):
    me = lax.axis_index("seq")
    lead, extra = (2 * s.modes, FORWARD_EXTRA) if forward else (s.modes, BACKWARD_EXTRA)
    in_ref, out_ref = wide if forward else (pay_ref, back_ref)
    if forward:
        widened(pay_ref, in_ref)
    rows = s.chunk_rows(lead, extra)
    for h in range(s.halves):
        lanes = pl.ds(pl.multiple_of((me + h * SUB) * LANES, LANES), LANES)
        rates = decay_ref[:, lanes]
        ends, extras = [], []
        for i in range(s.devices):
            e = i * rows + s.chunk_row(0, h, lead, extra)
            end = in_ref[e : e + s.modes, :]
            ends.append(end + in_ref[e + s.modes : e + lead, :] if forward else end)
            x = i * rows + s.chunk_row(lead, h, lead, extra)
            extras.append([in_ref[x + r : x + r + 1, :] for r in range(extra)])
        if forward:
            taps = [[filter_ref[i, tap : tap + 1, lanes] for tap in range(3)] for i in range(3)]
            result = forward_middle(s.length, rates, taps, ends, extras)
        else:
            result = backward_middle(s.length, rates, ends, extras)
        for i, (state, more) in enumerate(result):
            e = i * rows + s.chunk_row(0, h, lead, extra)
            if forward:
                out_ref[e : e + s.modes, :], out_ref[e + s.modes : e + lead, :] = split(state)
            else:
                out_ref[e : e + s.modes, :] = state
            x = i * rows + s.chunk_row(lead, h, lead, extra)
            for r in range(extra):
                out_ref[x + r : x + r + 1, :] = more[r]
    if forward:
        narrowed(out_ref, back_ref)


def exchange(s, pay, decay_rate, short_filter, forward):
    lead, extra = (2 * s.modes, FORWARD_EXTRA) if forward else (s.modes, BACKWARD_EXTRA)
    if s.direct:
        chunks = (s.devices, s.chunk_rows(lead, extra), LANES)
        got = lax.all_to_all(pay.reshape(chunks), "seq", 0, 0, tiled=True)
        back = pl.pallas_call(
            functools.partial(middle_kernel, s, forward),
            out_shape=jax.ShapeDtypeStruct(pay.shape, pay.dtype),
            scratch_shapes=[pltpu.VMEM(pay.shape, f32)] * 2 if forward else [],
            compiler_params=pltpu.CompilerParams(vmem_limit_bytes=GRANT),
        )(got.reshape(pay.shape), decay_rate, short_filter)
        return lax.all_to_all(back.reshape(chunks), "seq", 0, 0, tiled=True).reshape(pay.shape)
    rows = lead + extra
    width = s.channels // s.devices
    start = lax.axis_index("seq") * width
    rates = lax.dynamic_slice_in_dim(decay_rate, start, width, 1)
    part = lax.dynamic_slice_in_dim(short_filter, start, width, 2)
    pay = pay.reshape(rows, s.devices, width).transpose(1, 0, 2)
    got = lax.all_to_all(pay, "seq", 0, 0, tiled=True).astype(f32)
    ends = [got[i, : s.modes] for i in range(s.devices)]
    extras = [[got[i, lead + r][None] for r in range(extra)] for i in range(s.devices)]
    if forward:
        ends = [end + got[i, s.modes : lead] for i, end in enumerate(ends)]
        taps = [[part[i, tap][None] for tap in range(3)] for i in range(3)]
        result = forward_middle(s.length, rates, taps, ends, extras)
        highs = [lax.reduce_precision(state, 8, 7) for state, _ in result]
        result = [
            (jnp.concatenate([high, state - high]), more) for high, (state, more) in zip(highs, result)
        ]
    else:
        result = backward_middle(s.length, rates, ends, extras)
    back = jnp.stack([jnp.concatenate([state] + list(more)) for state, more in result])
    back = lax.all_to_all(back.astype(pay.dtype), "seq", 0, 0, tiled=True)
    return back.transpose(1, 0, 2).reshape(rows * s.tiles, LANES)


def inside_kernel(
    s, k_hbm, v_hbm, filter_hbm, decay_hbm, residue_hbm, inside_ref, first_ref, taps, poles, weights,
    kb, vb, fb, db, rb, ks, vs, prod, sems,
):
    pairs = [(decay_hbm, db), (residue_hbm, rb), (filter_hbm, fb), (k_hbm, kb), (v_hbm, vb)]
    copies = [pltpu.make_async_copy(a, b, sems.at[i]) for i, (a, b) in enumerate(pairs)]
    for copy in copies:
        copy.start()
    for copy in copies:
        copy.wait()
    stage_modes(s, db, poles, lambda x: jnp.exp(-x))
    stage_modes(s, rb, weights, lambda x: x)
    stage_taps(s, fb, taps)
    blank = jnp.zeros((SUB, LANES), f32)

    def half(h):
        taps_k, taps_v = (tap_tiles(s, taps, i, h) for i in (1, 2))

        products(s, kb, vb, ks, vs, prod, taps_k, taps_v, h)
        for i, (ref, part) in enumerate(((ks, taps_k), (vs, taps_v))):
            x0, x1 = (ref[staged(s, 0, offset, h), :] for offset in range(2))
            first_ref[major(s, 2 * i, h), :] = part[0] * x0
            first_ref[major(s, 2 * i + 1, h), :] = part[0] * x1 + part[1] * x0
        recur(s, prod, inside_ref, mode_tiles(s, poles, h), mode_tiles(s, weights, h), [blank] * s.modes, h)

    each_half(s, half)


def forward_kernel(
    s, inside_ref, first_ref, q_ref, stream_ref, cot_ref, back_ref, taps, poles, weights, gain_ref,
    conv_ref, sums_ref, near_ref,
    qs, xs, gs, back_s, squares, inners,
):
    widened(back_ref, back_s)
    steps = s.length // 16

    def half(h):
        p = mode_tiles(s, poles, h)
        w = mode_tiles(s, weights, h)
        gain = gain_ref[pl.ds(aligned(h * SUB, SUB), SUB), :]
        taps_q, taps_k, taps_v = (tap_tiles(s, taps, i, h) for i in range(3))
        near = [back_s[forward_slice(s, 2 * s.modes + r, h), :] for r in range(FORWARD_EXTRA)]
        for r, value in enumerate(near):
            near_ref[major(s, r, h), :] = value
        ka, kb, va, vb, qa, qb = near[:6]
        k0, k1, v0, v1 = (first_ref[major(s, r, h), :] for r in range(4))
        products = [
            (k0 + taps_k[1] * kb + taps_k[2] * ka) * (v0 + taps_v[1] * vb + taps_v[2] * va),
            (k1 + taps_k[2] * kb) * (v1 + taps_v[2] * vb),
        ]
        conv = []
        states = [
            back_s[forward_slice(s, m, h), :] + back_s[forward_slice(s, s.modes + m, h), :]
            for m in range(s.modes)
        ]
        for offset in range(2):
            states = [p[m] * states[m] + products[offset] for m in range(s.modes)]
            conv.append(total([w[m] * states[m] for m in range(s.modes)]))
        states = [w[m] * states[m] / (p[m] * p[m]) for m in range(s.modes)]
        first, ahead = [], states
        for offset in range(2):
            ahead = [p[m] * ahead[m] for m in range(s.modes)]
            first.append(conv[offset] - total(ahead))

        def bring(i):
            stage(s, q_ref, qs, i, h)
            stage(s, stream_ref, xs, i, h)
            stage(s, cot_ref, gs, i, h)

        def step(i, carry):
            (q1, q2), states = carry
            for block, offset in sixteen(0):
                rows = staged(s, 2 * i + block, offset, h)
                t = (2 * i + block) * SUB + offset
                out = major(s, t, h)
                inside = inside_ref[out, :]
                if block == 0 and offset < 2:
                    inside = jnp.where(i == 0, first[offset], inside)
                states = [p[m] * states[m] for m in range(s.modes)]
                conv = inside + total(states)
                conv_ref[out, :] = conv
                q0 = qs[rows, :]
                mixed = xs[rows, :] + mix(taps_q, q0, q1, q2) * conv
                part = pl.ds(pl.multiple_of(t * SUB, SUB), SUB)
                square, inner = mixed * mixed, gain * gs[rows, :] * mixed
                squares[part, :] = square + jnp.where(h == 0, 0.0, squares[part, :])
                inners[part, :] = inner + jnp.where(h == 0, 0.0, inners[part, :])
                q1, q2 = q0, q1
            bring(jnp.minimum(i + 1, steps - 1))
            return (q1, q2), states

        bring(0)
        lax.fori_loop(0, steps, step, ((qb, qa), states))

    each_half(s, half)
    for r, ref in enumerate((squares, inners)):
        parts = []
        for b in range(s.length // SUB):
            parts.append(
                total([ref[pl.ds(b * SUB * SUB + i, SUB, stride=SUB), :] for i in range(SUB)])
            )
        rows = jnp.concatenate(parts, axis=0)
        sums_ref[r : r + 1, :] = jnp.sum(rows.T, axis=0, keepdims=True)


def norm_kernel(
    s, width, sums_ref, conv_ref, q_ref, stream_ref, cot_ref, near_ref, taps, poles, gain_ref,
    normed_hbm, dstream_hbm, qgrad_hbm, dconv_ref, tail_ref, pay_ref,
    qs, xs, gs, ns, ds, normed_b, dstream_b, qgrad_b, inv_s, coef_s, sems,
):
    inverse = lax.rsqrt(sums_ref[0:1, :] / width + epsilon)
    coef = inverse * inverse * inverse * sums_ref[1:2, :] / width
    inv_s[...] = jnp.broadcast_to(inverse, (LANES, s.length)).T
    coef_s[...] = jnp.broadcast_to(coef, (LANES, s.length)).T
    blank = jnp.zeros((SUB, LANES), f32)
    steps = s.length // 16

    def pieces(h):
        cut = columns(h)
        sources = [
            (normed_b.at[:, cut], normed_hbm.at[:, cut]),
            (dstream_b.at[:, cut], dstream_hbm.at[:, cut]),
            (qgrad_b.at[pl.ds(16, s.length - 16), cut], qgrad_hbm.at[pl.ds(0, s.length - 16), cut]),
        ]
        return [pltpu.make_async_copy(a, b, sems.at[3 * h + i]) for i, (a, b) in enumerate(sources)]

    def half(h):
        gain = gain_ref[pl.ds(aligned(h * SUB, SUB), SUB), :]
        taps_q = tap_tiles(s, taps, 0, h)

        def bring(i):
            rows = jnp.minimum(i, steps - 1)
            stage(s, q_ref, qs, rows, h, i - rows + 1)
            stage(s, stream_ref, xs, rows, h)
            stage(s, cot_ref, gs, rows, h)

        def step(i, held):
            q1, q2, dq1, dq2 = held
            for block, offset in sixteen(0):
                rows = staged(s, 2 * i + block, offset, h)
                t = (2 * i + block) * SUB + offset
                out = major(s, t, h)
                inv = jnp.broadcast_to(inv_s[pl.ds(t, 1), :], (SUB, LANES))
                cf = jnp.broadcast_to(coef_s[pl.ds(t, 1), :], (SUB, LANES))
                q0 = qs[staged(s, 2 * i + block + 2, offset, h), :]
                qmix = mix(taps_q, q0, q1, q2)
                conv = conv_ref[out, :]
                mixed = xs[rows, :] + qmix * conv
                dmixed = inv * (gain * gs[rows, :]) - mixed * cf
                ns[rows, :] = mixed * inv * gain
                ds[rows, :] = dmixed
                dq0 = dmixed * conv
                dconv_ref[out, :] = dmixed * qmix
                qs[staged_before(s, 2 * i + block + 2, offset, h), :] = mix(taps_q, dq2, dq1, dq0)
                q1, q2, dq1, dq2 = q0, q1, dq0, dq1
            unstage(s, ns, normed_b, i, h)
            unstage(s, ds, dstream_b, i, h)
            unstage(s, qs, qgrad_b, i, h)
            bring(i + 1)
            return q1, q2, dq1, dq2

        bring(0)
        held = (near_ref[major(s, 5, h), :], near_ref[major(s, 4, h), :], blank, blank)
        _, _, dq1, dq2 = lax.fori_loop(0, steps, step, held)
        qs[staged(s, 2 * steps + 1, 6, h), :] = taps_q[0] * dq2 + taps_q[1] * dq1
        qs[staged(s, 2 * steps + 1, 7, h), :] = taps_q[0] * dq1
        for copy in pieces(h):
            copy.start()

    each_half(s, half)
    start = steps * 2 * s.tiles * SUB
    tail_ref[...] = qs[start : start + 2 * s.tiles * SUB, :]

    def ends(h):
        p = mode_tiles(s, poles, h)

        def step(i, states):
            for block, offset in sixteen(0, True):
                t = (2 * (steps - 1 - i) + block) * SUB + offset
                dconv = dconv_ref[major(s, t, h), :]
                states = [p[m] * states[m] + dconv for m in range(s.modes)]
            return states

        states = lax.fori_loop(0, steps, step, [blank] * s.modes)
        for m in range(s.modes):
            pay_ref[backward_slice(s, m, h), :] = states[m]
        first = [ds[staged(s, 0, offset, h), :] * conv_ref[major(s, offset, h), :] for offset in range(2)]
        for r, value in enumerate([dconv_ref[major(s, 0, h), :], *first, blank]):
            pay_ref[backward_slice(s, s.modes + r, h), :] = value

    each_half(s, ends)

    def finish(h):
        for copy in pieces(h):
            copy.wait()

    each_half(s, finish)


def backward_kernel(
    s, k_ref, v_ref, dconv_ref, tail_ref, near_ref, back_ref, taps, poles, weights, qgrad_in,
    qgrad_hbm, kgrad_hbm, vgrad_hbm,
    ks, vs, dprod, qs, kgrad_b, vgrad_b, qgrad_b, sems,
):
    del qgrad_in
    steps = s.length // 16

    def back(r, h):
        return back_ref[backward_slice(s, r, h), :]

    qs[...] = tail_ref[...]

    def tails(h):
        taps_q = tap_tiles(s, taps, 0, h)
        dq0, dq1 = back(s.modes + 1, h), back(s.modes + 2, h)
        rows = [staged(s, 1, offset, h) for offset in (6, 7)]
        qs[rows[0], :] = qs[rows[0], :] + taps_q[2] * dq0
        qs[rows[1], :] = qs[rows[1], :] + (taps_q[1] * dq0 + taps_q[2] * dq1)
        unstage(s, qs, qgrad_b, 0, h)

    each_half(s, tails)
    last = pltpu.make_async_copy(qgrad_b, qgrad_hbm.at[pl.ds(s.length - 16, 16), :], sems.at[2 * s.halves])
    last.start()

    def pieces(h):
        cut = columns(h)
        sources = [(kgrad_b, kgrad_hbm), (vgrad_b, vgrad_hbm)]
        return [
            pltpu.make_async_copy(a.at[:, cut], b.at[:, cut], sems.at[2 * h + i])
            for i, (a, b) in enumerate(sources)
        ]

    def half(h):
        p = mode_tiles(s, poles, h)
        w = mode_tiles(s, weights, h)
        arriving = [back(m, h) for m in range(s.modes)]
        recur(s, dconv_ref, dprod, p, w, arriving, h, reverse=True)
        taps_k, taps_v = (tap_tiles(s, taps, i, h) for i in (1, 2))

        def bring(i):
            stage(s, k_ref, ks, i, h, 1)
            stage(s, v_ref, vs, i, h, 1)

        def advance(inputs, grads, k2, v2, d):
            k0, k1, v0, v1 = inputs
            dk1, dk2, dv1, dv2 = grads
            dk0 = d * mix(taps_v, v0, v1, v2)
            dv0 = d * mix(taps_k, k0, k1, k2)
            out = mix(taps_k, dk0, dk1, dk2), mix(taps_v, dv0, dv1, dv2)
            return (k1, k2, v1, v2), (dk0, dk1, dv0, dv1), out

        bring(steps - 1)
        ka, kb, va, vb, _, _, kc, kd, vc, vd = (near_ref[major(s, r, h), :] for r in range(10))
        for ref, rows in ((ks, (ka, kb)), (vs, (va, vb))):
            for offset in range(2):
                ref[staged(s, 1, 6 + offset, h), :] = rows[offset]
        arriving = [back(m, h) for m in range(s.modes)]
        dconv0 = back(s.modes, h)
        d0 = total([w[m] * arriving[m] for m in range(s.modes)])
        d1 = total([w[m] * ((arriving[m] - dconv0) / p[m]) for m in range(s.modes)])
        ends = [staged(s, 2 * steps + 1, offset, h) for offset in (6, 7)]
        inputs = (kd, kc, vd, vc)
        grads = (jnp.zeros((SUB, LANES), f32),) * 4
        inputs, grads, _ = advance(inputs, grads, ks[ends[1], :], vs[ends[1], :], d1)
        inputs, grads, _ = advance(inputs, grads, ks[ends[0], :], vs[ends[0], :], d0)

        def step(i, carry):
            inputs, grads = carry
            i = steps - 1 - i

            @pl.when(i > 0)
            def _():
                bring(jnp.maximum(i - 1, 0))

            for block, offset in sixteen(0, True):
                d = dprod[major(s, (2 * i + block) * SUB + offset, h), :]
                rows = staged_before(s, 2 * i + block + 2, offset, h)
                inputs, grads, out = advance(inputs, grads, ks[rows, :], vs[rows, :], d)
                rows = staged(s, 2 * i + block + 2, offset, h)
                ks[rows, :], vs[rows, :] = out
            unstage(s, ks, kgrad_b, i + 1, h, i)
            unstage(s, vs, vgrad_b, i + 1, h, i)
            return inputs, grads

        lax.fori_loop(0, steps, step, (inputs, grads))
        for copy in pieces(h):
            copy.start()

    each_half(s, half)
    last.wait()

    def finish(h):
        for copy in pieces(h):
            copy.wait()

    each_half(s, finish)


def body(
    query_in, key_in, value_in, stream, short_filter, decay_rate, residue, norm_gain, cotangent
):
    length, channels = query_in.shape
    modes = decay_rate.shape[0]
    s = Sizes(length, channels, modes, lax.axis_size("seq"))
    total_width = channels * lax.axis_size("tp")
    wide = jax.ShapeDtypeStruct((length * s.tiles, LANES), f32)
    narrow = jax.ShapeDtypeStruct((length, channels), bf16)
    rows = 16 * s.tiles
    wide_s = pltpu.VMEM(wide.shape, f32)
    longer_s = pltpu.VMEM(((length + 16) * s.tiles, LANES), f32)
    narrow_s = pltpu.VMEM(narrow.shape, bf16)
    last_s = pltpu.VMEM((16, channels), bf16)
    tail_s = pltpu.VMEM((rows, LANES), f32)
    taps_s = pltpu.VMEM((3 * s.tiles * SUB, LANES), f32)
    mode_s = pltpu.VMEM((modes * s.tiles, LANES), f32)
    sum_s = pltpu.VMEM((length * SUB, LANES), f32)
    square_s = pltpu.VMEM((length, LANES), f32)
    gain = norm_gain.reshape(s.tiles, LANES)
    there = pl.BlockSpec(memory_space=pltpu.HBM)
    here = pl.BlockSpec(memory_space=pltpu.VMEM)

    def call(kernel, ins, outs, out_shape, scratch_shapes, operands, aliases={}, cost=None):
        return pl.pallas_call(
            functools.partial(kernel, s),
            in_specs=[there if c == "h" else here for c in ins],
            out_specs=[there if c == "h" else here for c in outs],
            out_shape=out_shape,
            scratch_shapes=scratch_shapes,
            input_output_aliases=aliases,
            cost_estimate=cost,
            compiler_params=pltpu.CompilerParams(vmem_limit_bytes=GRANT),
        )(*operands)

    forward_shape = s.exchange_shape(2 * modes, FORWARD_EXTRA)
    near_shape = jax.ShapeDtypeStruct((FORWARD_EXTRA * s.tiles, LANES), f32)

    def far(*arrays):
        return [pltpu.with_memory_space_constraint(x, pltpu.HBM) for x in arrays]

    def cost(per_element, arrays):
        return pl.CostEstimate(
            flops=per_element * length * channels, bytes_accessed=arrays * 4 * length * channels, transcendentals=0
        )

    filter_s = pltpu.VMEM(short_filter.shape, f32)
    rates_s = pltpu.VMEM(decay_rate.shape, f32)
    (pay,) = call(
        begin_kernel, "hhhhh", "v",
        (jax.ShapeDtypeStruct(forward_shape, bf16),),
        [narrow_s, narrow_s, last_s, filter_s, rates_s]
        + [wide_s] * 3 + [tail_s, pltpu.VMEM(forward_shape, f32), taps_s, mode_s]
        + [pltpu.SemaphoreType.DMA((3 + 2 * s.halves,))],
        far(query_in, key_in, value_in, short_filter, decay_rate),
    )
    inside, first, taps, poles, weights = call(
        inside_kernel, "hhhhh", "vvvvv",
        (wide, *(jax.ShapeDtypeStruct(x, f32) for x in ((4 * s.tiles, LANES), taps_s.shape, mode_s.shape, mode_s.shape))),
        [narrow_s, narrow_s, filter_s, rates_s, rates_s]
        + [wide_s] * 3 + [pltpu.SemaphoreType.DMA((5,))],
        far(key_in, value_in, short_filter, decay_rate, residue),
        cost=cost(75, 3),
    )
    back = exchange(s, pay, decay_rate, short_filter, True)
    conv, sums, near = call(
        forward_kernel, "v" * 10, "vvv",
        (wide, jax.ShapeDtypeStruct((2, length), f32), near_shape),
        [wide_s] * 3 + [pltpu.VMEM(forward_shape, f32), sum_s, sum_s],
        (inside, first, query_in, stream, cotangent, back, taps, poles, weights, gain),
        {0: 0},
    )
    sums = lax.psum(sums, "tp")
    normed, dstream, query_grad, dconv, tail, pay_back = call(
        lambda s, *refs: norm_kernel(s, total_width, *refs), "v" * 9, "hhhvvv",
        (narrow, narrow, narrow, wide, jax.ShapeDtypeStruct((rows, LANES), f32), jax.ShapeDtypeStruct(s.exchange_shape(modes, BACKWARD_EXTRA), f32)),
        [pltpu.VMEM(((length + 32) * s.tiles, LANES), f32)] + [longer_s] * 2 + [wide_s] * 2 + [narrow_s] * 2
        + [pltpu.VMEM((length + 16, channels), bf16)]
        + [square_s, square_s, pltpu.SemaphoreType.DMA((3 * s.halves,))],
        (sums, conv, query_in, stream, cotangent, near, taps, poles, gain),
    )
    back_back = exchange(s, pay_back, decay_rate, short_filter, False)
    query_grad, key_grad, value_grad = call(
        backward_kernel, "v" * 9 + "h", "hhh",
        (narrow, narrow, narrow),
        [longer_s] * 2 + [wide_s, tail_s] + [narrow_s] * 2 + [last_s]
        + [pltpu.SemaphoreType.DMA((1 + 2 * s.halves,))],
        (key_in, value_in, dconv, tail, near, back_back, taps, poles, weights, query_grad),
        {9: 0},
    )
    return (normed, dstream, query_grad, key_grad, value_grad)


def solution(mesh):
    cut = P("seq", "tp")
    return jax.shard_map(
        body,
        mesh=mesh,
        in_specs=(cut, cut, cut, cut, P(None, None, "tp"), P(None, "tp"), P(None, "tp"), P("tp"), cut),
        out_specs=(cut,) * 5,
        check_vma=False,
    )
```

```python
import functools

import jax
import jax.numpy as jnp
from jax import lax
from jax.experimental import pallas as pl
from jax.experimental.pallas import tpu as pltpu
from jax.sharding import PartitionSpec as P

f32 = jnp.float32
bf16 = jnp.bfloat16
epsilon = 1e-05
LANES = 128
SUB = 8
GROUP = LANES * SUB
FORWARD_EXTRA = 10
BACKWARD_EXTRA = 4
GRANT = 20 * 1024 * 1024


class Sizes:
    def __init__(self, length, channels, modes, devices):
        self.length, self.channels, self.modes, self.devices = length, channels, modes, devices
        self.tiles = channels // LANES
        self.halves = channels // GROUP
        self.direct = devices == SUB

    def chunk_row(self, r, h, lead, extra):
        if r < lead:
            return h * lead + r
        return self.halves * lead + h * extra + r - lead

    def chunk_rows(self, lead, extra):
        return -(-self.halves * (lead + extra) // SUB) * SUB

    def exchange_shape(self, lead, extra):
        if self.direct:
            return (self.devices * self.chunk_rows(lead, extra), LANES)
        return ((lead + extra) * self.tiles, LANES)

    def exchange_slice(self, r, h, lead, extra):
        if self.direct:
            return pl.ds(self.chunk_row(r, h, lead, extra), SUB, stride=self.chunk_rows(lead, extra))
        return pl.ds(r * self.tiles + h * SUB, SUB)


def staged(s, block, offset, h):
    start = block * (s.tiles * SUB) + (h * SUB * SUB + offset)
    return pl.ds(start, SUB, stride=SUB)


def major(s, t, h):
    start = t * s.tiles + h * SUB
    if not isinstance(start, int):
        start = pl.multiple_of(start, SUB)
    return pl.ds(start, SUB)


def staged_before(s, block, offset, h):
    if offset < 2:
        return staged(s, block - 1, offset + SUB - 2, h)
    return staged(s, block, offset - 2, h)


def aligned(start, unit):
    return start if isinstance(start, int) else pl.multiple_of(start, unit)


def columns(h):
    return pl.ds(aligned(h * GROUP, GROUP), GROUP)


def stage(s, x_ref, out_ref, i, h, pad=0):
    rows = x_ref[pl.ds(aligned(i * 16, 16), 16), columns(h)].astype(f32)
    base = (i + pad) * (2 * s.tiles * SUB) + h * (SUB * SUB)
    for part in range(2):
        for j in range(SUB):
            out_ref[pl.ds(aligned(base + (part * s.tiles + j) * SUB, SUB), SUB), :] = rows[
                part * SUB : (part + 1) * SUB, j * LANES : (j + 1) * LANES
            ]


def unstage(s, in_ref, x_ref, i, h, to=None):
    base = i * (2 * s.tiles * SUB) + h * (SUB * SUB)
    rows = [
        jnp.concatenate(
            [
                in_ref[pl.ds(aligned(base + (part * s.tiles + j) * SUB, SUB), SUB), :]
                for part in range(2)
            ],
            axis=0,
        )
        for j in range(SUB)
    ]
    to = i if to is None else to
    x_ref[pl.ds(aligned(to * 16, 16), 16), columns(h)] = jnp.concatenate(rows, axis=1).astype(bf16)


def stage_wide(s, x_ref, out_ref):
    for h in range(s.halves):
        stage(s, x_ref, out_ref, 0, h)


def each_half(s, body):
    def step(h, carry):
        body(h)
        return carry

    lax.fori_loop(0, s.halves, step, 0)


def sixteen(i, reverse=False):
    pairs = [(2 * i + part, offset) for part in range(2) for offset in range(SUB)]
    return pairs[::-1] if reverse else pairs


def stage_modes(s, x_ref, out_ref, f):
    for g in range(s.modes // SUB):
        rows = f(x_ref[g * SUB : (g + 1) * SUB, :])
        for j in range(s.tiles):
            start = (g * s.tiles + j) * SUB
            out_ref[start : start + SUB, :] = rows[:, j * LANES : (j + 1) * LANES]


def mode_tiles(s, ref, h):
    return [ref[staged(s, m // SUB, m % SUB, h), :] for m in range(s.modes)]


def stage_taps(s, filter_ref, out_ref):
    for i in range(3):
        rows = filter_ref[i]
        for j in range(s.tiles):
            start = (i * s.tiles + j) * SUB
            out_ref[start : start + 3, :] = rows[:, j * LANES : (j + 1) * LANES]


def tap_tiles(s, ref, i, h):
    return [ref[staged(s, i, tap, h), :] for tap in range(3)]


def total(parts):
    while len(parts) > 1:
        parts = [
            parts[i] + parts[i + 1] if i + 1 < len(parts) else parts[i]
            for i in range(0, len(parts), 2)
        ]
    return parts[0]


def mix(taps, now, before, before2):
    return taps[0] * now + taps[1] * before + taps[2] * before2


def recur(s, from_ref, to_ref, p, w, states, h, reverse=False):
    steps = s.length // 16

    def step(i, states):
        i = steps - 1 - i if reverse else i
        for block, offset in sixteen(0, reverse):
            rows = major(s, (2 * i + block) * SUB + offset, h)
            signal = from_ref[rows, :]
            states = [p[m] * states[m] + signal for m in range(s.modes)]
            to_ref[rows, :] = total([w[m] * states[m] for m in range(s.modes)])
        return states

    lax.fori_loop(0, steps, step, states)


def forward_slice(s, r, h):
    return s.exchange_slice(r, h, 2 * s.modes, FORWARD_EXTRA)


def split(x):
    high = x.astype(bf16).astype(f32)
    return high, x - high


def put_states(s, ref, states, h):
    for m in range(s.modes):
        high, low = split(states[m])
        ref[forward_slice(s, m, h), :] = high
        ref[forward_slice(s, s.modes + m, h), :] = low


def narrowed(from_ref, to_ref):
    rows = from_ref.shape[0]
    for i in range(0, rows, 16):
        to_ref[i : min(i + 16, rows), :] = from_ref[i : min(i + 16, rows), :].astype(bf16)


def widened(from_ref, to_ref):
    rows = from_ref.shape[0]
    for i in range(0, rows, 16):
        to_ref[i : min(i + 16, rows), :] = from_ref[i : min(i + 16, rows), :].astype(f32)


def backward_slice(s, r, h):
    return s.exchange_slice(r, h, s.modes, BACKWARD_EXTRA)


def begin_kernel(
    s, q_hbm, k_hbm, v_hbm, filter_hbm, decay_hbm, pay_ref,
    kb, vb, qb, fb, db, ks, vs, qs, pay_s, taps, poles, sems,
):
    copies = [(decay_hbm, db), (filter_hbm, fb), (q_hbm.at[pl.ds(s.length - 16, 16), :], qb)]
    for h in range(s.halves):
        cut = pl.ds(h * GROUP, GROUP)
        copies += [(k_hbm.at[:, cut], kb.at[:, cut]), (v_hbm.at[:, cut], vb.at[:, cut])]
    copies = [pltpu.make_async_copy(a, b, sems.at[i]) for i, (a, b) in enumerate(copies)]
    for copy in copies:
        copy.start()
    copies[0].wait()
    stage_modes(s, db, poles, lambda x: jnp.exp(-x))
    copies[1].wait()
    stage_taps(s, fb, taps)
    blank = jnp.zeros((SUB, LANES), f32)
    steps = s.length // 16
    copies[2].wait()
    stage_wide(s, qb, qs)

    def half(h):
        for i, (from_hbm, to) in enumerate(((k_hbm, kb), (v_hbm, vb))):
            cut = columns(h)
            pltpu.make_async_copy(from_hbm.at[:, cut], to.at[:, cut], sems.at[3 + 2 * h + i]).wait()
        p = mode_tiles(s, poles, h)
        taps_k, taps_v = (tap_tiles(s, taps, i, h) for i in (1, 2))

        def bring(i):
            stage(s, kb, ks, i, h)
            stage(s, vb, vs, i, h)

        def step(i, carry):
            (k1, k2, v1, v2), states = carry
            for block, offset in sixteen(0):
                rows = staged(s, 2 * i + block, offset, h)
                k0, v0 = ks[rows, :], vs[rows, :]
                product = mix(taps_k, k0, k1, k2) * mix(taps_v, v0, v1, v2)
                if block == 0 and offset < 2:
                    product = jnp.where(i == 0, 0.0, product)
                states = [p[m] * states[m] + product for m in range(s.modes)]
                k1, k2, v1, v2 = k0, k1, v0, v1
            bring(jnp.minimum(i + 1, steps - 1))
            return (k1, k2, v1, v2), states

        bring(0)
        held, states = lax.fori_loop(0, steps, step, ((blank,) * 4, [blank] * s.modes))
        put_states(s, pay_s, states, h)
        k1, k2, v1, v2 = held
        first = [staged(s, 0, offset, h) for offset in range(2)]
        last = [staged(s, 1, offset, h) for offset in (6, 7)]
        extra = [
            ks[first[0], :], ks[first[1], :], k2, k1,
            vs[first[0], :], vs[first[1], :], v2, v1,
            qs[last[0], :], qs[last[1], :],
        ]
        for r, value in enumerate(extra):
            pay_s[forward_slice(s, 2 * s.modes + r, h), :] = value

    each_half(s, half)
    narrowed(pay_s, pay_ref)


def forward_middle(length, rates, taps, ends, extras):
    devices = len(ends)
    whole, step0, step1 = (jnp.exp(-float(length - i) * rates) for i in range(3))
    blank = jnp.zeros_like(extras[0][0])
    arriving = jnp.zeros_like(ends[0])
    result = []
    for i in range(devices):
        k0, k1, _, _, v0, v1 = extras[i][:6]
        if i:
            _, _, ka, kb, _, _, va, vb, qa, qb = extras[i - 1][:10]
        else:
            ka = kb = va = vb = qa = qb = blank
        if i + 1 < devices:
            kc, kd, _, _, vc, vd = extras[i + 1][:6]
        else:
            kc = kd = vc = vd = blank
        prod0 = mix(taps[1], k0, kb, ka) * mix(taps[2], v0, vb, va)
        prod1 = mix(taps[1], k1, k0, kb) * mix(taps[2], v1, v0, vb)
        result.append((arriving, [ka, kb, va, vb, qa, qb, kc, kd, vc, vd]))
        arriving = whole * arriving + (ends[i] + step0 * prod0 + step1 * prod1)
    return result


def backward_middle(length, rates, ends, extras):
    devices = len(ends)
    whole = jnp.exp(-float(length) * rates)
    blank = jnp.zeros_like(extras[0][0])
    arriving = jnp.zeros_like(ends[0])
    result = [None] * devices
    for i in reversed(range(devices)):
        result[i] = (arriving, extras[i + 1] if i + 1 < devices else [blank] * len(extras[0]))
        arriving = whole * arriving + ends[i]
    return result


def middle_kernel(s, forward, pay_ref, decay_ref, filter_ref, back_ref, *wide):
    me = lax.axis_index("seq")
    lead, extra = (2 * s.modes, FORWARD_EXTRA) if forward else (s.modes, BACKWARD_EXTRA)
    in_ref, out_ref = wide if forward else (pay_ref, back_ref)
    if forward:
        widened(pay_ref, in_ref)
    rows = s.chunk_rows(lead, extra)
    for h in range(s.halves):
        lanes = pl.ds(pl.multiple_of((me + h * SUB) * LANES, LANES), LANES)
        rates = decay_ref[:, lanes]
        ends, extras = [], []
        for i in range(s.devices):
            e = i * rows + s.chunk_row(0, h, lead, extra)
            end = in_ref[e : e + s.modes, :]
            ends.append(end + in_ref[e + s.modes : e + lead, :] if forward else end)
            x = i * rows + s.chunk_row(lead, h, lead, extra)
            extras.append([in_ref[x + r : x + r + 1, :] for r in range(extra)])
        if forward:
            taps = [[filter_ref[i, tap : tap + 1, lanes] for tap in range(3)] for i in range(3)]
            result = forward_middle(s.length, rates, taps, ends, extras)
        else:
            result = backward_middle(s.length, rates, ends, extras)
        for i, (state, more) in enumerate(result):
            e = i * rows + s.chunk_row(0, h, lead, extra)
            if forward:
                out_ref[e : e + s.modes, :], out_ref[e + s.modes : e + lead, :] = split(state)
            else:
                out_ref[e : e + s.modes, :] = state
            x = i * rows + s.chunk_row(lead, h, lead, extra)
            for r in range(extra):
                out_ref[x + r : x + r + 1, :] = more[r]
    if forward:
        narrowed(out_ref, back_ref)


def exchange(s, pay, decay_rate, short_filter, forward):
    lead, extra = (2 * s.modes, FORWARD_EXTRA) if forward else (s.modes, BACKWARD_EXTRA)
    if s.direct:
        chunks = (s.devices, s.chunk_rows(lead, extra), LANES)
        got = lax.all_to_all(pay.reshape(chunks), "seq", 0, 0, tiled=True)
        back = pl.pallas_call(
            functools.partial(middle_kernel, s, forward),
            out_shape=jax.ShapeDtypeStruct(pay.shape, pay.dtype),
            scratch_shapes=[pltpu.VMEM(pay.shape, f32)] * 2 if forward else [],
            compiler_params=pltpu.CompilerParams(vmem_limit_bytes=GRANT),
        )(got.reshape(pay.shape), decay_rate, short_filter)
        return lax.all_to_all(back.reshape(chunks), "seq", 0, 0, tiled=True).reshape(pay.shape)
    rows = lead + extra
    width = s.channels // s.devices
    start = lax.axis_index("seq") * width
    rates = lax.dynamic_slice_in_dim(decay_rate, start, width, 1)
    part = lax.dynamic_slice_in_dim(short_filter, start, width, 2)
    pay = pay.reshape(rows, s.devices, width).transpose(1, 0, 2)
    got = lax.all_to_all(pay, "seq", 0, 0, tiled=True).astype(f32)
    ends = [got[i, : s.modes] for i in range(s.devices)]
    extras = [[got[i, lead + r][None] for r in range(extra)] for i in range(s.devices)]
    if forward:
        ends = [end + got[i, s.modes : lead] for i, end in enumerate(ends)]
        taps = [[part[i, tap][None] for tap in range(3)] for i in range(3)]
        result = forward_middle(s.length, rates, taps, ends, extras)
        highs = [lax.reduce_precision(state, 8, 7) for state, _ in result]
        result = [
            (jnp.concatenate([high, state - high]), more) for high, (state, more) in zip(highs, result)
        ]
    else:
        result = backward_middle(s.length, rates, ends, extras)
    back = jnp.stack([jnp.concatenate([state] + list(more)) for state, more in result])
    back = lax.all_to_all(back.astype(pay.dtype), "seq", 0, 0, tiled=True)
    return back.transpose(1, 0, 2).reshape(rows * s.tiles, LANES)


def inside_kernel(
    s, k_hbm, v_hbm, filter_hbm, decay_hbm, residue_hbm, inside_ref, first_ref,
    kb, vb, fb, db, rb, ks, vs, prod, taps, poles, weights, sems,
):
    pairs = [(decay_hbm, db), (residue_hbm, rb), (filter_hbm, fb), (k_hbm, kb), (v_hbm, vb)]
    copies = [pltpu.make_async_copy(a, b, sems.at[i]) for i, (a, b) in enumerate(pairs)]
    for copy in copies:
        copy.start()
    for copy in copies:
        copy.wait()
    stage_modes(s, db, poles, lambda x: jnp.exp(-x))
    stage_modes(s, rb, weights, lambda x: x)
    stage_taps(s, fb, taps)
    blank = jnp.zeros((SUB, LANES), f32)
    steps = s.length // 16

    def half(h):
        taps_k, taps_v = (tap_tiles(s, taps, i, h) for i in (1, 2))

        def products(i, held):
            stage(s, kb, ks, i, h)
            stage(s, vb, vs, i, h)
            k1, k2, v1, v2 = held
            for block, offset in sixteen(0):
                rows = staged(s, 2 * i + block, offset, h)
                k0, v0 = ks[rows, :], vs[rows, :]
                product = mix(taps_k, k0, k1, k2) * mix(taps_v, v0, v1, v2)
                if block == 0 and offset < 2:
                    product = jnp.where(i == 0, 0.0, product)
                prod[major(s, (2 * i + block) * SUB + offset, h), :] = product
                k1, k2, v1, v2 = k0, k1, v0, v1
            return k1, k2, v1, v2

        lax.fori_loop(0, steps, products, (blank,) * 4)
        for i, (ref, part) in enumerate(((ks, taps_k), (vs, taps_v))):
            x0, x1 = (ref[staged(s, 0, offset, h), :] for offset in range(2))
            first_ref[major(s, 2 * i, h), :] = part[0] * x0
            first_ref[major(s, 2 * i + 1, h), :] = part[0] * x1 + part[1] * x0
        recur(s, prod, inside_ref, mode_tiles(s, poles, h), mode_tiles(s, weights, h), [blank] * s.modes, h)

    each_half(s, half)


def forward_kernel(
    s, inside_ref, first_ref, q_ref, stream_ref, cot_ref, back_ref, filter_ref, decay_ref, residue_ref, gain_ref,
    conv_ref, sums_ref, near_ref,
    qs, xs, gs, back_s, taps, poles, weights, squares, inners,
):
    stage_modes(s, decay_ref, poles, lambda x: jnp.exp(-x))
    stage_modes(s, residue_ref, weights, lambda x: x)
    stage_taps(s, filter_ref, taps)

    widened(back_ref, back_s)
    steps = s.length // 16

    def half(h):
        p = mode_tiles(s, poles, h)
        w = mode_tiles(s, weights, h)
        gain = gain_ref[pl.ds(aligned(h * SUB, SUB), SUB), :]
        taps_q, taps_k, taps_v = (tap_tiles(s, taps, i, h) for i in range(3))
        near = [back_s[forward_slice(s, 2 * s.modes + r, h), :] for r in range(FORWARD_EXTRA)]
        for r, value in enumerate(near):
            near_ref[major(s, r, h), :] = value
        ka, kb, va, vb, qa, qb = near[:6]
        k0, k1, v0, v1 = (first_ref[major(s, r, h), :] for r in range(4))
        products = [
            (k0 + taps_k[1] * kb + taps_k[2] * ka) * (v0 + taps_v[1] * vb + taps_v[2] * va),
            (k1 + taps_k[2] * kb) * (v1 + taps_v[2] * vb),
        ]
        conv = []
        states = [
            back_s[forward_slice(s, m, h), :] + back_s[forward_slice(s, s.modes + m, h), :]
            for m in range(s.modes)
        ]
        for offset in range(2):
            states = [p[m] * states[m] + products[offset] for m in range(s.modes)]
            conv.append(total([w[m] * states[m] for m in range(s.modes)]))
        states = [w[m] * states[m] / (p[m] * p[m]) for m in range(s.modes)]
        first, ahead = [], states
        for offset in range(2):
            ahead = [p[m] * ahead[m] for m in range(s.modes)]
            first.append(conv[offset] - total(ahead))

        def bring(i):
            stage(s, q_ref, qs, i, h)
            stage(s, stream_ref, xs, i, h)
            stage(s, cot_ref, gs, i, h)

        def step(i, carry):
            (q1, q2), states = carry
            for block, offset in sixteen(0):
                rows = staged(s, 2 * i + block, offset, h)
                t = (2 * i + block) * SUB + offset
                out = major(s, t, h)
                inside = inside_ref[out, :]
                if block == 0 and offset < 2:
                    inside = jnp.where(i == 0, first[offset], inside)
                states = [p[m] * states[m] for m in range(s.modes)]
                conv = inside + total(states)
                conv_ref[out, :] = conv
                q0 = qs[rows, :]
                mixed = xs[rows, :] + mix(taps_q, q0, q1, q2) * conv
                part = pl.ds(pl.multiple_of(t * SUB, SUB), SUB)
                square, inner = mixed * mixed, gain * gs[rows, :] * mixed
                squares[part, :] = square + jnp.where(h == 0, 0.0, squares[part, :])
                inners[part, :] = inner + jnp.where(h == 0, 0.0, inners[part, :])
                q1, q2 = q0, q1
            bring(jnp.minimum(i + 1, steps - 1))
            return (q1, q2), states

        bring(0)
        lax.fori_loop(0, steps, step, ((qb, qa), states))

    each_half(s, half)
    for r, ref in enumerate((squares, inners)):
        parts = []
        for b in range(s.length // SUB):
            parts.append(
                total([ref[pl.ds(b * SUB * SUB + i, SUB, stride=SUB), :] for i in range(SUB)])
            )
        rows = jnp.concatenate(parts, axis=0)
        sums_ref[r : r + 1, :] = jnp.sum(rows.T, axis=0, keepdims=True)


def norm_kernel(
    s, width, sums_ref, conv_ref, q_ref, stream_ref, cot_ref, near_ref, filter_ref, decay_ref, gain_ref,
    normed_hbm, dstream_hbm, qgrad_hbm, dconv_hbm, tail_hbm, pay_ref,
    qs, xs, gs, ns, ds, dconv_ref, normed_b, dstream_b, qgrad_b, taps, poles, inv_s, coef_s, sems,
):
    inverse = lax.rsqrt(sums_ref[0:1, :] / width + epsilon)
    coef = inverse * inverse * inverse * sums_ref[1:2, :] / width
    inv_s[...] = jnp.broadcast_to(inverse, (LANES, s.length)).T
    coef_s[...] = jnp.broadcast_to(coef, (LANES, s.length)).T
    stage_modes(s, decay_ref, poles, lambda x: jnp.exp(-x))
    stage_taps(s, filter_ref, taps)
    blank = jnp.zeros((SUB, LANES), f32)
    steps = s.length // 16

    def pieces(h):
        cut = columns(h)
        sources = [
            (normed_b.at[:, cut], normed_hbm.at[:, cut]),
            (dstream_b.at[:, cut], dstream_hbm.at[:, cut]),
            (qgrad_b.at[pl.ds(16, s.length - 16), cut], qgrad_hbm.at[pl.ds(0, s.length - 16), cut]),
        ]
        return [pltpu.make_async_copy(a, b, sems.at[3 * h + i]) for i, (a, b) in enumerate(sources)]

    def half(h):
        gain = gain_ref[pl.ds(aligned(h * SUB, SUB), SUB), :]
        taps_q = tap_tiles(s, taps, 0, h)

        def bring(i):
            rows = jnp.minimum(i, steps - 1)
            stage(s, q_ref, qs, rows, h, i - rows + 1)
            stage(s, stream_ref, xs, rows, h)
            stage(s, cot_ref, gs, rows, h)

        def step(i, held):
            q1, q2, dq1, dq2 = held
            for block, offset in sixteen(0):
                rows = staged(s, 2 * i + block, offset, h)
                t = (2 * i + block) * SUB + offset
                out = major(s, t, h)
                inv = jnp.broadcast_to(inv_s[pl.ds(t, 1), :], (SUB, LANES))
                cf = jnp.broadcast_to(coef_s[pl.ds(t, 1), :], (SUB, LANES))
                q0 = qs[staged(s, 2 * i + block + 2, offset, h), :]
                qmix = mix(taps_q, q0, q1, q2)
                conv = conv_ref[out, :]
                mixed = xs[rows, :] + qmix * conv
                dmixed = inv * (gain * gs[rows, :]) - mixed * cf
                ns[rows, :] = mixed * inv * gain
                ds[rows, :] = dmixed
                dq0 = dmixed * conv
                dconv_ref[out, :] = dmixed * qmix
                qs[staged_before(s, 2 * i + block + 2, offset, h), :] = mix(taps_q, dq2, dq1, dq0)
                q1, q2, dq1, dq2 = q0, q1, dq0, dq1
            unstage(s, ns, normed_b, i, h)
            unstage(s, ds, dstream_b, i, h)
            unstage(s, qs, qgrad_b, i, h)
            bring(i + 1)
            return q1, q2, dq1, dq2

        bring(0)
        held = (near_ref[major(s, 5, h), :], near_ref[major(s, 4, h), :], blank, blank)
        _, _, dq1, dq2 = lax.fori_loop(0, steps, step, held)
        qs[staged(s, 2 * steps + 1, 6, h), :] = taps_q[0] * dq2 + taps_q[1] * dq1
        qs[staged(s, 2 * steps + 1, 7, h), :] = taps_q[0] * dq1
        for copy in pieces(h):
            copy.start()

    each_half(s, half)
    tail = pl.ds(steps * 2 * s.tiles * SUB, 2 * s.tiles * SUB)
    later = [
        pltpu.make_async_copy(dconv_ref, dconv_hbm, sems.at[3 * s.halves]),
        pltpu.make_async_copy(qs.at[tail], tail_hbm, sems.at[3 * s.halves + 1]),
    ]
    for copy in later:
        copy.start()

    def ends(h):
        p = mode_tiles(s, poles, h)

        def step(i, states):
            for block, offset in sixteen(0, True):
                t = (2 * (steps - 1 - i) + block) * SUB + offset
                dconv = dconv_ref[major(s, t, h), :]
                states = [p[m] * states[m] + dconv for m in range(s.modes)]
            return states

        states = lax.fori_loop(0, steps, step, [blank] * s.modes)
        for m in range(s.modes):
            pay_ref[backward_slice(s, m, h), :] = states[m]
        first = [ds[staged(s, 0, offset, h), :] * conv_ref[major(s, offset, h), :] for offset in range(2)]
        for r, value in enumerate([dconv_ref[major(s, 0, h), :], *first, blank]):
            pay_ref[backward_slice(s, s.modes + r, h), :] = value

    each_half(s, ends)

    def finish(h):
        for copy in pieces(h):
            copy.wait()

    each_half(s, finish)
    for copy in later:
        copy.wait()


def inside_back_kernel(s, dconv_hbm, decay_hbm, residue_hbm, inside_ref, cs, db, rb, poles, weights, sems):
    pairs = [(decay_hbm, db), (residue_hbm, rb), (dconv_hbm, cs)]
    copies = [pltpu.make_async_copy(a, b, sems.at[i]) for i, (a, b) in enumerate(pairs)]
    for copy in copies:
        copy.start()
    for copy in copies[:2]:
        copy.wait()
    stage_modes(s, db, poles, lambda x: jnp.exp(-x))
    stage_modes(s, rb, weights, lambda x: x)
    copies[2].wait()
    blank = jnp.zeros((SUB, LANES), f32)

    def half(h):
        p, w = mode_tiles(s, poles, h), mode_tiles(s, weights, h)
        recur(s, cs, inside_ref, p, w, [blank] * s.modes, h, reverse=True)

    each_half(s, half)


def backward_kernel(
    s, k_ref, v_ref, inside_ref, tail_hbm, near_ref, back_ref, filter_ref, decay_ref, residue_ref, qgrad_in,
    qgrad_hbm, kgrad_hbm, vgrad_hbm,
    ks, vs, qs, kgrad_b, vgrad_b, qgrad_b, taps, poles, weights, sems,
):
    del qgrad_in
    tail = pltpu.make_async_copy(tail_hbm, qs, sems.at[2 * s.halves + 1])
    tail.start()
    stage_modes(s, decay_ref, poles, lambda x: jnp.exp(-x))
    stage_modes(s, residue_ref, weights, lambda x: x)
    stage_taps(s, filter_ref, taps)
    steps = s.length // 16

    def back(r, h):
        return back_ref[backward_slice(s, r, h), :]

    def pieces(h):
        cut = columns(h)
        sources = [(kgrad_b, kgrad_hbm), (vgrad_b, vgrad_hbm)]
        return [
            pltpu.make_async_copy(a.at[:, cut], b.at[:, cut], sems.at[2 * h + i])
            for i, (a, b) in enumerate(sources)
        ]

    last = pltpu.make_async_copy(qgrad_b, qgrad_hbm.at[pl.ds(s.length - 16, 16), :], sems.at[2 * s.halves])

    def tails(h):
        taps_q = tap_tiles(s, taps, 0, h)
        dq0, dq1 = back(s.modes + 1, h), back(s.modes + 2, h)
        rows = [staged(s, 1, offset, h) for offset in (6, 7)]
        qs[rows[0], :] = qs[rows[0], :] + taps_q[2] * dq0
        qs[rows[1], :] = qs[rows[1], :] + (taps_q[1] * dq0 + taps_q[2] * dq1)
        unstage(s, qs, qgrad_b, 0, h)

    def half(h):
        p = mode_tiles(s, poles, h)
        w = mode_tiles(s, weights, h)
        taps_k, taps_v = (tap_tiles(s, taps, i, h) for i in (1, 2))

        def bring(i):
            stage(s, k_ref, ks, i, h, 1)
            stage(s, v_ref, vs, i, h, 1)

        def advance(inputs, grads, k2, v2, d):
            k0, k1, v0, v1 = inputs
            dk1, dk2, dv1, dv2 = grads
            dk0 = d * mix(taps_v, v0, v1, v2)
            dv0 = d * mix(taps_k, k0, k1, k2)
            out = mix(taps_k, dk0, dk1, dk2), mix(taps_v, dv0, dv1, dv2)
            return (k1, k2, v1, v2), (dk0, dk1, dv0, dv1), out

        bring(steps - 1)
        ka, kb, va, vb, _, _, kc, kd, vc, vd = (near_ref[major(s, r, h), :] for r in range(10))
        for ref, rows in ((ks, (ka, kb)), (vs, (va, vb))):
            for offset in range(2):
                ref[staged(s, 1, 6 + offset, h), :] = rows[offset]
        arriving = [back(m, h) for m in range(s.modes)]
        dconv0 = back(s.modes, h)
        d0 = total([w[m] * arriving[m] for m in range(s.modes)])
        d1 = total([w[m] * ((arriving[m] - dconv0) / p[m]) for m in range(s.modes)])
        ends = [staged(s, 2 * steps + 1, offset, h) for offset in (6, 7)]
        inputs = (kd, kc, vd, vc)
        grads = (jnp.zeros((SUB, LANES), f32),) * 4
        inputs, grads, _ = advance(inputs, grads, ks[ends[1], :], vs[ends[1], :], d1)
        inputs, grads, _ = advance(inputs, grads, ks[ends[0], :], vs[ends[0], :], d0)

        def step(i, carry):
            states, inputs, grads = carry
            i = steps - 1 - i

            @pl.when(i > 0)
            def _():
                bring(jnp.maximum(i - 1, 0))

            for block, offset in sixteen(0, True):
                states = [p[m] * states[m] for m in range(s.modes)]
                d = inside_ref[major(s, (2 * i + block) * SUB + offset, h), :] + total(states)
                rows = staged_before(s, 2 * i + block + 2, offset, h)
                inputs, grads, out = advance(inputs, grads, ks[rows, :], vs[rows, :], d)
                rows = staged(s, 2 * i + block + 2, offset, h)
                ks[rows, :], vs[rows, :] = out
            unstage(s, ks, kgrad_b, i + 1, h, i)
            unstage(s, vs, vgrad_b, i + 1, h, i)
            return states, inputs, grads

        states = [w[m] * arriving[m] for m in range(s.modes)]
        lax.fori_loop(0, steps, step, (states, inputs, grads))
        for copy in pieces(h):
            copy.start()

        @pl.when(h == 0)
        def _():
            tail.wait()
            each_half(s, tails)
            last.start()

    each_half(s, half)
    last.wait()

    def finish(h):
        for copy in pieces(h):
            copy.wait()

    each_half(s, finish)


def body(
    query_in, key_in, value_in, stream, short_filter, decay_rate, residue, norm_gain, cotangent
):
    length, channels = query_in.shape
    modes = decay_rate.shape[0]
    s = Sizes(length, channels, modes, lax.axis_size("seq"))
    total_width = channels * lax.axis_size("tp")
    wide = jax.ShapeDtypeStruct((length * s.tiles, LANES), f32)
    narrow = jax.ShapeDtypeStruct((length, channels), bf16)
    rows = 16 * s.tiles
    wide_s = pltpu.VMEM(wide.shape, f32)
    longer_s = pltpu.VMEM(((length + 16) * s.tiles, LANES), f32)
    narrow_s = pltpu.VMEM(narrow.shape, bf16)
    last_s = pltpu.VMEM((16, channels), bf16)
    tail_s = pltpu.VMEM((rows, LANES), f32)
    taps_s = pltpu.VMEM((3 * s.tiles * SUB, LANES), f32)
    mode_s = pltpu.VMEM((modes * s.tiles, LANES), f32)
    sum_s = pltpu.VMEM((length * SUB, LANES), f32)
    square_s = pltpu.VMEM((length, LANES), f32)
    gain = norm_gain.reshape(s.tiles, LANES)
    there = pl.BlockSpec(memory_space=pltpu.HBM)
    here = pl.BlockSpec(memory_space=pltpu.VMEM)

    def call(kernel, ins, outs, out_shape, scratch_shapes, operands, aliases={}, cost=None):
        return pl.pallas_call(
            functools.partial(kernel, s),
            in_specs=[there if c == "h" else here for c in ins],
            out_specs=[there if c == "h" else here for c in outs],
            out_shape=out_shape,
            scratch_shapes=scratch_shapes,
            input_output_aliases=aliases,
            cost_estimate=cost,
            compiler_params=pltpu.CompilerParams(vmem_limit_bytes=GRANT),
        )(*operands)

    forward_shape = s.exchange_shape(2 * modes, FORWARD_EXTRA)
    near_shape = jax.ShapeDtypeStruct((FORWARD_EXTRA * s.tiles, LANES), f32)

    def far(*arrays):
        return [pltpu.with_memory_space_constraint(x, pltpu.HBM) for x in arrays]

    def cost(per_element, arrays):
        return pl.CostEstimate(
            flops=per_element * length * channels, bytes_accessed=arrays * 4 * length * channels, transcendentals=0
        )

    filter_s = pltpu.VMEM(short_filter.shape, f32)
    rates_s = pltpu.VMEM(decay_rate.shape, f32)
    (pay,) = call(
        begin_kernel, "hhhhh", "v",
        (jax.ShapeDtypeStruct(forward_shape, bf16),),
        [narrow_s, narrow_s, last_s, filter_s, rates_s]
        + [wide_s, wide_s, tail_s, pltpu.VMEM(forward_shape, f32), taps_s, mode_s]
        + [pltpu.SemaphoreType.DMA((3 + 2 * s.halves,))],
        far(query_in, key_in, value_in, short_filter, decay_rate),
    )
    inside, first = call(
        inside_kernel, "hhhhh", "vv", (wide, jax.ShapeDtypeStruct((4 * s.tiles, LANES), f32)),
        [narrow_s, narrow_s, filter_s, rates_s, rates_s]
        + [wide_s] * 3 + [taps_s, mode_s, mode_s, pltpu.SemaphoreType.DMA((5,))],
        far(key_in, value_in, short_filter, decay_rate, residue),
        cost=cost(75, 3),
    )
    back = exchange(s, pay, decay_rate, short_filter, True)
    conv, sums, near = call(
        forward_kernel, "v" * 10, "vvv",
        (wide, jax.ShapeDtypeStruct((2, length), f32), near_shape),
        [wide_s] * 3 + [pltpu.VMEM(forward_shape, f32), taps_s, mode_s, mode_s, sum_s, sum_s],
        (inside, first, query_in, stream, cotangent, back, short_filter, decay_rate, residue, gain),
        {0: 0},
    )
    sums = lax.psum(sums, "tp")
    normed, dstream, query_grad, dconv, tail, pay_back = call(
        lambda s, *refs: norm_kernel(s, total_width, *refs), "v" * 9, "hhhhhv",
        (narrow, narrow, narrow, wide, jax.ShapeDtypeStruct((rows, LANES), f32), jax.ShapeDtypeStruct(s.exchange_shape(modes, BACKWARD_EXTRA), f32)),
        [pltpu.VMEM(((length + 32) * s.tiles, LANES), f32)] + [longer_s] * 2 + [wide_s] * 3 + [narrow_s] * 2
        + [pltpu.VMEM((length + 16, channels), bf16)]
        + [taps_s, mode_s, square_s, square_s, pltpu.SemaphoreType.DMA((3 * s.halves + 2,))],
        (sums, conv, query_in, stream, cotangent, near, short_filter, decay_rate, gain),
    )
    (inside_back,) = call(
        inside_back_kernel, "hhh", "v", (wide,),
        [wide_s, rates_s, rates_s, mode_s, mode_s, pltpu.SemaphoreType.DMA((3,))],
        far(dconv, decay_rate, residue),
        cost=cost(64, 3),
    )
    back_back = exchange(s, pay_back, decay_rate, short_filter, False)
    query_grad, key_grad, value_grad = call(
        backward_kernel, "vvvhvvvvvh", "hhh",
        (narrow, narrow, narrow),
        [longer_s] * 2 + [tail_s] + [narrow_s] * 2 + [last_s, taps_s, mode_s, mode_s]
        + [pltpu.SemaphoreType.DMA((2 + 2 * s.halves,))],
        (key_in, value_in, inside_back, tail, near, back_back, short_filter, decay_rate, residue, query_grad),
        {9: 0},
    )
    return (normed, dstream, query_grad, key_grad, value_grad)


def solution(mesh):
    cut = P("seq", "tp")
    return jax.shard_map(
        body,
        mesh=mesh,
        in_specs=(cut, cut, cut, cut, P(None, None, "tp"), P(None, "tp"), P(None, "tp"), P("tp"), cut),
        out_specs=(cut,) * 5,
        check_vma=False,
    )
```

```python
import functools

import jax
import jax.numpy as jnp
from jax import lax
from jax.experimental import pallas as pl
from jax.experimental.pallas import tpu as pltpu
from jax.sharding import PartitionSpec as P

f32 = jnp.float32
bf16 = jnp.bfloat16
epsilon = 1e-05
LANES = 128
SUB = 8
GROUP = LANES * SUB
FORWARD_EXTRA = 10
BACKWARD_EXTRA = 4
GRANT = 20 * 1024 * 1024


class Sizes:
    def __init__(self, length, channels, modes, devices):
        self.length, self.channels, self.modes, self.devices = length, channels, modes, devices
        self.tiles = channels // LANES
        self.halves = channels // GROUP
        self.direct = devices == SUB

    def chunk_row(self, r, h, lead, extra):
        if r < lead:
            return h * lead + r
        return self.halves * lead + h * extra + r - lead

    def chunk_rows(self, lead, extra):
        return -(-self.halves * (lead + extra) // SUB) * SUB

    def exchange_shape(self, lead, extra):
        if self.direct:
            return (self.devices * self.chunk_rows(lead, extra), LANES)
        return ((lead + extra) * self.tiles, LANES)

    def exchange_slice(self, r, h, lead, extra):
        if self.direct:
            return pl.ds(self.chunk_row(r, h, lead, extra), SUB, stride=self.chunk_rows(lead, extra))
        return pl.ds(r * self.tiles + h * SUB, SUB)


def staged(s, block, offset, h):
    start = block * (s.tiles * SUB) + (h * SUB * SUB + offset)
    return pl.ds(start, SUB, stride=SUB)


def major(s, t, h):
    start = t * s.tiles + h * SUB
    if not isinstance(start, int):
        start = pl.multiple_of(start, SUB)
    return pl.ds(start, SUB)


def staged_before(s, block, offset, h):
    if offset < 2:
        return staged(s, block - 1, offset + SUB - 2, h)
    return staged(s, block, offset - 2, h)


def aligned(start, unit):
    return start if isinstance(start, int) else pl.multiple_of(start, unit)


def columns(h):
    return pl.ds(aligned(h * GROUP, GROUP), GROUP)


def stage(s, x_ref, out_ref, i, h, pad=0):
    rows = x_ref[pl.ds(aligned(i * 16, 16), 16), columns(h)].astype(f32)
    base = (i + pad) * (2 * s.tiles * SUB) + h * (SUB * SUB)
    for part in range(2):
        for j in range(SUB):
            out_ref[pl.ds(aligned(base + (part * s.tiles + j) * SUB, SUB), SUB), :] = rows[
                part * SUB : (part + 1) * SUB, j * LANES : (j + 1) * LANES
            ]


def unstage(s, in_ref, x_ref, i, h, to=None):
    base = i * (2 * s.tiles * SUB) + h * (SUB * SUB)
    rows = [
        jnp.concatenate(
            [
                in_ref[pl.ds(aligned(base + (part * s.tiles + j) * SUB, SUB), SUB), :]
                for part in range(2)
            ],
            axis=0,
        )
        for j in range(SUB)
    ]
    to = i if to is None else to
    x_ref[pl.ds(aligned(to * 16, 16), 16), columns(h)] = jnp.concatenate(rows, axis=1).astype(bf16)


def stage_wide(s, x_ref, out_ref):
    for h in range(s.halves):
        stage(s, x_ref, out_ref, 0, h)


def each_half(s, body):
    def step(h, carry):
        body(h)
        return carry

    lax.fori_loop(0, s.halves, step, 0)


def sixteen(i, reverse=False):
    pairs = [(2 * i + part, offset) for part in range(2) for offset in range(SUB)]
    return pairs[::-1] if reverse else pairs


def stage_modes(s, x_ref, out_ref, f):
    for g in range(s.modes // SUB):
        rows = f(x_ref[g * SUB : (g + 1) * SUB, :])
        for j in range(s.tiles):
            start = (g * s.tiles + j) * SUB
            out_ref[start : start + SUB, :] = rows[:, j * LANES : (j + 1) * LANES]


def mode_tiles(s, ref, h):
    return [ref[staged(s, m // SUB, m % SUB, h), :] for m in range(s.modes)]


def stage_taps(s, filter_ref, out_ref):
    for i in range(3):
        rows = filter_ref[i]
        for j in range(s.tiles):
            start = (i * s.tiles + j) * SUB
            out_ref[start : start + 3, :] = rows[:, j * LANES : (j + 1) * LANES]


def tap_tiles(s, ref, i, h):
    return [ref[staged(s, i, tap, h), :] for tap in range(3)]


def total(parts):
    while len(parts) > 1:
        parts = [
            parts[i] + parts[i + 1] if i + 1 < len(parts) else parts[i]
            for i in range(0, len(parts), 2)
        ]
    return parts[0]


def mix(taps, now, before, before2):
    return taps[0] * now + taps[1] * before + taps[2] * before2


def products(s, k_ref, v_ref, ks, vs, to_ref, taps_k, taps_v, h):
    def step(i, held):
        stage(s, k_ref, ks, i, h)
        stage(s, v_ref, vs, i, h)
        k1, k2, v1, v2 = held
        for block, offset in sixteen(0):
            rows = staged(s, 2 * i + block, offset, h)
            k0, v0 = ks[rows, :], vs[rows, :]
            product = mix(taps_k, k0, k1, k2) * mix(taps_v, v0, v1, v2)
            if block == 0 and offset < 2:
                product = jnp.where(i == 0, 0.0, product)
            to_ref[major(s, (2 * i + block) * SUB + offset, h), :] = product
            k1, k2, v1, v2 = k0, k1, v0, v1
        return k1, k2, v1, v2

    return lax.fori_loop(0, s.length // 16, step, (jnp.zeros((SUB, LANES), f32),) * 4)


def recur(s, from_ref, to_ref, p, w, states, h, reverse=False):
    steps = s.length // 16

    def step(i, states):
        i = steps - 1 - i if reverse else i
        for block, offset in sixteen(0, reverse):
            rows = major(s, (2 * i + block) * SUB + offset, h)
            signal = from_ref[rows, :]
            states = [p[m] * states[m] + signal for m in range(s.modes)]
            to_ref[rows, :] = total([w[m] * states[m] for m in range(s.modes)])
        return states

    lax.fori_loop(0, steps, step, states)


def forward_slice(s, r, h):
    return s.exchange_slice(r, h, 2 * s.modes, FORWARD_EXTRA)


def split(x):
    high = x.astype(bf16).astype(f32)
    return high, x - high


def put_states(s, ref, states, h):
    for m in range(s.modes):
        high, low = split(states[m])
        ref[forward_slice(s, m, h), :] = high
        ref[forward_slice(s, s.modes + m, h), :] = low


def narrowed(from_ref, to_ref):
    rows = from_ref.shape[0]
    for i in range(0, rows, 16):
        to_ref[i : min(i + 16, rows), :] = from_ref[i : min(i + 16, rows), :].astype(bf16)


def widened(from_ref, to_ref):
    rows = from_ref.shape[0]
    for i in range(0, rows, 16):
        to_ref[i : min(i + 16, rows), :] = from_ref[i : min(i + 16, rows), :].astype(f32)


def backward_slice(s, r, h):
    return s.exchange_slice(r, h, s.modes, BACKWARD_EXTRA)


def begin_kernel(
    s, q_hbm, k_hbm, v_hbm, filter_hbm, decay_hbm, pay_ref,
    kb, vb, qb, fb, db, ks, vs, prod, qs, pay_s, taps, poles, sems,
):
    copies = [(decay_hbm, db), (filter_hbm, fb), (q_hbm.at[pl.ds(s.length - 16, 16), :], qb)]
    for h in range(s.halves):
        cut = pl.ds(h * GROUP, GROUP)
        copies += [(k_hbm.at[:, cut], kb.at[:, cut]), (v_hbm.at[:, cut], vb.at[:, cut])]
    copies = [pltpu.make_async_copy(a, b, sems.at[i]) for i, (a, b) in enumerate(copies)]
    for i, copy in enumerate(copies):
        copy.start(priority=i % 2)
    copies[0].wait()
    stage_modes(s, db, poles, lambda x: jnp.exp(-x))
    copies[1].wait()
    stage_taps(s, fb, taps)
    blank = jnp.zeros((SUB, LANES), f32)
    copies[2].wait()
    stage_wide(s, qb, qs)

    def half(h):
        for i, (from_hbm, to) in enumerate(((k_hbm, kb), (v_hbm, vb))):
            cut = columns(h)
            pltpu.make_async_copy(from_hbm.at[:, cut], to.at[:, cut], sems.at[3 + 2 * h + i]).wait()
        p = mode_tiles(s, poles, h)
        taps_k, taps_v = (tap_tiles(s, taps, i, h) for i in (1, 2))

        held = products(s, kb, vb, ks, vs, prod, taps_k, taps_v, h)

        def step(i, states):
            for block, offset in sixteen(0):
                product = prod[major(s, (2 * i + block) * SUB + offset, h), :]
                states = [p[m] * states[m] + product for m in range(s.modes)]
            return states

        states = lax.fori_loop(0, s.length // 16, step, [blank] * s.modes)
        put_states(s, pay_s, states, h)
        k1, k2, v1, v2 = held
        first = [staged(s, 0, offset, h) for offset in range(2)]
        last = [staged(s, 1, offset, h) for offset in (6, 7)]
        extra = [
            ks[first[0], :], ks[first[1], :], k2, k1,
            vs[first[0], :], vs[first[1], :], v2, v1,
            qs[last[0], :], qs[last[1], :],
        ]
        for r, value in enumerate(extra):
            pay_s[forward_slice(s, 2 * s.modes + r, h), :] = value

    each_half(s, half)
    narrowed(pay_s, pay_ref)


def forward_middle(length, rates, taps, ends, extras):
    devices = len(ends)
    whole, step0, step1 = (jnp.exp(-float(length - i) * rates) for i in range(3))
    blank = jnp.zeros_like(extras[0][0])
    arriving = jnp.zeros_like(ends[0])
    result = []
    for i in range(devices):
        k0, k1, _, _, v0, v1 = extras[i][:6]
        if i:
            _, _, ka, kb, _, _, va, vb, qa, qb = extras[i - 1][:10]
        else:
            ka = kb = va = vb = qa = qb = blank
        if i + 1 < devices:
            kc, kd, _, _, vc, vd = extras[i + 1][:6]
        else:
            kc = kd = vc = vd = blank
        prod0 = mix(taps[1], k0, kb, ka) * mix(taps[2], v0, vb, va)
        prod1 = mix(taps[1], k1, k0, kb) * mix(taps[2], v1, v0, vb)
        result.append((arriving, [ka, kb, va, vb, qa, qb, kc, kd, vc, vd]))
        arriving = whole * arriving + (ends[i] + step0 * prod0 + step1 * prod1)
    return result


def backward_middle(length, rates, ends, extras):
    devices = len(ends)
    whole = jnp.exp(-float(length) * rates)
    blank = jnp.zeros_like(extras[0][0])
    arriving = jnp.zeros_like(ends[0])
    result = [None] * devices
    for i in reversed(range(devices)):
        result[i] = (arriving, extras[i + 1] if i + 1 < devices else [blank] * len(extras[0]))
        arriving = whole * arriving + ends[i]
    return result


def middle_kernel(s, forward, pay_ref, decay_ref, filter_ref, back_ref, *wide):
    me = lax.axis_index("seq")
    lead, extra = (2 * s.modes, FORWARD_EXTRA) if forward else (s.modes, BACKWARD_EXTRA)
    in_ref, out_ref = wide if forward else (pay_ref, back_ref)
    if forward:
        widened(pay_ref, in_ref)
    rows = s.chunk_rows(lead, extra)
    for h in range(s.halves):
        lanes = pl.ds(pl.multiple_of((me + h * SUB) * LANES, LANES), LANES)
        rates = decay_ref[:, lanes]
        ends, extras = [], []
        for i in range(s.devices):
            e = i * rows + s.chunk_row(0, h, lead, extra)
            end = in_ref[e : e + s.modes, :]
            ends.append(end + in_ref[e + s.modes : e + lead, :] if forward else end)
            x = i * rows + s.chunk_row(lead, h, lead, extra)
            extras.append([in_ref[x + r : x + r + 1, :] for r in range(extra)])
        if forward:
            taps = [[filter_ref[i, tap : tap + 1, lanes] for tap in range(3)] for i in range(3)]
            result = forward_middle(s.length, rates, taps, ends, extras)
        else:
            result = backward_middle(s.length, rates, ends, extras)
        for i, (state, more) in enumerate(result):
            e = i * rows + s.chunk_row(0, h, lead, extra)
            if forward:
                out_ref[e : e + s.modes, :], out_ref[e + s.modes : e + lead, :] = split(state)
            else:
                out_ref[e : e + s.modes, :] = state
            x = i * rows + s.chunk_row(lead, h, lead, extra)
            for r in range(extra):
                out_ref[x + r : x + r + 1, :] = more[r]
    if forward:
        narrowed(out_ref, back_ref)


def exchange(s, pay, decay_rate, short_filter, forward):
    lead, extra = (2 * s.modes, FORWARD_EXTRA) if forward else (s.modes, BACKWARD_EXTRA)
    if s.direct:
        chunks = (s.devices, s.chunk_rows(lead, extra), LANES)
        got = lax.all_to_all(pay.reshape(chunks), "seq", 0, 0, tiled=True)
        back = pl.pallas_call(
            functools.partial(middle_kernel, s, forward),
            out_shape=jax.ShapeDtypeStruct(pay.shape, pay.dtype),
            scratch_shapes=[pltpu.VMEM(pay.shape, f32)] * 2 if forward else [],
            compiler_params=pltpu.CompilerParams(vmem_limit_bytes=GRANT),
        )(got.reshape(pay.shape), decay_rate, short_filter)
        return lax.all_to_all(back.reshape(chunks), "seq", 0, 0, tiled=True).reshape(pay.shape)
    rows = lead + extra
    width = s.channels // s.devices
    start = lax.axis_index("seq") * width
    rates = lax.dynamic_slice_in_dim(decay_rate, start, width, 1)
    part = lax.dynamic_slice_in_dim(short_filter, start, width, 2)
    pay = pay.reshape(rows, s.devices, width).transpose(1, 0, 2)
    got = lax.all_to_all(pay, "seq", 0, 0, tiled=True).astype(f32)
    ends = [got[i, : s.modes] for i in range(s.devices)]
    extras = [[got[i, lead + r][None] for r in range(extra)] for i in range(s.devices)]
    if forward:
        ends = [end + got[i, s.modes : lead] for i, end in enumerate(ends)]
        taps = [[part[i, tap][None] for tap in range(3)] for i in range(3)]
        result = forward_middle(s.length, rates, taps, ends, extras)
        highs = [lax.reduce_precision(state, 8, 7) for state, _ in result]
        result = [
            (jnp.concatenate([high, state - high]), more) for high, (state, more) in zip(highs, result)
        ]
    else:
        result = backward_middle(s.length, rates, ends, extras)
    back = jnp.stack([jnp.concatenate([state] + list(more)) for state, more in result])
    back = lax.all_to_all(back.astype(pay.dtype), "seq", 0, 0, tiled=True)
    return back.transpose(1, 0, 2).reshape(rows * s.tiles, LANES)


def inside_kernel(
    s, k_hbm, v_hbm, filter_hbm, decay_hbm, residue_hbm, inside_ref, first_ref,
    kb, vb, fb, db, rb, ks, vs, prod, taps, poles, weights, sems,
):
    pairs = [(decay_hbm, db), (residue_hbm, rb), (filter_hbm, fb), (k_hbm, kb), (v_hbm, vb)]
    copies = [pltpu.make_async_copy(a, b, sems.at[i]) for i, (a, b) in enumerate(pairs)]
    for i, copy in enumerate(copies):
        copy.start(priority=i % 2)
    for copy in copies:
        copy.wait()
    stage_modes(s, db, poles, lambda x: jnp.exp(-x))
    stage_modes(s, rb, weights, lambda x: x)
    stage_taps(s, fb, taps)
    blank = jnp.zeros((SUB, LANES), f32)
    steps = s.length // 16

    def half(h):
        taps_k, taps_v = (tap_tiles(s, taps, i, h) for i in (1, 2))

        products(s, kb, vb, ks, vs, prod, taps_k, taps_v, h)
        for i, (ref, part) in enumerate(((ks, taps_k), (vs, taps_v))):
            x0, x1 = (ref[staged(s, 0, offset, h), :] for offset in range(2))
            first_ref[major(s, 2 * i, h), :] = part[0] * x0
            first_ref[major(s, 2 * i + 1, h), :] = part[0] * x1 + part[1] * x0
        recur(s, prod, inside_ref, mode_tiles(s, poles, h), mode_tiles(s, weights, h), [blank] * s.modes, h)

    each_half(s, half)


def forward_kernel(
    s, inside_ref, first_ref, q_ref, stream_ref, cot_ref, back_ref, filter_ref, decay_ref, residue_ref, gain_ref,
    conv_ref, sums_ref, near_ref,
    qs, xs, gs, back_s, taps, poles, weights, squares, inners,
):
    stage_modes(s, decay_ref, poles, lambda x: jnp.exp(-x))
    stage_modes(s, residue_ref, weights, lambda x: x)
    stage_taps(s, filter_ref, taps)

    widened(back_ref, back_s)
    steps = s.length // 16

    def half(h):
        p = mode_tiles(s, poles, h)
        w = mode_tiles(s, weights, h)
        gain = gain_ref[pl.ds(aligned(h * SUB, SUB), SUB), :]
        taps_q, taps_k, taps_v = (tap_tiles(s, taps, i, h) for i in range(3))
        near = [back_s[forward_slice(s, 2 * s.modes + r, h), :] for r in range(FORWARD_EXTRA)]
        for r, value in enumerate(near):
            near_ref[major(s, r, h), :] = value
        ka, kb, va, vb, qa, qb = near[:6]
        k0, k1, v0, v1 = (first_ref[major(s, r, h), :] for r in range(4))
        products = [
            (k0 + taps_k[1] * kb + taps_k[2] * ka) * (v0 + taps_v[1] * vb + taps_v[2] * va),
            (k1 + taps_k[2] * kb) * (v1 + taps_v[2] * vb),
        ]
        conv = []
        states = [
            back_s[forward_slice(s, m, h), :] + back_s[forward_slice(s, s.modes + m, h), :]
            for m in range(s.modes)
        ]
        for offset in range(2):
            states = [p[m] * states[m] + products[offset] for m in range(s.modes)]
            conv.append(total([w[m] * states[m] for m in range(s.modes)]))
        states = [w[m] * states[m] / (p[m] * p[m]) for m in range(s.modes)]
        first, ahead = [], states
        for offset in range(2):
            ahead = [p[m] * ahead[m] for m in range(s.modes)]
            first.append(conv[offset] - total(ahead))

        def bring(i):
            stage(s, q_ref, qs, i, h)
            stage(s, stream_ref, xs, i, h)
            stage(s, cot_ref, gs, i, h)

        def step(i, carry):
            (q1, q2), states = carry
            for block, offset in sixteen(0):
                rows = staged(s, 2 * i + block, offset, h)
                t = (2 * i + block) * SUB + offset
                out = major(s, t, h)
                inside = inside_ref[out, :]
                if block == 0 and offset < 2:
                    inside = jnp.where(i == 0, first[offset], inside)
                states = [p[m] * states[m] for m in range(s.modes)]
                conv = inside + total(states)
                conv_ref[out, :] = conv
                q0 = qs[rows, :]
                mixed = xs[rows, :] + mix(taps_q, q0, q1, q2) * conv
                part = pl.ds(pl.multiple_of(t * SUB, SUB), SUB)
                square, inner = mixed * mixed, gain * gs[rows, :] * mixed
                squares[part, :] = square + jnp.where(h == 0, 0.0, squares[part, :])
                inners[part, :] = inner + jnp.where(h == 0, 0.0, inners[part, :])
                q1, q2 = q0, q1
            bring(jnp.minimum(i + 1, steps - 1))
            return (q1, q2), states

        bring(0)
        lax.fori_loop(0, steps, step, ((qb, qa), states))

    each_half(s, half)
    for r, ref in enumerate((squares, inners)):
        parts = []
        for b in range(s.length // SUB):
            parts.append(
                total([ref[pl.ds(b * SUB * SUB + i, SUB, stride=SUB), :] for i in range(SUB)])
            )
        rows = jnp.concatenate(parts, axis=0)
        sums_ref[r : r + 1, :] = jnp.sum(rows.T, axis=0, keepdims=True)


def norm_kernel(
    s, width, sums_ref, conv_ref, q_ref, stream_ref, cot_ref, near_ref, filter_ref, decay_ref, gain_ref,
    normed_hbm, dstream_hbm, qgrad_hbm, dconv_ref, tail_ref, pay_ref,
    qs, xs, gs, ns, ds, normed_b, dstream_b, qgrad_b, taps, poles, inv_s, coef_s, sems,
):
    inverse = lax.rsqrt(sums_ref[0:1, :] / width + epsilon)
    coef = inverse * inverse * inverse * sums_ref[1:2, :] / width
    inv_s[...] = jnp.broadcast_to(inverse, (LANES, s.length)).T
    coef_s[...] = jnp.broadcast_to(coef, (LANES, s.length)).T
    stage_modes(s, decay_ref, poles, lambda x: jnp.exp(-x))
    stage_taps(s, filter_ref, taps)
    blank = jnp.zeros((SUB, LANES), f32)
    steps = s.length // 16

    def pieces(h):
        cut = columns(h)
        sources = [
            (normed_b.at[:, cut], normed_hbm.at[:, cut]),
            (dstream_b.at[:, cut], dstream_hbm.at[:, cut]),
            (qgrad_b.at[pl.ds(16, s.length - 16), cut], qgrad_hbm.at[pl.ds(0, s.length - 16), cut]),
        ]
        return [pltpu.make_async_copy(a, b, sems.at[3 * h + i]) for i, (a, b) in enumerate(sources)]

    def half(h):
        gain = gain_ref[pl.ds(aligned(h * SUB, SUB), SUB), :]
        taps_q = tap_tiles(s, taps, 0, h)

        def bring(i):
            rows = jnp.minimum(i, steps - 1)
            stage(s, q_ref, qs, rows, h, i - rows + 1)
            stage(s, stream_ref, xs, rows, h)
            stage(s, cot_ref, gs, rows, h)

        def step(i, held):
            q1, q2, dq1, dq2 = held
            for block, offset in sixteen(0):
                rows = staged(s, 2 * i + block, offset, h)
                t = (2 * i + block) * SUB + offset
                out = major(s, t, h)
                inv = jnp.broadcast_to(inv_s[pl.ds(t, 1), :], (SUB, LANES))
                cf = jnp.broadcast_to(coef_s[pl.ds(t, 1), :], (SUB, LANES))
                q0 = qs[staged(s, 2 * i + block + 2, offset, h), :]
                qmix = mix(taps_q, q0, q1, q2)
                conv = conv_ref[out, :]
                mixed = xs[rows, :] + qmix * conv
                dmixed = inv * (gain * gs[rows, :]) - mixed * cf
                ns[rows, :] = mixed * inv * gain
                ds[rows, :] = dmixed
                dq0 = dmixed * conv
                dconv_ref[out, :] = dmixed * qmix
                qs[staged_before(s, 2 * i + block + 2, offset, h), :] = mix(taps_q, dq2, dq1, dq0)
                q1, q2, dq1, dq2 = q0, q1, dq0, dq1
            unstage(s, ns, normed_b, i, h)
            unstage(s, ds, dstream_b, i, h)
            unstage(s, qs, qgrad_b, i, h)
            bring(i + 1)
            return q1, q2, dq1, dq2

        bring(0)
        held = (near_ref[major(s, 5, h), :], near_ref[major(s, 4, h), :], blank, blank)
        _, _, dq1, dq2 = lax.fori_loop(0, steps, step, held)
        qs[staged(s, 2 * steps + 1, 6, h), :] = taps_q[0] * dq2 + taps_q[1] * dq1
        qs[staged(s, 2 * steps + 1, 7, h), :] = taps_q[0] * dq1
        for i, copy in enumerate(pieces(h)):
            copy.start(priority=i % 2)

    each_half(s, half)
    start = steps * 2 * s.tiles * SUB
    tail_ref[...] = qs[start : start + 2 * s.tiles * SUB, :]

    def ends(h):
        p = mode_tiles(s, poles, h)

        def step(i, states):
            for block, offset in sixteen(0, True):
                t = (2 * (steps - 1 - i) + block) * SUB + offset
                dconv = dconv_ref[major(s, t, h), :]
                states = [p[m] * states[m] + dconv for m in range(s.modes)]
            return states

        states = lax.fori_loop(0, steps, step, [blank] * s.modes)
        for m in range(s.modes):
            pay_ref[backward_slice(s, m, h), :] = states[m]
        first = [ds[staged(s, 0, offset, h), :] * conv_ref[major(s, offset, h), :] for offset in range(2)]
        for r, value in enumerate([dconv_ref[major(s, 0, h), :], *first, blank]):
            pay_ref[backward_slice(s, s.modes + r, h), :] = value

    each_half(s, ends)

    def finish(h):
        for copy in pieces(h):
            copy.wait()

    each_half(s, finish)


def backward_kernel(
    s, k_ref, v_ref, dconv_ref, tail_ref, near_ref, back_ref, filter_ref, decay_ref, residue_ref, qgrad_in,
    qgrad_hbm, kgrad_hbm, vgrad_hbm,
    ks, vs, dprod, qs, kgrad_b, vgrad_b, qgrad_b, taps, poles, weights, sems,
):
    del qgrad_in
    stage_modes(s, decay_ref, poles, lambda x: jnp.exp(-x))
    stage_modes(s, residue_ref, weights, lambda x: x)
    stage_taps(s, filter_ref, taps)
    steps = s.length // 16

    def back(r, h):
        return back_ref[backward_slice(s, r, h), :]

    qs[...] = tail_ref[...]

    def tails(h):
        taps_q = tap_tiles(s, taps, 0, h)
        dq0, dq1 = back(s.modes + 1, h), back(s.modes + 2, h)
        rows = [staged(s, 1, offset, h) for offset in (6, 7)]
        qs[rows[0], :] = qs[rows[0], :] + taps_q[2] * dq0
        qs[rows[1], :] = qs[rows[1], :] + (taps_q[1] * dq0 + taps_q[2] * dq1)
        unstage(s, qs, qgrad_b, 0, h)

    each_half(s, tails)
    last = pltpu.make_async_copy(qgrad_b, qgrad_hbm.at[pl.ds(s.length - 16, 16), :], sems.at[2 * s.halves])
    last.start()

    def pieces(h):
        cut = columns(h)
        sources = [(kgrad_b, kgrad_hbm), (vgrad_b, vgrad_hbm)]
        return [
            pltpu.make_async_copy(a.at[:, cut], b.at[:, cut], sems.at[2 * h + i])
            for i, (a, b) in enumerate(sources)
        ]

    def half(h):
        p = mode_tiles(s, poles, h)
        w = mode_tiles(s, weights, h)
        arriving = [back(m, h) for m in range(s.modes)]
        recur(s, dconv_ref, dprod, p, w, arriving, h, reverse=True)
        taps_k, taps_v = (tap_tiles(s, taps, i, h) for i in (1, 2))

        def bring(i):
            stage(s, k_ref, ks, i, h, 1)
            stage(s, v_ref, vs, i, h, 1)

        def advance(inputs, grads, k2, v2, d):
            k0, k1, v0, v1 = inputs
            dk1, dk2, dv1, dv2 = grads
            dk0 = d * mix(taps_v, v0, v1, v2)
            dv0 = d * mix(taps_k, k0, k1, k2)
            out = mix(taps_k, dk0, dk1, dk2), mix(taps_v, dv0, dv1, dv2)
            return (k1, k2, v1, v2), (dk0, dk1, dv0, dv1), out

        bring(steps - 1)
        ka, kb, va, vb, _, _, kc, kd, vc, vd = (near_ref[major(s, r, h), :] for r in range(10))
        for ref, rows in ((ks, (ka, kb)), (vs, (va, vb))):
            for offset in range(2):
                ref[staged(s, 1, 6 + offset, h), :] = rows[offset]
        arriving = [back(m, h) for m in range(s.modes)]
        dconv0 = back(s.modes, h)
        d0 = total([w[m] * arriving[m] for m in range(s.modes)])
        d1 = total([w[m] * ((arriving[m] - dconv0) / p[m]) for m in range(s.modes)])
        ends = [staged(s, 2 * steps + 1, offset, h) for offset in (6, 7)]
        inputs = (kd, kc, vd, vc)
        grads = (jnp.zeros((SUB, LANES), f32),) * 4
        inputs, grads, _ = advance(inputs, grads, ks[ends[1], :], vs[ends[1], :], d1)
        inputs, grads, _ = advance(inputs, grads, ks[ends[0], :], vs[ends[0], :], d0)

        def step(i, carry):
            inputs, grads = carry
            i = steps - 1 - i

            @pl.when(i > 0)
            def _():
                bring(jnp.maximum(i - 1, 0))

            for block, offset in sixteen(0, True):
                d = dprod[major(s, (2 * i + block) * SUB + offset, h), :]
                rows = staged_before(s, 2 * i + block + 2, offset, h)
                inputs, grads, out = advance(inputs, grads, ks[rows, :], vs[rows, :], d)
                rows = staged(s, 2 * i + block + 2, offset, h)
                ks[rows, :], vs[rows, :] = out
            unstage(s, ks, kgrad_b, i + 1, h, i)
            unstage(s, vs, vgrad_b, i + 1, h, i)
            return inputs, grads

        lax.fori_loop(0, steps, step, (inputs, grads))
        for i, copy in enumerate(pieces(h)):
            copy.start(priority=i % 2)

    each_half(s, half)
    last.wait()

    def finish(h):
        for copy in pieces(h):
            copy.wait()

    each_half(s, finish)


def body(
    query_in, key_in, value_in, stream, short_filter, decay_rate, residue, norm_gain, cotangent
):
    length, channels = query_in.shape
    modes = decay_rate.shape[0]
    s = Sizes(length, channels, modes, lax.axis_size("seq"))
    total_width = channels * lax.axis_size("tp")
    wide = jax.ShapeDtypeStruct((length * s.tiles, LANES), f32)
    narrow = jax.ShapeDtypeStruct((length, channels), bf16)
    rows = 16 * s.tiles
    wide_s = pltpu.VMEM(wide.shape, f32)
    longer_s = pltpu.VMEM(((length + 16) * s.tiles, LANES), f32)
    narrow_s = pltpu.VMEM(narrow.shape, bf16)
    last_s = pltpu.VMEM((16, channels), bf16)
    tail_s = pltpu.VMEM((rows, LANES), f32)
    taps_s = pltpu.VMEM((3 * s.tiles * SUB, LANES), f32)
    mode_s = pltpu.VMEM((modes * s.tiles, LANES), f32)
    sum_s = pltpu.VMEM((length * SUB, LANES), f32)
    square_s = pltpu.VMEM((length, LANES), f32)
    gain = norm_gain.reshape(s.tiles, LANES)
    there = pl.BlockSpec(memory_space=pltpu.HBM)
    here = pl.BlockSpec(memory_space=pltpu.VMEM)

    def call(kernel, ins, outs, out_shape, scratch_shapes, operands, aliases={}, cost=None):
        return pl.pallas_call(
            functools.partial(kernel, s),
            in_specs=[there if c == "h" else here for c in ins],
            out_specs=[there if c == "h" else here for c in outs],
            out_shape=out_shape,
            scratch_shapes=scratch_shapes,
            input_output_aliases=aliases,
            cost_estimate=cost,
            compiler_params=pltpu.CompilerParams(vmem_limit_bytes=GRANT),
        )(*operands)

    forward_shape = s.exchange_shape(2 * modes, FORWARD_EXTRA)
    near_shape = jax.ShapeDtypeStruct((FORWARD_EXTRA * s.tiles, LANES), f32)

    def far(*arrays):
        return [pltpu.with_memory_space_constraint(x, pltpu.HBM) for x in arrays]

    def cost(per_element, arrays):
        return pl.CostEstimate(
            flops=per_element * length * channels, bytes_accessed=arrays * 4 * length * channels, transcendentals=0
        )

    filter_s = pltpu.VMEM(short_filter.shape, f32)
    rates_s = pltpu.VMEM(decay_rate.shape, f32)
    (pay,) = call(
        begin_kernel, "hhhhh", "v",
        (jax.ShapeDtypeStruct(forward_shape, bf16),),
        [narrow_s, narrow_s, last_s, filter_s, rates_s]
        + [wide_s] * 3 + [tail_s, pltpu.VMEM(forward_shape, f32), taps_s, mode_s]
        + [pltpu.SemaphoreType.DMA((3 + 2 * s.halves,))],
        far(query_in, key_in, value_in, short_filter, decay_rate),
    )
    inside, first = call(
        inside_kernel, "hhhhh", "vv", (wide, jax.ShapeDtypeStruct((4 * s.tiles, LANES), f32)),
        [narrow_s, narrow_s, filter_s, rates_s, rates_s]
        + [wide_s] * 3 + [taps_s, mode_s, mode_s, pltpu.SemaphoreType.DMA((5,))],
        far(key_in, value_in, short_filter, decay_rate, residue),
        cost=cost(75, 3),
    )
    back = exchange(s, pay, decay_rate, short_filter, True)
    conv, sums, near = call(
        forward_kernel, "v" * 10, "vvv",
        (wide, jax.ShapeDtypeStruct((2, length), f32), near_shape),
        [wide_s] * 3 + [pltpu.VMEM(forward_shape, f32), taps_s, mode_s, mode_s, sum_s, sum_s],
        (inside, first, query_in, stream, cotangent, back, short_filter, decay_rate, residue, gain),
        {0: 0},
    )
    sums = lax.psum(sums, "tp")
    normed, dstream, query_grad, dconv, tail, pay_back = call(
        lambda s, *refs: norm_kernel(s, total_width, *refs), "v" * 9, "hhhvvv",
        (narrow, narrow, narrow, wide, jax.ShapeDtypeStruct((rows, LANES), f32), jax.ShapeDtypeStruct(s.exchange_shape(modes, BACKWARD_EXTRA), f32)),
        [pltpu.VMEM(((length + 32) * s.tiles, LANES), f32)] + [longer_s] * 2 + [wide_s] * 2 + [narrow_s] * 2
        + [pltpu.VMEM((length + 16, channels), bf16)]
        + [taps_s, mode_s, square_s, square_s, pltpu.SemaphoreType.DMA((3 * s.halves,))],
        (sums, conv, query_in, stream, cotangent, near, short_filter, decay_rate, gain),
    )
    back_back = exchange(s, pay_back, decay_rate, short_filter, False)
    query_grad, key_grad, value_grad = call(
        backward_kernel, "v" * 9 + "h", "hhh",
        (narrow, narrow, narrow),
        [longer_s] * 2 + [wide_s, tail_s] + [narrow_s] * 2 + [last_s, taps_s, mode_s, mode_s]
        + [pltpu.SemaphoreType.DMA((1 + 2 * s.halves,))],
        (key_in, value_in, dconv, tail, near, back_back, short_filter, decay_rate, residue, query_grad),
        {9: 0},
    )
    return (normed, dstream, query_grad, key_grad, value_grad)


def solution(mesh):
    cut = P("seq", "tp")
    return jax.shard_map(
        body,
        mesh=mesh,
        in_specs=(cut, cut, cut, cut, P(None, None, "tp"), P(None, "tp"), P(None, "tp"), P("tp"), cut),
        out_specs=(cut,) * 5,
        check_vma=False,
    )
```

```python
import functools

import jax
import jax.numpy as jnp
from jax import lax
from jax.experimental import pallas as pl
from jax.experimental.pallas import tpu as pltpu
from jax.sharding import PartitionSpec as P

f32 = jnp.float32
bf16 = jnp.bfloat16
epsilon = 1e-05
LANES = 128
SUB = 8
GROUP = LANES * SUB
FORWARD_EXTRA = 10
BACKWARD_EXTRA = 4
GRANT = 20 * 1024 * 1024


class Sizes:
    def __init__(self, length, channels, modes, devices):
        self.length, self.channels, self.modes, self.devices = length, channels, modes, devices
        self.tiles = channels // LANES
        self.halves = channels // GROUP
        self.direct = devices == SUB

    def chunk_row(self, r, h, lead, extra):
        if r < lead:
            return h * lead + r
        return self.halves * lead + h * extra + r - lead

    def chunk_rows(self, lead, extra):
        return -(-self.halves * (lead + extra) // SUB) * SUB

    def exchange_shape(self, lead, extra):
        if self.direct:
            return (self.devices * self.chunk_rows(lead, extra), LANES)
        return ((lead + extra) * self.tiles, LANES)

    def exchange_slice(self, r, h, lead, extra):
        if self.direct:
            return pl.ds(self.chunk_row(r, h, lead, extra), SUB, stride=self.chunk_rows(lead, extra))
        return pl.ds(r * self.tiles + h * SUB, SUB)


def staged(s, block, offset, h):
    start = block * (s.tiles * SUB) + (h * SUB * SUB + offset)
    return pl.ds(start, SUB, stride=SUB)


def major(s, t, h):
    start = t * s.tiles + h * SUB
    if not isinstance(start, int):
        start = pl.multiple_of(start, SUB)
    return pl.ds(start, SUB)


def staged_before(s, block, offset, h):
    if offset < 2:
        return staged(s, block - 1, offset + SUB - 2, h)
    return staged(s, block, offset - 2, h)


def aligned(start, unit):
    return start if isinstance(start, int) else pl.multiple_of(start, unit)


def columns(h):
    return pl.ds(aligned(h * GROUP, GROUP), GROUP)


def stage(s, x_ref, out_ref, i, h, pad=0):
    rows = x_ref[pl.ds(aligned(i * 16, 16), 16), columns(h)].astype(f32)
    base = (i + pad) * (2 * s.tiles * SUB) + h * (SUB * SUB)
    for part in range(2):
        for j in range(SUB):
            out_ref[pl.ds(aligned(base + (part * s.tiles + j) * SUB, SUB), SUB), :] = rows[
                part * SUB : (part + 1) * SUB, j * LANES : (j + 1) * LANES
            ]


def unstage(s, in_ref, x_ref, i, h, to=None):
    base = i * (2 * s.tiles * SUB) + h * (SUB * SUB)
    rows = [
        jnp.concatenate(
            [
                in_ref[pl.ds(aligned(base + (part * s.tiles + j) * SUB, SUB), SUB), :]
                for part in range(2)
            ],
            axis=0,
        )
        for j in range(SUB)
    ]
    to = i if to is None else to
    x_ref[pl.ds(aligned(to * 16, 16), 16), columns(h)] = jnp.concatenate(rows, axis=1).astype(bf16)


def stage_wide(s, x_ref, out_ref):
    for h in range(s.halves):
        stage(s, x_ref, out_ref, 0, h)


def each_half(s, body):
    def step(h, carry):
        body(h)
        return carry

    lax.fori_loop(0, s.halves, step, 0)


def sixteen(i, reverse=False):
    pairs = [(2 * i + part, offset) for part in range(2) for offset in range(SUB)]
    return pairs[::-1] if reverse else pairs


def long_steps(s):
    blocks = s.length // SUB
    return next(n for n in (4, 2, 1) if blocks % n == 0)


def positions(blocks, reverse=False):
    pairs = [(block, offset) for block in range(blocks) for offset in range(SUB)]
    return pairs[::-1] if reverse else pairs


def stage_modes(s, x_ref, out_ref, f):
    for g in range(s.modes // SUB):
        rows = f(x_ref[g * SUB : (g + 1) * SUB, :])
        for j in range(s.tiles):
            start = (g * s.tiles + j) * SUB
            out_ref[start : start + SUB, :] = rows[:, j * LANES : (j + 1) * LANES]


def mode_tiles(s, ref, h):
    return [ref[staged(s, m // SUB, m % SUB, h), :] for m in range(s.modes)]


def stage_taps(s, filter_ref, out_ref):
    for i in range(3):
        rows = filter_ref[i]
        for j in range(s.tiles):
            start = (i * s.tiles + j) * SUB
            out_ref[start : start + 3, :] = rows[:, j * LANES : (j + 1) * LANES]


def tap_tiles(s, ref, i, h):
    return [ref[staged(s, i, tap, h), :] for tap in range(3)]


def total(parts):
    while len(parts) > 1:
        parts = [
            parts[i] + parts[i + 1] if i + 1 < len(parts) else parts[i]
            for i in range(0, len(parts), 2)
        ]
    return parts[0]


def mix(taps, now, before, before2):
    return taps[0] * now + taps[1] * before + taps[2] * before2


def products(s, k_ref, v_ref, ks, vs, to_ref, taps_k, taps_v, h):
    def step(i, held):
        stage(s, k_ref, ks, i, h)
        stage(s, v_ref, vs, i, h)
        k1, k2, v1, v2 = held
        for block, offset in sixteen(0):
            rows = staged(s, 2 * i + block, offset, h)
            k0, v0 = ks[rows, :], vs[rows, :]
            product = mix(taps_k, k0, k1, k2) * mix(taps_v, v0, v1, v2)
            if block == 0 and offset < 2:
                product = jnp.where(i == 0, 0.0, product)
            to_ref[major(s, (2 * i + block) * SUB + offset, h), :] = product
            k1, k2, v1, v2 = k0, k1, v0, v1
        return k1, k2, v1, v2

    return lax.fori_loop(0, s.length // 16, step, (jnp.zeros((SUB, LANES), f32),) * 4)


def recur(s, from_ref, to_ref, p, w, states, h, reverse=False):
    blocks = long_steps(s)
    steps = s.length // (SUB * blocks)

    def step(i, states):
        i = steps - 1 - i if reverse else i
        for block, offset in positions(blocks, reverse):
            rows = major(s, (blocks * i + block) * SUB + offset, h)
            signal = from_ref[rows, :]
            states = [p[m] * states[m] + signal for m in range(s.modes)]
            to_ref[rows, :] = total([w[m] * states[m] for m in range(s.modes)])
        return states

    lax.fori_loop(0, steps, step, states)


def forward_slice(s, r, h):
    return s.exchange_slice(r, h, 2 * s.modes, FORWARD_EXTRA)


def split(x):
    high = x.astype(bf16).astype(f32)
    return high, x - high


def put_states(s, ref, states, h):
    for m in range(s.modes):
        high, low = split(states[m])
        ref[forward_slice(s, m, h), :] = high
        ref[forward_slice(s, s.modes + m, h), :] = low


def narrowed(from_ref, to_ref):
    rows = from_ref.shape[0]
    for i in range(0, rows, 16):
        to_ref[i : min(i + 16, rows), :] = from_ref[i : min(i + 16, rows), :].astype(bf16)


def widened(from_ref, to_ref):
    rows = from_ref.shape[0]
    for i in range(0, rows, 16):
        to_ref[i : min(i + 16, rows), :] = from_ref[i : min(i + 16, rows), :].astype(f32)


def backward_slice(s, r, h):
    return s.exchange_slice(r, h, s.modes, BACKWARD_EXTRA)


def begin_kernel(
    s, q_hbm, k_hbm, v_hbm, filter_hbm, decay_hbm, pay_ref,
    kb, vb, qb, fb, db, ks, vs, prod, qs, pay_s, taps, poles, sems,
):
    copies = [(decay_hbm, db), (filter_hbm, fb), (q_hbm.at[pl.ds(s.length - 16, 16), :], qb)]
    for h in range(s.halves):
        cut = pl.ds(h * GROUP, GROUP)
        copies += [(k_hbm.at[:, cut], kb.at[:, cut]), (v_hbm.at[:, cut], vb.at[:, cut])]
    copies = [pltpu.make_async_copy(a, b, sems.at[i]) for i, (a, b) in enumerate(copies)]
    for i, copy in enumerate(copies):
        copy.start(priority=i % 2)
    copies[0].wait()
    stage_modes(s, db, poles, lambda x: jnp.exp(-x))
    copies[1].wait()
    stage_taps(s, fb, taps)
    blank = jnp.zeros((SUB, LANES), f32)
    copies[2].wait()
    stage_wide(s, qb, qs)

    def half(h):
        for i, (from_hbm, to) in enumerate(((k_hbm, kb), (v_hbm, vb))):
            cut = columns(h)
            pltpu.make_async_copy(from_hbm.at[:, cut], to.at[:, cut], sems.at[3 + 2 * h + i]).wait()
        p = mode_tiles(s, poles, h)
        taps_k, taps_v = (tap_tiles(s, taps, i, h) for i in (1, 2))

        held = products(s, kb, vb, ks, vs, prod, taps_k, taps_v, h)

        blocks = long_steps(s)

        def step(i, states):
            for block, offset in positions(blocks):
                product = prod[major(s, (blocks * i + block) * SUB + offset, h), :]
                states = [p[m] * states[m] + product for m in range(s.modes)]
            return states

        states = lax.fori_loop(0, s.length // (SUB * blocks), step, [blank] * s.modes)
        put_states(s, pay_s, states, h)
        k1, k2, v1, v2 = held
        first = [staged(s, 0, offset, h) for offset in range(2)]
        last = [staged(s, 1, offset, h) for offset in (6, 7)]
        extra = [
            ks[first[0], :], ks[first[1], :], k2, k1,
            vs[first[0], :], vs[first[1], :], v2, v1,
            qs[last[0], :], qs[last[1], :],
        ]
        for r, value in enumerate(extra):
            pay_s[forward_slice(s, 2 * s.modes + r, h), :] = value

    each_half(s, half)
    narrowed(pay_s, pay_ref)


def forward_middle(length, rates, taps, ends, extras):
    devices = len(ends)
    whole, step0, step1 = (jnp.exp(-float(length - i) * rates) for i in range(3))
    blank = jnp.zeros_like(extras[0][0])
    arriving = jnp.zeros_like(ends[0])
    result = []
    for i in range(devices):
        k0, k1, _, _, v0, v1 = extras[i][:6]
        if i:
            _, _, ka, kb, _, _, va, vb, qa, qb = extras[i - 1][:10]
        else:
            ka = kb = va = vb = qa = qb = blank
        if i + 1 < devices:
            kc, kd, _, _, vc, vd = extras[i + 1][:6]
        else:
            kc = kd = vc = vd = blank
        prod0 = mix(taps[1], k0, kb, ka) * mix(taps[2], v0, vb, va)
        prod1 = mix(taps[1], k1, k0, kb) * mix(taps[2], v1, v0, vb)
        result.append((arriving, [ka, kb, va, vb, qa, qb, kc, kd, vc, vd]))
        arriving = whole * arriving + (ends[i] + step0 * prod0 + step1 * prod1)
    return result


def backward_middle(length, rates, ends, extras):
    devices = len(ends)
    whole = jnp.exp(-float(length) * rates)
    blank = jnp.zeros_like(extras[0][0])
    arriving = jnp.zeros_like(ends[0])
    result = [None] * devices
    for i in reversed(range(devices)):
        result[i] = (arriving, extras[i + 1] if i + 1 < devices else [blank] * len(extras[0]))
        arriving = whole * arriving + ends[i]
    return result


def middle_kernel(s, forward, pay_ref, decay_ref, filter_ref, back_ref, *wide):
    me = lax.axis_index("seq")
    lead, extra = (2 * s.modes, FORWARD_EXTRA) if forward else (s.modes, BACKWARD_EXTRA)
    in_ref, out_ref = wide if forward else (pay_ref, back_ref)
    if forward:
        widened(pay_ref, in_ref)
    rows = s.chunk_rows(lead, extra)
    for h in range(s.halves):
        lanes = pl.ds(pl.multiple_of((me + h * SUB) * LANES, LANES), LANES)
        rates = decay_ref[:, lanes]
        ends, extras = [], []
        for i in range(s.devices):
            e = i * rows + s.chunk_row(0, h, lead, extra)
            end = in_ref[e : e + s.modes, :]
            ends.append(end + in_ref[e + s.modes : e + lead, :] if forward else end)
            x = i * rows + s.chunk_row(lead, h, lead, extra)
            extras.append([in_ref[x + r : x + r + 1, :] for r in range(extra)])
        if forward:
            taps = [[filter_ref[i, tap : tap + 1, lanes] for tap in range(3)] for i in range(3)]
            result = forward_middle(s.length, rates, taps, ends, extras)
        else:
            result = backward_middle(s.length, rates, ends, extras)
        for i, (state, more) in enumerate(result):
            e = i * rows + s.chunk_row(0, h, lead, extra)
            if forward:
                out_ref[e : e + s.modes, :], out_ref[e + s.modes : e + lead, :] = split(state)
            else:
                out_ref[e : e + s.modes, :] = state
            x = i * rows + s.chunk_row(lead, h, lead, extra)
            for r in range(extra):
                out_ref[x + r : x + r + 1, :] = more[r]
    if forward:
        narrowed(out_ref, back_ref)


def exchange(s, pay, decay_rate, short_filter, forward):
    lead, extra = (2 * s.modes, FORWARD_EXTRA) if forward else (s.modes, BACKWARD_EXTRA)
    if s.direct:
        chunks = (s.devices, s.chunk_rows(lead, extra), LANES)
        got = lax.all_to_all(pay.reshape(chunks), "seq", 0, 0, tiled=True)
        back = pl.pallas_call(
            functools.partial(middle_kernel, s, forward),
            out_shape=jax.ShapeDtypeStruct(pay.shape, pay.dtype),
            scratch_shapes=[pltpu.VMEM(pay.shape, f32)] * 2 if forward else [],
            compiler_params=pltpu.CompilerParams(vmem_limit_bytes=GRANT),
        )(got.reshape(pay.shape), decay_rate, short_filter)
        return lax.all_to_all(back.reshape(chunks), "seq", 0, 0, tiled=True).reshape(pay.shape)
    rows = lead + extra
    width = s.channels // s.devices
    start = lax.axis_index("seq") * width
    rates = lax.dynamic_slice_in_dim(decay_rate, start, width, 1)
    part = lax.dynamic_slice_in_dim(short_filter, start, width, 2)
    pay = pay.reshape(rows, s.devices, width).transpose(1, 0, 2)
    got = lax.all_to_all(pay, "seq", 0, 0, tiled=True).astype(f32)
    ends = [got[i, : s.modes] for i in range(s.devices)]
    extras = [[got[i, lead + r][None] for r in range(extra)] for i in range(s.devices)]
    if forward:
        ends = [end + got[i, s.modes : lead] for i, end in enumerate(ends)]
        taps = [[part[i, tap][None] for tap in range(3)] for i in range(3)]
        result = forward_middle(s.length, rates, taps, ends, extras)
        highs = [lax.reduce_precision(state, 8, 7) for state, _ in result]
        result = [
            (jnp.concatenate([high, state - high]), more) for high, (state, more) in zip(highs, result)
        ]
    else:
        result = backward_middle(s.length, rates, ends, extras)
    back = jnp.stack([jnp.concatenate([state] + list(more)) for state, more in result])
    back = lax.all_to_all(back.astype(pay.dtype), "seq", 0, 0, tiled=True)
    return back.transpose(1, 0, 2).reshape(rows * s.tiles, LANES)


def inside_kernel(
    s, k_hbm, v_hbm, filter_hbm, decay_hbm, residue_hbm, inside_ref, first_ref,
    kb, vb, fb, db, rb, ks, vs, prod, taps, poles, weights, sems,
):
    pairs = [(decay_hbm, db), (residue_hbm, rb), (filter_hbm, fb), (k_hbm, kb), (v_hbm, vb)]
    copies = [pltpu.make_async_copy(a, b, sems.at[i]) for i, (a, b) in enumerate(pairs)]
    for i, copy in enumerate(copies):
        copy.start(priority=i % 2)
    for copy in copies:
        copy.wait()
    stage_modes(s, db, poles, lambda x: jnp.exp(-x))
    stage_modes(s, rb, weights, lambda x: x)
    stage_taps(s, fb, taps)
    blank = jnp.zeros((SUB, LANES), f32)
    steps = s.length // 16

    def half(h):
        taps_k, taps_v = (tap_tiles(s, taps, i, h) for i in (1, 2))

        products(s, kb, vb, ks, vs, prod, taps_k, taps_v, h)
        for i, (ref, part) in enumerate(((ks, taps_k), (vs, taps_v))):
            x0, x1 = (ref[staged(s, 0, offset, h), :] for offset in range(2))
            first_ref[major(s, 2 * i, h), :] = part[0] * x0
            first_ref[major(s, 2 * i + 1, h), :] = part[0] * x1 + part[1] * x0
        recur(s, prod, inside_ref, mode_tiles(s, poles, h), mode_tiles(s, weights, h), [blank] * s.modes, h)

    each_half(s, half)


def forward_kernel(
    s, inside_ref, first_ref, q_ref, stream_ref, cot_ref, back_ref, filter_ref, decay_ref, residue_ref, gain_ref,
    conv_ref, sums_ref, near_ref,
    qs, xs, gs, back_s, taps, poles, weights, squares, inners,
):
    stage_modes(s, decay_ref, poles, lambda x: jnp.exp(-x))
    stage_modes(s, residue_ref, weights, lambda x: x)
    stage_taps(s, filter_ref, taps)

    widened(back_ref, back_s)
    steps = s.length // 16

    def half(h):
        p = mode_tiles(s, poles, h)
        w = mode_tiles(s, weights, h)
        gain = gain_ref[pl.ds(aligned(h * SUB, SUB), SUB), :]
        taps_q, taps_k, taps_v = (tap_tiles(s, taps, i, h) for i in range(3))
        near = [back_s[forward_slice(s, 2 * s.modes + r, h), :] for r in range(FORWARD_EXTRA)]
        for r, value in enumerate(near):
            near_ref[major(s, r, h), :] = value
        ka, kb, va, vb, qa, qb = near[:6]
        k0, k1, v0, v1 = (first_ref[major(s, r, h), :] for r in range(4))
        products = [
            (k0 + taps_k[1] * kb + taps_k[2] * ka) * (v0 + taps_v[1] * vb + taps_v[2] * va),
            (k1 + taps_k[2] * kb) * (v1 + taps_v[2] * vb),
        ]
        conv = []
        states = [
            back_s[forward_slice(s, m, h), :] + back_s[forward_slice(s, s.modes + m, h), :]
            for m in range(s.modes)
        ]
        for offset in range(2):
            states = [p[m] * states[m] + products[offset] for m in range(s.modes)]
            conv.append(total([w[m] * states[m] for m in range(s.modes)]))
        states = [w[m] * states[m] / (p[m] * p[m]) for m in range(s.modes)]
        first, ahead = [], states
        for offset in range(2):
            ahead = [p[m] * ahead[m] for m in range(s.modes)]
            first.append(conv[offset] - total(ahead))

        def bring(i):
            stage(s, q_ref, qs, i, h)
            stage(s, stream_ref, xs, i, h)
            stage(s, cot_ref, gs, i, h)

        def step(i, carry):
            (q1, q2), states = carry
            for block, offset in sixteen(0):
                rows = staged(s, 2 * i + block, offset, h)
                t = (2 * i + block) * SUB + offset
                out = major(s, t, h)
                inside = inside_ref[out, :]
                if block == 0 and offset < 2:
                    inside = jnp.where(i == 0, first[offset], inside)
                states = [p[m] * states[m] for m in range(s.modes)]
                conv = inside + total(states)
                conv_ref[out, :] = conv
                q0 = qs[rows, :]
                mixed = xs[rows, :] + mix(taps_q, q0, q1, q2) * conv
                part = pl.ds(pl.multiple_of(t * SUB, SUB), SUB)
                square, inner = mixed * mixed, gain * gs[rows, :] * mixed
                squares[part, :] = square + jnp.where(h == 0, 0.0, squares[part, :])
                inners[part, :] = inner + jnp.where(h == 0, 0.0, inners[part, :])
                q1, q2 = q0, q1
            bring(jnp.minimum(i + 1, steps - 1))
            return (q1, q2), states

        bring(0)
        lax.fori_loop(0, steps, step, ((qb, qa), states))

    each_half(s, half)
    for r, ref in enumerate((squares, inners)):
        parts = []
        for b in range(s.length // SUB):
            parts.append(
                total([ref[pl.ds(b * SUB * SUB + i, SUB, stride=SUB), :] for i in range(SUB)])
            )
        rows = jnp.concatenate(parts, axis=0)
        sums_ref[r : r + 1, :] = jnp.sum(rows.T, axis=0, keepdims=True)


def norm_kernel(
    s, width, sums_ref, conv_ref, q_ref, stream_ref, cot_ref, near_ref, filter_ref, decay_ref, gain_ref,
    normed_hbm, dstream_hbm, qgrad_hbm, dconv_ref, tail_ref, pay_ref,
    qs, xs, gs, ns, ds, normed_b, dstream_b, qgrad_b, taps, poles, inv_s, coef_s, sems,
):
    inverse = lax.rsqrt(sums_ref[0:1, :] / width + epsilon)
    coef = inverse * inverse * inverse * sums_ref[1:2, :] / width
    inv_s[...] = jnp.broadcast_to(inverse, (LANES, s.length)).T
    coef_s[...] = jnp.broadcast_to(coef, (LANES, s.length)).T
    stage_modes(s, decay_ref, poles, lambda x: jnp.exp(-x))
    stage_taps(s, filter_ref, taps)
    blank = jnp.zeros((SUB, LANES), f32)
    steps = s.length // 16

    def pieces(h):
        cut = columns(h)
        sources = [
            (normed_b.at[:, cut], normed_hbm.at[:, cut]),
            (dstream_b.at[:, cut], dstream_hbm.at[:, cut]),
            (qgrad_b.at[pl.ds(16, s.length - 16), cut], qgrad_hbm.at[pl.ds(0, s.length - 16), cut]),
        ]
        return [pltpu.make_async_copy(a, b, sems.at[3 * h + i]) for i, (a, b) in enumerate(sources)]

    def half(h):
        gain = gain_ref[pl.ds(aligned(h * SUB, SUB), SUB), :]
        taps_q = tap_tiles(s, taps, 0, h)

        def bring(i):
            rows = jnp.minimum(i, steps - 1)
            stage(s, q_ref, qs, rows, h, i - rows + 1)
            stage(s, stream_ref, xs, rows, h)
            stage(s, cot_ref, gs, rows, h)

        def step(i, held):
            q1, q2, dq1, dq2 = held
            for block, offset in sixteen(0):
                rows = staged(s, 2 * i + block, offset, h)
                t = (2 * i + block) * SUB + offset
                out = major(s, t, h)
                inv = jnp.broadcast_to(inv_s[pl.ds(t, 1), :], (SUB, LANES))
                cf = jnp.broadcast_to(coef_s[pl.ds(t, 1), :], (SUB, LANES))
                q0 = qs[staged(s, 2 * i + block + 2, offset, h), :]
                qmix = mix(taps_q, q0, q1, q2)
                conv = conv_ref[out, :]
                mixed = xs[rows, :] + qmix * conv
                dmixed = inv * (gain * gs[rows, :]) - mixed * cf
                ns[rows, :] = mixed * inv * gain
                ds[rows, :] = dmixed
                dq0 = dmixed * conv
                dconv_ref[out, :] = dmixed * qmix
                qs[staged_before(s, 2 * i + block + 2, offset, h), :] = mix(taps_q, dq2, dq1, dq0)
                q1, q2, dq1, dq2 = q0, q1, dq0, dq1
            unstage(s, ns, normed_b, i, h)
            unstage(s, ds, dstream_b, i, h)
            unstage(s, qs, qgrad_b, i, h)
            bring(i + 1)
            return q1, q2, dq1, dq2

        bring(0)
        held = (near_ref[major(s, 5, h), :], near_ref[major(s, 4, h), :], blank, blank)
        _, _, dq1, dq2 = lax.fori_loop(0, steps, step, held)
        qs[staged(s, 2 * steps + 1, 6, h), :] = taps_q[0] * dq2 + taps_q[1] * dq1
        qs[staged(s, 2 * steps + 1, 7, h), :] = taps_q[0] * dq1
        for i, copy in enumerate(pieces(h)):
            copy.start(priority=i % 2)

    each_half(s, half)
    start = steps * 2 * s.tiles * SUB
    tail_ref[...] = qs[start : start + 2 * s.tiles * SUB, :]

    def ends(h):
        p = mode_tiles(s, poles, h)

        blocks = long_steps(s)
        many = s.length // (SUB * blocks)

        def step(i, states):
            for block, offset in positions(blocks, True):
                t = (blocks * (many - 1 - i) + block) * SUB + offset
                dconv = dconv_ref[major(s, t, h), :]
                states = [p[m] * states[m] + dconv for m in range(s.modes)]
            return states

        states = lax.fori_loop(0, many, step, [blank] * s.modes)
        for m in range(s.modes):
            pay_ref[backward_slice(s, m, h), :] = states[m]
        first = [ds[staged(s, 0, offset, h), :] * conv_ref[major(s, offset, h), :] for offset in range(2)]
        for r, value in enumerate([dconv_ref[major(s, 0, h), :], *first, blank]):
            pay_ref[backward_slice(s, s.modes + r, h), :] = value

    each_half(s, ends)

    def finish(h):
        for copy in pieces(h):
            copy.wait()

    each_half(s, finish)


def backward_kernel(
    s, k_ref, v_ref, dconv_ref, tail_ref, near_ref, back_ref, filter_ref, decay_ref, residue_ref, qgrad_in,
    qgrad_hbm, kgrad_hbm, vgrad_hbm,
    ks, vs, dprod, qs, kgrad_b, vgrad_b, qgrad_b, taps, poles, weights, sems,
):
    del qgrad_in
    stage_modes(s, decay_ref, poles, lambda x: jnp.exp(-x))
    stage_modes(s, residue_ref, weights, lambda x: x)
    stage_taps(s, filter_ref, taps)
    steps = s.length // 16

    def back(r, h):
        return back_ref[backward_slice(s, r, h), :]

    qs[...] = tail_ref[...]

    def tails(h):
        taps_q = tap_tiles(s, taps, 0, h)
        dq0, dq1 = back(s.modes + 1, h), back(s.modes + 2, h)
        rows = [staged(s, 1, offset, h) for offset in (6, 7)]
        qs[rows[0], :] = qs[rows[0], :] + taps_q[2] * dq0
        qs[rows[1], :] = qs[rows[1], :] + (taps_q[1] * dq0 + taps_q[2] * dq1)
        unstage(s, qs, qgrad_b, 0, h)

    each_half(s, tails)
    last = pltpu.make_async_copy(qgrad_b, qgrad_hbm.at[pl.ds(s.length - 16, 16), :], sems.at[2 * s.halves])
    last.start()

    def pieces(h):
        cut = columns(h)
        sources = [(kgrad_b, kgrad_hbm), (vgrad_b, vgrad_hbm)]
        return [
            pltpu.make_async_copy(a.at[:, cut], b.at[:, cut], sems.at[2 * h + i])
            for i, (a, b) in enumerate(sources)
        ]

    def half(h):
        p = mode_tiles(s, poles, h)
        w = mode_tiles(s, weights, h)
        arriving = [back(m, h) for m in range(s.modes)]
        recur(s, dconv_ref, dprod, p, w, arriving, h, reverse=True)
        taps_k, taps_v = (tap_tiles(s, taps, i, h) for i in (1, 2))

        def bring(i):
            stage(s, k_ref, ks, i, h, 1)
            stage(s, v_ref, vs, i, h, 1)

        def advance(inputs, grads, k2, v2, d):
            k0, k1, v0, v1 = inputs
            dk1, dk2, dv1, dv2 = grads
            dk0 = d * mix(taps_v, v0, v1, v2)
            dv0 = d * mix(taps_k, k0, k1, k2)
            out = mix(taps_k, dk0, dk1, dk2), mix(taps_v, dv0, dv1, dv2)
            return (k1, k2, v1, v2), (dk0, dk1, dv0, dv1), out

        bring(steps - 1)
        ka, kb, va, vb, _, _, kc, kd, vc, vd = (near_ref[major(s, r, h), :] for r in range(10))
        for ref, rows in ((ks, (ka, kb)), (vs, (va, vb))):
            for offset in range(2):
                ref[staged(s, 1, 6 + offset, h), :] = rows[offset]
        arriving = [back(m, h) for m in range(s.modes)]
        dconv0 = back(s.modes, h)
        d0 = total([w[m] * arriving[m] for m in range(s.modes)])
        d1 = total([w[m] * ((arriving[m] - dconv0) / p[m]) for m in range(s.modes)])
        ends = [staged(s, 2 * steps + 1, offset, h) for offset in (6, 7)]
        inputs = (kd, kc, vd, vc)
        grads = (jnp.zeros((SUB, LANES), f32),) * 4
        inputs, grads, _ = advance(inputs, grads, ks[ends[1], :], vs[ends[1], :], d1)
        inputs, grads, _ = advance(inputs, grads, ks[ends[0], :], vs[ends[0], :], d0)

        def step(i, carry):
            inputs, grads = carry
            i = steps - 1 - i

            @pl.when(i > 0)
            def _():
                bring(jnp.maximum(i - 1, 0))

            for block, offset in sixteen(0, True):
                d = dprod[major(s, (2 * i + block) * SUB + offset, h), :]
                rows = staged_before(s, 2 * i + block + 2, offset, h)
                inputs, grads, out = advance(inputs, grads, ks[rows, :], vs[rows, :], d)
                rows = staged(s, 2 * i + block + 2, offset, h)
                ks[rows, :], vs[rows, :] = out
            unstage(s, ks, kgrad_b, i + 1, h, i)
            unstage(s, vs, vgrad_b, i + 1, h, i)
            return inputs, grads

        lax.fori_loop(0, steps, step, (inputs, grads))
        for i, copy in enumerate(pieces(h)):
            copy.start(priority=i % 2)

    each_half(s, half)
    last.wait()

    def finish(h):
        for copy in pieces(h):
            copy.wait()

    each_half(s, finish)


def body(
    query_in, key_in, value_in, stream, short_filter, decay_rate, residue, norm_gain, cotangent
):
    length, channels = query_in.shape
    modes = decay_rate.shape[0]
    s = Sizes(length, channels, modes, lax.axis_size("seq"))
    total_width = channels * lax.axis_size("tp")
    wide = jax.ShapeDtypeStruct((length * s.tiles, LANES), f32)
    narrow = jax.ShapeDtypeStruct((length, channels), bf16)
    rows = 16 * s.tiles
    wide_s = pltpu.VMEM(wide.shape, f32)
    longer_s = pltpu.VMEM(((length + 16) * s.tiles, LANES), f32)
    narrow_s = pltpu.VMEM(narrow.shape, bf16)
    last_s = pltpu.VMEM((16, channels), bf16)
    tail_s = pltpu.VMEM((rows, LANES), f32)
    taps_s = pltpu.VMEM((3 * s.tiles * SUB, LANES), f32)
    mode_s = pltpu.VMEM((modes * s.tiles, LANES), f32)
    sum_s = pltpu.VMEM((length * SUB, LANES), f32)
    square_s = pltpu.VMEM((length, LANES), f32)
    gain = norm_gain.reshape(s.tiles, LANES)
    there = pl.BlockSpec(memory_space=pltpu.HBM)
    here = pl.BlockSpec(memory_space=pltpu.VMEM)

    def call(kernel, ins, outs, out_shape, scratch_shapes, operands, aliases={}, cost=None):
        return pl.pallas_call(
            functools.partial(kernel, s),
            in_specs=[there if c == "h" else here for c in ins],
            out_specs=[there if c == "h" else here for c in outs],
            out_shape=out_shape,
            scratch_shapes=scratch_shapes,
            input_output_aliases=aliases,
            cost_estimate=cost,
            compiler_params=pltpu.CompilerParams(vmem_limit_bytes=GRANT),
        )(*operands)

    forward_shape = s.exchange_shape(2 * modes, FORWARD_EXTRA)
    near_shape = jax.ShapeDtypeStruct((FORWARD_EXTRA * s.tiles, LANES), f32)

    def far(*arrays):
        return [pltpu.with_memory_space_constraint(x, pltpu.HBM) for x in arrays]

    def cost(per_element, arrays):
        return pl.CostEstimate(
            flops=per_element * length * channels, bytes_accessed=arrays * 4 * length * channels, transcendentals=0
        )

    filter_s = pltpu.VMEM(short_filter.shape, f32)
    rates_s = pltpu.VMEM(decay_rate.shape, f32)
    (pay,) = call(
        begin_kernel, "hhhhh", "v",
        (jax.ShapeDtypeStruct(forward_shape, bf16),),
        [narrow_s, narrow_s, last_s, filter_s, rates_s]
        + [wide_s] * 3 + [tail_s, pltpu.VMEM(forward_shape, f32), taps_s, mode_s]
        + [pltpu.SemaphoreType.DMA((3 + 2 * s.halves,))],
        far(query_in, key_in, value_in, short_filter, decay_rate),
    )
    inside, first = call(
        inside_kernel, "hhhhh", "vv", (wide, jax.ShapeDtypeStruct((4 * s.tiles, LANES), f32)),
        [narrow_s, narrow_s, filter_s, rates_s, rates_s]
        + [wide_s] * 3 + [taps_s, mode_s, mode_s, pltpu.SemaphoreType.DMA((5,))],
        far(key_in, value_in, short_filter, decay_rate, residue),
        cost=cost(75, 3),
    )
    back = exchange(s, pay, decay_rate, short_filter, True)
    conv, sums, near = call(
        forward_kernel, "v" * 10, "vvv",
        (wide, jax.ShapeDtypeStruct((2, length), f32), near_shape),
        [wide_s] * 3 + [pltpu.VMEM(forward_shape, f32), taps_s, mode_s, mode_s, sum_s, sum_s],
        (inside, first, query_in, stream, cotangent, back, short_filter, decay_rate, residue, gain),
        {0: 0},
    )
    sums = lax.psum(sums, "tp")
    normed, dstream, query_grad, dconv, tail, pay_back = call(
        lambda s, *refs: norm_kernel(s, total_width, *refs), "v" * 9, "hhhvvv",
        (narrow, narrow, narrow, wide, jax.ShapeDtypeStruct((rows, LANES), f32), jax.ShapeDtypeStruct(s.exchange_shape(modes, BACKWARD_EXTRA), f32)),
        [pltpu.VMEM(((length + 32) * s.tiles, LANES), f32)] + [longer_s] * 2 + [wide_s] * 2 + [narrow_s] * 2
        + [pltpu.VMEM((length + 16, channels), bf16)]
        + [taps_s, mode_s, square_s, square_s, pltpu.SemaphoreType.DMA((3 * s.halves,))],
        (sums, conv, query_in, stream, cotangent, near, short_filter, decay_rate, gain),
    )
    back_back = exchange(s, pay_back, decay_rate, short_filter, False)
    query_grad, key_grad, value_grad = call(
        backward_kernel, "v" * 9 + "h", "hhh",
        (narrow, narrow, narrow),
        [longer_s] * 2 + [wide_s, tail_s] + [narrow_s] * 2 + [last_s, taps_s, mode_s, mode_s]
        + [pltpu.SemaphoreType.DMA((1 + 2 * s.halves,))],
        (key_in, value_in, dconv, tail, near, back_back, short_filter, decay_rate, residue, query_grad),
        {9: 0},
    )
    return (normed, dstream, query_grad, key_grad, value_grad)


def solution(mesh):
    cut = P("seq", "tp")
    return jax.shard_map(
        body,
        mesh=mesh,
        in_specs=(cut, cut, cut, cut, P(None, None, "tp"), P(None, "tp"), P(None, "tp"), P("tp"), cut),
        out_specs=(cut,) * 5,
        check_vma=False,
    )
```

```python
import functools

import jax
import jax.numpy as jnp
from jax import lax
from jax.experimental import pallas as pl
from jax.experimental.pallas import tpu as pltpu
from jax.sharding import PartitionSpec as P

f32 = jnp.float32
bf16 = jnp.bfloat16
epsilon = 1e-05
LANES = 128
SUB = 8
GROUP = LANES * SUB
FORWARD_EXTRA = 10
BACKWARD_EXTRA = 4
GRANT = 20 * 1024 * 1024


class Sizes:
    def __init__(self, length, channels, modes, devices):
        self.length, self.channels, self.modes, self.devices = length, channels, modes, devices
        self.tiles = channels // LANES
        self.halves = channels // GROUP
        self.direct = devices == SUB

    def chunk_row(self, r, h, lead, extra):
        if r < lead:
            return h * lead + r
        return self.halves * lead + h * extra + r - lead

    def chunk_rows(self, lead, extra):
        return -(-self.halves * (lead + extra) // SUB) * SUB

    def exchange_shape(self, lead, extra):
        if self.direct:
            return (self.devices * self.chunk_rows(lead, extra), LANES)
        return ((lead + extra) * self.tiles, LANES)

    def exchange_slice(self, r, h, lead, extra):
        if self.direct:
            return pl.ds(self.chunk_row(r, h, lead, extra), SUB, stride=self.chunk_rows(lead, extra))
        return pl.ds(r * self.tiles + h * SUB, SUB)


def staged(s, block, offset, h):
    start = block * (s.tiles * SUB) + (h * SUB * SUB + offset)
    return pl.ds(start, SUB, stride=SUB)


def major(s, t, h):
    start = t * s.tiles + h * SUB
    if not isinstance(start, int):
        start = pl.multiple_of(start, SUB)
    return pl.ds(start, SUB)


def staged_before(s, block, offset, h):
    if offset < 2:
        return staged(s, block - 1, offset + SUB - 2, h)
    return staged(s, block, offset - 2, h)


def aligned(start, unit):
    return start if isinstance(start, int) else pl.multiple_of(start, unit)


def columns(h):
    return pl.ds(aligned(h * GROUP, GROUP), GROUP)


def stage(s, x_ref, out_ref, i, h, pad=0):
    rows = x_ref[pl.ds(aligned(i * 16, 16), 16), columns(h)].astype(f32)
    base = (i + pad) * (2 * s.tiles * SUB) + h * (SUB * SUB)
    for part in range(2):
        for j in range(SUB):
            out_ref[pl.ds(aligned(base + (part * s.tiles + j) * SUB, SUB), SUB), :] = rows[
                part * SUB : (part + 1) * SUB, j * LANES : (j + 1) * LANES
            ]


def unstage(s, in_ref, x_ref, i, h, to=None):
    base = i * (2 * s.tiles * SUB) + h * (SUB * SUB)
    rows = [
        jnp.concatenate(
            [
                in_ref[pl.ds(aligned(base + (part * s.tiles + j) * SUB, SUB), SUB), :]
                for part in range(2)
            ],
            axis=0,
        )
        for j in range(SUB)
    ]
    to = i if to is None else to
    x_ref[pl.ds(aligned(to * 16, 16), 16), columns(h)] = jnp.concatenate(rows, axis=1).astype(bf16)


def stage_wide(s, x_ref, out_ref):
    for h in range(s.halves):
        stage(s, x_ref, out_ref, 0, h)


def each_half(s, body):
    def step(h, carry):
        body(h)
        return carry

    lax.fori_loop(0, s.halves, step, 0)


def sixteen(i, reverse=False):
    pairs = [(2 * i + part, offset) for part in range(2) for offset in range(SUB)]
    return pairs[::-1] if reverse else pairs


def paired_loop(steps, step, carry):
    if steps % 2:
        return lax.fori_loop(0, steps, step, carry)
    return lax.fori_loop(0, steps // 2, lambda i, carry: step(2 * i + 1, step(2 * i, carry)), carry)


def long_steps(s):
    blocks = s.length // SUB
    return next(n for n in (4, 2, 1) if blocks % n == 0)


def positions(blocks, reverse=False):
    pairs = [(block, offset) for block in range(blocks) for offset in range(SUB)]
    return pairs[::-1] if reverse else pairs


def stage_modes(s, x_ref, out_ref, f):
    for g in range(s.modes // SUB):
        rows = f(x_ref[g * SUB : (g + 1) * SUB, :])
        for j in range(s.tiles):
            start = (g * s.tiles + j) * SUB
            out_ref[start : start + SUB, :] = rows[:, j * LANES : (j + 1) * LANES]


def mode_tiles(s, ref, h):
    return [ref[staged(s, m // SUB, m % SUB, h), :] for m in range(s.modes)]


def stage_taps(s, filter_ref, out_ref):
    for i in range(3):
        rows = filter_ref[i]
        for j in range(s.tiles):
            start = (i * s.tiles + j) * SUB
            out_ref[start : start + 3, :] = rows[:, j * LANES : (j + 1) * LANES]


def tap_tiles(s, ref, i, h):
    return [ref[staged(s, i, tap, h), :] for tap in range(3)]


def total(parts):
    while len(parts) > 1:
        parts = [
            parts[i] + parts[i + 1] if i + 1 < len(parts) else parts[i]
            for i in range(0, len(parts), 2)
        ]
    return parts[0]


def mix(taps, now, before, before2):
    return taps[0] * now + taps[1] * before + taps[2] * before2


def products(s, k_ref, v_ref, ks, vs, to_ref, taps_k, taps_v, h):
    def step(i, held):
        stage(s, k_ref, ks, i, h)
        stage(s, v_ref, vs, i, h)
        k1, k2, v1, v2 = held
        for block, offset in sixteen(0):
            rows = staged(s, 2 * i + block, offset, h)
            k0, v0 = ks[rows, :], vs[rows, :]
            product = mix(taps_k, k0, k1, k2) * mix(taps_v, v0, v1, v2)
            if block == 0 and offset < 2:
                product = jnp.where(i == 0, 0.0, product)
            to_ref[major(s, (2 * i + block) * SUB + offset, h), :] = product
            k1, k2, v1, v2 = k0, k1, v0, v1
        return k1, k2, v1, v2

    return paired_loop(s.length // 16, step, (jnp.zeros((SUB, LANES), f32),) * 4)


def recur(s, from_ref, to_ref, p, w, states, h, reverse=False):
    blocks = long_steps(s)
    steps = s.length // (SUB * blocks)

    def step(i, states):
        i = steps - 1 - i if reverse else i
        for block, offset in positions(blocks, reverse):
            rows = major(s, (blocks * i + block) * SUB + offset, h)
            signal = from_ref[rows, :]
            states = [p[m] * states[m] + signal for m in range(s.modes)]
            to_ref[rows, :] = total([w[m] * states[m] for m in range(s.modes)])
        return states

    lax.fori_loop(0, steps, step, states)


def forward_slice(s, r, h):
    return s.exchange_slice(r, h, 2 * s.modes, FORWARD_EXTRA)


def split(x):
    high = x.astype(bf16).astype(f32)
    return high, x - high


def put_states(s, ref, states, h):
    for m in range(s.modes):
        high, low = split(states[m])
        ref[forward_slice(s, m, h), :] = high
        ref[forward_slice(s, s.modes + m, h), :] = low


def narrowed(from_ref, to_ref):
    rows = from_ref.shape[0]
    for i in range(0, rows, 16):
        to_ref[i : min(i + 16, rows), :] = from_ref[i : min(i + 16, rows), :].astype(bf16)


def widened(from_ref, to_ref):
    rows = from_ref.shape[0]
    for i in range(0, rows, 16):
        to_ref[i : min(i + 16, rows), :] = from_ref[i : min(i + 16, rows), :].astype(f32)


def backward_slice(s, r, h):
    return s.exchange_slice(r, h, s.modes, BACKWARD_EXTRA)


def begin_kernel(
    s, q_hbm, k_hbm, v_hbm, filter_hbm, decay_hbm, pay_ref,
    kb, vb, qb, fb, db, ks, vs, prod, qs, pay_s, taps, poles, sems,
):
    copies = [(decay_hbm, db), (filter_hbm, fb), (q_hbm.at[pl.ds(s.length - 16, 16), :], qb)]
    for h in range(s.halves):
        cut = pl.ds(h * GROUP, GROUP)
        copies += [(k_hbm.at[:, cut], kb.at[:, cut]), (v_hbm.at[:, cut], vb.at[:, cut])]
    copies = [pltpu.make_async_copy(a, b, sems.at[i]) for i, (a, b) in enumerate(copies)]
    for i, copy in enumerate(copies):
        copy.start(priority=i % 2)
    copies[0].wait()
    stage_modes(s, db, poles, lambda x: jnp.exp(-x))
    copies[1].wait()
    stage_taps(s, fb, taps)
    blank = jnp.zeros((SUB, LANES), f32)
    copies[2].wait()
    stage_wide(s, qb, qs)

    def half(h):
        for i, (from_hbm, to) in enumerate(((k_hbm, kb), (v_hbm, vb))):
            cut = columns(h)
            pltpu.make_async_copy(from_hbm.at[:, cut], to.at[:, cut], sems.at[3 + 2 * h + i]).wait()
        p = mode_tiles(s, poles, h)
        taps_k, taps_v = (tap_tiles(s, taps, i, h) for i in (1, 2))

        held = products(s, kb, vb, ks, vs, prod, taps_k, taps_v, h)

        blocks = long_steps(s)

        def step(i, states):
            for block, offset in positions(blocks):
                product = prod[major(s, (blocks * i + block) * SUB + offset, h), :]
                states = [p[m] * states[m] + product for m in range(s.modes)]
            return states

        states = lax.fori_loop(0, s.length // (SUB * blocks), step, [blank] * s.modes)
        put_states(s, pay_s, states, h)
        k1, k2, v1, v2 = held
        first = [staged(s, 0, offset, h) for offset in range(2)]
        last = [staged(s, 1, offset, h) for offset in (6, 7)]
        extra = [
            ks[first[0], :], ks[first[1], :], k2, k1,
            vs[first[0], :], vs[first[1], :], v2, v1,
            qs[last[0], :], qs[last[1], :],
        ]
        for r, value in enumerate(extra):
            pay_s[forward_slice(s, 2 * s.modes + r, h), :] = value

    each_half(s, half)
    narrowed(pay_s, pay_ref)


def forward_middle(length, rates, taps, ends, extras):
    devices = len(ends)
    whole, step0, step1 = (jnp.exp(-float(length - i) * rates) for i in range(3))
    blank = jnp.zeros_like(extras[0][0])
    arriving = jnp.zeros_like(ends[0])
    result = []
    for i in range(devices):
        k0, k1, _, _, v0, v1 = extras[i][:6]
        if i:
            _, _, ka, kb, _, _, va, vb, qa, qb = extras[i - 1][:10]
        else:
            ka = kb = va = vb = qa = qb = blank
        if i + 1 < devices:
            kc, kd, _, _, vc, vd = extras[i + 1][:6]
        else:
            kc = kd = vc = vd = blank
        prod0 = mix(taps[1], k0, kb, ka) * mix(taps[2], v0, vb, va)
        prod1 = mix(taps[1], k1, k0, kb) * mix(taps[2], v1, v0, vb)
        result.append((arriving, [ka, kb, va, vb, qa, qb, kc, kd, vc, vd]))
        arriving = whole * arriving + (ends[i] + step0 * prod0 + step1 * prod1)
    return result


def backward_middle(length, rates, ends, extras):
    devices = len(ends)
    whole = jnp.exp(-float(length) * rates)
    blank = jnp.zeros_like(extras[0][0])
    arriving = jnp.zeros_like(ends[0])
    result = [None] * devices
    for i in reversed(range(devices)):
        result[i] = (arriving, extras[i + 1] if i + 1 < devices else [blank] * len(extras[0]))
        arriving = whole * arriving + ends[i]
    return result


def middle_kernel(s, forward, pay_ref, decay_ref, filter_ref, back_ref, *wide):
    me = lax.axis_index("seq")
    lead, extra = (2 * s.modes, FORWARD_EXTRA) if forward else (s.modes, BACKWARD_EXTRA)
    in_ref, out_ref = wide if forward else (pay_ref, back_ref)
    if forward:
        widened(pay_ref, in_ref)
    rows = s.chunk_rows(lead, extra)
    for h in range(s.halves):
        lanes = pl.ds(pl.multiple_of((me + h * SUB) * LANES, LANES), LANES)
        rates = decay_ref[:, lanes]
        ends, extras = [], []
        for i in range(s.devices):
            e = i * rows + s.chunk_row(0, h, lead, extra)
            end = in_ref[e : e + s.modes, :]
            ends.append(end + in_ref[e + s.modes : e + lead, :] if forward else end)
            x = i * rows + s.chunk_row(lead, h, lead, extra)
            extras.append([in_ref[x + r : x + r + 1, :] for r in range(extra)])
        if forward:
            taps = [[filter_ref[i, tap : tap + 1, lanes] for tap in range(3)] for i in range(3)]
            result = forward_middle(s.length, rates, taps, ends, extras)
        else:
            result = backward_middle(s.length, rates, ends, extras)
        for i, (state, more) in enumerate(result):
            e = i * rows + s.chunk_row(0, h, lead, extra)
            if forward:
                out_ref[e : e + s.modes, :], out_ref[e + s.modes : e + lead, :] = split(state)
            else:
                out_ref[e : e + s.modes, :] = state
            x = i * rows + s.chunk_row(lead, h, lead, extra)
            for r in range(extra):
                out_ref[x + r : x + r + 1, :] = more[r]
    if forward:
        narrowed(out_ref, back_ref)


def exchange(s, pay, decay_rate, short_filter, forward):
    lead, extra = (2 * s.modes, FORWARD_EXTRA) if forward else (s.modes, BACKWARD_EXTRA)
    if s.direct:
        chunks = (s.devices, s.chunk_rows(lead, extra), LANES)
        got = lax.all_to_all(pay.reshape(chunks), "seq", 0, 0, tiled=True)
        back = pl.pallas_call(
            functools.partial(middle_kernel, s, forward),
            out_shape=jax.ShapeDtypeStruct(pay.shape, pay.dtype),
            scratch_shapes=[pltpu.VMEM(pay.shape, f32)] * 2 if forward else [],
            compiler_params=pltpu.CompilerParams(vmem_limit_bytes=GRANT),
        )(got.reshape(pay.shape), decay_rate, short_filter)
        return lax.all_to_all(back.reshape(chunks), "seq", 0, 0, tiled=True).reshape(pay.shape)
    rows = lead + extra
    width = s.channels // s.devices
    start = lax.axis_index("seq") * width
    rates = lax.dynamic_slice_in_dim(decay_rate, start, width, 1)
    part = lax.dynamic_slice_in_dim(short_filter, start, width, 2)
    pay = pay.reshape(rows, s.devices, width).transpose(1, 0, 2)
    got = lax.all_to_all(pay, "seq", 0, 0, tiled=True).astype(f32)
    ends = [got[i, : s.modes] for i in range(s.devices)]
    extras = [[got[i, lead + r][None] for r in range(extra)] for i in range(s.devices)]
    if forward:
        ends = [end + got[i, s.modes : lead] for i, end in enumerate(ends)]
        taps = [[part[i, tap][None] for tap in range(3)] for i in range(3)]
        result = forward_middle(s.length, rates, taps, ends, extras)
        highs = [lax.reduce_precision(state, 8, 7) for state, _ in result]
        result = [
            (jnp.concatenate([high, state - high]), more) for high, (state, more) in zip(highs, result)
        ]
    else:
        result = backward_middle(s.length, rates, ends, extras)
    back = jnp.stack([jnp.concatenate([state] + list(more)) for state, more in result])
    back = lax.all_to_all(back.astype(pay.dtype), "seq", 0, 0, tiled=True)
    return back.transpose(1, 0, 2).reshape(rows * s.tiles, LANES)


def inside_kernel(
    s, k_hbm, v_hbm, filter_hbm, decay_hbm, residue_hbm, inside_ref, first_ref,
    kb, vb, fb, db, rb, ks, vs, prod, taps, poles, weights, sems,
):
    pairs = [(decay_hbm, db), (residue_hbm, rb), (filter_hbm, fb), (k_hbm, kb), (v_hbm, vb)]
    copies = [pltpu.make_async_copy(a, b, sems.at[i]) for i, (a, b) in enumerate(pairs)]
    for i, copy in enumerate(copies):
        copy.start(priority=i % 2)
    for copy in copies:
        copy.wait()
    stage_modes(s, db, poles, lambda x: jnp.exp(-x))
    stage_modes(s, rb, weights, lambda x: x)
    stage_taps(s, fb, taps)
    blank = jnp.zeros((SUB, LANES), f32)
    steps = s.length // 16

    def half(h):
        taps_k, taps_v = (tap_tiles(s, taps, i, h) for i in (1, 2))

        products(s, kb, vb, ks, vs, prod, taps_k, taps_v, h)
        for i, (ref, part) in enumerate(((ks, taps_k), (vs, taps_v))):
            x0, x1 = (ref[staged(s, 0, offset, h), :] for offset in range(2))
            first_ref[major(s, 2 * i, h), :] = part[0] * x0
            first_ref[major(s, 2 * i + 1, h), :] = part[0] * x1 + part[1] * x0
        recur(s, prod, inside_ref, mode_tiles(s, poles, h), mode_tiles(s, weights, h), [blank] * s.modes, h)

    each_half(s, half)


def forward_kernel(
    s, inside_ref, first_ref, q_ref, stream_ref, cot_ref, back_ref, filter_ref, decay_ref, residue_ref, gain_ref,
    conv_ref, sums_ref, near_ref,
    qs, xs, gs, back_s, taps, poles, weights, squares, inners,
):
    stage_modes(s, decay_ref, poles, lambda x: jnp.exp(-x))
    stage_modes(s, residue_ref, weights, lambda x: x)
    stage_taps(s, filter_ref, taps)

    widened(back_ref, back_s)
    steps = s.length // 16

    def half(h):
        p = mode_tiles(s, poles, h)
        w = mode_tiles(s, weights, h)
        gain = gain_ref[pl.ds(aligned(h * SUB, SUB), SUB), :]
        taps_q, taps_k, taps_v = (tap_tiles(s, taps, i, h) for i in range(3))
        near = [back_s[forward_slice(s, 2 * s.modes + r, h), :] for r in range(FORWARD_EXTRA)]
        for r, value in enumerate(near):
            near_ref[major(s, r, h), :] = value
        ka, kb, va, vb, qa, qb = near[:6]
        k0, k1, v0, v1 = (first_ref[major(s, r, h), :] for r in range(4))
        products = [
            (k0 + taps_k[1] * kb + taps_k[2] * ka) * (v0 + taps_v[1] * vb + taps_v[2] * va),
            (k1 + taps_k[2] * kb) * (v1 + taps_v[2] * vb),
        ]
        conv = []
        states = [
            back_s[forward_slice(s, m, h), :] + back_s[forward_slice(s, s.modes + m, h), :]
            for m in range(s.modes)
        ]
        for offset in range(2):
            states = [p[m] * states[m] + products[offset] for m in range(s.modes)]
            conv.append(total([w[m] * states[m] for m in range(s.modes)]))
        states = [w[m] * states[m] / (p[m] * p[m]) for m in range(s.modes)]
        first, ahead = [], states
        for offset in range(2):
            ahead = [p[m] * ahead[m] for m in range(s.modes)]
            first.append(conv[offset] - total(ahead))

        def bring(i):
            stage(s, q_ref, qs, i, h)
            stage(s, stream_ref, xs, i, h)
            stage(s, cot_ref, gs, i, h)

        def step(i, carry):
            (q1, q2), states = carry
            for block, offset in sixteen(0):
                rows = staged(s, 2 * i + block, offset, h)
                t = (2 * i + block) * SUB + offset
                out = major(s, t, h)
                inside = inside_ref[out, :]
                if block == 0 and offset < 2:
                    inside = jnp.where(i == 0, first[offset], inside)
                states = [p[m] * states[m] for m in range(s.modes)]
                conv = inside + total(states)
                conv_ref[out, :] = conv
                q0 = qs[rows, :]
                mixed = xs[rows, :] + mix(taps_q, q0, q1, q2) * conv
                part = pl.ds(pl.multiple_of(t * SUB, SUB), SUB)
                square, inner = mixed * mixed, gain * gs[rows, :] * mixed
                squares[part, :] = square + jnp.where(h == 0, 0.0, squares[part, :])
                inners[part, :] = inner + jnp.where(h == 0, 0.0, inners[part, :])
                q1, q2 = q0, q1
            bring(jnp.minimum(i + 1, steps - 1))
            return (q1, q2), states

        bring(0)
        paired_loop(steps, step, ((qb, qa), states))

    each_half(s, half)
    for r, ref in enumerate((squares, inners)):
        parts = []
        for b in range(s.length // SUB):
            parts.append(
                total([ref[pl.ds(b * SUB * SUB + i, SUB, stride=SUB), :] for i in range(SUB)])
            )
        rows = jnp.concatenate(parts, axis=0)
        sums_ref[r : r + 1, :] = jnp.sum(rows.T, axis=0, keepdims=True)


def norm_kernel(
    s, width, sums_ref, conv_ref, q_ref, stream_ref, cot_ref, near_ref, filter_ref, decay_ref, gain_ref,
    normed_hbm, dstream_hbm, qgrad_hbm, dconv_ref, tail_ref, pay_ref,
    qs, xs, gs, ns, ds, normed_b, dstream_b, qgrad_b, taps, poles, inv_s, coef_s, sems,
):
    inverse = lax.rsqrt(sums_ref[0:1, :] / width + epsilon)
    coef = inverse * inverse * inverse * sums_ref[1:2, :] / width
    inv_s[...] = jnp.broadcast_to(inverse, (LANES, s.length)).T
    coef_s[...] = jnp.broadcast_to(coef, (LANES, s.length)).T
    stage_modes(s, decay_ref, poles, lambda x: jnp.exp(-x))
    stage_taps(s, filter_ref, taps)
    blank = jnp.zeros((SUB, LANES), f32)
    steps = s.length // 16

    def pieces(h):
        cut = columns(h)
        sources = [
            (normed_b.at[:, cut], normed_hbm.at[:, cut]),
            (dstream_b.at[:, cut], dstream_hbm.at[:, cut]),
            (qgrad_b.at[pl.ds(16, s.length - 16), cut], qgrad_hbm.at[pl.ds(0, s.length - 16), cut]),
        ]
        return [pltpu.make_async_copy(a, b, sems.at[3 * h + i]) for i, (a, b) in enumerate(sources)]

    def half(h):
        gain = gain_ref[pl.ds(aligned(h * SUB, SUB), SUB), :]
        taps_q = tap_tiles(s, taps, 0, h)

        def bring(i):
            rows = jnp.minimum(i, steps - 1)
            stage(s, q_ref, qs, rows, h, i - rows + 1)
            stage(s, stream_ref, xs, rows, h)
            stage(s, cot_ref, gs, rows, h)

        def step(i, held):
            q1, q2, dq1, dq2 = held
            for block, offset in sixteen(0):
                rows = staged(s, 2 * i + block, offset, h)
                t = (2 * i + block) * SUB + offset
                out = major(s, t, h)
                inv = jnp.broadcast_to(inv_s[pl.ds(t, 1), :], (SUB, LANES))
                cf = jnp.broadcast_to(coef_s[pl.ds(t, 1), :], (SUB, LANES))
                q0 = qs[staged(s, 2 * i + block + 2, offset, h), :]
                qmix = mix(taps_q, q0, q1, q2)
                conv = conv_ref[out, :]
                mixed = xs[rows, :] + qmix * conv
                dmixed = inv * (gain * gs[rows, :]) - mixed * cf
                ns[rows, :] = mixed * inv * gain
                ds[rows, :] = dmixed
                dq0 = dmixed * conv
                dconv_ref[out, :] = dmixed * qmix
                qs[staged_before(s, 2 * i + block + 2, offset, h), :] = mix(taps_q, dq2, dq1, dq0)
                q1, q2, dq1, dq2 = q0, q1, dq0, dq1
            unstage(s, ns, normed_b, i, h)
            unstage(s, ds, dstream_b, i, h)
            unstage(s, qs, qgrad_b, i, h)
            bring(i + 1)
            return q1, q2, dq1, dq2

        bring(0)
        held = (near_ref[major(s, 5, h), :], near_ref[major(s, 4, h), :], blank, blank)
        _, _, dq1, dq2 = paired_loop(steps, step, held)
        qs[staged(s, 2 * steps + 1, 6, h), :] = taps_q[0] * dq2 + taps_q[1] * dq1
        qs[staged(s, 2 * steps + 1, 7, h), :] = taps_q[0] * dq1
        for i, copy in enumerate(pieces(h)):
            copy.start(priority=i % 2)

    each_half(s, half)
    start = steps * 2 * s.tiles * SUB
    tail_ref[...] = qs[start : start + 2 * s.tiles * SUB, :]

    def ends(h):
        p = mode_tiles(s, poles, h)

        blocks = long_steps(s)
        many = s.length // (SUB * blocks)

        def step(i, states):
            for block, offset in positions(blocks, True):
                t = (blocks * (many - 1 - i) + block) * SUB + offset
                dconv = dconv_ref[major(s, t, h), :]
                states = [p[m] * states[m] + dconv for m in range(s.modes)]
            return states

        states = lax.fori_loop(0, many, step, [blank] * s.modes)
        for m in range(s.modes):
            pay_ref[backward_slice(s, m, h), :] = states[m]
        first = [ds[staged(s, 0, offset, h), :] * conv_ref[major(s, offset, h), :] for offset in range(2)]
        for r, value in enumerate([dconv_ref[major(s, 0, h), :], *first, blank]):
            pay_ref[backward_slice(s, s.modes + r, h), :] = value

    each_half(s, ends)

    def finish(h):
        for copy in pieces(h):
            copy.wait()

    each_half(s, finish)


def backward_kernel(
    s, k_ref, v_ref, dconv_ref, tail_ref, near_ref, back_ref, filter_ref, decay_ref, residue_ref, qgrad_in,
    qgrad_hbm, kgrad_hbm, vgrad_hbm,
    ks, vs, dprod, qs, kgrad_b, vgrad_b, qgrad_b, taps, poles, weights, sems,
):
    del qgrad_in
    stage_modes(s, decay_ref, poles, lambda x: jnp.exp(-x))
    stage_modes(s, residue_ref, weights, lambda x: x)
    stage_taps(s, filter_ref, taps)
    steps = s.length // 16

    def back(r, h):
        return back_ref[backward_slice(s, r, h), :]

    qs[...] = tail_ref[...]

    def tails(h):
        taps_q = tap_tiles(s, taps, 0, h)
        dq0, dq1 = back(s.modes + 1, h), back(s.modes + 2, h)
        rows = [staged(s, 1, offset, h) for offset in (6, 7)]
        qs[rows[0], :] = qs[rows[0], :] + taps_q[2] * dq0
        qs[rows[1], :] = qs[rows[1], :] + (taps_q[1] * dq0 + taps_q[2] * dq1)
        unstage(s, qs, qgrad_b, 0, h)

    each_half(s, tails)
    last = pltpu.make_async_copy(qgrad_b, qgrad_hbm.at[pl.ds(s.length - 16, 16), :], sems.at[2 * s.halves])
    last.start()

    def pieces(h):
        cut = columns(h)
        sources = [(kgrad_b, kgrad_hbm), (vgrad_b, vgrad_hbm)]
        return [
            pltpu.make_async_copy(a.at[:, cut], b.at[:, cut], sems.at[2 * h + i])
            for i, (a, b) in enumerate(sources)
        ]

    def half(h):
        p = mode_tiles(s, poles, h)
        w = mode_tiles(s, weights, h)
        arriving = [back(m, h) for m in range(s.modes)]
        recur(s, dconv_ref, dprod, p, w, arriving, h, reverse=True)
        taps_k, taps_v = (tap_tiles(s, taps, i, h) for i in (1, 2))

        def bring(i):
            stage(s, k_ref, ks, i, h, 1)
            stage(s, v_ref, vs, i, h, 1)

        def advance(inputs, grads, k2, v2, d):
            k0, k1, v0, v1 = inputs
            dk1, dk2, dv1, dv2 = grads
            dk0 = d * mix(taps_v, v0, v1, v2)
            dv0 = d * mix(taps_k, k0, k1, k2)
            out = mix(taps_k, dk0, dk1, dk2), mix(taps_v, dv0, dv1, dv2)
            return (k1, k2, v1, v2), (dk0, dk1, dv0, dv1), out

        bring(steps - 1)
        ka, kb, va, vb, _, _, kc, kd, vc, vd = (near_ref[major(s, r, h), :] for r in range(10))
        for ref, rows in ((ks, (ka, kb)), (vs, (va, vb))):
            for offset in range(2):
                ref[staged(s, 1, 6 + offset, h), :] = rows[offset]
        arriving = [back(m, h) for m in range(s.modes)]
        dconv0 = back(s.modes, h)
        d0 = total([w[m] * arriving[m] for m in range(s.modes)])
        d1 = total([w[m] * ((arriving[m] - dconv0) / p[m]) for m in range(s.modes)])
        ends = [staged(s, 2 * steps + 1, offset, h) for offset in (6, 7)]
        inputs = (kd, kc, vd, vc)
        grads = (jnp.zeros((SUB, LANES), f32),) * 4
        inputs, grads, _ = advance(inputs, grads, ks[ends[1], :], vs[ends[1], :], d1)
        inputs, grads, _ = advance(inputs, grads, ks[ends[0], :], vs[ends[0], :], d0)

        def step(i, carry):
            inputs, grads = carry
            i = steps - 1 - i

            @pl.when(i > 0)
            def _():
                bring(jnp.maximum(i - 1, 0))

            for block, offset in sixteen(0, True):
                d = dprod[major(s, (2 * i + block) * SUB + offset, h), :]
                rows = staged_before(s, 2 * i + block + 2, offset, h)
                inputs, grads, out = advance(inputs, grads, ks[rows, :], vs[rows, :], d)
                rows = staged(s, 2 * i + block + 2, offset, h)
                ks[rows, :], vs[rows, :] = out
            unstage(s, ks, kgrad_b, i + 1, h, i)
            unstage(s, vs, vgrad_b, i + 1, h, i)
            return inputs, grads

        paired_loop(steps, step, (inputs, grads))
        for i, copy in enumerate(pieces(h)):
            copy.start(priority=i % 2)

    each_half(s, half)
    last.wait()

    def finish(h):
        for copy in pieces(h):
            copy.wait()

    each_half(s, finish)


def body(
    query_in, key_in, value_in, stream, short_filter, decay_rate, residue, norm_gain, cotangent
):
    length, channels = query_in.shape
    modes = decay_rate.shape[0]
    s = Sizes(length, channels, modes, lax.axis_size("seq"))
    total_width = channels * lax.axis_size("tp")
    wide = jax.ShapeDtypeStruct((length * s.tiles, LANES), f32)
    narrow = jax.ShapeDtypeStruct((length, channels), bf16)
    rows = 16 * s.tiles
    wide_s = pltpu.VMEM(wide.shape, f32)
    longer_s = pltpu.VMEM(((length + 16) * s.tiles, LANES), f32)
    narrow_s = pltpu.VMEM(narrow.shape, bf16)
    last_s = pltpu.VMEM((16, channels), bf16)
    tail_s = pltpu.VMEM((rows, LANES), f32)
    taps_s = pltpu.VMEM((3 * s.tiles * SUB, LANES), f32)
    mode_s = pltpu.VMEM((modes * s.tiles, LANES), f32)
    sum_s = pltpu.VMEM((length * SUB, LANES), f32)
    square_s = pltpu.VMEM((length, LANES), f32)
    gain = norm_gain.reshape(s.tiles, LANES)
    there = pl.BlockSpec(memory_space=pltpu.HBM)
    here = pl.BlockSpec(memory_space=pltpu.VMEM)

    def call(kernel, ins, outs, out_shape, scratch_shapes, operands, aliases={}, cost=None):
        return pl.pallas_call(
            functools.partial(kernel, s),
            in_specs=[there if c == "h" else here for c in ins],
            out_specs=[there if c == "h" else here for c in outs],
            out_shape=out_shape,
            scratch_shapes=scratch_shapes,
            input_output_aliases=aliases,
            cost_estimate=cost,
            compiler_params=pltpu.CompilerParams(vmem_limit_bytes=GRANT),
        )(*operands)

    forward_shape = s.exchange_shape(2 * modes, FORWARD_EXTRA)
    near_shape = jax.ShapeDtypeStruct((FORWARD_EXTRA * s.tiles, LANES), f32)

    def far(*arrays):
        return [pltpu.with_memory_space_constraint(x, pltpu.HBM) for x in arrays]

    def cost(per_element, arrays):
        return pl.CostEstimate(
            flops=per_element * length * channels, bytes_accessed=arrays * 4 * length * channels, transcendentals=0
        )

    filter_s = pltpu.VMEM(short_filter.shape, f32)
    rates_s = pltpu.VMEM(decay_rate.shape, f32)
    (pay,) = call(
        begin_kernel, "hhhhh", "v",
        (jax.ShapeDtypeStruct(forward_shape, bf16),),
        [narrow_s, narrow_s, last_s, filter_s, rates_s]
        + [wide_s] * 3 + [tail_s, pltpu.VMEM(forward_shape, f32), taps_s, mode_s]
        + [pltpu.SemaphoreType.DMA((3 + 2 * s.halves,))],
        far(query_in, key_in, value_in, short_filter, decay_rate),
    )
    inside, first = call(
        inside_kernel, "hhhhh", "vv", (wide, jax.ShapeDtypeStruct((4 * s.tiles, LANES), f32)),
        [narrow_s, narrow_s, filter_s, rates_s, rates_s]
        + [wide_s] * 3 + [taps_s, mode_s, mode_s, pltpu.SemaphoreType.DMA((5,))],
        far(key_in, value_in, short_filter, decay_rate, residue),
        cost=cost(75, 3),
    )
    back = exchange(s, pay, decay_rate, short_filter, True)
    conv, sums, near = call(
        forward_kernel, "v" * 10, "vvv",
        (wide, jax.ShapeDtypeStruct((2, length), f32), near_shape),
        [wide_s] * 3 + [pltpu.VMEM(forward_shape, f32), taps_s, mode_s, mode_s, sum_s, sum_s],
        (inside, first, query_in, stream, cotangent, back, short_filter, decay_rate, residue, gain),
        {0: 0},
    )
    sums = lax.psum(sums, "tp")
    normed, dstream, query_grad, dconv, tail, pay_back = call(
        lambda s, *refs: norm_kernel(s, total_width, *refs), "v" * 9, "hhhvvv",
        (narrow, narrow, narrow, wide, jax.ShapeDtypeStruct((rows, LANES), f32), jax.ShapeDtypeStruct(s.exchange_shape(modes, BACKWARD_EXTRA), f32)),
        [pltpu.VMEM(((length + 32) * s.tiles, LANES), f32)] + [longer_s] * 2 + [wide_s] * 2 + [narrow_s] * 2
        + [pltpu.VMEM((length + 16, channels), bf16)]
        + [taps_s, mode_s, square_s, square_s, pltpu.SemaphoreType.DMA((3 * s.halves,))],
        (sums, conv, query_in, stream, cotangent, near, short_filter, decay_rate, gain),
    )
    back_back = exchange(s, pay_back, decay_rate, short_filter, False)
    query_grad, key_grad, value_grad = call(
        backward_kernel, "v" * 9 + "h", "hhh",
        (narrow, narrow, narrow),
        [longer_s] * 2 + [wide_s, tail_s] + [narrow_s] * 2 + [last_s, taps_s, mode_s, mode_s]
        + [pltpu.SemaphoreType.DMA((1 + 2 * s.halves,))],
        (key_in, value_in, dconv, tail, near, back_back, short_filter, decay_rate, residue, query_grad),
        {9: 0},
    )
    return (normed, dstream, query_grad, key_grad, value_grad)


def solution(mesh):
    cut = P("seq", "tp")
    return jax.shard_map(
        body,
        mesh=mesh,
        in_specs=(cut, cut, cut, cut, P(None, None, "tp"), P(None, "tp"), P(None, "tp"), P("tp"), cut),
        out_specs=(cut,) * 5,
        check_vma=False,
    )
```

```python
import functools

import jax
import jax.numpy as jnp
from jax import lax
from jax.experimental import pallas as pl
from jax.experimental.pallas import tpu as pltpu
from jax.sharding import PartitionSpec as P

f32 = jnp.float32
bf16 = jnp.bfloat16
epsilon = 1e-05
LANES = 128
SUB = 8
GROUP = LANES * SUB
FORWARD_EXTRA = 10
BACKWARD_EXTRA = 4
GRANT = 20 * 1024 * 1024


class Sizes:
    def __init__(self, length, channels, modes, devices):
        self.length, self.channels, self.modes, self.devices = length, channels, modes, devices
        self.tiles = channels // LANES
        self.halves = channels // GROUP
        self.direct = devices == SUB

    def chunk_row(self, r, h, lead, extra):
        if r < lead:
            return h * lead + r
        return self.halves * lead + h * extra + r - lead

    def chunk_rows(self, lead, extra):
        return -(-self.halves * (lead + extra) // SUB) * SUB

    def exchange_shape(self, lead, extra):
        if self.direct:
            return (self.devices * self.chunk_rows(lead, extra), LANES)
        return ((lead + extra) * self.tiles, LANES)

    def exchange_slice(self, r, h, lead, extra):
        if self.direct:
            return pl.ds(self.chunk_row(r, h, lead, extra), SUB, stride=self.chunk_rows(lead, extra))
        return pl.ds(r * self.tiles + h * SUB, SUB)


def staged(s, block, offset, h):
    start = block * (s.tiles * SUB) + (h * SUB * SUB + offset)
    return pl.ds(start, SUB, stride=SUB)


def major(s, t, h):
    start = t * s.tiles + h * SUB
    if not isinstance(start, int):
        start = pl.multiple_of(start, SUB)
    return pl.ds(start, SUB)


def staged_before(s, block, offset, h):
    if offset < 2:
        return staged(s, block - 1, offset + SUB - 2, h)
    return staged(s, block, offset - 2, h)


def aligned(start, unit):
    return start if isinstance(start, int) else pl.multiple_of(start, unit)


def columns(h):
    return pl.ds(aligned(h * GROUP, GROUP), GROUP)


def stage(s, x_ref, out_ref, i, h, pad=0):
    rows = x_ref[pl.ds(aligned(i * 16, 16), 16), columns(h)].astype(f32)
    base = (i + pad) * (2 * s.tiles * SUB) + h * (SUB * SUB)
    for part in range(2):
        for j in range(SUB):
            out_ref[pl.ds(aligned(base + (part * s.tiles + j) * SUB, SUB), SUB), :] = rows[
                part * SUB : (part + 1) * SUB, j * LANES : (j + 1) * LANES
            ]


def unstage(s, in_ref, x_ref, i, h, to=None):
    base = i * (2 * s.tiles * SUB) + h * (SUB * SUB)
    rows = [
        jnp.concatenate(
            [
                in_ref[pl.ds(aligned(base + (part * s.tiles + j) * SUB, SUB), SUB), :]
                for part in range(2)
            ],
            axis=0,
        )
        for j in range(SUB)
    ]
    to = i if to is None else to
    x_ref[pl.ds(aligned(to * 16, 16), 16), columns(h)] = jnp.concatenate(rows, axis=1).astype(bf16)


def stage_wide(s, x_ref, out_ref):
    for h in range(s.halves):
        stage(s, x_ref, out_ref, 0, h)


def each_half(s, body):
    def step(h, carry):
        body(h)
        return carry

    lax.fori_loop(0, s.halves, step, 0)


def sixteen(i, reverse=False):
    pairs = [(2 * i + part, offset) for part in range(2) for offset in range(SUB)]
    return pairs[::-1] if reverse else pairs


def paired_loop(steps, step, carry):
    if steps % 2:
        return lax.fori_loop(0, steps, step, carry)
    return lax.fori_loop(0, steps // 2, lambda i, carry: step(2 * i + 1, step(2 * i, carry)), carry)


def long_steps(s):
    blocks = s.length // SUB
    return next(n for n in (4, 2, 1) if blocks % n == 0)


def positions(blocks, reverse=False):
    pairs = [(block, offset) for block in range(blocks) for offset in range(SUB)]
    return pairs[::-1] if reverse else pairs


def stage_modes(s, x_ref, out_ref, f):
    for g in range(s.modes // SUB):
        rows = f(x_ref[g * SUB : (g + 1) * SUB, :])
        for j in range(s.tiles):
            start = (g * s.tiles + j) * SUB
            out_ref[start : start + SUB, :] = rows[:, j * LANES : (j + 1) * LANES]


def mode_tiles(s, ref, h):
    return [ref[staged(s, m // SUB, m % SUB, h), :] for m in range(s.modes)]


def stage_taps(s, filter_ref, out_ref):
    for i in range(3):
        rows = filter_ref[i]
        for j in range(s.tiles):
            start = (i * s.tiles + j) * SUB
            out_ref[start : start + 3, :] = rows[:, j * LANES : (j + 1) * LANES]


def tap_tiles(s, ref, i, h):
    return [ref[staged(s, i, tap, h), :] for tap in range(3)]


def total(parts):
    while len(parts) > 1:
        parts = [
            parts[i] + parts[i + 1] if i + 1 < len(parts) else parts[i]
            for i in range(0, len(parts), 2)
        ]
    return parts[0]


def mix(taps, now, before, before2):
    return taps[0] * now + taps[1] * before + taps[2] * before2


def products(s, k_ref, v_ref, ks, vs, to_ref, taps_k, taps_v, h):
    def step(i, held):
        stage(s, k_ref, ks, i, h)
        stage(s, v_ref, vs, i, h)
        k1, k2, v1, v2 = held
        for block, offset in sixteen(0):
            rows = staged(s, 2 * i + block, offset, h)
            k0, v0 = ks[rows, :], vs[rows, :]
            product = mix(taps_k, k0, k1, k2) * mix(taps_v, v0, v1, v2)
            if block == 0 and offset < 2:
                product = jnp.where(i == 0, 0.0, product)
            to_ref[major(s, (2 * i + block) * SUB + offset, h), :] = product
            k1, k2, v1, v2 = k0, k1, v0, v1
        return k1, k2, v1, v2

    return paired_loop(s.length // 16, step, (jnp.zeros((SUB, LANES), f32),) * 4)


def recur(s, from_ref, to_ref, p, w, states, h, reverse=False):
    blocks = long_steps(s)
    steps = s.length // (SUB * blocks)

    def step(i, states):
        i = steps - 1 - i if reverse else i
        for block, offset in positions(blocks, reverse):
            rows = major(s, (blocks * i + block) * SUB + offset, h)
            signal = from_ref[rows, :]
            states = [p[m] * states[m] + signal for m in range(s.modes)]
            to_ref[rows, :] = total([w[m] * states[m] for m in range(s.modes)])
        return states

    lax.fori_loop(0, steps, step, states)


def forward_slice(s, r, h):
    return s.exchange_slice(r, h, 2 * s.modes, FORWARD_EXTRA)


def split(x):
    high = x.astype(bf16).astype(f32)
    return high, x - high


def put_states(s, ref, states, h):
    for m in range(s.modes):
        high, low = split(states[m])
        ref[forward_slice(s, m, h), :] = high
        ref[forward_slice(s, s.modes + m, h), :] = low


def narrowed(from_ref, to_ref):
    rows = from_ref.shape[0]
    for i in range(0, rows, 16):
        to_ref[i : min(i + 16, rows), :] = from_ref[i : min(i + 16, rows), :].astype(bf16)


def widened(from_ref, to_ref):
    rows = from_ref.shape[0]
    for i in range(0, rows, 16):
        to_ref[i : min(i + 16, rows), :] = from_ref[i : min(i + 16, rows), :].astype(f32)


def backward_slice(s, r, h):
    return s.exchange_slice(r, h, s.modes, BACKWARD_EXTRA)


def begin_kernel(
    s, q_hbm, k_hbm, v_hbm, filter_hbm, decay_hbm, pay_ref,
    kb, vb, qb, fb, db, ks, vs, prod, qs, pay_s, taps, poles, sems,
):
    copies = [(decay_hbm, db), (filter_hbm, fb), (q_hbm.at[pl.ds(s.length - 16, 16), :], qb)]
    for h in range(s.halves):
        cut = pl.ds(h * GROUP, GROUP)
        copies += [(k_hbm.at[:, cut], kb.at[:, cut]), (v_hbm.at[:, cut], vb.at[:, cut])]
    copies = [pltpu.make_async_copy(a, b, sems.at[i]) for i, (a, b) in enumerate(copies)]
    for i, copy in enumerate(copies):
        copy.start(priority=i % 2)
    copies[0].wait()
    stage_modes(s, db, poles, lambda x: jnp.exp(-x))
    copies[1].wait()
    stage_taps(s, fb, taps)
    blank = jnp.zeros((SUB, LANES), f32)
    copies[2].wait()
    stage_wide(s, qb, qs)

    def half(h):
        for i, (from_hbm, to) in enumerate(((k_hbm, kb), (v_hbm, vb))):
            cut = columns(h)
            pltpu.make_async_copy(from_hbm.at[:, cut], to.at[:, cut], sems.at[3 + 2 * h + i]).wait()
        p = mode_tiles(s, poles, h)
        taps_k, taps_v = (tap_tiles(s, taps, i, h) for i in (1, 2))

        held = products(s, kb, vb, ks, vs, prod, taps_k, taps_v, h)

        blocks = long_steps(s)

        def step(i, states):
            for block, offset in positions(blocks):
                product = prod[major(s, (blocks * i + block) * SUB + offset, h), :]
                states = [p[m] * states[m] + product for m in range(s.modes)]
            return states

        states = lax.fori_loop(0, s.length // (SUB * blocks), step, [blank] * s.modes)
        put_states(s, pay_s, states, h)
        k1, k2, v1, v2 = held
        first = [staged(s, 0, offset, h) for offset in range(2)]
        last = [staged(s, 1, offset, h) for offset in (6, 7)]
        extra = [
            ks[first[0], :], ks[first[1], :], k2, k1,
            vs[first[0], :], vs[first[1], :], v2, v1,
            qs[last[0], :], qs[last[1], :],
        ]
        for r, value in enumerate(extra):
            pay_s[forward_slice(s, 2 * s.modes + r, h), :] = value

    each_half(s, half)
    narrowed(pay_s, pay_ref)


def forward_middle(length, rates, taps, ends, extras):
    devices = len(ends)
    whole, step0, step1 = (jnp.exp(-float(length - i) * rates) for i in range(3))
    blank = jnp.zeros_like(extras[0][0])
    arriving = jnp.zeros_like(ends[0])
    result = []
    for i in range(devices):
        k0, k1, _, _, v0, v1 = extras[i][:6]
        if i:
            _, _, ka, kb, _, _, va, vb, qa, qb = extras[i - 1][:10]
        else:
            ka = kb = va = vb = qa = qb = blank
        if i + 1 < devices:
            kc, kd, _, _, vc, vd = extras[i + 1][:6]
        else:
            kc = kd = vc = vd = blank
        prod0 = mix(taps[1], k0, kb, ka) * mix(taps[2], v0, vb, va)
        prod1 = mix(taps[1], k1, k0, kb) * mix(taps[2], v1, v0, vb)
        result.append((arriving, [ka, kb, va, vb, qa, qb, kc, kd, vc, vd]))
        arriving = whole * arriving + (ends[i] + step0 * prod0 + step1 * prod1)
    return result


def backward_middle(length, rates, ends, extras):
    devices = len(ends)
    whole = jnp.exp(-float(length) * rates)
    blank = jnp.zeros_like(extras[0][0])
    arriving = jnp.zeros_like(ends[0])
    result = [None] * devices
    for i in reversed(range(devices)):
        result[i] = (arriving, extras[i + 1] if i + 1 < devices else [blank] * len(extras[0]))
        arriving = whole * arriving + ends[i]
    return result


def middle_kernel(s, forward, pay_ref, decay_ref, filter_ref, back_ref, *wide):
    me = lax.axis_index("seq")
    lead, extra = (2 * s.modes, FORWARD_EXTRA) if forward else (s.modes, BACKWARD_EXTRA)
    in_ref, out_ref = wide if forward else (pay_ref, back_ref)
    if forward:
        widened(pay_ref, in_ref)
    rows = s.chunk_rows(lead, extra)
    for h in range(s.halves):
        lanes = pl.ds(pl.multiple_of((me + h * SUB) * LANES, LANES), LANES)
        rates = decay_ref[:, lanes]
        ends, extras = [], []
        for i in range(s.devices):
            e = i * rows + s.chunk_row(0, h, lead, extra)
            end = in_ref[e : e + s.modes, :]
            ends.append(end + in_ref[e + s.modes : e + lead, :] if forward else end)
            x = i * rows + s.chunk_row(lead, h, lead, extra)
            extras.append([in_ref[x + r : x + r + 1, :] for r in range(extra)])
        if forward:
            taps = [[filter_ref[i, tap : tap + 1, lanes] for tap in range(3)] for i in range(3)]
            result = forward_middle(s.length, rates, taps, ends, extras)
        else:
            result = backward_middle(s.length, rates, ends, extras)
        for i, (state, more) in enumerate(result):
            e = i * rows + s.chunk_row(0, h, lead, extra)
            if forward:
                out_ref[e : e + s.modes, :], out_ref[e + s.modes : e + lead, :] = split(state)
            else:
                out_ref[e : e + s.modes, :] = state
            x = i * rows + s.chunk_row(lead, h, lead, extra)
            for r in range(extra):
                out_ref[x + r : x + r + 1, :] = more[r]
    if forward:
        narrowed(out_ref, back_ref)


def exchange(s, pay, decay_rate, short_filter, forward):
    lead, extra = (2 * s.modes, FORWARD_EXTRA) if forward else (s.modes, BACKWARD_EXTRA)
    if s.direct:
        chunks = (s.devices, s.chunk_rows(lead, extra), LANES)
        got = lax.all_to_all(pay.reshape(chunks), "seq", 0, 0, tiled=True)
        back = pl.pallas_call(
            functools.partial(middle_kernel, s, forward),
            out_shape=jax.ShapeDtypeStruct(pay.shape, pay.dtype),
            scratch_shapes=[pltpu.VMEM(pay.shape, f32)] * 2 if forward else [],
            compiler_params=pltpu.CompilerParams(vmem_limit_bytes=GRANT),
        )(got.reshape(pay.shape), decay_rate, short_filter)
        return lax.all_to_all(back.reshape(chunks), "seq", 0, 0, tiled=True).reshape(pay.shape)
    rows = lead + extra
    width = s.channels // s.devices
    start = lax.axis_index("seq") * width
    rates = lax.dynamic_slice_in_dim(decay_rate, start, width, 1)
    part = lax.dynamic_slice_in_dim(short_filter, start, width, 2)
    pay = pay.reshape(rows, s.devices, width).transpose(1, 0, 2)
    got = lax.all_to_all(pay, "seq", 0, 0, tiled=True).astype(f32)
    ends = [got[i, : s.modes] for i in range(s.devices)]
    extras = [[got[i, lead + r][None] for r in range(extra)] for i in range(s.devices)]
    if forward:
        ends = [end + got[i, s.modes : lead] for i, end in enumerate(ends)]
        taps = [[part[i, tap][None] for tap in range(3)] for i in range(3)]
        result = forward_middle(s.length, rates, taps, ends, extras)
        highs = [lax.reduce_precision(state, 8, 7) for state, _ in result]
        result = [
            (jnp.concatenate([high, state - high]), more) for high, (state, more) in zip(highs, result)
        ]
    else:
        result = backward_middle(s.length, rates, ends, extras)
    back = jnp.stack([jnp.concatenate([state] + list(more)) for state, more in result])
    back = lax.all_to_all(back.astype(pay.dtype), "seq", 0, 0, tiled=True)
    return back.transpose(1, 0, 2).reshape(rows * s.tiles, LANES)


def inside_kernel(
    s, k_hbm, v_hbm, filter_hbm, decay_hbm, residue_hbm, inside_ref, first_ref, taps, poles, weights,
    kb, vb, fb, db, rb, ks, vs, prod, sems,
):
    pairs = [(decay_hbm, db), (residue_hbm, rb), (filter_hbm, fb), (k_hbm, kb), (v_hbm, vb)]
    copies = [pltpu.make_async_copy(a, b, sems.at[i]) for i, (a, b) in enumerate(pairs)]
    for i, copy in enumerate(copies):
        copy.start(priority=i % 2)
    for copy in copies:
        copy.wait()
    stage_modes(s, db, poles, lambda x: jnp.exp(-x))
    stage_modes(s, rb, weights, lambda x: x)
    stage_taps(s, fb, taps)
    blank = jnp.zeros((SUB, LANES), f32)
    steps = s.length // 16

    def half(h):
        taps_k, taps_v = (tap_tiles(s, taps, i, h) for i in (1, 2))

        products(s, kb, vb, ks, vs, prod, taps_k, taps_v, h)
        for i, (ref, part) in enumerate(((ks, taps_k), (vs, taps_v))):
            x0, x1 = (ref[staged(s, 0, offset, h), :] for offset in range(2))
            first_ref[major(s, 2 * i, h), :] = part[0] * x0
            first_ref[major(s, 2 * i + 1, h), :] = part[0] * x1 + part[1] * x0
        recur(s, prod, inside_ref, mode_tiles(s, poles, h), mode_tiles(s, weights, h), [blank] * s.modes, h)

    each_half(s, half)


def forward_kernel(
    s, inside_ref, first_ref, q_ref, stream_ref, cot_ref, back_ref, taps, poles, weights, gain_ref,
    conv_ref, sums_ref, near_ref,
    qs, xs, gs, back_s, squares, inners,
):
    widened(back_ref, back_s)
    steps = s.length // 16

    def half(h):
        p = mode_tiles(s, poles, h)
        w = mode_tiles(s, weights, h)
        gain = gain_ref[pl.ds(aligned(h * SUB, SUB), SUB), :]
        taps_q, taps_k, taps_v = (tap_tiles(s, taps, i, h) for i in range(3))
        near = [back_s[forward_slice(s, 2 * s.modes + r, h), :] for r in range(FORWARD_EXTRA)]
        for r, value in enumerate(near):
            near_ref[major(s, r, h), :] = value
        ka, kb, va, vb, qa, qb = near[:6]
        k0, k1, v0, v1 = (first_ref[major(s, r, h), :] for r in range(4))
        products = [
            (k0 + taps_k[1] * kb + taps_k[2] * ka) * (v0 + taps_v[1] * vb + taps_v[2] * va),
            (k1 + taps_k[2] * kb) * (v1 + taps_v[2] * vb),
        ]
        conv = []
        states = [
            back_s[forward_slice(s, m, h), :] + back_s[forward_slice(s, s.modes + m, h), :]
            for m in range(s.modes)
        ]
        for offset in range(2):
            states = [p[m] * states[m] + products[offset] for m in range(s.modes)]
            conv.append(total([w[m] * states[m] for m in range(s.modes)]))
        states = [w[m] * states[m] / (p[m] * p[m]) for m in range(s.modes)]
        first, ahead = [], states
        for offset in range(2):
            ahead = [p[m] * ahead[m] for m in range(s.modes)]
            first.append(conv[offset] - total(ahead))

        def bring(i):
            stage(s, q_ref, qs, i, h)
            stage(s, stream_ref, xs, i, h)
            stage(s, cot_ref, gs, i, h)

        def step(i, carry):
            (q1, q2), states = carry
            for block, offset in sixteen(0):
                rows = staged(s, 2 * i + block, offset, h)
                t = (2 * i + block) * SUB + offset
                out = major(s, t, h)
                inside = inside_ref[out, :]
                if block == 0 and offset < 2:
                    inside = jnp.where(i == 0, first[offset], inside)
                states = [p[m] * states[m] for m in range(s.modes)]
                conv = inside + total(states)
                conv_ref[out, :] = conv
                q0 = qs[rows, :]
                mixed = xs[rows, :] + mix(taps_q, q0, q1, q2) * conv
                part = pl.ds(pl.multiple_of(t * SUB, SUB), SUB)
                square, inner = mixed * mixed, gain * gs[rows, :] * mixed
                squares[part, :] = square + jnp.where(h == 0, 0.0, squares[part, :])
                inners[part, :] = inner + jnp.where(h == 0, 0.0, inners[part, :])
                q1, q2 = q0, q1
            bring(jnp.minimum(i + 1, steps - 1))
            return (q1, q2), states

        bring(0)
        paired_loop(steps, step, ((qb, qa), states))

    each_half(s, half)
    for r, ref in enumerate((squares, inners)):
        parts = []
        for b in range(s.length // SUB):
            parts.append(
                total([ref[pl.ds(b * SUB * SUB + i, SUB, stride=SUB), :] for i in range(SUB)])
            )
        rows = jnp.concatenate(parts, axis=0)
        sums_ref[r : r + 1, :] = jnp.sum(rows.T, axis=0, keepdims=True)


def norm_kernel(
    s, width, sums_ref, conv_ref, q_ref, stream_ref, cot_ref, near_ref, filter_ref, decay_ref, gain_ref,
    normed_hbm, dstream_hbm, qgrad_hbm, dconv_ref, tail_ref, pay_ref,
    qs, xs, gs, ns, ds, normed_b, dstream_b, qgrad_b, taps, poles, inv_s, coef_s, sems,
):
    inverse = lax.rsqrt(sums_ref[0:1, :] / width + epsilon)
    coef = inverse * inverse * inverse * sums_ref[1:2, :] / width
    inv_s[...] = jnp.broadcast_to(inverse, (LANES, s.length)).T
    coef_s[...] = jnp.broadcast_to(coef, (LANES, s.length)).T
    stage_modes(s, decay_ref, poles, lambda x: jnp.exp(-x))
    stage_taps(s, filter_ref, taps)
    blank = jnp.zeros((SUB, LANES), f32)
    steps = s.length // 16

    def pieces(h):
        cut = columns(h)
        sources = [
            (normed_b.at[:, cut], normed_hbm.at[:, cut]),
            (dstream_b.at[:, cut], dstream_hbm.at[:, cut]),
            (qgrad_b.at[pl.ds(16, s.length - 16), cut], qgrad_hbm.at[pl.ds(0, s.length - 16), cut]),
        ]
        return [pltpu.make_async_copy(a, b, sems.at[3 * h + i]) for i, (a, b) in enumerate(sources)]

    def half(h):
        gain = gain_ref[pl.ds(aligned(h * SUB, SUB), SUB), :]
        taps_q = tap_tiles(s, taps, 0, h)

        def bring(i):
            rows = jnp.minimum(i, steps - 1)
            stage(s, q_ref, qs, rows, h, i - rows + 1)
            stage(s, stream_ref, xs, rows, h)
            stage(s, cot_ref, gs, rows, h)

        def step(i, held):
            q1, q2, dq1, dq2 = held
            for block, offset in sixteen(0):
                rows = staged(s, 2 * i + block, offset, h)
                t = (2 * i + block) * SUB + offset
                out = major(s, t, h)
                inv = jnp.broadcast_to(inv_s[pl.ds(t, 1), :], (SUB, LANES))
                cf = jnp.broadcast_to(coef_s[pl.ds(t, 1), :], (SUB, LANES))
                q0 = qs[staged(s, 2 * i + block + 2, offset, h), :]
                qmix = mix(taps_q, q0, q1, q2)
                conv = conv_ref[out, :]
                mixed = xs[rows, :] + qmix * conv
                dmixed = inv * (gain * gs[rows, :]) - mixed * cf
                ns[rows, :] = mixed * inv * gain
                ds[rows, :] = dmixed
                dq0 = dmixed * conv
                dconv_ref[out, :] = dmixed * qmix
                qs[staged_before(s, 2 * i + block + 2, offset, h), :] = mix(taps_q, dq2, dq1, dq0)
                q1, q2, dq1, dq2 = q0, q1, dq0, dq1
            unstage(s, ns, normed_b, i, h)
            unstage(s, ds, dstream_b, i, h)
            unstage(s, qs, qgrad_b, i, h)
            bring(i + 1)
            return q1, q2, dq1, dq2

        bring(0)
        held = (near_ref[major(s, 5, h), :], near_ref[major(s, 4, h), :], blank, blank)
        _, _, dq1, dq2 = paired_loop(steps, step, held)
        qs[staged(s, 2 * steps + 1, 6, h), :] = taps_q[0] * dq2 + taps_q[1] * dq1
        qs[staged(s, 2 * steps + 1, 7, h), :] = taps_q[0] * dq1
        for i, copy in enumerate(pieces(h)):
            copy.start(priority=i % 2)

    each_half(s, half)
    start = steps * 2 * s.tiles * SUB
    tail_ref[...] = qs[start : start + 2 * s.tiles * SUB, :]

    def ends(h):
        p = mode_tiles(s, poles, h)

        blocks = long_steps(s)
        many = s.length // (SUB * blocks)

        def step(i, states):
            for block, offset in positions(blocks, True):
                t = (blocks * (many - 1 - i) + block) * SUB + offset
                dconv = dconv_ref[major(s, t, h), :]
                states = [p[m] * states[m] + dconv for m in range(s.modes)]
            return states

        states = lax.fori_loop(0, many, step, [blank] * s.modes)
        for m in range(s.modes):
            pay_ref[backward_slice(s, m, h), :] = states[m]
        first = [ds[staged(s, 0, offset, h), :] * conv_ref[major(s, offset, h), :] for offset in range(2)]
        for r, value in enumerate([dconv_ref[major(s, 0, h), :], *first, blank]):
            pay_ref[backward_slice(s, s.modes + r, h), :] = value

    each_half(s, ends)

    def finish(h):
        for copy in pieces(h):
            copy.wait()

    each_half(s, finish)


def backward_kernel(
    s, k_ref, v_ref, dconv_ref, tail_ref, near_ref, back_ref, filter_ref, decay_ref, residue_ref, qgrad_in,
    qgrad_hbm, kgrad_hbm, vgrad_hbm,
    ks, vs, dprod, qs, kgrad_b, vgrad_b, qgrad_b, taps, poles, weights, sems,
):
    del qgrad_in
    stage_modes(s, decay_ref, poles, lambda x: jnp.exp(-x))
    stage_modes(s, residue_ref, weights, lambda x: x)
    stage_taps(s, filter_ref, taps)
    steps = s.length // 16

    def back(r, h):
        return back_ref[backward_slice(s, r, h), :]

    qs[...] = tail_ref[...]

    def tails(h):
        taps_q = tap_tiles(s, taps, 0, h)
        dq0, dq1 = back(s.modes + 1, h), back(s.modes + 2, h)
        rows = [staged(s, 1, offset, h) for offset in (6, 7)]
        qs[rows[0], :] = qs[rows[0], :] + taps_q[2] * dq0
        qs[rows[1], :] = qs[rows[1], :] + (taps_q[1] * dq0 + taps_q[2] * dq1)
        unstage(s, qs, qgrad_b, 0, h)

    each_half(s, tails)
    last = pltpu.make_async_copy(qgrad_b, qgrad_hbm.at[pl.ds(s.length - 16, 16), :], sems.at[2 * s.halves])
    last.start()

    def pieces(h):
        cut = columns(h)
        sources = [(kgrad_b, kgrad_hbm), (vgrad_b, vgrad_hbm)]
        return [
            pltpu.make_async_copy(a.at[:, cut], b.at[:, cut], sems.at[2 * h + i])
            for i, (a, b) in enumerate(sources)
        ]

    def half(h):
        p = mode_tiles(s, poles, h)
        w = mode_tiles(s, weights, h)
        arriving = [back(m, h) for m in range(s.modes)]
        recur(s, dconv_ref, dprod, p, w, arriving, h, reverse=True)
        taps_k, taps_v = (tap_tiles(s, taps, i, h) for i in (1, 2))

        def bring(i):
            stage(s, k_ref, ks, i, h, 1)
            stage(s, v_ref, vs, i, h, 1)

        def advance(inputs, grads, k2, v2, d):
            k0, k1, v0, v1 = inputs
            dk1, dk2, dv1, dv2 = grads
            dk0 = d * mix(taps_v, v0, v1, v2)
            dv0 = d * mix(taps_k, k0, k1, k2)
            out = mix(taps_k, dk0, dk1, dk2), mix(taps_v, dv0, dv1, dv2)
            return (k1, k2, v1, v2), (dk0, dk1, dv0, dv1), out

        bring(steps - 1)
        ka, kb, va, vb, _, _, kc, kd, vc, vd = (near_ref[major(s, r, h), :] for r in range(10))
        for ref, rows in ((ks, (ka, kb)), (vs, (va, vb))):
            for offset in range(2):
                ref[staged(s, 1, 6 + offset, h), :] = rows[offset]
        arriving = [back(m, h) for m in range(s.modes)]
        dconv0 = back(s.modes, h)
        d0 = total([w[m] * arriving[m] for m in range(s.modes)])
        d1 = total([w[m] * ((arriving[m] - dconv0) / p[m]) for m in range(s.modes)])
        ends = [staged(s, 2 * steps + 1, offset, h) for offset in (6, 7)]
        inputs = (kd, kc, vd, vc)
        grads = (jnp.zeros((SUB, LANES), f32),) * 4
        inputs, grads, _ = advance(inputs, grads, ks[ends[1], :], vs[ends[1], :], d1)
        inputs, grads, _ = advance(inputs, grads, ks[ends[0], :], vs[ends[0], :], d0)

        def step(i, carry):
            inputs, grads = carry
            i = steps - 1 - i

            @pl.when(i > 0)
            def _():
                bring(jnp.maximum(i - 1, 0))

            for block, offset in sixteen(0, True):
                d = dprod[major(s, (2 * i + block) * SUB + offset, h), :]
                rows = staged_before(s, 2 * i + block + 2, offset, h)
                inputs, grads, out = advance(inputs, grads, ks[rows, :], vs[rows, :], d)
                rows = staged(s, 2 * i + block + 2, offset, h)
                ks[rows, :], vs[rows, :] = out
            unstage(s, ks, kgrad_b, i + 1, h, i)
            unstage(s, vs, vgrad_b, i + 1, h, i)
            return inputs, grads

        paired_loop(steps, step, (inputs, grads))
        for i, copy in enumerate(pieces(h)):
            copy.start(priority=i % 2)

    each_half(s, half)
    last.wait()

    def finish(h):
        for copy in pieces(h):
            copy.wait()

    each_half(s, finish)


def body(
    query_in, key_in, value_in, stream, short_filter, decay_rate, residue, norm_gain, cotangent
):
    length, channels = query_in.shape
    modes = decay_rate.shape[0]
    s = Sizes(length, channels, modes, lax.axis_size("seq"))
    total_width = channels * lax.axis_size("tp")
    wide = jax.ShapeDtypeStruct((length * s.tiles, LANES), f32)
    narrow = jax.ShapeDtypeStruct((length, channels), bf16)
    rows = 16 * s.tiles
    wide_s = pltpu.VMEM(wide.shape, f32)
    longer_s = pltpu.VMEM(((length + 16) * s.tiles, LANES), f32)
    narrow_s = pltpu.VMEM(narrow.shape, bf16)
    last_s = pltpu.VMEM((16, channels), bf16)
    tail_s = pltpu.VMEM((rows, LANES), f32)
    taps_s = pltpu.VMEM((3 * s.tiles * SUB, LANES), f32)
    mode_s = pltpu.VMEM((modes * s.tiles, LANES), f32)
    sum_s = pltpu.VMEM((length * SUB, LANES), f32)
    square_s = pltpu.VMEM((length, LANES), f32)
    gain = norm_gain.reshape(s.tiles, LANES)
    there = pl.BlockSpec(memory_space=pltpu.HBM)
    here = pl.BlockSpec(memory_space=pltpu.VMEM)

    def call(kernel, ins, outs, out_shape, scratch_shapes, operands, aliases={}, cost=None):
        return pl.pallas_call(
            functools.partial(kernel, s),
            in_specs=[there if c == "h" else here for c in ins],
            out_specs=[there if c == "h" else here for c in outs],
            out_shape=out_shape,
            scratch_shapes=scratch_shapes,
            input_output_aliases=aliases,
            cost_estimate=cost,
            compiler_params=pltpu.CompilerParams(vmem_limit_bytes=GRANT),
        )(*operands)

    forward_shape = s.exchange_shape(2 * modes, FORWARD_EXTRA)
    near_shape = jax.ShapeDtypeStruct((FORWARD_EXTRA * s.tiles, LANES), f32)

    def far(*arrays):
        return [pltpu.with_memory_space_constraint(x, pltpu.HBM) for x in arrays]

    def cost(per_element, arrays):
        return pl.CostEstimate(
            flops=per_element * length * channels, bytes_accessed=arrays * 4 * length * channels, transcendentals=0
        )

    filter_s = pltpu.VMEM(short_filter.shape, f32)
    rates_s = pltpu.VMEM(decay_rate.shape, f32)
    (pay,) = call(
        begin_kernel, "hhhhh", "v",
        (jax.ShapeDtypeStruct(forward_shape, bf16),),
        [narrow_s, narrow_s, last_s, filter_s, rates_s]
        + [wide_s] * 3 + [tail_s, pltpu.VMEM(forward_shape, f32), taps_s, mode_s]
        + [pltpu.SemaphoreType.DMA((3 + 2 * s.halves,))],
        far(query_in, key_in, value_in, short_filter, decay_rate),
    )
    tiled = [jax.ShapeDtypeStruct(x.shape, f32) for x in (taps_s, mode_s, mode_s)]
    inside, first, *tiled = call(
        inside_kernel, "hhhhh", "vvvvv",
        (wide, jax.ShapeDtypeStruct((4 * s.tiles, LANES), f32), *tiled),
        [narrow_s, narrow_s, filter_s, rates_s, rates_s]
        + [wide_s] * 3 + [pltpu.SemaphoreType.DMA((5,))],
        far(key_in, value_in, short_filter, decay_rate, residue),
        cost=cost(75, 3),
    )
    back = exchange(s, pay, decay_rate, short_filter, True)
    conv, sums, near = call(
        forward_kernel, "v" * 10, "vvv",
        (wide, jax.ShapeDtypeStruct((2, length), f32), near_shape),
        [wide_s] * 3 + [pltpu.VMEM(forward_shape, f32), sum_s, sum_s],
        (inside, first, query_in, stream, cotangent, back, *tiled, gain),
        {0: 0},
    )
    sums = lax.psum(sums, "tp")
    normed, dstream, query_grad, dconv, tail, pay_back = call(
        lambda s, *refs: norm_kernel(s, total_width, *refs), "v" * 9, "hhhvvv",
        (narrow, narrow, narrow, wide, jax.ShapeDtypeStruct((rows, LANES), f32), jax.ShapeDtypeStruct(s.exchange_shape(modes, BACKWARD_EXTRA), f32)),
        [pltpu.VMEM(((length + 32) * s.tiles, LANES), f32)] + [longer_s] * 2 + [wide_s] * 2 + [narrow_s] * 2
        + [pltpu.VMEM((length + 16, channels), bf16)]
        + [taps_s, mode_s, square_s, square_s, pltpu.SemaphoreType.DMA((3 * s.halves,))],
        (sums, conv, query_in, stream, cotangent, near, short_filter, decay_rate, gain),
    )
    back_back = exchange(s, pay_back, decay_rate, short_filter, False)
    query_grad, key_grad, value_grad = call(
        backward_kernel, "v" * 9 + "h", "hhh",
        (narrow, narrow, narrow),
        [longer_s] * 2 + [wide_s, tail_s] + [narrow_s] * 2 + [last_s, taps_s, mode_s, mode_s]
        + [pltpu.SemaphoreType.DMA((1 + 2 * s.halves,))],
        (key_in, value_in, dconv, tail, near, back_back, short_filter, decay_rate, residue, query_grad),
        {9: 0},
    )
    return (normed, dstream, query_grad, key_grad, value_grad)


def solution(mesh):
    cut = P("seq", "tp")
    return jax.shard_map(
        body,
        mesh=mesh,
        in_specs=(cut, cut, cut, cut, P(None, None, "tp"), P(None, "tp"), P(None, "tp"), P("tp"), cut),
        out_specs=(cut,) * 5,
        check_vma=False,
    )
```
